32 devices in a mesh: frames: 8 (over z, y), tiles: 4 (over x, core).
Axes of the slice: x: 2, y: 2, z: 4, core: 2. Of those that a mesh axis runs over, the one named last changes fastest.
Arguments:
- frames: bfloat16 [32, 3, 128, 1024], P(('frames', 'tiles')), may hold values from -6 to 6
- weight_map: bfloat16 [32, 128, 1024], P(('frames', 'tiles')), may hold values from 0.049804688 to 1
- seam_mask: int32 [32, 128, 64], P(('frames', 'tiles')), may hold values 0 or 1
- strip_cell: int32 [32], P(('frames', 'tiles')), may hold values from 0 to 60
- partner: int32 [32], P(('frames', 'tiles')), may hold values from 0 to 31, as said below
- tile_group: int32 [32, 32, 1], P(('frames', 'tiles')), may hold values from 0 to 7; in each aligned block of 32 rows (0 to 31, 32 to 63, ..., all dimensions but the last counted through in order) at most 8 rows name the same one
- tile_position_in_group: int32 [32, 32], P(('frames', 'tiles')), may hold values from 0 to 15
Outputs:
- panorama: float32 [128, 3, 4096], P(('frames', 'tiles'))
The draws below stay inside these ranges and needn't reach their ends.
Inputs may be any that keep to these rules, and one draw needn't show every extreme that they name: partner[partner[f]] = f. Writing f = (g * 4 + t) + j with t < 4 and j < 1, partner[f] = ((g XOR m_(t,j)) * 4 + t) + j, with one nonzero m_(t,j) below 8 for each pair t, j; among these masks are 4 and 1. `tile_group`: within the rows of one device (32 rows), no value occurs more than 8 times, and some value occurs exactly 8 times.
All inputs are finite; a program needn't handle non-finite values. No bound on the sum of `seam_mask` on one device may be relied on, other than what follows from the above.
Results may differ from the reference program's by a relative error of at most 0.0028.
Values may be sent and summed in bfloat16 or wider, within the bound.
No kernel may reach another device: no remote copies, remote signals or barrier semaphores. Data moves between devices by JAX's collectives and lax.ppermute only.
A program may use at most 128 MiB of HBM per device.

```python
import math
import jax
import jax.numpy as jnp
import numpy as np
from jax import lax

COLOUR_CHANNELS = 3
LEVELS = 5
BS = 64
SW = 64
FR_DEV = 1
FH = 128
FW = 1024
FRAMES = 32
QB = 32
TG = 16
PANORAMA_TILES = 128
CAP = 8
BLOCK_VALUES = 5456
N_FRAMES = 8
N_TILES = 4


def draw_partner(key, part):
    mask_count = N_TILES * FR_DEV
    mask_key = jax.random.fold_in(key, 11)
    order_key = jax.random.fold_in(key, 23)
    masks = jax.random.randint(mask_key, (mask_count,), 1, N_FRAMES).astype(jnp.int32)
    order = jax.random.permutation(order_key, mask_count)
    masks = masks.at[order[0]].set(N_FRAMES // 2)
    masks = masks.at[order[1]].set(1)
    index_all = jnp.arange(FRAMES, dtype=jnp.int32)
    slot_of = index_all % FR_DEV
    tile_of = index_all // FR_DEV % N_TILES
    group_of = index_all // (FR_DEV * N_TILES)
    partner_group = jnp.bitwise_xor(group_of, masks[tile_of * FR_DEV + slot_of])
    return ((partner_group * N_TILES + tile_of) * FR_DEV + slot_of).astype(jnp.int32)


def set_ends(drawn, stream_key, smallest, top_value):
    spot = [jax.random.randint(jax.random.fold_in(stream_key, axis), (), 0, length) for axis, length in enumerate(drawn.shape)]
    widest = drawn.shape.index(max(drawn.shape))
    neighbour = spot[:widest] + [(spot[widest] + 1) % drawn.shape[widest]] + spot[widest + 1:]
    return drawn.at[tuple(spot)].set(smallest).at[tuple(neighbour)].set(top_value)


def steps_of(key, shape, cuts, low, high):
    level = 1.0
    for axis_at, blocks in cuts:
        heights = jax.random.uniform(jax.random.fold_in(jax.random.fold_in(key, 6), axis_at), (blocks,), jnp.float32, low / len(cuts), high / len(cuts))
        level = level * jnp.repeat(jnp.exp(heights), shape[axis_at] // blocks).reshape((-1,) + (1,) * (len(shape) - 1 - axis_at))
    return level


def assign_block(own_key, own, number, rows, number_of, top, reach, lean):
    sequence = jax.random.permutation(own_key, number_of)
    crowded, usual = portions_of(number_of, rows * top, reach, lean, True), portions_of(number_of, rows * top, reach, lean, False)
    places = jnp.arange(number_of)

    def named(sizes, offset_by):
        used = int((sizes > 0).sum())
        fixed = max(1, used // 4)
        shifted = fixed + (places - fixed + offset_by * (used - fixed)) % max(1, number_of - fixed)
        return jnp.zeros((number_of,), jnp.int32).at[sequence[jnp.where(places < fixed, places, shifted)]].set(jnp.asarray(sizes, jnp.int32))

    sizes = jnp.where(number % 4 == 0, named(crowded, number // 4), named(usual, number - number // 4 - 1))
    mixed = jax.random.permutation(jax.random.fold_in(own, 3), number_of)
    donor, sink = mixed[0:number_of // 2 * 2:2], mixed[1:number_of // 2 * 2:2]
    room = jnp.minimum(sizes[donor] - 1, reach - sizes[sink]) // 2
    room = jnp.where((donor == sequence[0]) | (sink == sequence[0]) | (sizes[sink] == 0), 0, jnp.maximum(room, 0))
    shifted = jax.random.randint(jax.random.fold_in(own, 4), (number_of // 2,), 0, 1 << 20) % (room + 1)
    sizes = sizes.at[donor].add(-shifted).at[sink].add(shifted)
    labels = jnp.searchsorted(jnp.cumsum(sizes), jnp.arange(rows * top), side="right").astype(jnp.int32)
    listing = labels.reshape(top, rows).T
    listing = listing[jax.random.permutation(jax.random.fold_in(own, 1), rows)]
    offset_by = jax.random.randint(jax.random.fold_in(own, 2), (rows, 1), 0, top)
    return jnp.take_along_axis(listing, (jnp.arange(top)[None, :] + offset_by) % top, axis=1)


def portions_of(amount, total, most, skew, full):
    loads = [(1 << 20) // math.isqrt(grade ** skew) + 1 for grade in range(1, amount + 1)]
    largest = most if full else min(most, max(-(-total // amount), total * loads[0] // sum(loads)))
    least = 1 if total - largest >= amount - 1 else 0
    given, spare = [largest] + [least] * (amount - 1), total - largest - least * (amount - 1)
    while spare > 0:
        candidates = [i for i in range(1, amount) if given[i] < largest] or [i for i in range(1, amount) if given[i] < most]
        mass, remaining = sum([loads[i] for i in candidates]), spare
        for i in candidates:
            extra = min(most - given[i], max(1, remaining * loads[i] // mass), spare)
            given[i] = given[i] + extra
            spare = spare - extra
    return np.array(given)


def scatter_about(own_key, dims, spread, bound, cuts=(), held_as=jnp.bfloat16):
    array = spread * jax.random.normal(own_key, dims, jnp.float32)
    if cuts:
        array = array * steps_of(own_key, dims, cuts, -0.22, 0.18)
    return jnp.clip(array, -bound, bound).astype(held_as)


def setup_inputs(seed: int = 0) -> dict:
    arg_keys = jax.random.split(jax.random.key(seed), 8)
    frames = scatter_about(arg_keys[0], (FRAMES, COLOUR_CHANNELS, FH, FW), 1.0, 6.0, ((0, 32),))
    weight_map = jnp.clip(jnp.exp(math.log(1.0) - 2.9996462 * jax.random.uniform(arg_keys[1], (FRAMES, FH, FW), jnp.float32) ** steps_of(arg_keys[1], (FRAMES, FH, FW), ((0, 32),), -0.2, 0.2)), 0.049804688, 1.0).astype(jnp.bfloat16)
    seam_mask = set_ends((jax.random.randint(arg_keys[2], (FRAMES, FH, SW), 0, 2) < 1).astype(jnp.int32), jax.random.fold_in(arg_keys[2], 1), 0, 1)
    strip_cell = set_ends(jax.random.randint(arg_keys[3], (FRAMES,), 0, (FW - SW) // 16 + 1), jax.random.fold_in(arg_keys[3], 1), 0, ((FW - SW) // 16 + 1) - 1).astype(jnp.int32)
    partner = draw_partner(jax.random.fold_in(arg_keys[7], 71), 0)
    tile_group_keys = jax.random.split(jax.random.fold_in(arg_keys[5], 1), FRAMES * QB // (FR_DEV * QB))
    tile_group_turns = jax.random.permutation(jax.random.fold_in(arg_keys[5], 3), FRAMES * QB // (FR_DEV * QB))
    tile_group = jax.vmap(lambda own, number: assign_block(jax.random.fold_in(arg_keys[5], 2), own, number, FR_DEV * QB, N_FRAMES, 1, CAP, 2))(tile_group_keys, tile_group_turns).reshape((FRAMES, QB, 1))
    tile_position_in_group = set_ends(jax.random.randint(arg_keys[6], (FRAMES, QB), 0, TG), jax.random.fold_in(arg_keys[6], 1), 0, TG - 1).astype(jnp.int32)
    return dict(frames=frames, weight_map=weight_map, seam_mask=seam_mask, strip_cell=strip_cell, partner=partner, tile_group=tile_group, tile_position_in_group=tile_position_in_group)


TAPS = (1.0, 4.0, 6.0, 4.0, 1.0)


def shrink_axis(values, along):
    length = values.shape[along]
    padding = [(0, 0)] * values.ndim
    padding[along] = (2, 2)
    padded = jnp.pad(values, padding, mode="edge")
    total = TAPS[0] * lax.slice_in_dim(padded, 0, length - 1, 2, along)
    for offset in range(1, 5):
        total = total + TAPS[offset] * lax.slice_in_dim(padded, offset, offset + length - 1, 2, along)
    return total / 16.0


def grow_axis(values, along):
    length = values.shape[along]
    padding = [(0, 0)] * values.ndim
    padding[along] = (1, 1)
    padded = jnp.pad(values, padding, mode="edge")
    before = lax.slice_in_dim(padded, 0, length, 1, along)
    middle = lax.slice_in_dim(padded, 1, length + 1, 1, along)
    after_rows = lax.slice_in_dim(padded, 2, length + 2, 1, along)
    even_rows = (before + 6.0 * middle + after_rows) / 8.0
    odd_rows = (middle + after_rows) / 2.0
    stacked = jnp.stack((even_rows, odd_rows), axis=along + 1)
    new_shape = list(values.shape)
    new_shape[along] = 2 * length
    return stacked.reshape(new_shape)


def shrink(values):
    return shrink_axis(shrink_axis(values, values.ndim - 2), values.ndim - 1)


def grow(values):
    return grow_axis(grow_axis(values, values.ndim - 2), values.ndim - 1)


def gaussian_levels(image):
    levels = [image]
    for level_k in range(LEVELS - 1):
        levels.append(shrink(levels[-1]))
    return levels


def band_levels(image):
    gaussian = gaussian_levels(image)
    return [gaussian[level_k] - grow(gaussian[level_k + 1]) for level_k in range(LEVELS - 1)] + [gaussian[-1]]


def frame_strips(bands, cell_index):
    pieces = []
    for level_k in range(LEVELS):
        column_start = (cell_index * (16 >> level_k)).astype(jnp.int32)
        strip_piece = lax.dynamic_slice_in_dim(bands[level_k], column_start, SW >> level_k, 2)
        pieces.append(strip_piece.reshape(-1))
    return jnp.concatenate(pieces).astype(jnp.bfloat16)


def blend_frame(bands, level_weights, mask_levels, cell_index, partner_vec):
    offset_now = 0
    outputs = []
    blocks_high = FH // BS
    blocks_wide = FW // BS
    for level_k in range(LEVELS):
        band_now = bands[level_k]
        column_start = (cell_index * (16 >> level_k)).astype(jnp.int32)
        strip_width = SW >> level_k
        rows_here = FH >> level_k
        count_of_values = COLOUR_CHANNELS * rows_here * strip_width
        remote = partner_vec[offset_now:offset_now + count_of_values].reshape(COLOUR_CHANNELS, rows_here, strip_width).astype(jnp.float32)
        offset_now += count_of_values
        own_strip = lax.dynamic_slice_in_dim(band_now, column_start, strip_width, 2)
        mask_share = mask_levels[level_k][None]
        mixed_band = lax.dynamic_update_slice_in_dim(band_now, mask_share * own_strip + (1.0 - mask_share) * remote, column_start, 2)
        weights = level_weights[level_k][None]
        stacked = jnp.concatenate((weights * mixed_band, weights), axis=0).astype(jnp.bfloat16)
        block_side = BS >> level_k
        tiled_blocks = stacked.reshape(COLOUR_CHANNELS + 1, blocks_high, block_side, blocks_wide, block_side).transpose(1, 3, 0, 2, 4)
        outputs.append(tiled_blocks.reshape(blocks_high * blocks_wide, COLOUR_CHANNELS + 1, block_side * block_side))
    return jnp.concatenate(outputs, axis=2)


def collapse(summed_totals):
    normal = summed_totals[:, :COLOUR_CHANNELS] / jnp.maximum(summed_totals[:, COLOUR_CHANNELS:], 1.0)
    offset_now = 0
    levels = []
    for level_k in range(LEVELS):
        block_side = BS >> level_k
        levels.append(normal[:, :, offset_now:offset_now + block_side * block_side].reshape(normal.shape[0], COLOUR_CHANNELS, block_side, block_side))
        offset_now += block_side * block_side
    merged = levels[-1]
    for level_k in range(LEVELS - 2, -1, -1):
        merged = levels[level_k] + grow(merged)
    return merged.reshape(merged.shape[0], COLOUR_CHANNELS, BS * BS)


def reference(frames, weight_map, seam_mask, strip_cell, partner, tile_group, tile_position_in_group):
    def strips_of(inputs):
        image, cell_index = inputs
        return frame_strips(band_levels(image.astype(jnp.float32)), cell_index)

    all_strips = lax.map(strips_of, (frames, strip_cell))
    partner_strips = all_strips[partner]
    tile_ids = (tile_group[:, :, 0] * TG + tile_position_in_group).astype(jnp.int32)

    def accumulate(summed_totals, inputs):
        image, weight_image, mask_image, cell_index, partner_vec, row_ids = inputs
        bands = band_levels(image.astype(jnp.float32))
        level_weights = gaussian_levels(weight_image.astype(jnp.float32))
        mask_levels = gaussian_levels(mask_image.astype(jnp.float32))
        blocks = blend_frame(bands, level_weights, mask_levels, cell_index, partner_vec)
        return summed_totals.at[row_ids].add(blocks.astype(jnp.float32)), None

    summed_totals = jnp.zeros((PANORAMA_TILES, COLOUR_CHANNELS + 1, BLOCK_VALUES), jnp.float32)
    summed_totals, unused = lax.scan(accumulate, summed_totals, (frames, weight_map, seam_mask, strip_cell, partner_strips, tile_ids))
    return collapse(summed_totals)
```

```python
import functools

import jax
import jax.numpy as jnp
import numpy as np
from jax import lax
from jax.experimental import pallas as pl
from jax.experimental.pallas import tpu as pltpu
from jax.sharding import PartitionSpec as P

COLOURS = 3
FH = 128
FW = 1024
QB = 32
WIN = 256
TILE_DEV = 4
F32 = jnp.float32
BF16 = jnp.bfloat16


def shrink_matrix(n):
    m = np.zeros((n // 2, n), np.float32)
    for i in range(n // 2):
        for d, tap in zip(range(-2, 3), (1, 4, 6, 4, 1)):
            m[i, min(max(2 * i + d, 0), n - 1)] += tap / 16.0
    return m


def grow_matrix(n):
    m = np.zeros((2 * n, n), np.float32)
    for i in range(n):
        lo, hi = max(i - 1, 0), min(i + 1, n - 1)
        m[2 * i, lo] += 1 / 8
        m[2 * i, i] += 6 / 8
        m[2 * i, hi] += 1 / 8
        m[2 * i + 1, i] += 1 / 2
        m[2 * i + 1, hi] += 1 / 2
    return m


def padded(m, rows, cols):
    return np.pad(m, ((0, rows - m.shape[0]), (0, cols - m.shape[1])))


def row_order():
    m = np.zeros((FH, FH), np.float32)
    for r in range(2):
        for par in range(2):
            for i in range(32):
                m[r * 64 + par * 32 + i, r * 64 + 2 * i + par] = 1
    return m


def vertical():
    v = {1: shrink_matrix(128), 2: shrink_matrix(64), 3: shrink_matrix(32)}
    spread = np.zeros((16, 8), np.float32)
    for r in range(2):
        for i in range(4):
            spread[r * 8 + i, r * 4 + i] = 1
    v[4] = spread @ shrink_matrix(16)
    g = {0: row_order() @ grow_matrix(64), 1: grow_matrix(32), 2: grow_matrix(16)}
    g[3] = grow_matrix(8) @ spread.T
    return v, g


def horizontal(width, pad_last):
    s = {k: shrink_matrix(width >> (k - 1)).T for k in range(1, 5)}
    g = {k: grow_matrix(width >> (k + 1)).T for k in range(4)}
    if pad_last:
        s[4] = padded(s[4], s[4].shape[0], pad_last)
        g[3] = padded(g[3], pad_last, g[3].shape[1])
    return s, g


def const(m):
    return jnp.asarray(m, BF16)


def mm(a, b):
    return jnp.dot(a, b, preferred_element_type=F32)


def split(v):
    hi = v.astype(BF16)
    return hi, (v - hi.astype(F32)).astype(BF16)


def rdot(v, m):
    hi, lo = split(v)
    return mm(hi, m) + mm(lo, m)


def ldot(m, v):
    hi, lo = split(v)
    return mm(m, hi) + mm(m, lo)


def pyramid(planes, v, s):
    n = len(planes)
    t = jnp.concatenate([mm(v[1], p) for p in planes], axis=0)
    levels = {1: rdot(t, s[1])}
    for k in range(2, 5):
        prev = levels[k - 1]
        rows = prev.shape[0] // n
        t = jnp.concatenate([ldot(v[k], prev[i * rows : (i + 1) * rows]) for i in range(n)], axis=0)
        levels[k] = rdot(t, s[k])
    return levels


def grown(level, n, gv, gh):
    h = rdot(level, gh)
    rows = level.shape[0] // n
    return [ldot(gv, h[i * rows : (i + 1) * rows]) for i in range(n)]


def place(rows, cols, base, width, offset):
    i = lax.broadcasted_iota(jnp.int32, (rows, cols), 0)
    c = lax.broadcasted_iota(jnp.int32, (rows, cols), 1)
    hit = (i >= base) & (i < base + width) & (c - i == offset - base)
    return jnp.where(hit, 1.0, 0.0).astype(BF16)


def strips_kernel(cell, xa, xb, *refs):
    mats, (out, acc) = refs[:-2], refs[-2:]
    v = {k: mats[k - 1][...] for k in range(1, 5)}
    gv = {k: mats[4 + k][...] for k in range(4)}
    s = {k: mats[7 + k][...] for k in range(1, 5)}
    gh = {k: mats[12 + k][...] for k in range(4)}
    order = mats[16][...]
    first = window_tile(cell[0]) * 128
    planes = [jnp.concatenate([xa[0, c], xb[0, c]], axis=1) for c in range(COLOURS)]
    levels = pyramid(planes, v, s)
    back = grown(levels[1], COLOURS, gv[0], gh[0])
    b0 = jnp.concatenate([mm(order, planes[c]) - back[c] for c in range(COLOURS)], axis=0)
    bands = [b0.astype(BF16)]
    for k in range(1, 4):
        back = grown(levels[k + 1], COLOURS, gv[k], gh[k])
        bands.append((levels[k] - jnp.concatenate(back, axis=0)).astype(BF16))
    bands.append(levels[4].astype(BF16))
    start = cell[0] * 16 - first

    def pick(band, base, k):
        i = lax.broadcasted_iota(jnp.int32, (band.shape[1], 128), 0)
        c = lax.broadcasted_iota(jnp.int32, (band.shape[1], 128), 1)
        hit = (c >= base) & (c < base + (64 >> k)) & (i - c == (start >> k) - base)
        return mm(band, jnp.where(hit, 1.0, 0.0).astype(BF16))

    out[0:192, :] = (pick(bands[0][0:192], 0, 0) + pick(bands[0][192:384], 64, 0)).astype(BF16)
    acc[...] = pick(bands[1][0:96], 0, 1) + pick(bands[1][96:192], 32, 1) + pick(bands[2], 64, 2)
    acc[0:48, :] = acc[0:48, :] + pick(bands[3], 80, 3) + pick(bands[4], 88, 4)
    out[192:288, :] = acc[...].astype(BF16)


def window_tile(cell):
    return jnp.clip((cell - 3) >> 3, 0, (FW - WIN) // 128)


def full_spec(a):
    return pl.BlockSpec(a.shape, lambda *_: (0,) * a.ndim)


def strips_of(frames, cell):
    v, g = vertical()
    s, gh = horizontal(WIN, 0)
    mats = [const(v[k]) for k in range(1, 5)] + [const(g[k]) for k in range(4)]
    mats += [const(s[k]) for k in range(1, 5)] + [const(gh[k]) for k in range(4)]
    mats.append(const(row_order()))
    grid_spec = pltpu.PrefetchScalarGridSpec(
        num_scalar_prefetch=1,
        grid=(1,),
        in_specs=[
            pl.BlockSpec((1, COLOURS, FH, 128), lambda i, c: (0, 0, 0, window_tile(c[0]))),
            pl.BlockSpec((1, COLOURS, FH, 128), lambda i, c: (0, 0, 0, window_tile(c[0]) + 1)),
        ]
        + [full_spec(m) for m in mats],
        out_specs=pl.BlockSpec((288, 128), lambda i, c: (0, 0)),
        scratch_shapes=[pltpu.VMEM((96, 128), F32)],
    )
    return pl.pallas_call(
        strips_kernel,
        grid_spec=grid_spec,
        out_shape=jax.ShapeDtypeStruct((288, 128), BF16),
        compiler_params=pltpu.CompilerParams(vmem_limit_bytes=48 << 20),
        cost_estimate=pl.CostEstimate(flops=2 * 10**9, bytes_accessed=10**6, transcendentals=0),
        name="strips",
    )(cell, frames, frames, *mats)


def lane_index():
    return lax.broadcasted_iota(jnp.int32, (1, 128), 1)


def fold_level0(p, store):
    left = lane_index() < 64
    for r in range(2):
        for j in range(8):
            even = p[r * 64 : r * 64 + 32, j * 128 : j * 128 + 128]
            odd = p[r * 64 + 32 : r * 64 + 64, j * 128 : j * 128 + 128]
            store(r * 16 + 2 * j, jnp.where(left, even, pltpu.roll(odd, 64, 1)))
            store(r * 16 + 2 * j + 1, jnp.where(left, pltpu.roll(even, 64, 1), odd))


def gather_channels(parts, width, cc, base):
    groups = 128 // width
    group = lane_index() // width
    out = jnp.zeros_like(parts[0])
    for ch in range(4):
        out = jnp.where(group == (cc + ch) % groups, parts[ch], out)
    return pltpu.roll(out, (base - cc * width) % 128, 1)


def bands_kernel(x, w, m, *refs):
    mats, outs = refs[:21], refs[21:]
    v = {k: mats[k - 1][...] for k in range(1, 5)}
    gv = {k: mats[4 + k][...] for k in range(4)}
    s = {k: mats[7 + k][...] for k in range(1, 5)}
    gh = {k: mats[12 + k][...] for k in range(4)}
    order = mats[16][...]
    sm = {k: mats[16 + k][...] for k in range(1, 5)}
    wblocks, b0, b1, b2, b3, b4, wp, w1, w2, w3, w4, n0, n1, n2, n3, n4 = outs
    planes = [x[0, c] for c in range(COLOURS)] + [w[0]]
    weights = mm(order, planes[3])
    wp[...] = weights.astype(BF16)

    def store(q, piece):
        wblocks[q] = piece.astype(BF16)

    fold_level0(weights, store)
    levels = pyramid(planes, v, s)
    bands, wl = (b1, b2, b3), (w1, w2, w3, w4)
    for k in range(1, 5):
        rows = levels[k].shape[0] // 4
        wl[k - 1][...] = levels[k][3 * rows :]
    back = grown(levels[1][: 3 * 64], COLOURS, gv[0], gh[0])
    for c in range(COLOURS):
        b0[c] = mm(order, planes[c]) - back[c]
    for k in range(1, 4):
        rows = levels[k].shape[0] // 4
        below = levels[k + 1].shape[0] // 4
        back = grown(levels[k + 1][: 3 * below], COLOURS, gv[k], gh[k])
        for c in range(COLOURS):
            bands[k - 1][c] = levels[k][c * rows : (c + 1) * rows] - back[c]
    for c in range(COLOURS):
        b4[c] = levels[4][c * 16 : (c + 1) * 16]
    other = (1.0 - m[0].astype(F32)).astype(BF16)
    n0[...] = mm(order, other)
    masks = pyramid([other], v, sm)
    for k, ref in enumerate((n1, n2, n3, n4)):
        ref[...] = masks[k + 1]


def bands_of(frames, weight_map, seam_mask):
    v, g = vertical()
    s, gh = horizontal(FW, 128)
    sm, _ = horizontal(64, 0)
    mats = [const(v[k]) for k in range(1, 5)] + [const(g[k]) for k in range(4)]
    mats += [const(s[k]) for k in range(1, 5)] + [const(gh[k]) for k in range(4)]
    mats.append(const(row_order()))
    mats += [const(sm[k]) for k in range(1, 5)]
    out_shape = [jax.ShapeDtypeStruct((QB, 32, 128), BF16)]
    shapes = [(128, 1024), (64, 512), (32, 256), (16, 128), (16, 128)]
    out_shape += [jax.ShapeDtypeStruct((COLOURS,) + sh, F32) for sh in shapes]
    out_shape += [jax.ShapeDtypeStruct(shapes[0], BF16)]
    out_shape += [jax.ShapeDtypeStruct(sh, F32) for sh in shapes[1:]]
    out_shape += [jax.ShapeDtypeStruct(sh, F32) for sh in ((128, 64), (64, 32), (32, 16), (16, 8), (16, 4))]
    return pl.pallas_call(
        bands_kernel,
        out_shape=out_shape,
        compiler_params=pltpu.CompilerParams(vmem_limit_bytes=48 << 20),
        cost_estimate=pl.CostEstimate(flops=8 * 10**9, bytes_accessed=6 * 10**6, transcendentals=0),
        name="bands",
    )(frames, weight_map, seam_mask, *mats)


def blend_kernel(cell, strips, b0, b1, b2, b3, b4, wp, w1, w2, w3, w4, n0, n1, n2, n3, n4, first, second):
    start = cell[0] * 16
    low = strips[192:288]

    def mixed(band, remote, share):
        return band + share * (remote - band)

    widths = (1024, 512, 256, 128, 128)
    share0 = mm(n0[...].astype(BF16), place(64, 1024, 0, 64, start))
    share = [share0]
    for k, ref in enumerate((n1, n2, n3, n4)):
        share.append(rdot(ref[...], place(64 >> (k + 1), widths[k + 1], 0, 64 >> (k + 1), start >> (k + 1))))
    top = strips[0:192]
    remote0 = [mm(top, place(128, 1024, 0, 64, start)), mm(top, place(128, 1024, 64, 64, start))]
    remote0 = jnp.concatenate(remote0, axis=0)
    weights = wp[...].astype(F32)
    for c in range(COLOURS):
        p = weights * mixed(b0[c], remote0[c * 128 : (c + 1) * 128], share[0])
        out, row = (first, 0) if c == 0 else (second, 32 * (c - 1))

        def store(q, piece, out=out, row=row):
            out[q, row : row + 32, :] = piece.astype(BF16)

        fold_level0(p, store)
    remote1 = [mm(low, place(128, 512, 0, 32, start >> 1)), mm(low, place(128, 512, 32, 32, start >> 1))]
    remote1 = jnp.concatenate(remote1, axis=0)
    parts = [w1[...] * mixed(b1[c], remote1[c * 64 : (c + 1) * 64], share[1]) for c in range(COLOURS)] + [w1[...]]
    for r in range(2):
        for j in range(4):
            turned = [parts[ch][r * 32 : r * 32 + 32, j * 128 : j * 128 + 128] for ch in range(4)]
            turned = [turned[0]] + [pltpu.roll(turned[ch], 32 * ch, 1) for ch in range(1, 4)]
            for cc in range(4):
                first[r * 16 + 4 * j + cc, 32:64, :] = gather_channels(turned, 32, cc, 0).astype(BF16)
    remote2 = mm(low, place(128, 256, 64, 16, start >> 2))
    remote3 = mm(low[0:48], place(128, 128, 80, 8, start >> 3))
    remote4 = mm(low[0:48], place(128, 128, 88, 4, start >> 4))
    parts2 = [w2[...] * mixed(b2[c], remote2[c * 32 : (c + 1) * 32], share[2]) for c in range(COLOURS)] + [w2[...]]
    parts3 = [w3[...] * mixed(b3[c], remote3[c * 16 : (c + 1) * 16], share[3]) for c in range(COLOURS)] + [w3[...]]
    parts4 = [w4[...] * mixed(b4[c], remote4[c * 16 : (c + 1) * 16], share[4]) for c in range(COLOURS)] + [w4[...]]
    lane = lane_index()
    for r in range(2):
        turned3 = [pltpu.roll(parts3[ch][r * 8 : r * 8 + 8], 8 * ch, 1) for ch in range(4)]
        turned4 = [pltpu.roll(parts4[ch][r * 8 : r * 8 + 8], 4 * ch, 1) for ch in range(4)]
        for j in range(2):
            turned2 = [parts2[ch][r * 16 : r * 16 + 16, j * 128 : j * 128 + 128] for ch in range(4)]
            turned2 = [pltpu.roll(turned2[ch], 16 * ch, 1) for ch in range(4)]
            for cc in range(8):
                c = j * 8 + cc
                two = gather_channels(turned2, 16, cc, 0)
                three = gather_channels(turned3, 8, c, 64)
                four = gather_channels(turned4, 4, c, 96)
                head = jnp.where(lane < 64, two[0:8], jnp.where(lane < 96, three, four))
                tail = jnp.where(lane < 64, two[8:16], 0.0)
                first[r * 16 + c, 64:80, :] = jnp.concatenate([head, tail], axis=0).astype(BF16)


def blend(cell, strips, parts):
    vmem = pl.BlockSpec(memory_space=pltpu.VMEM)
    return pl.pallas_call(
        blend_kernel,
        in_specs=[pl.BlockSpec(memory_space=pltpu.SMEM)] + [vmem] * 16,
        out_shape=[jax.ShapeDtypeStruct((QB, 80, 128), BF16), jax.ShapeDtypeStruct((QB, 64, 128), BF16)],
        compiler_params=pltpu.CompilerParams(vmem_limit_bytes=48 << 20),
        cost_estimate=pl.CostEstimate(flops=4 * 10**9, bytes_accessed=4 * 10**6, transcendentals=0),
        name="blend",
    )(cell, strips, *parts)


def gather_kernel(spot, a, b, c, d, out, acc):
    acc[...] = jnp.zeros_like(acc)
    for source, ref in enumerate((a, b, c, d)):

        def body(q, carry, source=source, ref=ref):
            at = spot[source, q]

            @pl.when(at >= 0)
            def _():
                acc[at] = acc[at] + ref[q].astype(F32)

            return carry

        lax.fori_loop(0, QB, body, 0)
    out[...] = acc[...].astype(BF16)


def gather_rows(spot, rows, tiles):
    height = rows[0].shape[1]
    vmem = pl.BlockSpec(memory_space=pltpu.VMEM)
    return pl.pallas_call(
        gather_kernel,
        in_specs=[pl.BlockSpec(memory_space=pltpu.SMEM)] + [vmem] * 4,
        out_shape=jax.ShapeDtypeStruct((tiles, height, 128), BF16),
        scratch_shapes=[pltpu.VMEM((tiles, height, 128), F32)],
        compiler_params=pltpu.CompilerParams(vmem_limit_bytes=48 << 20),
        cost_estimate=pl.CostEstimate(flops=10**9, bytes_accessed=4 * 10**6, transcendentals=0),
        name="gather_rows",
    )(spot, *rows)


def collapse_matrices():
    def across(src, dst, width, copies=1):
        g = grow_matrix(width).T
        m = np.zeros((128, 128), np.float32)
        for ch in range(COLOURS):
            m[src + ch * width : src + (ch + 1) * width, dst + ch * 2 * width : dst + (ch + 1) * 2 * width] = g
        return m

    last = np.zeros((128, 384), np.float32)
    g = grow_matrix(32).T
    for ch in range(COLOURS):
        for half in range(2):
            last[ch * 32 : ch * 32 + 32, ch * 128 + half * 64 : ch * 128 + half * 64 + 64] = g

    def down(n, rows_in, rows_out, pick=None):
        g = grow_matrix(n)
        g = g if pick is None else g[pick::2]
        m = np.zeros((TILE_DEV * rows_out, TILE_DEV * rows_in), np.float32)
        for t in range(TILE_DEV):
            m[t * rows_out : t * rows_out + g.shape[0], t * rows_in : t * rows_in + n] = g
        return m

    return [
        across(96, 64, 4),
        across(64, 0, 8),
        across(0, 0, 16),
        last,
        down(4, 16, 16),
        down(8, 16, 16),
        down(16, 16, 32),
        down(32, 32, 32, 0),
        down(32, 32, 32, 1),
    ]


def collapse_kernel(a, b, c, m43, m32, m21, m10, d43, d32, d21, even, odd, out, level0):
    def total(ref, lo, hi):
        acc = ref[0, :, lo:hi, :].astype(F32)
        for source in range(1, ref.shape[0]):
            acc = acc + ref[source, :, lo:hi, :].astype(F32)
        return acc.reshape(TILE_DEV * (hi - lo), 128)

    lane = lane_index()
    small = total(b, 64, 80)
    bottom = small
    for lo, width, chans in ((0, 16, 3), (64, 8, 3), (96, 4, 3)):
        for ch in range(chans):
            inside = (lane >= lo + ch * width) & (lane < lo + (ch + 1) * width)
            bottom = jnp.where(inside, pltpu.roll(small, (128 - (3 - ch) * width) % 128, 1), bottom)
    small = small / jnp.maximum(bottom, 1.0)
    three = small + ldot(d43[...], rdot(small, m43[...]))
    two = small + ldot(d32[...], rdot(three, m32[...]))
    one = total(b, 32, 64)
    bottom = one
    for ch in range(3):
        inside = (lane >= ch * 32) & (lane < (ch + 1) * 32)
        bottom = jnp.where(inside, pltpu.roll(one, (128 - (3 - ch) * 32) % 128, 1), bottom)
    one = one / jnp.maximum(bottom, 1.0) + ldot(d21[...], rdot(two, m21[...]))
    wide = rdot(one, m10[...])
    hi, lo = split(wide)
    up = mm(even[...], hi) + mm(even[...], lo)
    down = mm(odd[...], hi) + mm(odd[...], lo)
    bottom = jnp.maximum(total(a, 0, 32), 1.0)
    for ch in range(COLOURS):
        own = total(b, 0, 32) if ch == 0 else total(c, 32 * (ch - 1), 32 * ch)
        back = jnp.where(lane < 64, up[:, ch * 128 : ch * 128 + 128], down[:, ch * 128 : ch * 128 + 128])
        level0[ch * 128 : ch * 128 + 128, :] = own / bottom + back
    for t in range(TILE_DEV):
        for row in range(32):
            out[t, :, row * 128 : row * 128 + 128] = level0[pl.ds(t * 32 + row, COLOURS, stride=128), :]


def collapse(a, b, c):
    mats = [const(m) for m in collapse_matrices()]
    return pl.pallas_call(
        collapse_kernel,
        out_shape=jax.ShapeDtypeStruct((TILE_DEV, COLOURS, 4096), F32),
        scratch_shapes=[pltpu.VMEM((COLOURS * 128, 128), F32)],
        compiler_params=pltpu.CompilerParams(vmem_limit_bytes=56 << 20),
        cost_estimate=pl.CostEstimate(flops=10**9, bytes_accessed=3 * 10**6, transcendentals=0),
        name="collapse",
    )(a, b, c, *mats)


def swap(value, axis, bit):
    size = lax.axis_size(axis)
    return lax.ppermute(value, axis, [(i, i ^ bit) for i in range(size)])


def local(frames, weight_map, seam_mask, strip_cell, partner, tile_group, tile_position_in_group):
    groups = lax.axis_size("frames")
    parts = lax.axis_size("tiles")
    mine = lax.axis_index("tiles")
    mask = lax.bitwise_xor(partner[0] // parts, lax.axis_index("frames"))

    ids = tile_group.reshape(QB) * (parts * TILE_DEV) + tile_position_in_group.reshape(QB)
    ids_core = swap(ids, "tiles", 1)
    ids_far = swap(ids, "tiles", 2)
    ids_far_core = swap(ids_far, "tiles", 1)
    ids = jnp.stack([ids, ids_core, ids_far, ids_far_core])
    group_size = parts * TILE_DEV
    owner = ids % group_size // TILE_DEV
    spot = jnp.where(owner == mine, ids // group_size * TILE_DEV + ids % TILE_DEV, -1)

    strips = strips_of(frames, strip_cell)
    bit = 1
    while bit < groups:
        strips = jnp.where((mask & bit) != 0, swap(strips, "frames", bit), strips)
        bit *= 2

    bands = bands_of(frames, weight_map, seam_mask)
    weights = bands[0]

    def send(rows):
        far = swap(rows, "tiles", 2)
        near = swap(rows, "tiles", 1)
        far_near = swap(far, "tiles", 1)
        sums = gather_rows(spot, (rows, near, far, far_near), groups * TILE_DEV)
        sums = sums.reshape(groups, TILE_DEV, rows.shape[1], 128)
        return lax.all_to_all(sums, "frames", split_axis=0, concat_axis=0, tiled=True)

    got_weights = send(weights)
    first, second = blend(strip_cell, strips, bands[1:])
    got_first = send(first)
    got_second = send(second)
    return collapse(got_weights, got_first, got_second)


def solution(mesh):
    in_specs = (
        P(("frames", "tiles"), None, None, None),
        P(("frames", "tiles"), None, None),
        P(("frames", "tiles"), None, None),
        P(("frames", "tiles")),
        P(("frames", "tiles")),
        P(("frames", "tiles"), None, None),
        P(("frames", "tiles"), None),
    )
    out_specs = P(("frames", "tiles"), None, None)
    return jax.shard_map(local, mesh=mesh, in_specs=in_specs, out_specs=out_specs, check_vma=False)
```

```python
import functools

import jax
import jax.numpy as jnp
import numpy as np
from jax import lax
from jax.experimental import pallas as pl
from jax.experimental.pallas import tpu as pltpu
from jax.sharding import PartitionSpec as P

COLOURS = 3
FH = 128
FW = 1024
QB = 32
WIN = 256
TILE_DEV = 4
VMEM = 30 << 20
ROUTE = 4096
F32 = jnp.float32
BF16 = jnp.bfloat16


def shrink_matrix(n):
    m = np.zeros((n // 2, n), np.float32)
    for i in range(n // 2):
        for d, tap in zip(range(-2, 3), (1, 4, 6, 4, 1)):
            m[i, min(max(2 * i + d, 0), n - 1)] += tap / 16.0
    return m


def grow_matrix(n):
    m = np.zeros((2 * n, n), np.float32)
    for i in range(n):
        lo, hi = max(i - 1, 0), min(i + 1, n - 1)
        m[2 * i, lo] += 1 / 8
        m[2 * i, i] += 6 / 8
        m[2 * i, hi] += 1 / 8
        m[2 * i + 1, i] += 1 / 2
        m[2 * i + 1, hi] += 1 / 2
    return m


def padded(m, rows, cols):
    return np.pad(m, ((0, rows - m.shape[0]), (0, cols - m.shape[1])))


def row_order():
    m = np.zeros((FH, FH), np.float32)
    for r in range(2):
        for par in range(2):
            for i in range(32):
                m[r * 64 + par * 32 + i, r * 64 + 2 * i + par] = 1
    return m


def vertical():
    v = {1: shrink_matrix(128), 2: shrink_matrix(64), 3: shrink_matrix(32)}
    spread = np.zeros((16, 8), np.float32)
    for r in range(2):
        for i in range(4):
            spread[r * 8 + i, r * 4 + i] = 1
    v[4] = spread @ shrink_matrix(16)
    g = {0: row_order() @ grow_matrix(64), 1: grow_matrix(32), 2: grow_matrix(16)}
    g[3] = grow_matrix(8) @ spread.T
    return v, g


def horizontal(width, pad_last):
    s = {k: shrink_matrix(width >> (k - 1)).T for k in range(1, 5)}
    g = {k: grow_matrix(width >> (k + 1)).T for k in range(4)}
    if pad_last:
        s[4] = padded(s[4], s[4].shape[0], pad_last)
        g[3] = padded(g[3], pad_last, g[3].shape[1])
    return s, g


def pack(mats, width):
    places, row, col, height = {}, 0, 0, 0
    for name in sorted(mats, key=lambda n: (-mats[n].shape[0], -mats[n].shape[1], n)):
        h, w = mats[name].shape
        wide = -(-w // 128) * 128
        if col + wide > width:
            row, col, height = row + height, 0, 0
        height = max(height, -(-h // 16) * 16)
        places[name] = (row, col, h, w)
        col += wide
    out = np.zeros((row + height, width), np.float32)
    for name, (r, c, h, w) in places.items():
        out[r : r + h, c : c + w] = mats[name]
    return jnp.asarray(out, BF16), places


def unpack(ref, places):
    return {name: ref[r : r + h, c : c + w] for name, (r, c, h, w) in places.items()}


def small_matrices():
    v, g = vertical()
    s, gh = horizontal(WIN, 0)
    sm, _ = horizontal(64, 0)
    mats = {f"v{k}": m for k, m in v.items()} | {f"g{k}": m for k, m in g.items()}
    mats |= {f"s{k}": m for k, m in s.items()} | {f"h{k}": m for k, m in gh.items()}
    mats |= {f"m{k}": m for k, m in sm.items()} | {"order": row_order()}
    return pack(mats, 512)


def large_matrices():
    s, gh = horizontal(FW, 128)
    mats = {f"s{k}": m for k, m in s.items()} | {f"h{k}": m for k, m in gh.items()}
    return pack(mats, 1024)


def levels_of(mats, letter):
    return {int(n[1:]): m for n, m in mats.items() if n[0] == letter and n[1:].isdigit()}


def mm(a, b):
    return jnp.dot(a, b, preferred_element_type=F32)


def split(v):
    hi = v.astype(BF16)
    return hi, (v - hi.astype(F32)).astype(BF16)


def rdot(v, m):
    hi, lo = split(v)
    return mm(hi, m) + mm(lo, m)


def ldot(m, v):
    hi, lo = split(v)
    return mm(m, hi) + mm(m, lo)


def mmt(a, b):
    return lax.dot_general(a, b, (((1,), (1,)), ((), ())), preferred_element_type=F32)


def pyramid(planes, v, s, product=mm):
    n = len(planes)
    t = jnp.concatenate([product(v[1], p) for p in planes], axis=0)
    levels = {1: rdot(t, s[1])}
    for k in range(2, 5):
        prev = levels[k - 1]
        rows = prev.shape[0] // n
        t = jnp.concatenate([ldot(v[k], prev[i * rows : (i + 1) * rows]) for i in range(n)], axis=0)
        levels[k] = rdot(t, s[k])
    return levels


def grown(level, n, gv, gh):
    h = rdot(level, gh)
    rows = level.shape[0] // n
    return [ldot(gv, h[i * rows : (i + 1) * rows]) for i in range(n)]


def place(rows, cols, base, width, offset):
    i = lax.broadcasted_iota(jnp.int32, (rows, cols), 0)
    c = lax.broadcasted_iota(jnp.int32, (rows, cols), 1)
    hit = (i >= base) & (i < base + width) & (c - i == offset - base)
    return jnp.where(hit, 1.0, 0.0).astype(BF16)


def strips_kernel(places, cell, xa, xb, packed, out, acc):
    mats = unpack(packed, places)
    v, gv, s, gh = (levels_of(mats, letter) for letter in "vgsh")
    order = mats["order"]
    first = window_tile(cell[0]) * 128
    planes = [jnp.concatenate([xa[0, c], xb[0, c]], axis=1) for c in range(COLOURS)]
    levels = pyramid(planes, v, s)
    back = grown(levels[1], COLOURS, gv[0], gh[0])
    b0 = jnp.concatenate([mm(order, planes[c]) - back[c] for c in range(COLOURS)], axis=0)
    bands = [b0.astype(BF16)]
    for k in range(1, 4):
        back = grown(levels[k + 1], COLOURS, gv[k], gh[k])
        bands.append((levels[k] - jnp.concatenate(back, axis=0)).astype(BF16))
    bands.append(levels[4].astype(BF16))
    start = cell[0] * 16 - first

    def pick(band, base, k):
        i = lax.broadcasted_iota(jnp.int32, (band.shape[1], 128), 0)
        c = lax.broadcasted_iota(jnp.int32, (band.shape[1], 128), 1)
        hit = (c >= base) & (c < base + (64 >> k)) & (i - c == (start >> k) - base)
        return mm(band, jnp.where(hit, 1.0, 0.0).astype(BF16))

    out[0:192, :] = (pick(bands[0][0:192], 0, 0) + pick(bands[0][192:384], 64, 0)).astype(BF16)
    acc[...] = pick(bands[1][0:96], 0, 1) + pick(bands[1][96:192], 32, 1) + pick(bands[2], 64, 2)
    acc[0:48, :] = acc[0:48, :] + pick(bands[3], 80, 3) + pick(bands[4], 88, 4)
    out[192:288, :] = acc[...].astype(BF16)


def window_tile(cell):
    return jnp.clip((cell - 3) >> 3, 0, (FW - WIN) // 128)


def full_spec(a):
    return pl.BlockSpec(a.shape, lambda *_: (0,) * a.ndim)


def strips_of(frames, cell):
    packed, places = small_matrices()
    grid_spec = pltpu.PrefetchScalarGridSpec(
        num_scalar_prefetch=1,
        grid=(1,),
        in_specs=[
            pl.BlockSpec((1, COLOURS, FH, 128), lambda i, c: (0, 0, 0, window_tile(c[0]))),
            pl.BlockSpec((1, COLOURS, FH, 128), lambda i, c: (0, 0, 0, window_tile(c[0]) + 1)),
        ]
        + [full_spec(packed)],
        out_specs=pl.BlockSpec((288, 128), lambda i, c: (0, 0)),
        scratch_shapes=[pltpu.VMEM((96, 128), F32)],
    )
    return pl.pallas_call(
        functools.partial(strips_kernel, places),
        grid_spec=grid_spec,
        out_shape=jax.ShapeDtypeStruct((288, 128), BF16),
        compiler_params=pltpu.CompilerParams(vmem_limit_bytes=VMEM),
        cost_estimate=pl.CostEstimate(flops=2 * 10**9, bytes_accessed=10**6, transcendentals=0),
        name="strips",
    )(cell, frames, frames, packed)


def lane_index():
    return lax.broadcasted_iota(jnp.int32, (1, 128), 1)


def fold_level0(p, store):
    left = lane_index() < 64
    for r in range(2):
        for j in range(8):
            even = p[r * 64 : r * 64 + 32, j * 128 : j * 128 + 128]
            odd = p[r * 64 + 32 : r * 64 + 64, j * 128 : j * 128 + 128]
            store(r * 16 + 2 * j, jnp.where(left, even, pltpu.roll(odd, 64, 1)))
            store(r * 16 + 2 * j + 1, jnp.where(left, pltpu.roll(even, 64, 1), odd))


def gather_channels(parts, width, cc, base):
    groups = 128 // width
    group = lane_index() // width
    out = jnp.zeros_like(parts[0])
    for ch in range(4):
        out = jnp.where(group == (cc + ch) % groups, parts[ch], out)
    return pltpu.roll(out, (base - cc * width) % 128, 1)


STATE_ROWS = 816


def state_views(state):
    at = lambda r, h, c, w: (slice(r, r + h), slice(c, c + w))
    b0 = [at(128 * c, 128, 0, 1024) for c in range(3)]
    l1 = [at(384, 64, 0, 512), at(384, 64, 512, 512), at(448, 64, 0, 512), at(448, 64, 512, 512)]
    l2 = [at(512, 32, 256 * c, 256) for c in range(4)]
    l3 = [at(544, 16, 128 * c, 128) for c in range(4)]
    l4 = [at(544, 16, 512 + 128 * c, 128) for c in range(4)]
    levels = [b0 + [at(560, 128, 0, 1024)], l1, l2, l3, l4]
    masks = [at(688, 128 >> k, 128 * k, 64 >> k) for k in range(4)] + [at(688, 16, 512, 4)]
    return levels, masks


def bands_kernel(small_places, large_places, x, w, m, small, large, wblocks, state):
    mats = unpack(small, small_places)
    v, gv, sm = (levels_of(mats, letter) for letter in "vgm")
    order = mats["order"]
    mats = unpack(large, large_places)
    s, gh = (levels_of(mats, letter) for letter in "sh")
    views, mask_views = state_views(state)
    planes = [x[0, c] for c in range(COLOURS)] + [w[0]]
    weights = mm(order, planes[3])
    state[views[0][3]] = weights

    def store(q, piece):
        wblocks[q] = piece.astype(BF16)

    fold_level0(weights, store)
    levels = pyramid(planes, v, s)
    for k in range(1, 5):
        rows = levels[k].shape[0] // 4
        state[views[k][3]] = levels[k][3 * rows :]
    back = grown(levels[1][: 3 * 64], COLOURS, gv[0], gh[0])
    for c in range(COLOURS):
        state[views[0][c]] = mm(order, planes[c]) - back[c]
    for k in range(1, 4):
        rows = levels[k].shape[0] // 4
        below = levels[k + 1].shape[0] // 4
        back = grown(levels[k + 1][: 3 * below], COLOURS, gv[k], gh[k])
        for c in range(COLOURS):
            state[views[k][c]] = levels[k][c * rows : (c + 1) * rows] - back[c]
    for c in range(COLOURS):
        state[views[4][c]] = levels[4][c * 16 : (c + 1) * 16]
    other = (1.0 - m[0].astype(F32)).astype(BF16)
    state[mask_views[0]] = mmt(order, other)
    masks = pyramid([other], v, sm, mmt)
    for k in range(1, 5):
        state[mask_views[k]] = masks[k]


def bands_of(frames, weight_map, seam_mask):
    small, small_places = small_matrices()
    large, large_places = large_matrices()
    return pl.pallas_call(
        functools.partial(bands_kernel, small_places, large_places),
        out_shape=[jax.ShapeDtypeStruct((QB, 32, 128), BF16), jax.ShapeDtypeStruct((STATE_ROWS, FW), F32)],
        compiler_params=pltpu.CompilerParams(vmem_limit_bytes=VMEM),
        cost_estimate=pl.CostEstimate(flops=8 * 10**9, bytes_accessed=6 * 10**6, transcendentals=0),
        name="bands",
    )(frames, weight_map, jnp.swapaxes(seam_mask, 1, 2), small, large)


def blend_kernel(cell, strips, state, first, second):
    views, mask_views = state_views(state)
    (b0, b1, b2, b3, b4) = [[state[view] for view in views[k][:3]] for k in range(5)]
    (wp, w1, w2, w3, w4) = [state[views[k][3]] for k in range(5)]
    (n0, n1, n2, n3, n4) = [state[view] for view in mask_views]
    start = cell[0] * 16
    low = strips[192:288]

    def mixed(band, remote, share):
        return band + share * (remote - band)

    widths = (1024, 512, 256, 128, 128)
    share0 = mm(n0.astype(BF16), place(64, 1024, 0, 64, start))
    share = [share0]
    for k, ref in enumerate((n1, n2, n3, n4)):
        share.append(rdot(ref, place(64 >> (k + 1), widths[k + 1], 0, 64 >> (k + 1), start >> (k + 1))))
    top = strips[0:192]
    remote0 = [mm(top, place(128, 1024, 0, 64, start)), mm(top, place(128, 1024, 64, 64, start))]
    remote0 = jnp.concatenate(remote0, axis=0)
    weights = wp
    for c in range(COLOURS):
        p = weights * mixed(b0[c], remote0[c * 128 : (c + 1) * 128], share[0])
        out, row = (first, 0) if c == 0 else (second, 32 * (c - 1))

        def store(q, piece, out=out, row=row):
            out[q, row : row + 32, :] = piece.astype(BF16)

        fold_level0(p, store)
    remote1 = [mm(low, place(128, 512, 0, 32, start >> 1)), mm(low, place(128, 512, 32, 32, start >> 1))]
    remote1 = jnp.concatenate(remote1, axis=0)
    parts = [w1 * mixed(b1[c], remote1[c * 64 : (c + 1) * 64], share[1]) for c in range(COLOURS)] + [w1]
    for r in range(2):
        for j in range(4):
            turned = [parts[ch][r * 32 : r * 32 + 32, j * 128 : j * 128 + 128] for ch in range(4)]
            turned = [turned[0]] + [pltpu.roll(turned[ch], 32 * ch, 1) for ch in range(1, 4)]
            for cc in range(4):
                first[r * 16 + 4 * j + cc, 32:64, :] = gather_channels(turned, 32, cc, 0).astype(BF16)
    remote2 = mm(low, place(128, 256, 64, 16, start >> 2))
    remote3 = mm(low[0:48], place(128, 128, 80, 8, start >> 3))
    remote4 = mm(low[0:48], place(128, 128, 88, 4, start >> 4))
    parts2 = [w2 * mixed(b2[c], remote2[c * 32 : (c + 1) * 32], share[2]) for c in range(COLOURS)] + [w2]
    parts3 = [w3 * mixed(b3[c], remote3[c * 16 : (c + 1) * 16], share[3]) for c in range(COLOURS)] + [w3]
    parts4 = [w4 * mixed(b4[c], remote4[c * 16 : (c + 1) * 16], share[4]) for c in range(COLOURS)] + [w4]
    lane = lane_index()
    for r in range(2):
        turned3 = [pltpu.roll(parts3[ch][r * 8 : r * 8 + 8], 8 * ch, 1) for ch in range(4)]
        turned4 = [pltpu.roll(parts4[ch][r * 8 : r * 8 + 8], 4 * ch, 1) for ch in range(4)]
        for j in range(2):
            turned2 = [parts2[ch][r * 16 : r * 16 + 16, j * 128 : j * 128 + 128] for ch in range(4)]
            turned2 = [pltpu.roll(turned2[ch], 16 * ch, 1) for ch in range(4)]
            for cc in range(8):
                c = j * 8 + cc
                two = gather_channels(turned2, 16, cc, 0)
                three = gather_channels(turned3, 8, c, 64)
                four = gather_channels(turned4, 4, c, 96)
                head = jnp.where(lane < 64, two[0:8], jnp.where(lane < 96, three, four))
                tail = jnp.where(lane < 64, two[8:16], 0.0)
                first[r * 16 + c, 64:80, :] = jnp.concatenate([head, tail], axis=0).astype(BF16)


def blend(cell, strips, state):
    vmem = pl.BlockSpec(memory_space=pltpu.VMEM)
    return pl.pallas_call(
        blend_kernel,
        in_specs=[pl.BlockSpec(memory_space=pltpu.SMEM)] + [vmem] * 2,
        out_shape=[jax.ShapeDtypeStruct((QB, 80, 128), BF16), jax.ShapeDtypeStruct((QB, 64, 128), BF16)],
        compiler_params=pltpu.CompilerParams(vmem_limit_bytes=VMEM),
        cost_estimate=pl.CostEstimate(flops=4 * 10**9, bytes_accessed=4 * 10**6, transcendentals=0),
        name="blend",
    )(cell, strips, state)


def routes_kernel(spot, lists, counts):
    for source in range(4):

        def body(q, count, source=source):
            at = spot[source, q]
            lists[source, count] = q * ROUTE + at
            return jnp.where(at >= 0, count + 1, count)

        counts[source] = lax.fori_loop(0, QB, body, 0)


def routes_of(spot):
    smem = pl.BlockSpec(memory_space=pltpu.SMEM)
    return pl.pallas_call(
        routes_kernel,
        in_specs=[smem],
        out_specs=[smem, smem],
        out_shape=[jax.ShapeDtypeStruct((4, QB + 1), jnp.int32), jax.ShapeDtypeStruct((4,), jnp.int32)],
        name="routes",
    )(spot)


def gather_kernel(lists, counts, a, b, c, d, out, acc):
    acc[...] = jnp.zeros_like(acc)
    for source, ref in enumerate((a, b, c, d)):

        def body(i, carry, source=source, ref=ref):
            entry = lists[source, i]
            q, at = entry // ROUTE, entry % ROUTE
            acc[at] = acc[at] + ref[q].astype(F32)
            return carry

        lax.fori_loop(0, counts[source], body, 0)
    out[...] = acc[...].astype(BF16)


def gather_rows(routes, rows, tiles):
    height = rows[0].shape[1]
    vmem = pl.BlockSpec(memory_space=pltpu.VMEM)
    return pl.pallas_call(
        gather_kernel,
        in_specs=[pl.BlockSpec(memory_space=pltpu.SMEM)] * 2 + [vmem] * 4,
        out_shape=jax.ShapeDtypeStruct((tiles, height, 128), BF16),
        scratch_shapes=[pltpu.VMEM((tiles, height, 128), F32)],
        compiler_params=pltpu.CompilerParams(vmem_limit_bytes=VMEM),
        cost_estimate=pl.CostEstimate(flops=10**9, bytes_accessed=4 * 10**6, transcendentals=0),
        name="gather_rows",
    )(*routes, *rows)


def collapse_matrices():
    def across(src, dst, width):
        g = grow_matrix(width).T
        m = np.zeros((128, 128), np.float32)
        for ch in range(COLOURS):
            m[src + ch * width : src + (ch + 1) * width, dst + ch * 2 * width : dst + (ch + 1) * 2 * width] = g
        return m

    last = np.zeros((128, 384), np.float32)
    g = grow_matrix(32).T
    for ch in range(COLOURS):
        for half in range(2):
            last[ch * 32 : ch * 32 + 32, ch * 128 + half * 64 : ch * 128 + half * 64 + 64] = g

    def down(n, rows_in, rows_out, pick=None):
        g = grow_matrix(n)
        g = g if pick is None else g[pick::2]
        m = np.zeros((TILE_DEV * rows_out, TILE_DEV * rows_in), np.float32)
        for t in range(TILE_DEV):
            m[t * rows_out : t * rows_out + g.shape[0], t * rows_in : t * rows_in + n] = g
        return m

    mats = {"m43": across(96, 64, 4), "m32": across(64, 0, 8), "m21": across(0, 0, 16), "m10": last}
    mats |= {"d43": down(4, 16, 16), "d32": down(8, 16, 16), "d21": down(16, 16, 32)}
    mats |= {"even": down(32, 32, 32, 0), "odd": down(32, 32, 32, 1)}
    return pack(mats, 1280)


def collapse_kernel(places, a, b, c, packed, out, level0):
    mats = unpack(packed, places)

    def total(ref, lo, hi):
        acc = ref[0, :, lo:hi, :].astype(F32)
        for source in range(1, ref.shape[0]):
            acc = acc + ref[source, :, lo:hi, :].astype(F32)
        return acc.reshape(TILE_DEV * (hi - lo), 128)

    lane = lane_index()
    small = total(b, 64, 80)
    bottom = small
    for lo, width, chans in ((0, 16, 3), (64, 8, 3), (96, 4, 3)):
        for ch in range(chans):
            inside = (lane >= lo + ch * width) & (lane < lo + (ch + 1) * width)
            bottom = jnp.where(inside, pltpu.roll(small, (128 - (3 - ch) * width) % 128, 1), bottom)
    small = small / jnp.maximum(bottom, 1.0)
    three = small + ldot(mats["d43"], rdot(small, mats["m43"]))
    two = small + ldot(mats["d32"], rdot(three, mats["m32"]))
    one = total(b, 32, 64)
    bottom = one
    for ch in range(3):
        inside = (lane >= ch * 32) & (lane < (ch + 1) * 32)
        bottom = jnp.where(inside, pltpu.roll(one, (128 - (3 - ch) * 32) % 128, 1), bottom)
    one = one / jnp.maximum(bottom, 1.0) + ldot(mats["d21"], rdot(two, mats["m21"]))
    wide = rdot(one, mats["m10"])
    hi, lo = split(wide)
    up = mm(mats["even"], hi) + mm(mats["even"], lo)
    down = mm(mats["odd"], hi) + mm(mats["odd"], lo)
    bottom = jnp.maximum(total(a, 0, 32), 1.0)
    for ch in range(COLOURS):
        own = total(b, 0, 32) if ch == 0 else total(c, 32 * (ch - 1), 32 * ch)
        back = jnp.where(lane < 64, up[:, ch * 128 : ch * 128 + 128], down[:, ch * 128 : ch * 128 + 128])
        level0[ch * 128 : ch * 128 + 128, :] = own / bottom + back
    for ch in range(COLOURS):
        for row in range(32):
            out[ch, :, row * 128 : row * 128 + 128] = level0[pl.ds(ch * 128 + row, TILE_DEV, stride=32), :]


def collapse(a, b, c):
    packed, places = collapse_matrices()
    tiles = pl.pallas_call(
        functools.partial(collapse_kernel, places),
        out_shape=jax.ShapeDtypeStruct((COLOURS, TILE_DEV, 4096), F32),
        scratch_shapes=[pltpu.VMEM((COLOURS * 128, 128), F32)],
        compiler_params=pltpu.CompilerParams(vmem_limit_bytes=VMEM),
        cost_estimate=pl.CostEstimate(flops=10**9, bytes_accessed=3 * 10**6, transcendentals=0),
        name="collapse",
    )(a, b, c, packed)
    return jnp.swapaxes(tiles, 0, 1)


def swap(value, axis, bit):
    size = lax.axis_size(axis)
    return lax.ppermute(value, axis, [(i, i ^ bit) for i in range(size)])


def local(frames, weight_map, seam_mask, strip_cell, partner, tile_group, tile_position_in_group):
    groups = lax.axis_size("frames")
    parts = lax.axis_size("tiles")
    mine = lax.axis_index("tiles")
    mask = lax.bitwise_xor(partner[0] // parts, lax.axis_index("frames"))

    ids = tile_group.reshape(QB) * (parts * TILE_DEV) + tile_position_in_group.reshape(QB)
    ids_core = swap(ids, "tiles", 1)
    ids_far = swap(ids, "tiles", 2)
    ids_far_core = swap(ids_far, "tiles", 1)
    ids = jnp.stack([ids, ids_core, ids_far, ids_far_core])
    group_size = parts * TILE_DEV
    owner = ids % group_size // TILE_DEV
    spot = jnp.where(owner == mine, ids // group_size * TILE_DEV + ids % TILE_DEV, -1)

    strips = strips_of(frames, strip_cell)
    bit = 1
    while bit < groups:
        strips = jnp.where((mask & bit) != 0, swap(strips, "frames", bit), strips)
        bit *= 2

    weights, state = bands_of(frames, weight_map, seam_mask)
    routes = routes_of(spot)

    def spread(rows):
        far = swap(rows, "tiles", 2)
        return rows, swap(rows, "tiles", 1), far

    def send(rows, near, far):
        sums = gather_rows(routes, (rows, near, far, swap(far, "tiles", 1)), groups * TILE_DEV)
        sums = sums.reshape(groups, TILE_DEV, rows.shape[1], 128)
        return lax.all_to_all(sums, "frames", split_axis=0, concat_axis=0, tiled=True)

    weight_rows = spread(weights)
    weight_rows, routes, strips = lax.optimization_barrier((weight_rows, routes, strips))
    first, second = blend(strip_cell, strips, state)
    first_rows = spread(first)
    second_rows = spread(second)
    got_weights = send(*weight_rows)
    got_first = send(*first_rows)
    got_second = send(*second_rows)
    return collapse(got_weights, got_first, got_second)


def solution(mesh):
    in_specs = (
        P(("frames", "tiles"), None, None, None),
        P(("frames", "tiles"), None, None),
        P(("frames", "tiles"), None, None),
        P(("frames", "tiles")),
        P(("frames", "tiles")),
        P(("frames", "tiles"), None, None),
        P(("frames", "tiles"), None),
    )
    out_specs = P(("frames", "tiles"), None, None)
    return jax.shard_map(local, mesh=mesh, in_specs=in_specs, out_specs=out_specs, check_vma=False)
```

```python
import functools

import jax
import jax.numpy as jnp
import numpy as np
from jax import lax
from jax.experimental import pallas as pl
from jax.experimental.pallas import tpu as pltpu
from jax.sharding import PartitionSpec as P

COLOURS = 3
FH = 128
FW = 1024
QB = 32
WIN = 256
TILE_DEV = 4
VMEM = 30 << 20
ROUTE = 4096
F32 = jnp.float32
BF16 = jnp.bfloat16


def shrink_matrix(n):
    m = np.zeros((n // 2, n), np.float32)
    for i in range(n // 2):
        for d, tap in zip(range(-2, 3), (1, 4, 6, 4, 1)):
            m[i, min(max(2 * i + d, 0), n - 1)] += tap / 16.0
    return m


def grow_matrix(n):
    m = np.zeros((2 * n, n), np.float32)
    for i in range(n):
        lo, hi = max(i - 1, 0), min(i + 1, n - 1)
        m[2 * i, lo] += 1 / 8
        m[2 * i, i] += 6 / 8
        m[2 * i, hi] += 1 / 8
        m[2 * i + 1, i] += 1 / 2
        m[2 * i + 1, hi] += 1 / 2
    return m


def padded(m, rows, cols):
    return np.pad(m, ((0, rows - m.shape[0]), (0, cols - m.shape[1])))


def row_order():
    m = np.zeros((FH, FH), np.float32)
    for r in range(2):
        for par in range(2):
            for i in range(32):
                m[r * 64 + par * 32 + i, r * 64 + 2 * i + par] = 1
    return m


def vertical():
    v = {1: shrink_matrix(128), 2: shrink_matrix(64), 3: shrink_matrix(32)}
    spread = np.zeros((16, 8), np.float32)
    for r in range(2):
        for i in range(4):
            spread[r * 8 + i, r * 4 + i] = 1
    v[4] = spread @ shrink_matrix(16)
    g = {0: row_order() @ grow_matrix(64), 1: grow_matrix(32), 2: grow_matrix(16)}
    g[3] = grow_matrix(8) @ spread.T
    return v, g


def horizontal(width):
    s = {k: shrink_matrix(width >> (k - 1)).T for k in range(1, 5)}
    g = {k: grow_matrix(width >> (k + 1)).T for k in range(4)}
    return s, g


def shrink_window():
    m = np.zeros((512, 128), np.float32)
    for i in range(128):
        for d, tap in zip(range(-2, 3), (1, 4, 6, 4, 1)):
            m[128 + 2 * i + d, i] = tap / 16.0
    return m


def grow_window():
    m = np.zeros((384, 256), np.float32)
    for i in range(128):
        for d, tap in zip(range(-1, 2), (1, 6, 1)):
            m[128 + i + d, 2 * i] = tap / 8.0
        m[128 + i, 2 * i + 1] = m[128 + i + 1, 2 * i + 1] = 0.5
    return m


def pack(mats, width):
    places, row, col, height = {}, 0, 0, 0
    for name in sorted(mats, key=lambda n: (-mats[n].shape[0], -mats[n].shape[1], n)):
        h, w = mats[name].shape
        wide = -(-w // 128) * 128
        if col + wide > width:
            row, col, height = row + height, 0, 0
        height = max(height, -(-h // 16) * 16)
        places[name] = (row, col, h, w)
        col += wide
    out = np.zeros((row + height, width), np.float32)
    for name, (r, c, h, w) in places.items():
        out[r : r + h, c : c + w] = mats[name]
    return jnp.asarray(out, BF16), places


def unpack(ref, places):
    return {name: ref[r : r + h, c : c + w] for name, (r, c, h, w) in places.items()}


def small_matrices():
    v, g = vertical()
    s, gh = horizontal(WIN)
    sm, _ = horizontal(64)
    mats = {f"v{k}": m for k, m in v.items()} | {f"g{k}": m for k, m in g.items()}
    mats |= {f"s{k}": m for k, m in s.items()} | {f"h{k}": m for k, m in gh.items()}
    mats |= {f"m{k}": m for k, m in sm.items()} | {"order": row_order()}
    return pack(mats, 512)


def large_matrices():
    mats = {"shrink": shrink_window(), "grow": grow_window()}
    mats["last"] = padded(shrink_matrix(128).T, 128, 128)
    mats["least"] = padded(grow_matrix(64).T, 128, 128)
    return pack(mats, 640)


def levels_of(mats, letter):
    return {int(n[1:]): m for n, m in mats.items() if n[0] == letter and n[1:].isdigit()}


def mm(a, b):
    return jnp.dot(a, b, preferred_element_type=F32)


def split(v):
    hi = v.astype(BF16)
    return hi, (v - hi.astype(F32)).astype(BF16)


def rdot(v, m):
    hi, lo = split(v)
    return mm(hi, m) + mm(lo, m)


def ldot(m, v):
    hi, lo = split(v)
    return mm(m, hi) + mm(m, lo)


def mmt(a, b):
    return lax.dot_general(a, b, (((1,), (1,)), ((), ())), preferred_element_type=F32)


def windows(v, m, step):
    rows, width = v.shape
    both = jnp.concatenate(split(v), axis=0)
    left = jnp.broadcast_to(both[:, :1], (2 * rows, 128))
    right = jnp.broadcast_to(both[:, width - 1 :], (2 * rows, 128))
    both = jnp.concatenate([left, both, right], axis=1)
    pieces = []
    for n in range(width // step):
        piece = mm(both[:, n * step : n * step + step + 256], m)
        pieces.append(piece[:rows] + piece[rows:])
    return jnp.concatenate(pieces, axis=1)


def right_of(m):
    return lambda v: rdot(v, m)


def pyramid(planes, v, shrinks, product=mm):
    n = len(planes)
    t = jnp.concatenate([product(v[1], p) for p in planes], axis=0)
    levels = {1: shrinks[1](t)}
    for k in range(2, 5):
        prev = levels[k - 1]
        rows = prev.shape[0] // n
        t = jnp.concatenate([ldot(v[k], prev[i * rows : (i + 1) * rows]) for i in range(n)], axis=0)
        levels[k] = shrinks[k](t)
    return levels


def grown(level, n, gv, grow):
    h = grow(level)
    rows = level.shape[0] // n
    return [ldot(gv, h[i * rows : (i + 1) * rows]) for i in range(n)]


def place(rows, cols, base, width, offset):
    i = lax.broadcasted_iota(jnp.int32, (rows, cols), 0)
    c = lax.broadcasted_iota(jnp.int32, (rows, cols), 1)
    hit = (i >= base) & (i < base + width) & (c - i == offset - base)
    return jnp.where(hit, 1.0, 0.0).astype(BF16)


def strips_kernel(places, cell, xa, xb, packed, out, acc):
    mats = unpack(packed, places)
    v, gv, s, gh = (levels_of(mats, letter) for letter in "vgsh")
    s, gh = ({k: right_of(m) for k, m in each.items()} for each in (s, gh))
    order = mats["order"]
    first = window_tile(cell[0]) * 128
    planes = [jnp.concatenate([xa[0, c], xb[0, c]], axis=1) for c in range(COLOURS)]
    levels = pyramid(planes, v, s)
    back = grown(levels[1], COLOURS, gv[0], gh[0])
    b0 = jnp.concatenate([mm(order, planes[c]) - back[c] for c in range(COLOURS)], axis=0)
    bands = [b0.astype(BF16)]
    for k in range(1, 4):
        back = grown(levels[k + 1], COLOURS, gv[k], gh[k])
        bands.append((levels[k] - jnp.concatenate(back, axis=0)).astype(BF16))
    bands.append(levels[4].astype(BF16))
    start = cell[0] * 16 - first

    def pick(band, base, k):
        i = lax.broadcasted_iota(jnp.int32, (band.shape[1], 128), 0)
        c = lax.broadcasted_iota(jnp.int32, (band.shape[1], 128), 1)
        hit = (c >= base) & (c < base + (64 >> k)) & (i - c == (start >> k) - base)
        return mm(band, jnp.where(hit, 1.0, 0.0).astype(BF16))

    out[0:192, :] = (pick(bands[0][0:192], 0, 0) + pick(bands[0][192:384], 64, 0)).astype(BF16)
    acc[...] = pick(bands[1][0:96], 0, 1) + pick(bands[1][96:192], 32, 1) + pick(bands[2], 64, 2)
    acc[0:48, :] = acc[0:48, :] + pick(bands[3], 80, 3) + pick(bands[4], 88, 4)
    out[192:288, :] = acc[...].astype(BF16)


def window_tile(cell):
    return jnp.clip((cell - 3) >> 3, 0, (FW - WIN) // 128)


def full_spec(a):
    return pl.BlockSpec(a.shape, lambda *_: (0,) * a.ndim)


def strips_of(frames, cell):
    packed, places = small_matrices()
    grid_spec = pltpu.PrefetchScalarGridSpec(
        num_scalar_prefetch=1,
        grid=(1,),
        in_specs=[
            pl.BlockSpec((1, COLOURS, FH, 128), lambda i, c: (0, 0, 0, window_tile(c[0]))),
            pl.BlockSpec((1, COLOURS, FH, 128), lambda i, c: (0, 0, 0, window_tile(c[0]) + 1)),
        ]
        + [full_spec(packed)],
        out_specs=pl.BlockSpec((288, 128), lambda i, c: (0, 0)),
        scratch_shapes=[pltpu.VMEM((96, 128), F32)],
    )
    return pl.pallas_call(
        functools.partial(strips_kernel, places),
        grid_spec=grid_spec,
        out_shape=jax.ShapeDtypeStruct((288, 128), BF16),
        compiler_params=pltpu.CompilerParams(vmem_limit_bytes=VMEM),
        cost_estimate=pl.CostEstimate(flops=2 * 10**9, bytes_accessed=10**6, transcendentals=0),
        name="strips",
    )(cell, frames, frames, packed)


def lane_index():
    return lax.broadcasted_iota(jnp.int32, (1, 128), 1)


def fold_level0(p, store):
    left = lane_index() < 64
    for r in range(2):
        for j in range(8):
            even = p[r * 64 : r * 64 + 32, j * 128 : j * 128 + 128]
            odd = p[r * 64 + 32 : r * 64 + 64, j * 128 : j * 128 + 128]
            store(r * 16 + 2 * j, jnp.where(left, even, pltpu.roll(odd, 64, 1)))
            store(r * 16 + 2 * j + 1, jnp.where(left, pltpu.roll(even, 64, 1), odd))


def gather_channels(parts, width, cc, base):
    groups = 128 // width
    group = lane_index() // width
    out = jnp.zeros_like(parts[0])
    for ch in range(4):
        out = jnp.where(group == (cc + ch) % groups, parts[ch], out)
    return pltpu.roll(out, (base - cc * width) % 128, 1)


STATE_ROWS = 816


def state_views(state):
    at = lambda r, h, c, w: (slice(r, r + h), slice(c, c + w))
    b0 = [at(128 * c, 128, 0, 1024) for c in range(3)]
    l1 = [at(384, 64, 0, 512), at(384, 64, 512, 512), at(448, 64, 0, 512), at(448, 64, 512, 512)]
    l2 = [at(512, 32, 256 * c, 256) for c in range(4)]
    l3 = [at(544, 16, 128 * c, 128) for c in range(4)]
    l4 = [at(544, 16, 512 + 128 * c, 128) for c in range(4)]
    levels = [b0 + [at(560, 128, 0, 1024)], l1, l2, l3, l4]
    masks = [at(688, 128 >> k, 128 * k, 64 >> k) for k in range(4)] + [at(688, 16, 512, 4)]
    return levels, masks


def bands_kernel(small_places, large_places, x, w, m, small, large, wblocks, state):
    mats = unpack(small, small_places)
    v, gv, sm = (levels_of(mats, letter) for letter in "vgm")
    order = mats["order"]
    sm = {k: right_of(each) for k, each in sm.items()}
    mats = unpack(large, large_places)
    half = lambda each: windows(each, mats["shrink"], 256)
    twice = lambda each: windows(each, mats["grow"], 128)
    s = {1: half, 2: half, 3: half, 4: right_of(mats["last"])}
    gh = {0: twice, 1: twice, 2: twice, 3: right_of(mats["least"])}
    views, mask_views = state_views(state)
    planes = [x[0, c] for c in range(COLOURS)] + [w[0]]
    weights = mm(order, planes[3])
    state[views[0][3]] = weights

    def store(q, piece):
        wblocks[q] = piece.astype(BF16)

    fold_level0(weights, store)
    levels = pyramid(planes, v, s)
    for k in range(1, 5):
        rows = levels[k].shape[0] // 4
        state[views[k][3]] = levels[k][3 * rows :]
    back = grown(levels[1][: 3 * 64], COLOURS, gv[0], gh[0])
    for c in range(COLOURS):
        state[views[0][c]] = mm(order, planes[c]) - back[c]
    for k in range(1, 4):
        rows = levels[k].shape[0] // 4
        below = levels[k + 1].shape[0] // 4
        back = grown(levels[k + 1][: 3 * below], COLOURS, gv[k], gh[k])
        for c in range(COLOURS):
            state[views[k][c]] = levels[k][c * rows : (c + 1) * rows] - back[c]
    for c in range(COLOURS):
        state[views[4][c]] = levels[4][c * 16 : (c + 1) * 16]
    other = (1.0 - m[0].astype(F32)).astype(BF16)
    state[mask_views[0]] = mmt(order, other)
    masks = pyramid([other], v, sm, mmt)
    for k in range(1, 5):
        state[mask_views[k]] = masks[k]


def bands_of(frames, weight_map, seam_mask):
    small, small_places = small_matrices()
    large, large_places = large_matrices()
    return pl.pallas_call(
        functools.partial(bands_kernel, small_places, large_places),
        out_shape=[jax.ShapeDtypeStruct((QB, 32, 128), BF16), jax.ShapeDtypeStruct((STATE_ROWS, FW), F32)],
        compiler_params=pltpu.CompilerParams(vmem_limit_bytes=VMEM),
        cost_estimate=pl.CostEstimate(flops=8 * 10**9, bytes_accessed=6 * 10**6, transcendentals=0),
        name="bands",
    )(frames, weight_map, jnp.swapaxes(seam_mask, 1, 2), small, large)


def blend_kernel(cell, strips, state, first, second):
    views, mask_views = state_views(state)
    (b0, b1, b2, b3, b4) = [[state[view] for view in views[k][:3]] for k in range(5)]
    (wp, w1, w2, w3, w4) = [state[views[k][3]] for k in range(5)]
    (n0, n1, n2, n3, n4) = [state[view] for view in mask_views]
    start = cell[0] * 16
    low = strips[192:288]

    def mixed(band, remote, share):
        return band + share * (remote - band)

    widths = (1024, 512, 256, 128, 128)
    share0 = mm(n0.astype(BF16), place(64, 1024, 0, 64, start))
    share = [share0]
    for k, ref in enumerate((n1, n2, n3, n4)):
        share.append(rdot(ref, place(64 >> (k + 1), widths[k + 1], 0, 64 >> (k + 1), start >> (k + 1))))
    top = strips[0:192]
    remote0 = [mm(top, place(128, 1024, 0, 64, start)), mm(top, place(128, 1024, 64, 64, start))]
    remote0 = jnp.concatenate(remote0, axis=0)
    weights = wp
    for c in range(COLOURS):
        p = weights * mixed(b0[c], remote0[c * 128 : (c + 1) * 128], share[0])
        out, row = (first, 0) if c == 0 else (second, 32 * (c - 1))

        def store(q, piece, out=out, row=row):
            out[q, row : row + 32, :] = piece.astype(BF16)

        fold_level0(p, store)
    remote1 = [mm(low, place(128, 512, 0, 32, start >> 1)), mm(low, place(128, 512, 32, 32, start >> 1))]
    remote1 = jnp.concatenate(remote1, axis=0)
    parts = [w1 * mixed(b1[c], remote1[c * 64 : (c + 1) * 64], share[1]) for c in range(COLOURS)] + [w1]
    for r in range(2):
        for j in range(4):
            turned = [parts[ch][r * 32 : r * 32 + 32, j * 128 : j * 128 + 128] for ch in range(4)]
            turned = [turned[0]] + [pltpu.roll(turned[ch], 32 * ch, 1) for ch in range(1, 4)]
            for cc in range(4):
                first[r * 16 + 4 * j + cc, 32:64, :] = gather_channels(turned, 32, cc, 0).astype(BF16)
    remote2 = mm(low, place(128, 256, 64, 16, start >> 2))
    remote3 = mm(low[0:48], place(128, 128, 80, 8, start >> 3))
    remote4 = mm(low[0:48], place(128, 128, 88, 4, start >> 4))
    parts2 = [w2 * mixed(b2[c], remote2[c * 32 : (c + 1) * 32], share[2]) for c in range(COLOURS)] + [w2]
    parts3 = [w3 * mixed(b3[c], remote3[c * 16 : (c + 1) * 16], share[3]) for c in range(COLOURS)] + [w3]
    parts4 = [w4 * mixed(b4[c], remote4[c * 16 : (c + 1) * 16], share[4]) for c in range(COLOURS)] + [w4]
    lane = lane_index()
    for r in range(2):
        turned3 = [pltpu.roll(parts3[ch][r * 8 : r * 8 + 8], 8 * ch, 1) for ch in range(4)]
        turned4 = [pltpu.roll(parts4[ch][r * 8 : r * 8 + 8], 4 * ch, 1) for ch in range(4)]
        for j in range(2):
            turned2 = [parts2[ch][r * 16 : r * 16 + 16, j * 128 : j * 128 + 128] for ch in range(4)]
            turned2 = [pltpu.roll(turned2[ch], 16 * ch, 1) for ch in range(4)]
            for cc in range(8):
                c = j * 8 + cc
                two = gather_channels(turned2, 16, cc, 0)
                three = gather_channels(turned3, 8, c, 64)
                four = gather_channels(turned4, 4, c, 96)
                head = jnp.where(lane < 64, two[0:8], jnp.where(lane < 96, three, four))
                tail = jnp.where(lane < 64, two[8:16], 0.0)
                first[r * 16 + c, 64:80, :] = jnp.concatenate([head, tail], axis=0).astype(BF16)


def blend(cell, strips, state):
    vmem = pl.BlockSpec(memory_space=pltpu.VMEM)
    return pl.pallas_call(
        blend_kernel,
        in_specs=[pl.BlockSpec(memory_space=pltpu.SMEM)] + [vmem] * 2,
        out_shape=[jax.ShapeDtypeStruct((QB, 80, 128), BF16), jax.ShapeDtypeStruct((QB, 64, 128), BF16)],
        compiler_params=pltpu.CompilerParams(vmem_limit_bytes=VMEM),
        cost_estimate=pl.CostEstimate(flops=4 * 10**9, bytes_accessed=4 * 10**6, transcendentals=0),
        name="blend",
    )(cell, strips, state)


def routes_kernel(spot, lists, counts):
    for source in range(4):

        def body(q, count, source=source):
            at = spot[source, q]
            lists[source, count] = q * ROUTE + at
            return jnp.where(at >= 0, count + 1, count)

        counts[source] = lax.fori_loop(0, QB, body, 0)


def routes_of(spot):
    smem = pl.BlockSpec(memory_space=pltpu.SMEM)
    return pl.pallas_call(
        routes_kernel,
        in_specs=[smem],
        out_specs=[smem, smem],
        out_shape=[jax.ShapeDtypeStruct((4, QB + 1), jnp.int32), jax.ShapeDtypeStruct((4,), jnp.int32)],
        name="routes",
    )(spot)


def gather_kernel(lists, counts, a, b, c, d, home, away, acc):
    acc[...] = jnp.zeros_like(acc)
    for source, ref in enumerate((a, b, c, d)):

        def body(i, carry, source=source, ref=ref):
            entry = lists[source, i]
            q, at = entry // ROUTE, entry % ROUTE
            acc[at] = acc[at] + ref[q].astype(F32)
            return carry

        lax.fori_loop(0, counts[source], body, 0)
    tiles = home.shape[0]
    home[...] = acc[0:tiles]
    away[...] = acc[tiles : 2 * tiles].astype(BF16)


def gather_rows(routes, rows, tiles):
    height = rows[0].shape[1]
    vmem = pl.BlockSpec(memory_space=pltpu.VMEM)
    shape = (tiles // 2, height, 128)
    return pl.pallas_call(
        gather_kernel,
        in_specs=[pl.BlockSpec(memory_space=pltpu.SMEM)] * 2 + [vmem] * 4,
        out_shape=[jax.ShapeDtypeStruct(shape, F32), jax.ShapeDtypeStruct(shape, BF16)],
        scratch_shapes=[pltpu.VMEM((tiles, height, 128), F32)],
        compiler_params=pltpu.CompilerParams(vmem_limit_bytes=VMEM),
        cost_estimate=pl.CostEstimate(flops=10**9, bytes_accessed=4 * 10**6, transcendentals=0),
        name="gather_rows",
    )(*routes, *rows)


def add_kernel(home, got, own, *away):
    for j in range(len(away) + 1):
        lo = j * TILE_DEV
        total = home[lo : lo + TILE_DEV] + got[lo : lo + TILE_DEV].astype(F32)
        if j == 0:
            own[...] = total
        else:
            away[j - 1][...] = total.astype(BF16)


def add_halves(home, got):
    shape = (TILE_DEV,) + home.shape[1:]
    others = home.shape[0] // TILE_DEV - 1
    return pl.pallas_call(
        add_kernel,
        out_shape=[jax.ShapeDtypeStruct(shape, F32)] + [jax.ShapeDtypeStruct(shape, BF16)] * others,
        compiler_params=pltpu.CompilerParams(vmem_limit_bytes=VMEM),
        cost_estimate=pl.CostEstimate(flops=10**8, bytes_accessed=2 * 10**6, transcendentals=0),
        name="add_halves",
    )(home, got)


def collapse_matrices():
    def across(src, dst, width):
        g = grow_matrix(width).T
        m = np.zeros((128, 128), np.float32)
        for ch in range(COLOURS):
            m[src + ch * width : src + (ch + 1) * width, dst + ch * 2 * width : dst + (ch + 1) * 2 * width] = g
        return m

    last = np.zeros((128, 384), np.float32)
    g = grow_matrix(32).T
    for ch in range(COLOURS):
        for half in range(2):
            last[ch * 32 : ch * 32 + 32, ch * 128 + half * 64 : ch * 128 + half * 64 + 64] = g

    def down(n, rows_in, rows_out, pick=None):
        g = grow_matrix(n)
        g = g if pick is None else g[pick::2]
        m = np.zeros((TILE_DEV * rows_out, TILE_DEV * rows_in), np.float32)
        for t in range(TILE_DEV):
            m[t * rows_out : t * rows_out + g.shape[0], t * rows_in : t * rows_in + n] = g
        return m

    mats = {"m43": across(96, 64, 4), "m32": across(64, 0, 8), "m21": across(0, 0, 16), "m10": last}
    mats |= {"d43": down(4, 16, 16), "d32": down(8, 16, 16), "d21": down(16, 16, 32)}
    mats |= {"even": down(32, 32, 32, 0), "odd": down(32, 32, 32, 1)}
    return pack(mats, 1280)


def collapse_kernel(places, each, packed, *refs):
    mats = unpack(packed, places)
    a, b, c = (refs[i * each : (i + 1) * each] for i in range(3))
    out, level0 = refs[3 * each :]

    def total(sources, lo, hi):
        acc = sources[0][:, lo:hi, :]
        for source in sources[1:]:
            acc = acc + source[:, lo:hi, :].astype(F32)
        return acc.reshape(TILE_DEV * (hi - lo), 128)

    lane = lane_index()
    small = total(b, 64, 80)
    bottom = small
    for lo, width, chans in ((0, 16, 3), (64, 8, 3), (96, 4, 3)):
        for ch in range(chans):
            inside = (lane >= lo + ch * width) & (lane < lo + (ch + 1) * width)
            bottom = jnp.where(inside, pltpu.roll(small, (128 - (3 - ch) * width) % 128, 1), bottom)
    small = small / jnp.maximum(bottom, 1.0)
    three = small + ldot(mats["d43"], rdot(small, mats["m43"]))
    two = small + ldot(mats["d32"], rdot(three, mats["m32"]))
    one = total(b, 32, 64)
    bottom = one
    for ch in range(3):
        inside = (lane >= ch * 32) & (lane < (ch + 1) * 32)
        bottom = jnp.where(inside, pltpu.roll(one, (128 - (3 - ch) * 32) % 128, 1), bottom)
    one = one / jnp.maximum(bottom, 1.0) + ldot(mats["d21"], rdot(two, mats["m21"]))
    wide = rdot(one, mats["m10"])
    hi, lo = split(wide)
    up = mm(mats["even"], hi) + mm(mats["even"], lo)
    down = mm(mats["odd"], hi) + mm(mats["odd"], lo)
    bottom = jnp.maximum(total(a, 0, 32), 1.0)
    for ch in range(COLOURS):
        own = total(b, 0, 32) if ch == 0 else total(c, 32 * (ch - 1), 32 * ch)
        back = jnp.where(lane < 64, up[:, ch * 128 : ch * 128 + 128], down[:, ch * 128 : ch * 128 + 128])
        level0[ch * 128 : ch * 128 + 128, :] = own / bottom + back
    for ch in range(COLOURS):
        for row in range(32):
            out[ch, :, row * 128 : row * 128 + 128] = level0[pl.ds(ch * 128 + row, TILE_DEV, stride=32), :]


def collapse(a, b, c):
    packed, places = collapse_matrices()
    tiles = pl.pallas_call(
        functools.partial(collapse_kernel, places, len(a)),
        out_shape=jax.ShapeDtypeStruct((COLOURS, TILE_DEV, 4096), F32),
        scratch_shapes=[pltpu.VMEM((COLOURS * 128, 128), F32)],
        compiler_params=pltpu.CompilerParams(vmem_limit_bytes=VMEM),
        cost_estimate=pl.CostEstimate(flops=10**9, bytes_accessed=3 * 10**6, transcendentals=0),
        name="collapse",
    )(packed, *a, *b, *c)
    return jnp.swapaxes(tiles, 0, 1)


def swap(value, axis, bit):
    size = lax.axis_size(axis)
    return lax.ppermute(value, axis, [(i, i ^ bit) for i in range(size)])


def local(frames, weight_map, seam_mask, strip_cell, partner, tile_group, tile_position_in_group):
    groups = lax.axis_size("frames")
    parts = lax.axis_size("tiles")
    mine = lax.axis_index("tiles")
    mask = lax.bitwise_xor(partner[0] // parts, lax.axis_index("frames"))

    ids = tile_group.reshape(QB) * (parts * TILE_DEV) + tile_position_in_group.reshape(QB)
    ids_core = swap(ids, "tiles", 1)
    ids_far = swap(ids, "tiles", 2)
    ids_far_core = swap(ids_far, "tiles", 1)
    ids = jnp.stack([ids, ids_core, ids_far, ids_far_core])
    group_size = parts * TILE_DEV
    owner = ids % group_size // TILE_DEV
    relative = lax.bitwise_xor(ids // group_size, lax.axis_index("frames"))
    relative = (relative & 1) * (groups // 2) + (relative >> 1)
    spot = jnp.where(owner == mine, relative * TILE_DEV + ids % TILE_DEV, -1)

    strips = strips_of(frames, strip_cell)
    strips, frames = lax.optimization_barrier((strips, frames))
    bit = 1
    while bit < groups:
        strips = jnp.where((mask & bit) != 0, swap(strips, "frames", bit), strips)
        bit *= 2

    weights, state = bands_of(frames, weight_map, seam_mask)
    routes = routes_of(spot)

    def spread(rows):
        far = swap(rows, "tiles", 2)
        return rows, swap(rows, "tiles", 1), far

    def send(rows, near, far):
        home, away = gather_rows(routes, (rows, near, far, swap(far, "tiles", 1)), groups * TILE_DEV)
        own, *away = add_halves(home, swap(away, "frames", 1))
        return [own] + [swap(part, "frames", 2 * (j + 1)) for j, part in enumerate(away)]

    weight_rows = spread(weights)
    weight_rows, routes, strips = lax.optimization_barrier((weight_rows, routes, strips))
    first, second = blend(strip_cell, strips, state)
    first_rows = spread(first)
    second_rows = spread(second)
    got_weights = send(*weight_rows)
    got_first = send(*first_rows)
    got_second = send(*second_rows)
    return collapse(got_weights, got_first, got_second)


def solution(mesh):
    in_specs = (
        P(("frames", "tiles"), None, None, None),
        P(("frames", "tiles"), None, None),
        P(("frames", "tiles"), None, None),
        P(("frames", "tiles")),
        P(("frames", "tiles")),
        P(("frames", "tiles"), None, None),
        P(("frames", "tiles"), None),
    )
    out_specs = P(("frames", "tiles"), None, None)
    return jax.shard_map(local, mesh=mesh, in_specs=in_specs, out_specs=out_specs, check_vma=False)
```

```python
import functools

import jax
import jax.numpy as jnp
import numpy as np
from jax import lax
from jax.experimental import pallas as pl
from jax.experimental.pallas import tpu as pltpu
from jax.sharding import PartitionSpec as P

COLOURS = 3
FH = 128
FW = 1024
QB = 32
WIN = 256
TILE_DEV = 4
VMEM = 30 << 20
ROUTE = 4096
F32 = jnp.float32
BF16 = jnp.bfloat16


def shrink_matrix(n):
    m = np.zeros((n // 2, n), np.float32)
    for i in range(n // 2):
        for d, tap in zip(range(-2, 3), (1, 4, 6, 4, 1)):
            m[i, min(max(2 * i + d, 0), n - 1)] += tap / 16.0
    return m


def grow_matrix(n):
    m = np.zeros((2 * n, n), np.float32)
    for i in range(n):
        lo, hi = max(i - 1, 0), min(i + 1, n - 1)
        m[2 * i, lo] += 1 / 8
        m[2 * i, i] += 6 / 8
        m[2 * i, hi] += 1 / 8
        m[2 * i + 1, i] += 1 / 2
        m[2 * i + 1, hi] += 1 / 2
    return m


def padded(m, rows, cols):
    return np.pad(m, ((0, rows - m.shape[0]), (0, cols - m.shape[1])))


def row_order():
    m = np.zeros((FH, FH), np.float32)
    for r in range(2):
        for par in range(2):
            for i in range(32):
                m[r * 64 + par * 32 + i, r * 64 + 2 * i + par] = 1
    return m


def vertical():
    v = {1: shrink_matrix(128), 2: shrink_matrix(64), 3: shrink_matrix(32)}
    spread = np.zeros((16, 8), np.float32)
    for r in range(2):
        for i in range(4):
            spread[r * 8 + i, r * 4 + i] = 1
    v[4] = spread @ shrink_matrix(16)
    g = {0: row_order() @ grow_matrix(64), 1: grow_matrix(32), 2: grow_matrix(16)}
    g[3] = grow_matrix(8) @ spread.T
    return v, g


def horizontal(width):
    s = {k: shrink_matrix(width >> (k - 1)).T for k in range(1, 5)}
    g = {k: grow_matrix(width >> (k + 1)).T for k in range(4)}
    return s, g


def shrink_window():
    m = np.zeros((512, 128), np.float32)
    for i in range(128):
        for d, tap in zip(range(-2, 3), (1, 4, 6, 4, 1)):
            m[128 + 2 * i + d, i] = tap / 16.0
    return m


def grow_window():
    m = np.zeros((384, 256), np.float32)
    for i in range(128):
        for d, tap in zip(range(-1, 2), (1, 6, 1)):
            m[128 + i + d, 2 * i] = tap / 8.0
        m[128 + i, 2 * i + 1] = m[128 + i + 1, 2 * i + 1] = 0.5
    return m


def pack(mats, width):
    places, row, col, height = {}, 0, 0, 0
    for name in sorted(mats, key=lambda n: (-mats[n].shape[0], -mats[n].shape[1], n)):
        h, w = mats[name].shape
        wide = -(-w // 128) * 128
        if col + wide > width:
            row, col, height = row + height, 0, 0
        height = max(height, -(-h // 16) * 16)
        places[name] = (row, col, h, w)
        col += wide
    out = np.zeros((row + height, width), np.float32)
    for name, (r, c, h, w) in places.items():
        out[r : r + h, c : c + w] = mats[name]
    return jnp.asarray(out, BF16), places


def unpack(ref, places):
    return {name: ref[r : r + h, c : c + w] for name, (r, c, h, w) in places.items()}


def small_matrices():
    v, g = vertical()
    s, gh = horizontal(WIN)
    sm, _ = horizontal(64)
    mats = {f"v{k}": m for k, m in v.items()} | {f"g{k}": m for k, m in g.items()}
    mats |= {f"s{k}": m for k, m in s.items()} | {f"h{k}": m for k, m in gh.items()}
    mats |= {f"m{k}": m for k, m in sm.items()} | {"order": row_order()}
    return pack(mats, 512)


def large_matrices():
    mats = {"shrink": shrink_window(), "grow": grow_window()}
    mats["last"] = padded(shrink_matrix(128).T, 128, 128)
    mats["least"] = padded(grow_matrix(64).T, 128, 128)
    return pack(mats, 640)


def levels_of(mats, letter):
    return {int(n[1:]): m for n, m in mats.items() if n[0] == letter and n[1:].isdigit()}


def mm(a, b):
    return jnp.dot(a, b, preferred_element_type=F32)


def split(v):
    hi = v.astype(BF16)
    return hi, (v - hi.astype(F32)).astype(BF16)


def rdot(v, m):
    hi, lo = split(v)
    return mm(hi, m) + mm(lo, m)


def ldot(m, v):
    hi, lo = split(v)
    return mm(m, hi) + mm(m, lo)


def mmt(a, b):
    return lax.dot_general(a, b, (((1,), (1,)), ((), ())), preferred_element_type=F32)


def windows(v, m, step):
    rows, width = v.shape
    both = jnp.concatenate(split(v), axis=0)
    left = jnp.broadcast_to(both[:, :1], (2 * rows, 128))
    right = jnp.broadcast_to(both[:, width - 1 :], (2 * rows, 128))
    both = jnp.concatenate([left, both, right], axis=1)
    pieces = []
    for n in range(width // step):
        piece = mm(both[:, n * step : n * step + step + 256], m)
        pieces.append(piece[:rows] + piece[rows:])
    return jnp.concatenate(pieces, axis=1)


def right_of(m):
    return lambda v: rdot(v, m)


def pyramid(planes, v, shrinks, product=mm):
    n = len(planes)
    t = jnp.concatenate([product(v[1], p) for p in planes], axis=0)
    levels = {1: shrinks[1](t)}
    for k in range(2, 5):
        prev = levels[k - 1]
        rows = prev.shape[0] // n
        t = jnp.concatenate([ldot(v[k], prev[i * rows : (i + 1) * rows]) for i in range(n)], axis=0)
        levels[k] = shrinks[k](t)
    return levels


def grown(level, n, gv, grow):
    h = grow(level)
    rows = level.shape[0] // n
    return [ldot(gv, h[i * rows : (i + 1) * rows]) for i in range(n)]


def place(rows, cols, base, width, offset):
    i = lax.broadcasted_iota(jnp.int32, (rows, cols), 0)
    c = lax.broadcasted_iota(jnp.int32, (rows, cols), 1)
    hit = (i >= base) & (i < base + width) & (c - i == offset - base)
    return jnp.where(hit, 1.0, 0.0).astype(BF16)


def strips_kernel(places, cell, xa, xb, packed, out, acc):
    mats = unpack(packed, places)
    v, gv, s, gh = (levels_of(mats, letter) for letter in "vgsh")
    s, gh = ({k: right_of(m) for k, m in each.items()} for each in (s, gh))
    order = mats["order"]
    first = window_tile(cell[0]) * 128
    planes = [jnp.concatenate([xa[0, c], xb[0, c]], axis=1) for c in range(COLOURS)]
    levels = pyramid(planes, v, s)
    back = grown(levels[1], COLOURS, gv[0], gh[0])
    b0 = jnp.concatenate([mm(order, planes[c]) - back[c] for c in range(COLOURS)], axis=0)
    bands = [b0.astype(BF16)]
    for k in range(1, 4):
        back = grown(levels[k + 1], COLOURS, gv[k], gh[k])
        bands.append((levels[k] - jnp.concatenate(back, axis=0)).astype(BF16))
    bands.append(levels[4].astype(BF16))
    start = cell[0] * 16 - first

    def pick(band, base, k):
        i = lax.broadcasted_iota(jnp.int32, (band.shape[1], 128), 0)
        c = lax.broadcasted_iota(jnp.int32, (band.shape[1], 128), 1)
        hit = (c >= base) & (c < base + (64 >> k)) & (i - c == (start >> k) - base)
        return mm(band, jnp.where(hit, 1.0, 0.0).astype(BF16))

    out[0:192, :] = (pick(bands[0][0:192], 0, 0) + pick(bands[0][192:384], 64, 0)).astype(BF16)
    acc[...] = pick(bands[1][0:96], 0, 1) + pick(bands[1][96:192], 32, 1) + pick(bands[2], 64, 2)
    acc[0:48, :] = acc[0:48, :] + pick(bands[3], 80, 3) + pick(bands[4], 88, 4)
    out[192:288, :] = acc[...].astype(BF16)


def window_tile(cell):
    return jnp.clip((cell - 3) >> 3, 0, (FW - WIN) // 128)


def full_spec(a):
    return pl.BlockSpec(a.shape, lambda *_: (0,) * a.ndim)


def strips_of(frames, cell):
    packed, places = small_matrices()
    grid_spec = pltpu.PrefetchScalarGridSpec(
        num_scalar_prefetch=1,
        grid=(1,),
        in_specs=[
            pl.BlockSpec((1, COLOURS, FH, 128), lambda i, c: (0, 0, 0, window_tile(c[0]))),
            pl.BlockSpec((1, COLOURS, FH, 128), lambda i, c: (0, 0, 0, window_tile(c[0]) + 1)),
        ]
        + [full_spec(packed)],
        out_specs=pl.BlockSpec((288, 128), lambda i, c: (0, 0)),
        scratch_shapes=[pltpu.VMEM((96, 128), F32)],
    )
    return pl.pallas_call(
        functools.partial(strips_kernel, places),
        grid_spec=grid_spec,
        out_shape=jax.ShapeDtypeStruct((288, 128), BF16),
        compiler_params=pltpu.CompilerParams(vmem_limit_bytes=VMEM),
        cost_estimate=pl.CostEstimate(flops=2 * 10**9, bytes_accessed=10**6, transcendentals=0),
        name="strips",
    )(cell, frames, frames, packed)


def lane_index():
    return lax.broadcasted_iota(jnp.int32, (1, 128), 1)


def fold_level0(p, store):
    left = lane_index() < 64
    for r in range(2):
        for j in range(8):
            even = p[r * 64 : r * 64 + 32, j * 128 : j * 128 + 128]
            odd = p[r * 64 + 32 : r * 64 + 64, j * 128 : j * 128 + 128]
            store(r * 16 + 2 * j, jnp.where(left, even, pltpu.roll(odd, 64, 1)))
            store(r * 16 + 2 * j + 1, jnp.where(left, pltpu.roll(even, 64, 1), odd))


def gather_channels(parts, width, cc, base):
    groups = 128 // width
    group = lane_index() // width
    out = jnp.zeros_like(parts[0])
    for ch in range(4):
        out = jnp.where(group == (cc + ch) % groups, parts[ch], out)
    return pltpu.roll(out, (base - cc * width) % 128, 1)


STATE_ROWS = 816


def state_views(state):
    at = lambda r, h, c, w: (slice(r, r + h), slice(c, c + w))
    b0 = [at(128 * c, 128, 0, 1024) for c in range(3)]
    l1 = [at(384, 64, 0, 512), at(384, 64, 512, 512), at(448, 64, 0, 512), at(448, 64, 512, 512)]
    l2 = [at(512, 32, 256 * c, 256) for c in range(4)]
    l3 = [at(544, 16, 128 * c, 128) for c in range(4)]
    l4 = [at(544, 16, 512 + 128 * c, 128) for c in range(4)]
    levels = [b0 + [at(560, 128, 0, 1024)], l1, l2, l3, l4]
    masks = [at(688, 128 >> k, 128 * k, 64 >> k) for k in range(4)] + [at(688, 16, 512, 4)]
    return levels, masks


def bands_kernel(small_places, large_places, x, w, m, small, large, wblocks, state):
    mats = unpack(small, small_places)
    v, gv, sm = (levels_of(mats, letter) for letter in "vgm")
    order = mats["order"]
    sm = {k: right_of(each) for k, each in sm.items()}
    mats = unpack(large, large_places)
    half = lambda each: windows(each, mats["shrink"], 256)
    twice = lambda each: windows(each, mats["grow"], 128)
    s = {1: half, 2: half, 3: half, 4: right_of(mats["last"])}
    gh = {0: twice, 1: twice, 2: twice, 3: right_of(mats["least"])}
    views, mask_views = state_views(state)
    planes = [x[0, c] for c in range(COLOURS)] + [w[0]]
    weights = mm(order, planes[3])
    state[views[0][3]] = weights

    def store(q, piece):
        wblocks[q] = piece.astype(BF16)

    fold_level0(weights, store)
    levels = pyramid(planes, v, s)
    for k in range(1, 5):
        rows = levels[k].shape[0] // 4
        state[views[k][3]] = levels[k][3 * rows :]
    back = grown(levels[1][: 3 * 64], COLOURS, gv[0], gh[0])
    for c in range(COLOURS):
        state[views[0][c]] = mm(order, planes[c]) - back[c]
    for k in range(1, 4):
        rows = levels[k].shape[0] // 4
        below = levels[k + 1].shape[0] // 4
        back = grown(levels[k + 1][: 3 * below], COLOURS, gv[k], gh[k])
        for c in range(COLOURS):
            state[views[k][c]] = levels[k][c * rows : (c + 1) * rows] - back[c]
    for c in range(COLOURS):
        state[views[4][c]] = levels[4][c * 16 : (c + 1) * 16]
    other = (1.0 - m[0].astype(F32)).astype(BF16)
    state[mask_views[0]] = mmt(order, other)
    masks = pyramid([other], v, sm, mmt)
    for k in range(1, 5):
        state[mask_views[k]] = masks[k]


def bands_of(frames, weight_map, seam_mask):
    small, small_places = small_matrices()
    large, large_places = large_matrices()
    return pl.pallas_call(
        functools.partial(bands_kernel, small_places, large_places),
        out_shape=[jax.ShapeDtypeStruct((QB, 32, 128), BF16), jax.ShapeDtypeStruct((STATE_ROWS, FW), F32)],
        compiler_params=pltpu.CompilerParams(vmem_limit_bytes=VMEM),
        cost_estimate=pl.CostEstimate(flops=8 * 10**9, bytes_accessed=6 * 10**6, transcendentals=0),
        name="bands",
    )(frames, weight_map, jnp.swapaxes(seam_mask, 1, 2), small, large)


def blend_kernel(cell, strips, state, first, second):
    views, mask_views = state_views(state)
    (b0, b1, b2, b3, b4) = [[state[view] for view in views[k][:3]] for k in range(5)]
    (wp, w1, w2, w3, w4) = [state[views[k][3]] for k in range(5)]
    (n0, n1, n2, n3, n4) = [state[view] for view in mask_views]
    start = cell[0] * 16
    low = strips[192:288]

    def mixed(band, remote, share):
        return band + share * (remote - band)

    widths = (1024, 512, 256, 128, 128)
    share0 = mm(n0.astype(BF16), place(64, 1024, 0, 64, start))
    share = [share0]
    for k, ref in enumerate((n1, n2, n3, n4)):
        share.append(rdot(ref, place(64 >> (k + 1), widths[k + 1], 0, 64 >> (k + 1), start >> (k + 1))))
    top = strips[0:192]
    remote0 = [mm(top, place(128, 1024, 0, 64, start)), mm(top, place(128, 1024, 64, 64, start))]
    remote0 = jnp.concatenate(remote0, axis=0)
    weights = wp
    for c in range(COLOURS):
        p = weights * mixed(b0[c], remote0[c * 128 : (c + 1) * 128], share[0])
        out, row = (first, 0) if c == 0 else (second, 32 * (c - 1))

        def store(q, piece, out=out, row=row):
            out[q, row : row + 32, :] = piece.astype(BF16)

        fold_level0(p, store)
    remote1 = [mm(low, place(128, 512, 0, 32, start >> 1)), mm(low, place(128, 512, 32, 32, start >> 1))]
    remote1 = jnp.concatenate(remote1, axis=0)
    parts = [w1 * mixed(b1[c], remote1[c * 64 : (c + 1) * 64], share[1]) for c in range(COLOURS)] + [w1]
    for r in range(2):
        for j in range(4):
            turned = [parts[ch][r * 32 : r * 32 + 32, j * 128 : j * 128 + 128] for ch in range(4)]
            turned = [turned[0]] + [pltpu.roll(turned[ch], 32 * ch, 1) for ch in range(1, 4)]
            for cc in range(4):
                first[r * 16 + 4 * j + cc, 32:64, :] = gather_channels(turned, 32, cc, 0).astype(BF16)
    remote2 = mm(low, place(128, 256, 64, 16, start >> 2))
    remote3 = mm(low[0:48], place(128, 128, 80, 8, start >> 3))
    remote4 = mm(low[0:48], place(128, 128, 88, 4, start >> 4))
    parts2 = [w2 * mixed(b2[c], remote2[c * 32 : (c + 1) * 32], share[2]) for c in range(COLOURS)] + [w2]
    parts3 = [w3 * mixed(b3[c], remote3[c * 16 : (c + 1) * 16], share[3]) for c in range(COLOURS)] + [w3]
    parts4 = [w4 * mixed(b4[c], remote4[c * 16 : (c + 1) * 16], share[4]) for c in range(COLOURS)] + [w4]
    lane = lane_index()
    for r in range(2):
        turned3 = [pltpu.roll(parts3[ch][r * 8 : r * 8 + 8], 8 * ch, 1) for ch in range(4)]
        turned4 = [pltpu.roll(parts4[ch][r * 8 : r * 8 + 8], 4 * ch, 1) for ch in range(4)]
        for j in range(2):
            turned2 = [parts2[ch][r * 16 : r * 16 + 16, j * 128 : j * 128 + 128] for ch in range(4)]
            turned2 = [pltpu.roll(turned2[ch], 16 * ch, 1) for ch in range(4)]
            for cc in range(8):
                c = j * 8 + cc
                two = gather_channels(turned2, 16, cc, 0)
                three = gather_channels(turned3, 8, c, 64)
                four = gather_channels(turned4, 4, c, 96)
                head = jnp.where(lane < 64, two[0:8], jnp.where(lane < 96, three, four))
                tail = jnp.where(lane < 64, two[8:16], 0.0)
                first[r * 16 + c, 64:80, :] = jnp.concatenate([head, tail], axis=0).astype(BF16)


def blend(cell, strips, state):
    vmem = pl.BlockSpec(memory_space=pltpu.VMEM)
    return pl.pallas_call(
        blend_kernel,
        in_specs=[pl.BlockSpec(memory_space=pltpu.SMEM)] + [vmem] * 2,
        out_shape=[jax.ShapeDtypeStruct((QB, 80, 128), BF16), jax.ShapeDtypeStruct((QB, 64, 128), BF16)],
        compiler_params=pltpu.CompilerParams(vmem_limit_bytes=VMEM),
        cost_estimate=pl.CostEstimate(flops=4 * 10**9, bytes_accessed=4 * 10**6, transcendentals=0),
        name="blend",
    )(cell, strips, state)


def routes_kernel(spot, lists, counts):
    for source in range(4):

        def body(q, count, source=source):
            at = spot[source, q]
            lists[source, count] = q * ROUTE + at
            return jnp.where(at >= 0, count + 1, count)

        counts[source] = lax.fori_loop(0, QB, body, 0)


def routes_of(spot):
    smem = pl.BlockSpec(memory_space=pltpu.SMEM)
    return pl.pallas_call(
        routes_kernel,
        in_specs=[smem],
        out_specs=[smem, smem],
        out_shape=[jax.ShapeDtypeStruct((4, QB + 1), jnp.int32), jax.ShapeDtypeStruct((4,), jnp.int32)],
        name="routes",
    )(spot)


def gather_kernel(lists, counts, a, b, c, d, home, away, acc):
    acc[...] = jnp.zeros_like(acc)
    for source, ref in enumerate((a, b, c, d)):

        def body(i, carry, source=source, ref=ref):
            entry = lists[source, i]
            q, at = entry // ROUTE, entry % ROUTE
            acc[at] = acc[at] + ref[q].astype(F32)
            return carry

        lax.fori_loop(0, counts[source], body, 0)
    tiles = home.shape[0]
    home[...] = acc[0:tiles]
    away[...] = acc[tiles : 2 * tiles].astype(BF16)


def gather_rows(routes, rows, tiles):
    height = rows[0].shape[1]
    vmem = pl.BlockSpec(memory_space=pltpu.VMEM)
    shape = (tiles // 2, height, 128)
    return pl.pallas_call(
        gather_kernel,
        in_specs=[pl.BlockSpec(memory_space=pltpu.SMEM)] * 2 + [vmem] * 4,
        out_shape=[jax.ShapeDtypeStruct(shape, F32), jax.ShapeDtypeStruct(shape, BF16)],
        scratch_shapes=[pltpu.VMEM((tiles, height, 128), F32)],
        compiler_params=pltpu.CompilerParams(vmem_limit_bytes=VMEM),
        cost_estimate=pl.CostEstimate(flops=10**9, bytes_accessed=4 * 10**6, transcendentals=0),
        name="gather_rows",
    )(*routes, *rows)


def add_kernel(home, got, own, *away):
    for j in range(len(away) + 1):
        lo = j * TILE_DEV
        total = home[lo : lo + TILE_DEV] + got[lo : lo + TILE_DEV].astype(F32)
        if j == 0:
            own[...] = total
        else:
            away[j - 1][...] = total.astype(BF16)


def add_halves(home, got):
    shape = (TILE_DEV,) + home.shape[1:]
    others = home.shape[0] // TILE_DEV - 1
    return pl.pallas_call(
        add_kernel,
        out_shape=[jax.ShapeDtypeStruct(shape, F32)] + [jax.ShapeDtypeStruct(shape, BF16)] * others,
        compiler_params=pltpu.CompilerParams(vmem_limit_bytes=VMEM),
        cost_estimate=pl.CostEstimate(flops=10**8, bytes_accessed=2 * 10**6, transcendentals=0),
        name="add_halves",
    )(home, got)


def collapse_matrices():
    def across(src, dst, width):
        g = grow_matrix(width).T
        m = np.zeros((128, 128), np.float32)
        for ch in range(COLOURS):
            m[src + ch * width : src + (ch + 1) * width, dst + ch * 2 * width : dst + (ch + 1) * 2 * width] = g
        return m

    last = np.zeros((128, 384), np.float32)
    g = grow_matrix(32).T
    for ch in range(COLOURS):
        for half in range(2):
            last[ch * 32 : ch * 32 + 32, ch * 128 + half * 64 : ch * 128 + half * 64 + 64] = g

    def down(n, rows_in, rows_out, pick=None):
        g = grow_matrix(n)
        g = g if pick is None else g[pick::2]
        m = np.zeros((TILE_DEV * rows_out, TILE_DEV * rows_in), np.float32)
        for t in range(TILE_DEV):
            m[t * rows_out : t * rows_out + g.shape[0], t * rows_in : t * rows_in + n] = g
        return m

    mats = {"m43": across(96, 64, 4), "m32": across(64, 0, 8), "m21": across(0, 0, 16), "m10": last}
    mats |= {"d43": down(4, 16, 16), "d32": down(8, 16, 16), "d21": down(16, 16, 32)}
    mats |= {"even": down(32, 32, 32, 0), "odd": down(32, 32, 32, 1)}
    return pack(mats, 1280)


def collapse_kernel(places, each, packed, *refs):
    mats = unpack(packed, places)
    a, b, c = (refs[i * each : (i + 1) * each] for i in range(3))
    out, level0 = refs[3 * each :]

    def total(sources, lo, hi):
        acc = sources[0][:, lo:hi, :]
        for source in sources[1:]:
            acc = acc + source[:, lo:hi, :].astype(F32)
        return acc.reshape(TILE_DEV * (hi - lo), 128)

    lane = lane_index()
    small = total(b, 64, 80)
    bottom = small
    for lo, width, chans in ((0, 16, 3), (64, 8, 3), (96, 4, 3)):
        for ch in range(chans):
            inside = (lane >= lo + ch * width) & (lane < lo + (ch + 1) * width)
            bottom = jnp.where(inside, pltpu.roll(small, (128 - (3 - ch) * width) % 128, 1), bottom)
    small = small / jnp.maximum(bottom, 1.0)
    three = small + ldot(mats["d43"], rdot(small, mats["m43"]))
    two = small + ldot(mats["d32"], rdot(three, mats["m32"]))
    one = total(b, 32, 64)
    bottom = one
    for ch in range(3):
        inside = (lane >= ch * 32) & (lane < (ch + 1) * 32)
        bottom = jnp.where(inside, pltpu.roll(one, (128 - (3 - ch) * 32) % 128, 1), bottom)
    one = one / jnp.maximum(bottom, 1.0) + ldot(mats["d21"], rdot(two, mats["m21"]))
    wide = rdot(one, mats["m10"])
    hi, lo = split(wide)
    up = mm(mats["even"], hi) + mm(mats["even"], lo)
    down = mm(mats["odd"], hi) + mm(mats["odd"], lo)
    bottom = jnp.maximum(total(a, 0, 32), 1.0)
    for ch in range(COLOURS):
        own = total(b, 0, 32) if ch == 0 else total(c, 32 * (ch - 1), 32 * ch)
        back = jnp.where(lane < 64, up[:, ch * 128 : ch * 128 + 128], down[:, ch * 128 : ch * 128 + 128])
        level0[ch * 128 : ch * 128 + 128, :] = own / bottom + back
    for ch in range(COLOURS):
        for row in range(32):
            out[ch, :, row * 128 : row * 128 + 128] = level0[pl.ds(ch * 128 + row, TILE_DEV, stride=32), :]


def collapse(a, b, c):
    packed, places = collapse_matrices()
    tiles = pl.pallas_call(
        functools.partial(collapse_kernel, places, len(a)),
        out_shape=jax.ShapeDtypeStruct((COLOURS, TILE_DEV, 4096), F32),
        scratch_shapes=[pltpu.VMEM((COLOURS * 128, 128), F32)],
        compiler_params=pltpu.CompilerParams(vmem_limit_bytes=VMEM),
        cost_estimate=pl.CostEstimate(flops=10**9, bytes_accessed=3 * 10**6, transcendentals=0),
        name="collapse",
    )(packed, *a, *b, *c)
    return jnp.swapaxes(tiles, 0, 1)


def swap(value, axis, bit):
    size = lax.axis_size(axis)
    return lax.ppermute(value, axis, [(i, i ^ bit) for i in range(size)])


def local(frames, weight_map, seam_mask, strip_cell, partner, tile_group, tile_position_in_group):
    groups = lax.axis_size("frames")
    parts = lax.axis_size("tiles")
    mine = lax.axis_index("tiles")
    mask = lax.bitwise_xor(partner[0] // parts, lax.axis_index("frames"))

    ids = tile_group.reshape(QB) * (parts * TILE_DEV) + tile_position_in_group.reshape(QB)
    ids_core = swap(ids, "tiles", 1)
    ids_far = swap(ids, "tiles", 2)
    ids_far_core = swap(ids_far, "tiles", 1)
    ids = jnp.stack([ids, ids_core, ids_far, ids_far_core])
    group_size = parts * TILE_DEV
    owner = ids % group_size // TILE_DEV
    relative = lax.bitwise_xor(ids // group_size, lax.axis_index("frames"))
    relative = (relative & 1) * (groups // 2) + (relative >> 1)
    spot = jnp.where(owner == mine, relative * TILE_DEV + ids % TILE_DEV, -1)

    routes = routes_of(spot)
    strips = strips_of(frames, strip_cell)
    strips, frames = lax.optimization_barrier((strips, frames))
    weights, state = bands_of(frames, weight_map, seam_mask)
    bit = 1
    while bit < groups:
        got = swap(strips, "frames", bit)
        if bit == 1:
            got, weights, state = lax.optimization_barrier((got, weights, state))
        strips = jnp.where((mask & bit) != 0, got, strips)
        bit *= 2

    tie = lax.optimization_barrier

    def gather(rows, near, far, far_near):
        return gather_rows(routes, (rows, near, far, far_near), groups * TILE_DEV)

    def along(own, *away):
        return [own] + [swap(part, "frames", 2 * (j + 1)) for j, part in enumerate(away)]

    far = swap(weights, "tiles", 2)
    home, away = gather(weights, swap(weights, "tiles", 1), far, swap(far, "tiles", 1))
    home, away, strips = tie((home, away, strips))
    first, second = blend(strip_cell, strips, state)
    far = swap(first, "tiles", 2)
    near = swap(first, "tiles", 1)
    sums = add_halves(home, swap(away, "frames", 1))
    far, near, sums, second = tie((far, near, sums, second))
    got_weights = along(*sums)
    far_second = swap(second, "tiles", 2)
    near_second = swap(second, "tiles", 1)
    home, away = gather(first, near, far, swap(far, "tiles", 1))
    got = swap(away, "frames", 1)
    far_second, got, got_weights = tie((far_second, got, got_weights))
    far_near = swap(far_second, "tiles", 1)
    sums = add_halves(home, got)
    far_near, sums = tie((far_near, sums))
    got_first = along(*sums)
    home, away = gather(second, near_second, far_second, far_near)
    got = swap(away, "frames", 1)
    got, got_first = tie((got, got_first))
    got_second = along(*add_halves(home, got))
    return collapse(got_weights, got_first, got_second)


def solution(mesh):
    in_specs = (
        P(("frames", "tiles"), None, None, None),
        P(("frames", "tiles"), None, None),
        P(("frames", "tiles"), None, None),
        P(("frames", "tiles")),
        P(("frames", "tiles")),
        P(("frames", "tiles"), None, None),
        P(("frames", "tiles"), None),
    )
    out_specs = P(("frames", "tiles"), None, None)
    return jax.shard_map(local, mesh=mesh, in_specs=in_specs, out_specs=out_specs, check_vma=False)
```

```python
import functools

import jax
import jax.numpy as jnp
import numpy as np
from jax import lax
from jax.experimental import pallas as pl
from jax.experimental.pallas import tpu as pltpu
from jax.sharding import PartitionSpec as P

COLOURS = 3
FH = 128
FW = 1024
QB = 32
WIN = 256
TILE_DEV = 4
VMEM = 30 << 20
ROUTE = 4096
FREE = 28
PATCH = 144
HALF = 96
F32 = jnp.float32
BF16 = jnp.bfloat16


def shrink_matrix(n):
    m = np.zeros((n // 2, n), np.float32)
    for i in range(n // 2):
        for d, tap in zip(range(-2, 3), (1, 4, 6, 4, 1)):
            m[i, min(max(2 * i + d, 0), n - 1)] += tap / 16.0
    return m


def grow_matrix(n):
    m = np.zeros((2 * n, n), np.float32)
    for i in range(n):
        lo, hi = max(i - 1, 0), min(i + 1, n - 1)
        m[2 * i, lo] += 1 / 8
        m[2 * i, i] += 6 / 8
        m[2 * i, hi] += 1 / 8
        m[2 * i + 1, i] += 1 / 2
        m[2 * i + 1, hi] += 1 / 2
    return m


def padded(m, rows, cols):
    return np.pad(m, ((0, rows - m.shape[0]), (0, cols - m.shape[1])))


def row_order():
    m = np.zeros((FH, FH), np.float32)
    for r in range(2):
        for par in range(2):
            for i in range(32):
                m[r * 64 + par * 32 + i, r * 64 + 2 * i + par] = 1
    return m


def vertical():
    v = {1: shrink_matrix(128), 2: shrink_matrix(64), 3: shrink_matrix(32)}
    spread = np.zeros((16, 8), np.float32)
    for r in range(2):
        for i in range(4):
            spread[r * 8 + i, r * 4 + i] = 1
    v[4] = spread @ shrink_matrix(16)
    g = {0: row_order() @ grow_matrix(64), 1: grow_matrix(32), 2: grow_matrix(16)}
    g[3] = grow_matrix(8) @ spread.T
    return v, g


def horizontal(width):
    s = {k: shrink_matrix(width >> (k - 1)).T for k in range(1, 5)}
    g = {k: grow_matrix(width >> (k + 1)).T for k in range(4)}
    return s, g


def shrink_window():
    m = np.zeros((512, 128), np.float32)
    for i in range(128):
        for d, tap in zip(range(-2, 3), (1, 4, 6, 4, 1)):
            m[128 + 2 * i + d, i] = tap / 16.0
    return m


def grow_window():
    m = np.zeros((384, 256), np.float32)
    for i in range(128):
        for d, tap in zip(range(-1, 2), (1, 6, 1)):
            m[128 + i + d, 2 * i] = tap / 8.0
        m[128 + i, 2 * i + 1] = m[128 + i + 1, 2 * i + 1] = 0.5
    return m


def pack(mats, width):
    places, row, col, height = {}, 0, 0, 0
    for name in sorted(mats, key=lambda n: (-mats[n].shape[0], -mats[n].shape[1], n)):
        h, w = mats[name].shape
        wide = -(-w // 128) * 128
        if col + wide > width:
            row, col, height = row + height, 0, 0
        height = max(height, -(-h // 16) * 16)
        places[name] = (row, col, h, w)
        col += wide
    out = np.zeros((row + height, width), np.float32)
    for name, (r, c, h, w) in places.items():
        out[r : r + h, c : c + w] = mats[name]
    return jnp.asarray(out, BF16), places


def unpack(ref, places):
    return {name: ref[r : r + h, c : c + w] for name, (r, c, h, w) in places.items()}


def small_matrices():
    v, g = vertical()
    s, gh = horizontal(WIN)
    sm, _ = horizontal(64)
    mats = {f"v{k}": m for k, m in v.items()} | {f"g{k}": m for k, m in g.items()}
    mats |= {f"s{k}": m for k, m in s.items()} | {f"h{k}": m for k, m in gh.items()}
    mats |= {f"m{k}": m for k, m in sm.items()} | {"order": row_order()}
    return pack(mats, 512)


def large_matrices():
    mats = {"shrink": shrink_window(), "grow": grow_window()}
    mats["last"] = padded(shrink_matrix(128).T, 128, 128)
    mats["least"] = padded(grow_matrix(64).T, 128, 128)
    return pack(mats, 640)


def levels_of(mats, letter):
    return {int(n[1:]): m for n, m in mats.items() if n[0] == letter and n[1:].isdigit()}


def mm(a, b):
    return jnp.dot(a, b, preferred_element_type=F32)


def split(v):
    hi = v.astype(BF16)
    return hi, (v - hi.astype(F32)).astype(BF16)


def rdot(v, m):
    hi, lo = split(v)
    return mm(hi, m) + mm(lo, m)


def ldot(m, v):
    hi, lo = split(v)
    return mm(m, hi) + mm(m, lo)


def mmt(a, b):
    return lax.dot_general(a, b, (((1,), (1,)), ((), ())), preferred_element_type=F32)


def windows(v, m, step):
    rows, width = v.shape
    both = jnp.concatenate(split(v), axis=0)
    left = jnp.broadcast_to(both[:, :1], (2 * rows, 128))
    right = jnp.broadcast_to(both[:, width - 1 :], (2 * rows, 128))
    both = jnp.concatenate([left, both, right], axis=1)
    pieces = []
    for n in range(width // step):
        piece = mm(both[:, n * step : n * step + step + 256], m)
        pieces.append(piece[:rows] + piece[rows:])
    return jnp.concatenate(pieces, axis=1)


def right_of(m):
    return lambda v: rdot(v, m)


def pyramid(planes, v, shrinks, product=mm):
    n = len(planes)
    t = jnp.concatenate([product(v[1], p) for p in planes], axis=0)
    levels = {1: shrinks[1](t)}
    for k in range(2, 5):
        prev = levels[k - 1]
        rows = prev.shape[0] // n
        t = jnp.concatenate([ldot(v[k], prev[i * rows : (i + 1) * rows]) for i in range(n)], axis=0)
        levels[k] = shrinks[k](t)
    return levels


def grown(level, n, gv, grow):
    h = grow(level)
    rows = level.shape[0] // n
    return [ldot(gv, h[i * rows : (i + 1) * rows]) for i in range(n)]


def place(rows, cols, base, width, offset):
    i = lax.broadcasted_iota(jnp.int32, (rows, cols), 0)
    c = lax.broadcasted_iota(jnp.int32, (rows, cols), 1)
    hit = (i >= base) & (i < base + width) & (c - i == offset - base)
    return jnp.where(hit, 1.0, 0.0).astype(BF16)


def strips_kernel(places, cell, xa, xb, packed, out, acc):
    mats = unpack(packed, places)
    v, gv, s, gh = (levels_of(mats, letter) for letter in "vgsh")
    s, gh = ({k: right_of(m) for k, m in each.items()} for each in (s, gh))
    order = mats["order"]
    first = window_tile(cell[0]) * 128
    planes = [jnp.concatenate([xa[0, c], xb[0, c]], axis=1) for c in range(COLOURS)]
    levels = pyramid(planes, v, s)
    back = grown(levels[1], COLOURS, gv[0], gh[0])
    b0 = jnp.concatenate([mm(order, planes[c]) - back[c] for c in range(COLOURS)], axis=0)
    bands = [b0.astype(BF16)]
    for k in range(1, 4):
        back = grown(levels[k + 1], COLOURS, gv[k], gh[k])
        bands.append((levels[k] - jnp.concatenate(back, axis=0)).astype(BF16))
    bands.append(levels[4].astype(BF16))
    start = cell[0] * 16 - first

    def pick(band, base, k):
        i = lax.broadcasted_iota(jnp.int32, (band.shape[1], 128), 0)
        c = lax.broadcasted_iota(jnp.int32, (band.shape[1], 128), 1)
        hit = (c >= base) & (c < base + (64 >> k)) & (i - c == (start >> k) - base)
        return mm(band, jnp.where(hit, 1.0, 0.0).astype(BF16))

    out[0:192, :] = (pick(bands[0][0:192], 0, 0) + pick(bands[0][192:384], 64, 0)).astype(BF16)
    acc[...] = pick(bands[1][0:96], 0, 1) + pick(bands[1][96:192], 32, 1) + pick(bands[2], 64, 2)
    acc[0:48, :] = acc[0:48, :] + pick(bands[3], 80, 3) + pick(bands[4], 88, 4)
    out[192:288, :] = acc[...].astype(BF16)


def window_tile(cell):
    return jnp.clip((cell - 3) >> 3, 0, (FW - WIN) // 128)


def full_spec(a):
    return pl.BlockSpec(a.shape, lambda *_: (0,) * a.ndim)


def strips_of(frames, cell):
    packed, places = small_matrices()
    grid_spec = pltpu.PrefetchScalarGridSpec(
        num_scalar_prefetch=1,
        grid=(1,),
        in_specs=[
            pl.BlockSpec((1, COLOURS, FH, 128), lambda i, c: (0, 0, 0, window_tile(c[0]))),
            pl.BlockSpec((1, COLOURS, FH, 128), lambda i, c: (0, 0, 0, window_tile(c[0]) + 1)),
        ]
        + [full_spec(packed)],
        out_specs=pl.BlockSpec((288, 128), lambda i, c: (0, 0)),
        scratch_shapes=[pltpu.VMEM((96, 128), F32)],
    )
    return pl.pallas_call(
        functools.partial(strips_kernel, places),
        grid_spec=grid_spec,
        out_shape=jax.ShapeDtypeStruct((288, 128), BF16),
        compiler_params=pltpu.CompilerParams(vmem_limit_bytes=VMEM),
        cost_estimate=pl.CostEstimate(flops=10**6, bytes_accessed=10**4, transcendentals=0),
        name="strips",
    )(cell, frames, frames, packed)


def lane_index():
    return lax.broadcasted_iota(jnp.int32, (1, 128), 1)


def slot_of(c, left):
    return jnp.where(c < left, c, jnp.where(c < left + 2, c - left + 14, c - 2))


def left_column(cell):
    return jnp.minimum(cell // 4, 14)


def fold_level0(p, store):
    left = lane_index() < 64
    for r in range(2):
        for j in range(8):
            even = p[r * 64 : r * 64 + 32, j * 128 : j * 128 + 128]
            odd = p[r * 64 + 32 : r * 64 + 64, j * 128 : j * 128 + 128]
            store(r, 2 * j, jnp.where(left, even, pltpu.roll(odd, 64, 1)))
            store(r, 2 * j + 1, jnp.where(left, pltpu.roll(even, 64, 1), odd))


def cut(level0, parts1, parts2, parts3, parts4, put):
    for ch in range(COLOURS):
        row = (0, 32, 96)[ch]
        fold_level0(level0(ch), lambda r, c, piece, row=row: put(r, c, row, piece))
    for r in range(2):
        for j in range(4):
            turned = [parts1[ch][r * 32 : r * 32 + 32, j * 128 : j * 128 + 128] for ch in range(4)]
            turned = [turned[0]] + [pltpu.roll(turned[ch], 32 * ch, 1) for ch in range(1, 4)]
            for cc in range(4):
                put(r, 4 * j + cc, 64, gather_channels(turned, 32, cc, 0))
    lane = lane_index()
    for r in range(2):
        turned3 = [pltpu.roll(parts3[ch][r * 8 : r * 8 + 8], 8 * ch, 1) for ch in range(4)]
        turned4 = [pltpu.roll(parts4[ch][r * 8 : r * 8 + 8], 4 * ch, 1) for ch in range(4)]
        for j in range(2):
            turned2 = [parts2[ch][r * 16 : r * 16 + 16, j * 128 : j * 128 + 128] for ch in range(4)]
            turned2 = [pltpu.roll(turned2[ch], 16 * ch, 1) for ch in range(4)]
            for cc in range(8):
                c = j * 8 + cc
                two = gather_channels(turned2, 16, cc, 0)
                three = gather_channels(turned3, 8, c, 64)
                four = gather_channels(turned4, 4, c, 96)
                head = jnp.where(lane < 64, two[0:8], jnp.where(lane < 96, three, four))
                tail = jnp.where(lane < 64, two[8:16], 0.0)
                put(r, c, 128, jnp.concatenate([head, tail], axis=0))


def gather_channels(parts, width, cc, base):
    groups = 128 // width
    group = lane_index() // width
    out = jnp.zeros_like(parts[0])
    for ch in range(4):
        out = jnp.where(group == (cc + ch) % groups, parts[ch], out)
    return pltpu.roll(out, (base - cc * width) % 128, 1)


STATE_ROWS = 816


def state_views(state):
    at = lambda r, h, c, w: (slice(r, r + h), slice(c, c + w))
    b0 = [at(128 * c, 128, 0, 1024) for c in range(3)]
    l1 = [at(384, 64, 0, 512), at(384, 64, 512, 512), at(448, 64, 0, 512), at(448, 64, 512, 512)]
    l2 = [at(512, 32, 256 * c, 256) for c in range(4)]
    l3 = [at(544, 16, 128 * c, 128) for c in range(4)]
    l4 = [at(544, 16, 512 + 128 * c, 128) for c in range(4)]
    levels = [b0 + [at(560, 128, 0, 1024)], l1, l2, l3, l4]
    masks = [at(688, 128 >> k, 128 * k, 64 >> k) for k in range(4)] + [at(688, 16, 512, 4)]
    return levels, masks


def bands_kernel(small_places, large_places, cell, x, w, m, small, large, wblocks, first, second, state):
    mats = unpack(small, small_places)
    v, gv, sm = (levels_of(mats, letter) for letter in "vgm")
    order = mats["order"]
    sm = {k: right_of(each) for k, each in sm.items()}
    mats = unpack(large, large_places)
    half = lambda each: windows(each, mats["shrink"], 256)
    twice = lambda each: windows(each, mats["grow"], 128)
    s = {1: half, 2: half, 3: half, 4: right_of(mats["last"])}
    gh = {0: twice, 1: twice, 2: twice, 3: right_of(mats["least"])}
    views, mask_views = state_views(state)
    planes = [x[0, c] for c in range(COLOURS)] + [w[0]]
    weights = mm(order, planes[3])
    state[views[0][3]] = weights

    left = left_column(cell[0])

    def store(r, c, piece):
        wblocks[slot_of(c, left) * 2 + r] = piece.astype(BF16)

    fold_level0(weights, store)
    levels = pyramid(planes, v, s)
    for k in range(1, 5):
        rows = levels[k].shape[0] // 4
        state[views[k][3]] = levels[k][3 * rows :]
    back = grown(levels[1][: 3 * 64], COLOURS, gv[0], gh[0])
    for c in range(COLOURS):
        state[views[0][c]] = mm(order, planes[c]) - back[c]
    for k in range(1, 4):
        rows = levels[k].shape[0] // 4
        below = levels[k + 1].shape[0] // 4
        back = grown(levels[k + 1][: 3 * below], COLOURS, gv[k], gh[k])
        for c in range(COLOURS):
            state[views[k][c]] = levels[k][c * rows : (c + 1) * rows] - back[c]
    for c in range(COLOURS):
        state[views[4][c]] = levels[4][c * 16 : (c + 1) * 16]
    other = (1.0 - m[0].astype(F32)).astype(BF16)
    state[mask_views[0]] = mmt(order, other)
    masks = pyramid([other], v, sm, mmt)
    for k in range(1, 5):
        state[mask_views[k]] = masks[k]

    def put(r, c, row, piece):
        slot = slot_of(c, left)
        out, at = (first, row) if row < HALF else (second, row - HALF)

        @pl.when(slot < 14)
        def _():
            out[slot * 2 + r, at : at + piece.shape[0], :] = piece.astype(BF16)

    parts = [None]
    for k in range(1, 5):
        wk = state[views[k][3]]
        parts.append([wk * state[views[k][c]] for c in range(COLOURS)] + [wk])
    cut(lambda ch: weights * state[views[0][ch]], *parts[1:], put)


def bands_of(cell, frames, weight_map, seam_mask):
    small, small_places = small_matrices()
    large, large_places = large_matrices()
    return pl.pallas_call(
        functools.partial(bands_kernel, small_places, large_places),
        in_specs=[pl.BlockSpec(memory_space=pltpu.SMEM)] + [pl.BlockSpec(memory_space=pltpu.VMEM)] * 5,
        out_shape=[
            jax.ShapeDtypeStruct((QB, 32, 128), BF16),
            jax.ShapeDtypeStruct((FREE, HALF, 128), BF16),
            jax.ShapeDtypeStruct((FREE, PATCH - HALF, 128), BF16),
            jax.ShapeDtypeStruct((STATE_ROWS, FW), F32),
        ],
        compiler_params=pltpu.CompilerParams(vmem_limit_bytes=VMEM),
        cost_estimate=pl.CostEstimate(flops=10**6, bytes_accessed=10**4, transcendentals=0),
        name="bands",
    )(cell, frames, weight_map, jnp.swapaxes(seam_mask, 1, 2), small, large)


def blend_kernel(cell, strips, state, patch):
    views, mask_views = state_views(state)
    (b0, b1, b2, b3, b4) = [[state[view] for view in views[k][:3]] for k in range(5)]
    (wp, w1, w2, w3, w4) = [state[views[k][3]] for k in range(5)]
    (n0, n1, n2, n3, n4) = [state[view] for view in mask_views]
    start = cell[0] * 16
    low = strips[192:288]

    def mixed(band, remote, share):
        return band + share * (remote - band)

    widths = (1024, 512, 256, 128, 128)
    share0 = mm(n0.astype(BF16), place(64, 1024, 0, 64, start))
    share = [share0]
    for k, ref in enumerate((n1, n2, n3, n4)):
        share.append(rdot(ref, place(64 >> (k + 1), widths[k + 1], 0, 64 >> (k + 1), start >> (k + 1))))
    top = strips[0:192]
    remote0 = [mm(top, place(128, 1024, 0, 64, start)), mm(top, place(128, 1024, 64, 64, start))]
    remote0 = jnp.concatenate(remote0, axis=0)

    left = left_column(cell[0])

    def put(r, c, row, piece):
        slot = slot_of(c, left)

        @pl.when(slot >= 14)
        def _():
            patch[(slot - 14) * 2 + r, row : row + piece.shape[0], :] = piece.astype(BF16)

    remote1 = [mm(low, place(128, 512, 0, 32, start >> 1)), mm(low, place(128, 512, 32, 32, start >> 1))]
    remote1 = jnp.concatenate(remote1, axis=0)
    parts1 = [w1 * mixed(b1[c], remote1[c * 64 : (c + 1) * 64], share[1]) for c in range(COLOURS)] + [w1]
    remote2 = mm(low, place(128, 256, 64, 16, start >> 2))
    remote3 = mm(low[0:48], place(128, 128, 80, 8, start >> 3))
    remote4 = mm(low[0:48], place(128, 128, 88, 4, start >> 4))
    parts2 = [w2 * mixed(b2[c], remote2[c * 32 : (c + 1) * 32], share[2]) for c in range(COLOURS)] + [w2]
    parts3 = [w3 * mixed(b3[c], remote3[c * 16 : (c + 1) * 16], share[3]) for c in range(COLOURS)] + [w3]
    parts4 = [w4 * mixed(b4[c], remote4[c * 16 : (c + 1) * 16], share[4]) for c in range(COLOURS)] + [w4]
    cut(lambda c: wp * mixed(b0[c], remote0[c * 128 : (c + 1) * 128], share[0]), parts1, parts2, parts3, parts4, put)


def blend(cell, strips, state):
    vmem = pl.BlockSpec(memory_space=pltpu.VMEM)
    return pl.pallas_call(
        blend_kernel,
        in_specs=[pl.BlockSpec(memory_space=pltpu.SMEM)] + [vmem] * 2,
        out_shape=jax.ShapeDtypeStruct((QB - FREE, PATCH, 128), BF16),
        compiler_params=pltpu.CompilerParams(vmem_limit_bytes=VMEM),
        cost_estimate=pl.CostEstimate(flops=10**6, bytes_accessed=10**4, transcendentals=0),
        name="blend",
    )(cell, strips, state)


def routes_kernel(spot, lists, counts):
    for source in range(4):

        def body(q, count, source=source):
            at = spot[source, q]
            lists[source, count] = q * ROUTE + at
            return jnp.where(at >= 0, count + 1, count)

        free = lax.fori_loop(0, FREE, body, 0)
        counts[source] = free
        counts[4 + source] = lax.fori_loop(FREE, QB, body, free)


def routes_of(spot):
    smem = pl.BlockSpec(memory_space=pltpu.SMEM)
    return pl.pallas_call(
        routes_kernel,
        in_specs=[smem],
        out_specs=[smem, smem],
        out_shape=[jax.ShapeDtypeStruct((4, QB + 1), jnp.int32), jax.ShapeDtypeStruct((8,), jnp.int32)],
        name="routes",
    )(spot)


def gather_kernel(row, lists, counts, *refs):
    home, away, acc = refs[-3:]
    sources, patches = refs[:4], refs[4:-3]
    height = acc.shape[1]
    acc[...] = jnp.zeros_like(acc)

    def add(source, lo, hi, load):
        def body(i, carry):
            entry = lists[source, i]
            at = entry % ROUTE
            acc[at] = acc[at] + load(entry // ROUTE).astype(F32)
            return carry

        lax.fori_loop(lo, hi, body, 0)

    for source in range(4):
        ref = sources[source]
        if patches:
            patch = patches[source]
            add(source, 0, counts[source], lambda q, ref=ref: ref[q])
            load = lambda q, ref=patch: ref[q - FREE, row : row + height, :]
            add(source, counts[source], counts[4 + source], load)
        else:
            add(source, 0, counts[4 + source], lambda q, ref=ref: ref[q])
    tiles = home.shape[0]
    home[...] = acc[0:tiles]
    away[...] = acc[tiles : 2 * tiles].astype(BF16)


def gather_rows(routes, rows, patches, row, tiles):
    height = rows[0].shape[1]
    vmem = pl.BlockSpec(memory_space=pltpu.VMEM)
    shape = (tiles // 2, height, 128)
    return pl.pallas_call(
        functools.partial(gather_kernel, row),
        in_specs=[pl.BlockSpec(memory_space=pltpu.SMEM)] * 2 + [vmem] * len(rows + patches),
        out_shape=[jax.ShapeDtypeStruct(shape, F32), jax.ShapeDtypeStruct(shape, BF16)],
        scratch_shapes=[pltpu.VMEM((tiles, height, 128), F32)],
        compiler_params=pltpu.CompilerParams(vmem_limit_bytes=VMEM),
        cost_estimate=pl.CostEstimate(flops=10**6, bytes_accessed=10**4, transcendentals=0),
        name="gather_rows",
    )(*routes, *rows, *patches)


def add_kernel(home, got, own, *away):
    for j in range(len(away) + 1):
        lo = j * TILE_DEV
        total = home[lo : lo + TILE_DEV] + got[lo : lo + TILE_DEV].astype(F32)
        if j == 0:
            own[...] = total
        else:
            away[j - 1][...] = total.astype(BF16)


def add_halves(home, got):
    shape = (TILE_DEV,) + home.shape[1:]
    others = home.shape[0] // TILE_DEV - 1
    return pl.pallas_call(
        add_kernel,
        out_shape=[jax.ShapeDtypeStruct(shape, F32)] + [jax.ShapeDtypeStruct(shape, BF16)] * others,
        compiler_params=pltpu.CompilerParams(vmem_limit_bytes=VMEM),
        cost_estimate=pl.CostEstimate(flops=10**6, bytes_accessed=10**4, transcendentals=0),
        name="add_halves",
    )(home, got)


def collapse_matrices():
    def across(src, dst, width):
        g = grow_matrix(width).T
        m = np.zeros((128, 128), np.float32)
        for ch in range(COLOURS):
            m[src + ch * width : src + (ch + 1) * width, dst + ch * 2 * width : dst + (ch + 1) * 2 * width] = g
        return m

    last = np.zeros((128, 384), np.float32)
    g = grow_matrix(32).T
    for ch in range(COLOURS):
        for half in range(2):
            last[ch * 32 : ch * 32 + 32, ch * 128 + half * 64 : ch * 128 + half * 64 + 64] = g

    def down(n, rows_in, rows_out, pick=None):
        g = grow_matrix(n)
        g = g if pick is None else g[pick::2]
        m = np.zeros((TILE_DEV * rows_out, TILE_DEV * rows_in), np.float32)
        for t in range(TILE_DEV):
            m[t * rows_out : t * rows_out + g.shape[0], t * rows_in : t * rows_in + n] = g
        return m

    mats = {"m43": across(96, 64, 4), "m32": across(64, 0, 8), "m21": across(0, 0, 16), "m10": last}
    mats |= {"d43": down(4, 16, 16), "d32": down(8, 16, 16), "d21": down(16, 16, 32)}
    mats |= {"even": down(32, 32, 32, 0), "odd": down(32, 32, 32, 1)}
    return pack(mats, 1280)


def collapse_kernel(places, each, packed, *refs):
    mats = unpack(packed, places)
    a, b, c = (refs[i * each : (i + 1) * each] for i in range(3))
    out, level0 = refs[3 * each :]

    def total(sources, lo, hi):
        acc = sources[0][:, lo:hi, :]
        for source in sources[1:]:
            acc = acc + source[:, lo:hi, :].astype(F32)
        return acc.reshape(TILE_DEV * (hi - lo), 128)

    lane = lane_index()
    small = total(c, 32, 48)
    bottom = small
    for lo, width, chans in ((0, 16, 3), (64, 8, 3), (96, 4, 3)):
        for ch in range(chans):
            inside = (lane >= lo + ch * width) & (lane < lo + (ch + 1) * width)
            bottom = jnp.where(inside, pltpu.roll(small, (128 - (3 - ch) * width) % 128, 1), bottom)
    small = small / jnp.maximum(bottom, 1.0)
    three = small + ldot(mats["d43"], rdot(small, mats["m43"]))
    two = small + ldot(mats["d32"], rdot(three, mats["m32"]))
    one = total(b, 64, 96)
    bottom = one
    for ch in range(3):
        inside = (lane >= ch * 32) & (lane < (ch + 1) * 32)
        bottom = jnp.where(inside, pltpu.roll(one, (128 - (3 - ch) * 32) % 128, 1), bottom)
    one = one / jnp.maximum(bottom, 1.0) + ldot(mats["d21"], rdot(two, mats["m21"]))
    wide = rdot(one, mats["m10"])
    hi, lo = split(wide)
    up = mm(mats["even"], hi) + mm(mats["even"], lo)
    down = mm(mats["odd"], hi) + mm(mats["odd"], lo)
    bottom = jnp.maximum(total(a, 0, 32), 1.0)
    for ch in range(COLOURS):
        own = total(b, 32 * ch, 32 * ch + 32) if ch < 2 else total(c, 0, 32)
        back = jnp.where(lane < 64, up[:, ch * 128 : ch * 128 + 128], down[:, ch * 128 : ch * 128 + 128])
        level0[ch * 128 : ch * 128 + 128, :] = own / bottom + back
    for ch in range(COLOURS):
        for row in range(32):
            out[ch, :, row * 128 : row * 128 + 128] = level0[pl.ds(ch * 128 + row, TILE_DEV, stride=32), :]


def collapse(a, b, c):
    packed, places = collapse_matrices()
    tiles = pl.pallas_call(
        functools.partial(collapse_kernel, places, len(a)),
        out_shape=jax.ShapeDtypeStruct((COLOURS, TILE_DEV, 4096), F32),
        scratch_shapes=[pltpu.VMEM((COLOURS * 128, 128), F32)],
        compiler_params=pltpu.CompilerParams(vmem_limit_bytes=VMEM),
        cost_estimate=pl.CostEstimate(flops=10**6, bytes_accessed=10**4, transcendentals=0),
        name="collapse",
    )(packed, *a, *b, *c)
    return jnp.swapaxes(tiles, 0, 1)


def swap(value, axis, bit):
    size = lax.axis_size(axis)
    return lax.ppermute(value, axis, [(i, i ^ bit) for i in range(size)])


def local(frames, weight_map, seam_mask, strip_cell, partner, tile_group, tile_position_in_group):
    groups = lax.axis_size("frames")
    parts = lax.axis_size("tiles")
    mine = lax.axis_index("tiles")
    mask = lax.bitwise_xor(partner[0] // parts, lax.axis_index("frames"))

    strips = strips_of(frames, strip_cell)
    ids = tile_group.reshape(QB) * (parts * TILE_DEV) + tile_position_in_group.reshape(QB)
    columns = jnp.arange(QB, dtype=jnp.int32) % 16
    slots = slot_of(columns, left_column(strip_cell[0])) * 2 + jnp.arange(QB, dtype=jnp.int32) // 16
    ids = jnp.sum(jnp.where(slots[None, :] == jnp.arange(QB, dtype=jnp.int32)[:, None], ids[None, :], 0), axis=1)
    strips, frames, ids = lax.optimization_barrier((strips, frames, ids))
    ids_far = swap(ids, "tiles", 2)
    ids = jnp.stack([ids, swap(ids, "tiles", 1), ids_far, swap(ids_far, "tiles", 1)])
    group_size = parts * TILE_DEV
    owner = ids % group_size // TILE_DEV
    relative = lax.bitwise_xor(ids // group_size, lax.axis_index("frames"))
    relative = (relative & 1) * (groups // 2) + (relative >> 1)
    spot = jnp.where(owner == mine, relative * TILE_DEV + ids % TILE_DEV, -1)

    routes = routes_of(spot)
    tie = lax.optimization_barrier
    weights, first, second, state = bands_of(strip_cell, frames, weight_map, seam_mask)
    bit = 1
    while bit < groups:
        got = swap(strips, "frames", bit)
        if bit == 1:
            got, weights, first, second, state = tie((got, weights, first, second, state))
            far_weights, near_weights = swap(weights, "tiles", 2), swap(weights, "tiles", 1)
        if bit == 2:
            got, far_weights, near_weights, first = tie((got, far_weights, near_weights, first))
        if bit == groups // 2:
            got, routes = tie((got, routes))
        strips = jnp.where((mask & bit) != 0, got, strips)
        bit *= 2

    def gather(rows, patches=(), row=0):
        return gather_rows(routes, rows, patches, row, groups * TILE_DEV)

    def along(own, *away):
        return [own] + [swap(part, "frames", 2 * (j + 1)) for j, part in enumerate(away)]

    far_first, near_first = swap(first, "tiles", 2), swap(first, "tiles", 1)
    patch = blend(strip_cell, strips, state)
    far_patch, near_patch = swap(patch, "tiles", 2), swap(patch, "tiles", 1)
    near_patch, second = tie((near_patch, second))
    far_second, near_second = swap(second, "tiles", 2), swap(second, "tiles", 1)
    home, away = gather((weights, near_weights, far_weights, swap(far_weights, "tiles", 1)))
    away_got = swap(away, "frames", 1)
    far_first, near_first, far_patch, near_patch, home, away_got = tie(
        (far_first, near_first, far_patch, near_patch, home, away_got)
    )
    patches = (patch, near_patch, far_patch, swap(far_patch, "tiles", 1))
    sums = add_halves(home, away_got)
    far_near = swap(far_first, "tiles", 1)
    far_near, sums = tie((far_near, sums))
    got_weights = along(*sums)
    home, away = gather((first, near_first, far_first, far_near), patches, 0)
    got = swap(away, "frames", 1)
    far_second, home, got_weights = tie((far_second, home, got_weights))
    far_near = swap(far_second, "tiles", 1)
    sums = add_halves(home, got)
    far_near, sums = tie((far_near, sums))
    got_first = along(*sums)
    home, away = gather((second, near_second, far_second, far_near), patches, HALF)
    got = swap(away, "frames", 1)
    got, got_first = tie((got, got_first))
    got_second = along(*add_halves(home, got))
    return collapse(got_weights, got_first, got_second)


def solution(mesh):
    in_specs = (
        P(("frames", "tiles"), None, None, None),
        P(("frames", "tiles"), None, None),
        P(("frames", "tiles"), None, None),
        P(("frames", "tiles")),
        P(("frames", "tiles")),
        P(("frames", "tiles"), None, None),
        P(("frames", "tiles"), None),
    )
    out_specs = P(("frames", "tiles"), None, None)
    return jax.shard_map(local, mesh=mesh, in_specs=in_specs, out_specs=out_specs, check_vma=False)
```

```python
import functools

import jax
import jax.numpy as jnp
import numpy as np
from jax import lax
from jax.experimental import pallas as pl
from jax.experimental.pallas import tpu as pltpu
from jax.sharding import PartitionSpec as P

COLOURS = 3
FH = 128
FW = 1024
QB = 32
WIN = 256
TILE_DEV = 4
VMEM = 30 << 20
ROUTE = 4096
F32 = jnp.float32
BF16 = jnp.bfloat16


def shrink_matrix(n):
    m = np.zeros((n // 2, n), np.float32)
    for i in range(n // 2):
        for d, tap in zip(range(-2, 3), (1, 4, 6, 4, 1)):
            m[i, min(max(2 * i + d, 0), n - 1)] += tap / 16.0
    return m


def grow_matrix(n):
    m = np.zeros((2 * n, n), np.float32)
    for i in range(n):
        lo, hi = max(i - 1, 0), min(i + 1, n - 1)
        m[2 * i, lo] += 1 / 8
        m[2 * i, i] += 6 / 8
        m[2 * i, hi] += 1 / 8
        m[2 * i + 1, i] += 1 / 2
        m[2 * i + 1, hi] += 1 / 2
    return m


def padded(m, rows, cols):
    return np.pad(m, ((0, rows - m.shape[0]), (0, cols - m.shape[1])))


def row_order():
    m = np.zeros((FH, FH), np.float32)
    for r in range(2):
        for par in range(2):
            for i in range(32):
                m[r * 64 + par * 32 + i, r * 64 + 2 * i + par] = 1
    return m


def vertical():
    v = {1: shrink_matrix(128), 2: shrink_matrix(64), 3: shrink_matrix(32)}
    spread = np.zeros((16, 8), np.float32)
    for r in range(2):
        for i in range(4):
            spread[r * 8 + i, r * 4 + i] = 1
    v[4] = spread @ shrink_matrix(16)
    g = {0: row_order() @ grow_matrix(64), 1: grow_matrix(32), 2: grow_matrix(16)}
    g[3] = grow_matrix(8) @ spread.T
    return v, g


def horizontal(width):
    s = {k: shrink_matrix(width >> (k - 1)).T for k in range(1, 5)}
    g = {k: grow_matrix(width >> (k + 1)).T for k in range(4)}
    return s, g


def shrink_window():
    m = np.zeros((512, 128), np.float32)
    for i in range(128):
        for d, tap in zip(range(-2, 3), (1, 4, 6, 4, 1)):
            m[128 + 2 * i + d, i] = tap / 16.0
    return m


def grow_window():
    m = np.zeros((384, 256), np.float32)
    for i in range(128):
        for d, tap in zip(range(-1, 2), (1, 6, 1)):
            m[128 + i + d, 2 * i] = tap / 8.0
        m[128 + i, 2 * i + 1] = m[128 + i + 1, 2 * i + 1] = 0.5
    return m


def pack(mats, width):
    places, row, col, height = {}, 0, 0, 0
    for name in sorted(mats, key=lambda n: (-mats[n].shape[0], -mats[n].shape[1], n)):
        h, w = mats[name].shape
        wide = -(-w // 128) * 128
        if col + wide > width:
            row, col, height = row + height, 0, 0
        height = max(height, -(-h // 16) * 16)
        places[name] = (row, col, h, w)
        col += wide
    out = np.zeros((row + height, width), np.float32)
    for name, (r, c, h, w) in places.items():
        out[r : r + h, c : c + w] = mats[name]
    return jnp.asarray(out, BF16), places


def unpack(ref, places):
    return {name: ref[r : r + h, c : c + w] for name, (r, c, h, w) in places.items()}


def small_matrices():
    v, g = vertical()
    s, gh = horizontal(WIN)
    sm, _ = horizontal(64)
    mats = {f"v{k}": m for k, m in v.items()} | {f"g{k}": m for k, m in g.items()}
    mats |= {f"s{k}": m for k, m in s.items()} | {f"h{k}": m for k, m in gh.items()}
    mats |= {f"m{k}": m for k, m in sm.items()} | {"order": row_order()}
    return pack(mats, 512)


def large_matrices():
    mats = {"shrink": shrink_window(), "grow": grow_window()}
    mats["last"] = padded(shrink_matrix(128).T, 128, 128)
    mats["least"] = padded(grow_matrix(64).T, 128, 128)
    return pack(mats, 640)


def levels_of(mats, letter):
    return {int(n[1:]): m for n, m in mats.items() if n[0] == letter and n[1:].isdigit()}


def mm(a, b):
    return jnp.dot(a, b, preferred_element_type=F32)


def split(v):
    hi = v.astype(BF16)
    return hi, (v - hi.astype(F32)).astype(BF16)


def rdot(v, m):
    hi, lo = split(v)
    return mm(hi, m) + mm(lo, m)


def ldot(m, v):
    hi, lo = split(v)
    return mm(m, hi) + mm(m, lo)


def mmt(a, b):
    return lax.dot_general(a, b, (((1,), (1,)), ((), ())), preferred_element_type=F32)


def windows(v, m, step):
    rows, width = v.shape
    both = jnp.concatenate(split(v), axis=0)
    left = jnp.broadcast_to(both[:, :1], (2 * rows, 128))
    right = jnp.broadcast_to(both[:, width - 1 :], (2 * rows, 128))
    both = jnp.concatenate([left, both, right], axis=1)
    pieces = []
    for n in range(width // step):
        piece = mm(both[:, n * step : n * step + step + 256], m)
        pieces.append(piece[:rows] + piece[rows:])
    return jnp.concatenate(pieces, axis=1)


def right_of(m):
    return lambda v: rdot(v, m)


def pyramid(planes, v, shrinks, product=mm):
    n = len(planes)
    t = jnp.concatenate([product(v[1], p) for p in planes], axis=0)
    levels = {1: shrinks[1](t)}
    for k in range(2, 5):
        prev = levels[k - 1]
        rows = prev.shape[0] // n
        t = jnp.concatenate([ldot(v[k], prev[i * rows : (i + 1) * rows]) for i in range(n)], axis=0)
        levels[k] = shrinks[k](t)
    return levels


def grown(level, n, gv, grow):
    h = grow(level)
    rows = level.shape[0] // n
    return [ldot(gv, h[i * rows : (i + 1) * rows]) for i in range(n)]


def place(rows, cols, base, width, offset):
    i = lax.broadcasted_iota(jnp.int32, (rows, cols), 0)
    c = lax.broadcasted_iota(jnp.int32, (rows, cols), 1)
    hit = (i >= base) & (i < base + width) & (c - i == offset - base)
    return jnp.where(hit, 1.0, 0.0).astype(BF16)


def strips_kernel(places, cell, xa, xb, packed, out, acc):
    mats = unpack(packed, places)
    v, gv, s, gh = (levels_of(mats, letter) for letter in "vgsh")
    s, gh = ({k: right_of(m) for k, m in each.items()} for each in (s, gh))
    order = mats["order"]
    first = window_tile(cell[0]) * 128
    planes = [jnp.concatenate([xa[0, c], xb[0, c]], axis=1) for c in range(COLOURS)]
    levels = pyramid(planes, v, s)
    back = grown(levels[1], COLOURS, gv[0], gh[0])
    b0 = jnp.concatenate([mm(order, planes[c]) - back[c] for c in range(COLOURS)], axis=0)
    bands = [b0.astype(BF16)]
    for k in range(1, 4):
        back = grown(levels[k + 1], COLOURS, gv[k], gh[k])
        bands.append((levels[k] - jnp.concatenate(back, axis=0)).astype(BF16))
    bands.append(levels[4].astype(BF16))
    start = cell[0] * 16 - first

    def pick(band, base, k):
        i = lax.broadcasted_iota(jnp.int32, (band.shape[1], 128), 0)
        c = lax.broadcasted_iota(jnp.int32, (band.shape[1], 128), 1)
        hit = (c >= base) & (c < base + (64 >> k)) & (i - c == (start >> k) - base)
        return mm(band, jnp.where(hit, 1.0, 0.0).astype(BF16))

    out[0:192, :] = (pick(bands[0][0:192], 0, 0) + pick(bands[0][192:384], 64, 0)).astype(BF16)
    acc[...] = pick(bands[1][0:96], 0, 1) + pick(bands[1][96:192], 32, 1) + pick(bands[2], 64, 2)
    acc[0:48, :] = acc[0:48, :] + pick(bands[3], 80, 3) + pick(bands[4], 88, 4)
    out[192:288, :] = acc[...].astype(BF16)


def window_tile(cell):
    return jnp.clip((cell - 3) >> 3, 0, (FW - WIN) // 128)


def full_spec(a):
    return pl.BlockSpec(a.shape, lambda *_: (0,) * a.ndim)


def strips_of(frames, cell):
    packed, places = small_matrices()
    grid_spec = pltpu.PrefetchScalarGridSpec(
        num_scalar_prefetch=1,
        grid=(1,),
        in_specs=[
            pl.BlockSpec((1, COLOURS, FH, 128), lambda i, c: (0, 0, 0, window_tile(c[0]))),
            pl.BlockSpec((1, COLOURS, FH, 128), lambda i, c: (0, 0, 0, window_tile(c[0]) + 1)),
        ]
        + [full_spec(packed)],
        out_specs=pl.BlockSpec((288, 128), lambda i, c: (0, 0)),
        scratch_shapes=[pltpu.VMEM((96, 128), F32)],
    )
    return pl.pallas_call(
        functools.partial(strips_kernel, places),
        grid_spec=grid_spec,
        out_shape=jax.ShapeDtypeStruct((288, 128), BF16),
        compiler_params=pltpu.CompilerParams(vmem_limit_bytes=VMEM),
        cost_estimate=pl.CostEstimate(flops=2 * 10**9, bytes_accessed=10**6, transcendentals=0),
        name="strips",
    )(cell, frames, frames, packed)


def lane_index():
    return lax.broadcasted_iota(jnp.int32, (1, 128), 1)


def fold_level0(p, store):
    left = lane_index() < 64
    for r in range(2):
        for j in range(8):
            even = p[r * 64 : r * 64 + 32, j * 128 : j * 128 + 128]
            odd = p[r * 64 + 32 : r * 64 + 64, j * 128 : j * 128 + 128]
            store(r * 16 + 2 * j, jnp.where(left, even, pltpu.roll(odd, 64, 1)))
            store(r * 16 + 2 * j + 1, jnp.where(left, pltpu.roll(even, 64, 1), odd))


def gather_channels(parts, width, cc, base):
    groups = 128 // width
    group = lane_index() // width
    out = jnp.zeros_like(parts[0])
    for ch in range(4):
        out = jnp.where(group == (cc + ch) % groups, parts[ch], out)
    return pltpu.roll(out, (base - cc * width) % 128, 1)


STATE_ROWS = 816


def state_views(state):
    at = lambda r, h, c, w: (slice(r, r + h), slice(c, c + w))
    b0 = [at(128 * c, 128, 0, 1024) for c in range(3)]
    l1 = [at(384, 64, 0, 512), at(384, 64, 512, 512), at(448, 64, 0, 512), at(448, 64, 512, 512)]
    l2 = [at(512, 32, 256 * c, 256) for c in range(4)]
    l3 = [at(544, 16, 128 * c, 128) for c in range(4)]
    l4 = [at(544, 16, 512 + 128 * c, 128) for c in range(4)]
    levels = [b0 + [at(560, 128, 0, 1024)], l1, l2, l3, l4]
    masks = [at(688, 128 >> k, 128 * k, 64 >> k) for k in range(4)] + [at(688, 16, 512, 4)]
    return levels, masks


def bands_kernel(small_places, large_places, x, w, m, small, large, wblocks, state):
    mats = unpack(small, small_places)
    v, gv, sm = (levels_of(mats, letter) for letter in "vgm")
    order = mats["order"]
    sm = {k: right_of(each) for k, each in sm.items()}
    mats = unpack(large, large_places)
    half = lambda each: windows(each, mats["shrink"], 256)
    twice = lambda each: windows(each, mats["grow"], 128)
    s = {1: half, 2: half, 3: half, 4: right_of(mats["last"])}
    gh = {0: twice, 1: twice, 2: twice, 3: right_of(mats["least"])}
    views, mask_views = state_views(state)
    planes = [x[0, c] for c in range(COLOURS)] + [w[0]]
    weights = mm(order, planes[3])
    state[views[0][3]] = weights

    def store(q, piece):
        wblocks[q] = piece.astype(BF16)

    fold_level0(weights, store)
    levels = pyramid(planes, v, s)
    for k in range(1, 5):
        rows = levels[k].shape[0] // 4
        state[views[k][3]] = levels[k][3 * rows :]
    back = grown(levels[1][: 3 * 64], COLOURS, gv[0], gh[0])
    for c in range(COLOURS):
        state[views[0][c]] = mm(order, planes[c]) - back[c]
    for k in range(1, 4):
        rows = levels[k].shape[0] // 4
        below = levels[k + 1].shape[0] // 4
        back = grown(levels[k + 1][: 3 * below], COLOURS, gv[k], gh[k])
        for c in range(COLOURS):
            state[views[k][c]] = levels[k][c * rows : (c + 1) * rows] - back[c]
    for c in range(COLOURS):
        state[views[4][c]] = levels[4][c * 16 : (c + 1) * 16]
    other = (1.0 - m[0].astype(F32)).astype(BF16)
    state[mask_views[0]] = mmt(order, other)
    masks = pyramid([other], v, sm, mmt)
    for k in range(1, 5):
        state[mask_views[k]] = masks[k]


def bands_of(frames, weight_map, seam_mask):
    small, small_places = small_matrices()
    large, large_places = large_matrices()
    return pl.pallas_call(
        functools.partial(bands_kernel, small_places, large_places),
        out_shape=[jax.ShapeDtypeStruct((QB, 32, 128), BF16), jax.ShapeDtypeStruct((STATE_ROWS, FW), F32)],
        compiler_params=pltpu.CompilerParams(vmem_limit_bytes=VMEM),
        cost_estimate=pl.CostEstimate(flops=8 * 10**9, bytes_accessed=6 * 10**6, transcendentals=0),
        name="bands",
    )(frames, weight_map, jnp.swapaxes(seam_mask, 1, 2), small, large)


def blend_kernel(cell, strips, state, first, second):
    views, mask_views = state_views(state)
    (b0, b1, b2, b3, b4) = [[state[view] for view in views[k][:3]] for k in range(5)]
    (wp, w1, w2, w3, w4) = [state[views[k][3]] for k in range(5)]
    (n0, n1, n2, n3, n4) = [state[view] for view in mask_views]
    start = cell[0] * 16
    low = strips[192:288]

    def mixed(band, remote, share):
        return band + share * (remote - band)

    widths = (1024, 512, 256, 128, 128)
    share0 = mm(n0.astype(BF16), place(64, 1024, 0, 64, start))
    share = [share0]
    for k, ref in enumerate((n1, n2, n3, n4)):
        share.append(rdot(ref, place(64 >> (k + 1), widths[k + 1], 0, 64 >> (k + 1), start >> (k + 1))))
    top = strips[0:192]
    remote0 = [mm(top, place(128, 1024, 0, 64, start)), mm(top, place(128, 1024, 64, 64, start))]
    remote0 = jnp.concatenate(remote0, axis=0)
    weights = wp
    for c in range(COLOURS):
        p = weights * mixed(b0[c], remote0[c * 128 : (c + 1) * 128], share[0])
        out, row = (first, 0) if c == 0 else (second, 32 * (c - 1))

        def store(q, piece, out=out, row=row):
            out[q, row : row + 32, :] = piece.astype(BF16)

        fold_level0(p, store)
    remote1 = [mm(low, place(128, 512, 0, 32, start >> 1)), mm(low, place(128, 512, 32, 32, start >> 1))]
    remote1 = jnp.concatenate(remote1, axis=0)
    parts = [w1 * mixed(b1[c], remote1[c * 64 : (c + 1) * 64], share[1]) for c in range(COLOURS)] + [w1]
    for r in range(2):
        for j in range(4):
            turned = [parts[ch][r * 32 : r * 32 + 32, j * 128 : j * 128 + 128] for ch in range(4)]
            turned = [turned[0]] + [pltpu.roll(turned[ch], 32 * ch, 1) for ch in range(1, 4)]
            for cc in range(4):
                first[r * 16 + 4 * j + cc, 32:64, :] = gather_channels(turned, 32, cc, 0).astype(BF16)
    remote2 = mm(low, place(128, 256, 64, 16, start >> 2))
    remote3 = mm(low[0:48], place(128, 128, 80, 8, start >> 3))
    remote4 = mm(low[0:48], place(128, 128, 88, 4, start >> 4))
    parts2 = [w2 * mixed(b2[c], remote2[c * 32 : (c + 1) * 32], share[2]) for c in range(COLOURS)] + [w2]
    parts3 = [w3 * mixed(b3[c], remote3[c * 16 : (c + 1) * 16], share[3]) for c in range(COLOURS)] + [w3]
    parts4 = [w4 * mixed(b4[c], remote4[c * 16 : (c + 1) * 16], share[4]) for c in range(COLOURS)] + [w4]
    lane = lane_index()
    for r in range(2):
        turned3 = [pltpu.roll(parts3[ch][r * 8 : r * 8 + 8], 8 * ch, 1) for ch in range(4)]
        turned4 = [pltpu.roll(parts4[ch][r * 8 : r * 8 + 8], 4 * ch, 1) for ch in range(4)]
        for j in range(2):
            turned2 = [parts2[ch][r * 16 : r * 16 + 16, j * 128 : j * 128 + 128] for ch in range(4)]
            turned2 = [pltpu.roll(turned2[ch], 16 * ch, 1) for ch in range(4)]
            for cc in range(8):
                c = j * 8 + cc
                two = gather_channels(turned2, 16, cc, 0)
                three = gather_channels(turned3, 8, c, 64)
                four = gather_channels(turned4, 4, c, 96)
                head = jnp.where(lane < 64, two[0:8], jnp.where(lane < 96, three, four))
                tail = jnp.where(lane < 64, two[8:16], 0.0)
                first[r * 16 + c, 64:80, :] = jnp.concatenate([head, tail], axis=0).astype(BF16)


def blend(cell, strips, state):
    vmem = pl.BlockSpec(memory_space=pltpu.VMEM)
    return pl.pallas_call(
        blend_kernel,
        in_specs=[pl.BlockSpec(memory_space=pltpu.SMEM)] + [vmem] * 2,
        out_shape=[jax.ShapeDtypeStruct((QB, 80, 128), BF16), jax.ShapeDtypeStruct((QB, 64, 128), BF16)],
        compiler_params=pltpu.CompilerParams(vmem_limit_bytes=VMEM),
        cost_estimate=pl.CostEstimate(flops=10**6, bytes_accessed=10**4, transcendentals=0),
        name="blend",
    )(cell, strips, state)


def routes_kernel(spot, lists, counts):
    for source in range(4):

        def body(q, count, source=source):
            at = spot[source, q]
            lists[source, count] = q * ROUTE + at
            return jnp.where(at >= 0, count + 1, count)

        counts[source] = lax.fori_loop(0, QB, body, 0)


def routes_of(spot):
    smem = pl.BlockSpec(memory_space=pltpu.SMEM)
    return pl.pallas_call(
        routes_kernel,
        in_specs=[smem],
        out_specs=[smem, smem],
        out_shape=[jax.ShapeDtypeStruct((4, QB + 1), jnp.int32), jax.ShapeDtypeStruct((4,), jnp.int32)],
        name="routes",
    )(spot)


def gather_kernel(lists, counts, a, b, c, d, home, away, acc):
    acc[...] = jnp.zeros_like(acc)
    for source, ref in enumerate((a, b, c, d)):

        def body(i, carry, source=source, ref=ref):
            entry = lists[source, i]
            q, at = entry // ROUTE, entry % ROUTE
            acc[at] = acc[at] + ref[q].astype(F32)
            return carry

        lax.fori_loop(0, counts[source], body, 0)
    tiles = home.shape[0]
    home[...] = acc[0:tiles]
    away[...] = acc[tiles : 2 * tiles].astype(BF16)


def gather_rows(routes, rows, tiles):
    height = rows[0].shape[1]
    vmem = pl.BlockSpec(memory_space=pltpu.VMEM)
    shape = (tiles // 2, height, 128)
    return pl.pallas_call(
        gather_kernel,
        in_specs=[pl.BlockSpec(memory_space=pltpu.SMEM)] * 2 + [vmem] * 4,
        out_shape=[jax.ShapeDtypeStruct(shape, F32), jax.ShapeDtypeStruct(shape, BF16)],
        scratch_shapes=[pltpu.VMEM((tiles, height, 128), F32)],
        compiler_params=pltpu.CompilerParams(vmem_limit_bytes=VMEM),
        cost_estimate=pl.CostEstimate(flops=10**6, bytes_accessed=10**4, transcendentals=0),
        name="gather_rows",
    )(*routes, *rows)


def add_kernel(home, got, own, *away):
    for j in range(len(away) + 1):
        lo = j * TILE_DEV
        total = home[lo : lo + TILE_DEV] + got[lo : lo + TILE_DEV].astype(F32)
        if j == 0:
            own[...] = total
        else:
            away[j - 1][...] = total.astype(BF16)


def add_halves(home, got):
    shape = (TILE_DEV,) + home.shape[1:]
    others = home.shape[0] // TILE_DEV - 1
    return pl.pallas_call(
        add_kernel,
        out_shape=[jax.ShapeDtypeStruct(shape, F32)] + [jax.ShapeDtypeStruct(shape, BF16)] * others,
        compiler_params=pltpu.CompilerParams(vmem_limit_bytes=VMEM),
        cost_estimate=pl.CostEstimate(flops=10**6, bytes_accessed=10**4, transcendentals=0),
        name="add_halves",
    )(home, got)


def collapse_matrices():
    def across(src, dst, width):
        g = grow_matrix(width).T
        m = np.zeros((128, 128), np.float32)
        for ch in range(COLOURS):
            m[src + ch * width : src + (ch + 1) * width, dst + ch * 2 * width : dst + (ch + 1) * 2 * width] = g
        return m

    last = np.zeros((128, 384), np.float32)
    g = grow_matrix(32).T
    for ch in range(COLOURS):
        for half in range(2):
            last[ch * 32 : ch * 32 + 32, ch * 128 + half * 64 : ch * 128 + half * 64 + 64] = g

    def down(n, rows_in, rows_out, pick=None):
        g = grow_matrix(n)
        g = g if pick is None else g[pick::2]
        m = np.zeros((TILE_DEV * rows_out, TILE_DEV * rows_in), np.float32)
        for t in range(TILE_DEV):
            m[t * rows_out : t * rows_out + g.shape[0], t * rows_in : t * rows_in + n] = g
        return m

    mats = {"m43": across(96, 64, 4), "m32": across(64, 0, 8), "m21": across(0, 0, 16), "m10": last}
    mats |= {"d43": down(4, 16, 16), "d32": down(8, 16, 16), "d21": down(16, 16, 32)}
    mats |= {"even": down(32, 32, 32, 0), "odd": down(32, 32, 32, 1)}
    return pack(mats, 1280)


def collapse_kernel(places, each, packed, *refs):
    mats = unpack(packed, places)
    a, b, c = (refs[i * each : (i + 1) * each] for i in range(3))
    out, level0 = refs[3 * each :]

    def total(sources, lo, hi):
        acc = sources[0][:, lo:hi, :]
        for source in sources[1:]:
            acc = acc + source[:, lo:hi, :].astype(F32)
        return acc.reshape(TILE_DEV * (hi - lo), 128)

    lane = lane_index()
    small = total(b, 64, 80)
    bottom = small
    for lo, width, chans in ((0, 16, 3), (64, 8, 3), (96, 4, 3)):
        for ch in range(chans):
            inside = (lane >= lo + ch * width) & (lane < lo + (ch + 1) * width)
            bottom = jnp.where(inside, pltpu.roll(small, (128 - (3 - ch) * width) % 128, 1), bottom)
    small = small / jnp.maximum(bottom, 1.0)
    three = small + ldot(mats["d43"], rdot(small, mats["m43"]))
    two = small + ldot(mats["d32"], rdot(three, mats["m32"]))
    one = total(b, 32, 64)
    bottom = one
    for ch in range(3):
        inside = (lane >= ch * 32) & (lane < (ch + 1) * 32)
        bottom = jnp.where(inside, pltpu.roll(one, (128 - (3 - ch) * 32) % 128, 1), bottom)
    one = one / jnp.maximum(bottom, 1.0) + ldot(mats["d21"], rdot(two, mats["m21"]))
    wide = rdot(one, mats["m10"])
    hi, lo = split(wide)
    up = mm(mats["even"], hi) + mm(mats["even"], lo)
    down = mm(mats["odd"], hi) + mm(mats["odd"], lo)
    bottom = jnp.maximum(total(a, 0, 32), 1.0)
    for ch in range(COLOURS):
        own = total(b, 0, 32) if ch == 0 else total(c, 32 * (ch - 1), 32 * ch)
        back = jnp.where(lane < 64, up[:, ch * 128 : ch * 128 + 128], down[:, ch * 128 : ch * 128 + 128])
        level0[ch * 128 : ch * 128 + 128, :] = own / bottom + back
    for ch in range(COLOURS):
        for row in range(32):
            out[ch, :, row * 128 : row * 128 + 128] = level0[pl.ds(ch * 128 + row, TILE_DEV, stride=32), :]


def collapse(a, b, c):
    packed, places = collapse_matrices()
    tiles = pl.pallas_call(
        functools.partial(collapse_kernel, places, len(a)),
        out_shape=jax.ShapeDtypeStruct((COLOURS, TILE_DEV, 4096), F32),
        scratch_shapes=[pltpu.VMEM((COLOURS * 128, 128), F32)],
        compiler_params=pltpu.CompilerParams(vmem_limit_bytes=VMEM),
        cost_estimate=pl.CostEstimate(flops=10**6, bytes_accessed=10**4, transcendentals=0),
        name="collapse",
    )(packed, *a, *b, *c)
    return jnp.swapaxes(tiles, 0, 1)


def swap(value, axis, bit):
    size = lax.axis_size(axis)
    return lax.ppermute(value, axis, [(i, i ^ bit) for i in range(size)])


def local(frames, weight_map, seam_mask, strip_cell, partner, tile_group, tile_position_in_group):
    groups = lax.axis_size("frames")
    parts = lax.axis_size("tiles")
    mine = lax.axis_index("tiles")
    mask = lax.bitwise_xor(partner[0] // parts, lax.axis_index("frames"))

    strips = strips_of(frames, strip_cell)
    ids = tile_group.reshape(QB) * (parts * TILE_DEV) + tile_position_in_group.reshape(QB)
    strips, frames, ids = lax.optimization_barrier((strips, frames, ids))
    ids_core = swap(ids, "tiles", 1)
    ids_far = swap(ids, "tiles", 2)
    ids_far_core = swap(ids_far, "tiles", 1)
    ids = jnp.stack([ids, ids_core, ids_far, ids_far_core])
    group_size = parts * TILE_DEV
    owner = ids % group_size // TILE_DEV
    relative = lax.bitwise_xor(ids // group_size, lax.axis_index("frames"))
    relative = (relative & 1) * (groups // 2) + (relative >> 1)
    spot = jnp.where(owner == mine, relative * TILE_DEV + ids % TILE_DEV, -1)

    routes = routes_of(spot)
    tie = lax.optimization_barrier
    weights, state = bands_of(frames, weight_map, seam_mask)
    bit = 1
    while bit < groups:
        got = swap(strips, "frames", bit)
        if bit == 1:
            got, weights, state = tie((got, weights, state))
            far, near = swap(weights, "tiles", 2), swap(weights, "tiles", 1)
        if bit == groups // 2:
            got, routes, near = tie((got, routes, near))
        strips = jnp.where((mask & bit) != 0, got, strips)
        bit *= 2

    def gather(rows, near, far, far_near):
        return gather_rows(routes, (rows, near, far, far_near), groups * TILE_DEV)

    def along(own, *away):
        return [own] + [swap(part, "frames", 2 * (j + 1)) for j, part in enumerate(away)]

    first, second = blend(strip_cell, strips, state)
    far_first, near_first = swap(first, "tiles", 2), swap(first, "tiles", 1)
    near_first, far, second = tie((near_first, far, second))
    far_second, near_second = swap(second, "tiles", 2), swap(second, "tiles", 1)
    home, away = gather(weights, near, far, swap(far, "tiles", 1))
    sums = add_halves(home, swap(away, "frames", 1))
    far_first, sums = tie((far_first, sums))
    got_weights = along(*sums)
    home, away = gather(first, near_first, far_first, swap(far_first, "tiles", 1))
    got = swap(away, "frames", 1)
    far_second, got = tie((far_second, got))
    far_near = swap(far_second, "tiles", 1)
    sums = add_halves(home, got)
    far_near, sums, got_weights = tie((far_near, sums, got_weights))
    got_first = along(*sums)
    home, away = gather(second, near_second, far_second, far_near)
    got_second = along(*add_halves(home, swap(away, "frames", 1)))
    return collapse(got_weights, got_first, got_second)


def solution(mesh):
    in_specs = (
        P(("frames", "tiles"), None, None, None),
        P(("frames", "tiles"), None, None),
        P(("frames", "tiles"), None, None),
        P(("frames", "tiles")),
        P(("frames", "tiles")),
        P(("frames", "tiles"), None, None),
        P(("frames", "tiles"), None),
    )
    out_specs = P(("frames", "tiles"), None, None)
    return jax.shard_map(local, mesh=mesh, in_specs=in_specs, out_specs=out_specs, check_vma=False)
```

```python
import functools

import jax
import jax.numpy as jnp
import numpy as np
from jax import lax
from jax.experimental import pallas as pl
from jax.experimental.pallas import tpu as pltpu
from jax.sharding import PartitionSpec as P

COLOURS = 3
FH = 128
FW = 1024
QB = 32
WIN = 256
TILE_DEV = 4
VMEM = 30 << 20
ROUTE = 4096
F32 = jnp.float32
BF16 = jnp.bfloat16


def shrink_matrix(n):
    m = np.zeros((n // 2, n), np.float32)
    for i in range(n // 2):
        for d, tap in zip(range(-2, 3), (1, 4, 6, 4, 1)):
            m[i, min(max(2 * i + d, 0), n - 1)] += tap / 16.0
    return m


def grow_matrix(n):
    m = np.zeros((2 * n, n), np.float32)
    for i in range(n):
        lo, hi = max(i - 1, 0), min(i + 1, n - 1)
        m[2 * i, lo] += 1 / 8
        m[2 * i, i] += 6 / 8
        m[2 * i, hi] += 1 / 8
        m[2 * i + 1, i] += 1 / 2
        m[2 * i + 1, hi] += 1 / 2
    return m


def padded(m, rows, cols):
    return np.pad(m, ((0, rows - m.shape[0]), (0, cols - m.shape[1])))


def row_order():
    m = np.zeros((FH, FH), np.float32)
    for r in range(2):
        for par in range(2):
            for i in range(32):
                m[r * 64 + par * 32 + i, r * 64 + 2 * i + par] = 1
    return m


def vertical():
    v = {1: shrink_matrix(128), 2: shrink_matrix(64), 3: shrink_matrix(32)}
    spread = np.zeros((16, 8), np.float32)
    for r in range(2):
        for i in range(4):
            spread[r * 8 + i, r * 4 + i] = 1
    v[4] = spread @ shrink_matrix(16)
    g = {0: row_order() @ grow_matrix(64), 1: grow_matrix(32), 2: grow_matrix(16)}
    g[3] = grow_matrix(8) @ spread.T
    return v, g


def horizontal(width):
    s = {k: shrink_matrix(width >> (k - 1)).T for k in range(1, 5)}
    g = {k: grow_matrix(width >> (k + 1)).T for k in range(4)}
    return s, g


def shrink_window():
    m = np.zeros((512, 128), np.float32)
    for i in range(128):
        for d, tap in zip(range(-2, 3), (1, 4, 6, 4, 1)):
            m[128 + 2 * i + d, i] = tap / 16.0
    return m


def grow_window():
    m = np.zeros((384, 256), np.float32)
    for i in range(128):
        for d, tap in zip(range(-1, 2), (1, 6, 1)):
            m[128 + i + d, 2 * i] = tap / 8.0
        m[128 + i, 2 * i + 1] = m[128 + i + 1, 2 * i + 1] = 0.5
    return m


def pack(mats, width):
    places, row, col, height = {}, 0, 0, 0
    for name in sorted(mats, key=lambda n: (-mats[n].shape[0], -mats[n].shape[1], n)):
        h, w = mats[name].shape
        wide = -(-w // 128) * 128
        if col + wide > width:
            row, col, height = row + height, 0, 0
        height = max(height, -(-h // 16) * 16)
        places[name] = (row, col, h, w)
        col += wide
    out = np.zeros((row + height, width), np.float32)
    for name, (r, c, h, w) in places.items():
        out[r : r + h, c : c + w] = mats[name]
    return jnp.asarray(out, BF16), places


def unpack(ref, places):
    return {name: ref[r : r + h, c : c + w] for name, (r, c, h, w) in places.items()}


def small_matrices():
    v, g = vertical()
    s, gh = horizontal(WIN)
    sm, _ = horizontal(64)
    mats = {f"v{k}": m for k, m in v.items()} | {f"g{k}": m for k, m in g.items()}
    mats |= {f"s{k}": m for k, m in s.items()} | {f"h{k}": m for k, m in gh.items()}
    mats |= {f"m{k}": m for k, m in sm.items()} | {"order": row_order()}
    return pack(mats, 512)


def large_matrices():
    mats = {"shrink": shrink_window(), "grow": grow_window()}
    mats["last"] = padded(shrink_matrix(128).T, 128, 128)
    mats["least"] = padded(grow_matrix(64).T, 128, 128)
    return pack(mats, 640)


def levels_of(mats, letter):
    return {int(n[1:]): m for n, m in mats.items() if n[0] == letter and n[1:].isdigit()}


def mm(a, b):
    return jnp.dot(a, b, preferred_element_type=F32)


def split(v):
    hi = v.astype(BF16)
    return hi, (v - hi.astype(F32)).astype(BF16)


def rdot(v, m):
    hi, lo = split(v)
    return mm(hi, m) + mm(lo, m)


def ldot(m, v):
    hi, lo = split(v)
    return mm(m, hi) + mm(m, lo)


def mmt(a, b):
    return lax.dot_general(a, b, (((1,), (1,)), ((), ())), preferred_element_type=F32)


def windows(v, m, step):
    rows, width = v.shape
    both = jnp.concatenate(split(v), axis=0)
    left = jnp.broadcast_to(both[:, :1], (2 * rows, 128))
    right = jnp.broadcast_to(both[:, width - 1 :], (2 * rows, 128))
    both = jnp.concatenate([left, both, right], axis=1)
    pieces = []
    for n in range(width // step):
        piece = mm(both[:, n * step : n * step + step + 256], m)
        pieces.append(piece[:rows] + piece[rows:])
    return jnp.concatenate(pieces, axis=1)


def right_of(m):
    return lambda v: rdot(v, m)


def pyramid(planes, v, shrinks, product=mm):
    n = len(planes)
    t = jnp.concatenate([product(v[1], p) for p in planes], axis=0)
    levels = {1: shrinks[1](t)}
    for k in range(2, 5):
        prev = levels[k - 1]
        rows = prev.shape[0] // n
        t = jnp.concatenate([ldot(v[k], prev[i * rows : (i + 1) * rows]) for i in range(n)], axis=0)
        levels[k] = shrinks[k](t)
    return levels


def grown(level, n, gv, grow):
    h = grow(level)
    rows = level.shape[0] // n
    return [ldot(gv, h[i * rows : (i + 1) * rows]) for i in range(n)]


def place(rows, cols, base, width, offset):
    i = lax.broadcasted_iota(jnp.int32, (rows, cols), 0)
    c = lax.broadcasted_iota(jnp.int32, (rows, cols), 1)
    hit = (i >= base) & (i < base + width) & (c - i == offset - base)
    return jnp.where(hit, 1.0, 0.0).astype(BF16)


def strips_kernel(places, cell, xa, xb, packed, out, acc):
    mats = unpack(packed, places)
    v, gv, s, gh = (levels_of(mats, letter) for letter in "vgsh")
    s, gh = ({k: right_of(m) for k, m in each.items()} for each in (s, gh))
    order = mats["order"]
    first = window_tile(cell[0]) * 128
    planes = [jnp.concatenate([xa[0, c], xb[0, c]], axis=1) for c in range(COLOURS)]
    levels = pyramid(planes, v, s)
    back = grown(levels[1], COLOURS, gv[0], gh[0])
    b0 = jnp.concatenate([mm(order, planes[c]) - back[c] for c in range(COLOURS)], axis=0)
    bands = [b0.astype(BF16)]
    for k in range(1, 4):
        back = grown(levels[k + 1], COLOURS, gv[k], gh[k])
        bands.append((levels[k] - jnp.concatenate(back, axis=0)).astype(BF16))
    bands.append(levels[4].astype(BF16))
    start = cell[0] * 16 - first

    def pick(band, base, k):
        i = lax.broadcasted_iota(jnp.int32, (band.shape[1], 128), 0)
        c = lax.broadcasted_iota(jnp.int32, (band.shape[1], 128), 1)
        hit = (c >= base) & (c < base + (64 >> k)) & (i - c == (start >> k) - base)
        return mm(band, jnp.where(hit, 1.0, 0.0).astype(BF16))

    out[0:192, :] = (pick(bands[0][0:192], 0, 0) + pick(bands[0][192:384], 64, 0)).astype(BF16)
    acc[...] = pick(bands[1][0:96], 0, 1) + pick(bands[1][96:192], 32, 1) + pick(bands[2], 64, 2)
    acc[0:48, :] = acc[0:48, :] + pick(bands[3], 80, 3) + pick(bands[4], 88, 4)
    out[192:288, :] = acc[...].astype(BF16)


def window_tile(cell):
    return jnp.clip((cell - 3) >> 3, 0, (FW - WIN) // 128)


def full_spec(a):
    return pl.BlockSpec(a.shape, lambda *_: (0,) * a.ndim)


def strips_of(frames, cell):
    packed, places = small_matrices()
    grid_spec = pltpu.PrefetchScalarGridSpec(
        num_scalar_prefetch=1,
        grid=(1,),
        in_specs=[
            pl.BlockSpec((1, COLOURS, FH, 128), lambda i, c: (0, 0, 0, window_tile(c[0]))),
            pl.BlockSpec((1, COLOURS, FH, 128), lambda i, c: (0, 0, 0, window_tile(c[0]) + 1)),
        ]
        + [full_spec(packed)],
        out_specs=pl.BlockSpec((288, 128), lambda i, c: (0, 0)),
        scratch_shapes=[pltpu.VMEM((96, 128), F32)],
    )
    return pl.pallas_call(
        functools.partial(strips_kernel, places),
        grid_spec=grid_spec,
        out_shape=jax.ShapeDtypeStruct((288, 128), BF16),
        compiler_params=pltpu.CompilerParams(vmem_limit_bytes=VMEM),
        cost_estimate=pl.CostEstimate(flops=2 * 10**9, bytes_accessed=10**6, transcendentals=0),
        name="strips",
    )(cell, frames, frames, packed)


def lane_index():
    return lax.broadcasted_iota(jnp.int32, (1, 128), 1)


def fold_level0(p, store):
    left = lane_index() < 64
    for r in range(2):
        for j in range(8):
            even = p[r * 64 : r * 64 + 32, j * 128 : j * 128 + 128]
            odd = p[r * 64 + 32 : r * 64 + 64, j * 128 : j * 128 + 128]
            store(r * 16 + 2 * j, jnp.where(left, even, pltpu.roll(odd, 64, 1)))
            store(r * 16 + 2 * j + 1, jnp.where(left, pltpu.roll(even, 64, 1), odd))


def gather_channels(parts, width, cc, base):
    groups = 128 // width
    group = lane_index() // width
    out = jnp.zeros_like(parts[0])
    for ch in range(4):
        out = jnp.where(group == (cc + ch) % groups, parts[ch], out)
    return pltpu.roll(out, (base - cc * width) % 128, 1)


STATE_ROWS = 816


def state_views(state):
    at = lambda r, h, c, w: (slice(r, r + h), slice(c, c + w))
    b0 = [at(128 * c, 128, 0, 1024) for c in range(3)]
    l1 = [at(384, 64, 0, 512), at(384, 64, 512, 512), at(448, 64, 0, 512), at(448, 64, 512, 512)]
    l2 = [at(512, 32, 256 * c, 256) for c in range(4)]
    l3 = [at(544, 16, 128 * c, 128) for c in range(4)]
    l4 = [at(544, 16, 512 + 128 * c, 128) for c in range(4)]
    levels = [b0 + [at(560, 128, 0, 1024)], l1, l2, l3, l4]
    masks = [at(688, 128 >> k, 128 * k, 64 >> k) for k in range(4)] + [at(688, 16, 512, 4)]
    return levels, masks


def bands_kernel(small_places, large_places, x, w, m, small, large, wblocks, state):
    mats = unpack(small, small_places)
    v, gv, sm = (levels_of(mats, letter) for letter in "vgm")
    order = mats["order"]
    sm = {k: right_of(each) for k, each in sm.items()}
    mats = unpack(large, large_places)
    half = lambda each: windows(each, mats["shrink"], 256)
    twice = lambda each: windows(each, mats["grow"], 128)
    s = {1: half, 2: half, 3: half, 4: right_of(mats["last"])}
    gh = {0: twice, 1: twice, 2: twice, 3: right_of(mats["least"])}
    views, mask_views = state_views(state)
    planes = [x[0, c] for c in range(COLOURS)] + [w[0]]
    weights = mm(order, planes[3])
    state[views[0][3]] = weights

    def store(q, piece):
        wblocks[q] = piece.astype(BF16)

    fold_level0(weights, store)
    levels = pyramid(planes, v, s)
    for k in range(1, 5):
        rows = levels[k].shape[0] // 4
        state[views[k][3]] = levels[k][3 * rows :]
    back = grown(levels[1][: 3 * 64], COLOURS, gv[0], gh[0])
    for c in range(COLOURS):
        state[views[0][c]] = mm(order, planes[c]) - back[c]
    for k in range(1, 4):
        rows = levels[k].shape[0] // 4
        below = levels[k + 1].shape[0] // 4
        back = grown(levels[k + 1][: 3 * below], COLOURS, gv[k], gh[k])
        for c in range(COLOURS):
            state[views[k][c]] = levels[k][c * rows : (c + 1) * rows] - back[c]
    for c in range(COLOURS):
        state[views[4][c]] = levels[4][c * 16 : (c + 1) * 16]
    other = (1.0 - m[0].astype(F32)).astype(BF16)
    state[mask_views[0]] = mmt(order, other)
    masks = pyramid([other], v, sm, mmt)
    for k in range(1, 5):
        state[mask_views[k]] = masks[k]


def bands_of(frames, weight_map, seam_mask):
    small, small_places = small_matrices()
    large, large_places = large_matrices()
    return pl.pallas_call(
        functools.partial(bands_kernel, small_places, large_places),
        out_shape=[jax.ShapeDtypeStruct((QB, 32, 128), BF16), jax.ShapeDtypeStruct((STATE_ROWS, FW), F32)],
        compiler_params=pltpu.CompilerParams(vmem_limit_bytes=VMEM),
        cost_estimate=pl.CostEstimate(flops=8 * 10**9, bytes_accessed=6 * 10**6, transcendentals=0),
        name="bands",
    )(frames, weight_map, jnp.swapaxes(seam_mask, 1, 2), small, large)


def blend_kernel(cell, strips, state, first, second):
    views, mask_views = state_views(state)
    (b0, b1, b2, b3, b4) = [[state[view] for view in views[k][:3]] for k in range(5)]
    (wp, w1, w2, w3, w4) = [state[views[k][3]] for k in range(5)]
    (n0, n1, n2, n3, n4) = [state[view] for view in mask_views]
    start = cell[0] * 16
    low = strips[192:288]

    def mixed(band, remote, share):
        return band + share * (remote - band)

    widths = (1024, 512, 256, 128, 128)
    share0 = mm(n0.astype(BF16), place(64, 1024, 0, 64, start))
    share = [share0]
    for k, ref in enumerate((n1, n2, n3, n4)):
        share.append(rdot(ref, place(64 >> (k + 1), widths[k + 1], 0, 64 >> (k + 1), start >> (k + 1))))
    top = strips[0:192]
    remote0 = [mm(top, place(128, 1024, 0, 64, start)), mm(top, place(128, 1024, 64, 64, start))]
    remote0 = jnp.concatenate(remote0, axis=0)
    weights = wp
    for c in range(COLOURS):
        p = weights * mixed(b0[c], remote0[c * 128 : (c + 1) * 128], share[0])
        out, row = (first, 0) if c == 0 else (second, 32 * (c - 1))

        def store(q, piece, out=out, row=row):
            out[q, row : row + 32, :] = piece.astype(BF16)

        fold_level0(p, store)
    remote1 = [mm(low, place(128, 512, 0, 32, start >> 1)), mm(low, place(128, 512, 32, 32, start >> 1))]
    remote1 = jnp.concatenate(remote1, axis=0)
    parts = [w1 * mixed(b1[c], remote1[c * 64 : (c + 1) * 64], share[1]) for c in range(COLOURS)] + [w1]
    for r in range(2):
        for j in range(4):
            turned = [parts[ch][r * 32 : r * 32 + 32, j * 128 : j * 128 + 128] for ch in range(4)]
            turned = [turned[0]] + [pltpu.roll(turned[ch], 32 * ch, 1) for ch in range(1, 4)]
            for cc in range(4):
                first[r * 16 + 4 * j + cc, 32:64, :] = gather_channels(turned, 32, cc, 0).astype(BF16)
    remote2 = mm(low, place(128, 256, 64, 16, start >> 2))
    remote3 = mm(low[0:48], place(128, 128, 80, 8, start >> 3))
    remote4 = mm(low[0:48], place(128, 128, 88, 4, start >> 4))
    parts2 = [w2 * mixed(b2[c], remote2[c * 32 : (c + 1) * 32], share[2]) for c in range(COLOURS)] + [w2]
    parts3 = [w3 * mixed(b3[c], remote3[c * 16 : (c + 1) * 16], share[3]) for c in range(COLOURS)] + [w3]
    parts4 = [w4 * mixed(b4[c], remote4[c * 16 : (c + 1) * 16], share[4]) for c in range(COLOURS)] + [w4]
    lane = lane_index()
    for r in range(2):
        turned3 = [pltpu.roll(parts3[ch][r * 8 : r * 8 + 8], 8 * ch, 1) for ch in range(4)]
        turned4 = [pltpu.roll(parts4[ch][r * 8 : r * 8 + 8], 4 * ch, 1) for ch in range(4)]
        for j in range(2):
            turned2 = [parts2[ch][r * 16 : r * 16 + 16, j * 128 : j * 128 + 128] for ch in range(4)]
            turned2 = [pltpu.roll(turned2[ch], 16 * ch, 1) for ch in range(4)]
            for cc in range(8):
                c = j * 8 + cc
                two = gather_channels(turned2, 16, cc, 0)
                three = gather_channels(turned3, 8, c, 64)
                four = gather_channels(turned4, 4, c, 96)
                head = jnp.where(lane < 64, two[0:8], jnp.where(lane < 96, three, four))
                tail = jnp.where(lane < 64, two[8:16], 0.0)
                first[r * 16 + c, 64:80, :] = jnp.concatenate([head, tail], axis=0).astype(BF16)


def blend(cell, strips, state):
    vmem = pl.BlockSpec(memory_space=pltpu.VMEM)
    return pl.pallas_call(
        blend_kernel,
        in_specs=[pl.BlockSpec(memory_space=pltpu.SMEM)] + [vmem] * 2,
        out_shape=[jax.ShapeDtypeStruct((QB, 80, 128), BF16), jax.ShapeDtypeStruct((QB, 64, 128), BF16)],
        compiler_params=pltpu.CompilerParams(vmem_limit_bytes=VMEM),
        cost_estimate=pl.CostEstimate(flops=10**6, bytes_accessed=10**4, transcendentals=0),
        name="blend",
    )(cell, strips, state)


def routes_kernel(spot, lists, counts):
    for source in range(4):

        def body(q, count, source=source):
            at = spot[source, q]
            lists[source, count] = q * ROUTE + at
            return jnp.where(at >= 0, count + 1, count)

        counts[source] = lax.fori_loop(0, QB, body, 0)


def routes_of(spot):
    smem = pl.BlockSpec(memory_space=pltpu.SMEM)
    return pl.pallas_call(
        routes_kernel,
        in_specs=[smem],
        out_specs=[smem, smem],
        out_shape=[jax.ShapeDtypeStruct((4, QB + 1), jnp.int32), jax.ShapeDtypeStruct((4,), jnp.int32)],
        name="routes",
    )(spot)


def gather_kernel(lists, counts, a, b, c, d, home, away, acc):
    acc[...] = jnp.zeros_like(acc)
    for source, ref in enumerate((a, b, c, d)):

        def body(i, carry, source=source, ref=ref):
            entry = lists[source, i]
            q, at = entry // ROUTE, entry % ROUTE
            acc[at] = acc[at] + ref[q].astype(F32)
            return carry

        lax.fori_loop(0, counts[source], body, 0)
    tiles = home.shape[0]
    home[...] = acc[0:tiles]
    away[...] = acc[tiles : 2 * tiles].astype(BF16)


def gather_rows(routes, rows, tiles):
    height = rows[0].shape[1]
    vmem = pl.BlockSpec(memory_space=pltpu.VMEM)
    shape = (tiles // 2, height, 128)
    return pl.pallas_call(
        gather_kernel,
        in_specs=[pl.BlockSpec(memory_space=pltpu.SMEM)] * 2 + [vmem] * 4,
        out_shape=[jax.ShapeDtypeStruct(shape, F32), jax.ShapeDtypeStruct(shape, BF16)],
        scratch_shapes=[pltpu.VMEM((tiles, height, 128), F32)],
        compiler_params=pltpu.CompilerParams(vmem_limit_bytes=VMEM),
        cost_estimate=pl.CostEstimate(flops=10**6, bytes_accessed=10**4, transcendentals=0),
        name="gather_rows",
    )(*routes, *rows)


def add_kernel(home, got, own, *away):
    for j in range(len(away) + 1):
        lo = j * TILE_DEV
        total = home[lo : lo + TILE_DEV] + got[lo : lo + TILE_DEV].astype(F32)
        if j == 0:
            own[...] = total
        else:
            away[j - 1][...] = total.astype(BF16)


def add_halves(home, got):
    shape = (TILE_DEV,) + home.shape[1:]
    others = home.shape[0] // TILE_DEV - 1
    return pl.pallas_call(
        add_kernel,
        out_shape=[jax.ShapeDtypeStruct(shape, F32)] + [jax.ShapeDtypeStruct(shape, BF16)] * others,
        compiler_params=pltpu.CompilerParams(vmem_limit_bytes=VMEM),
        cost_estimate=pl.CostEstimate(flops=10**6, bytes_accessed=10**4, transcendentals=0),
        name="add_halves",
    )(home, got)


def collapse_matrices():
    def across(src, dst, width):
        g = grow_matrix(width).T
        m = np.zeros((128, 128), np.float32)
        for ch in range(COLOURS):
            m[src + ch * width : src + (ch + 1) * width, dst + ch * 2 * width : dst + (ch + 1) * 2 * width] = g
        return m

    last = np.zeros((128, 384), np.float32)
    g = grow_matrix(32).T
    for ch in range(COLOURS):
        for half in range(2):
            last[ch * 32 : ch * 32 + 32, ch * 128 + half * 64 : ch * 128 + half * 64 + 64] = g

    def down(n, rows_in, rows_out, pick=None):
        g = grow_matrix(n)
        g = g if pick is None else g[pick::2]
        m = np.zeros((TILE_DEV * rows_out, TILE_DEV * rows_in), np.float32)
        for t in range(TILE_DEV):
            m[t * rows_out : t * rows_out + g.shape[0], t * rows_in : t * rows_in + n] = g
        return m

    mats = {"m43": across(96, 64, 4), "m32": across(64, 0, 8), "m21": across(0, 0, 16), "m10": last}
    mats |= {"d43": down(4, 16, 16), "d32": down(8, 16, 16), "d21": down(16, 16, 32)}
    mats |= {"even": down(32, 32, 32, 0), "odd": down(32, 32, 32, 1)}
    return pack(mats, 1280)


def collapse_kernel(places, each, packed, *refs):
    mats = unpack(packed, places)
    a, b, c = (refs[i * each : (i + 1) * each] for i in range(3))
    out, level0 = refs[3 * each :]

    def total(sources, lo, hi):
        acc = sources[0][:, lo:hi, :]
        for source in sources[1:]:
            acc = acc + source[:, lo:hi, :].astype(F32)
        return acc.reshape(TILE_DEV * (hi - lo), 128)

    lane = lane_index()
    small = total(b, 64, 80)
    bottom = small
    for lo, width, chans in ((0, 16, 3), (64, 8, 3), (96, 4, 3)):
        for ch in range(chans):
            inside = (lane >= lo + ch * width) & (lane < lo + (ch + 1) * width)
            bottom = jnp.where(inside, pltpu.roll(small, (128 - (3 - ch) * width) % 128, 1), bottom)
    small = small / jnp.maximum(bottom, 1.0)
    three = small + ldot(mats["d43"], rdot(small, mats["m43"]))
    two = small + ldot(mats["d32"], rdot(three, mats["m32"]))
    one = total(b, 32, 64)
    bottom = one
    for ch in range(3):
        inside = (lane >= ch * 32) & (lane < (ch + 1) * 32)
        bottom = jnp.where(inside, pltpu.roll(one, (128 - (3 - ch) * 32) % 128, 1), bottom)
    one = one / jnp.maximum(bottom, 1.0) + ldot(mats["d21"], rdot(two, mats["m21"]))
    wide = rdot(one, mats["m10"])
    hi, lo = split(wide)
    up = mm(mats["even"], hi) + mm(mats["even"], lo)
    down = mm(mats["odd"], hi) + mm(mats["odd"], lo)
    bottom = jnp.maximum(total(a, 0, 32), 1.0)
    for ch in range(COLOURS):
        own = total(b, 0, 32) if ch == 0 else total(c, 32 * (ch - 1), 32 * ch)
        back = jnp.where(lane < 64, up[:, ch * 128 : ch * 128 + 128], down[:, ch * 128 : ch * 128 + 128])
        level0[ch * 128 : ch * 128 + 128, :] = own / bottom + back
    for ch in range(COLOURS):
        for row in range(32):
            out[ch, :, row * 128 : row * 128 + 128] = level0[pl.ds(ch * 128 + row, TILE_DEV, stride=32), :]


def collapse(a, b, c):
    packed, places = collapse_matrices()
    tiles = pl.pallas_call(
        functools.partial(collapse_kernel, places, len(a)),
        out_shape=jax.ShapeDtypeStruct((COLOURS, TILE_DEV, 4096), F32),
        scratch_shapes=[pltpu.VMEM((COLOURS * 128, 128), F32)],
        compiler_params=pltpu.CompilerParams(vmem_limit_bytes=VMEM),
        cost_estimate=pl.CostEstimate(flops=10**6, bytes_accessed=10**4, transcendentals=0),
        name="collapse",
    )(packed, *a, *b, *c)
    return jnp.swapaxes(tiles, 0, 1)


def swap(value, axis, bit):
    size = lax.axis_size(axis)
    return lax.ppermute(value, axis, [(i, i ^ bit) for i in range(size)])


def local(frames, weight_map, seam_mask, strip_cell, partner, tile_group, tile_position_in_group):
    groups = lax.axis_size("frames")
    parts = lax.axis_size("tiles")
    mine = lax.axis_index("tiles")
    mask = lax.bitwise_xor(partner[0] // parts, lax.axis_index("frames"))

    tie = lax.optimization_barrier
    strips = strips_of(frames, strip_cell)
    ids = tile_group.reshape(QB) * (parts * TILE_DEV) + tile_position_in_group.reshape(QB)
    strips, frames, ids = tie((strips, frames, ids))
    ids = jnp.stack([ids, swap(ids, "tiles", 1)])
    ids_x = jnp.concatenate([ids, swap(ids, "tiles", 2)])
    ids_y = jnp.concatenate([ids, swap(ids, "frames", 1)])

    def relative(ids):
        group, tile = ids // (parts * TILE_DEV), ids % (parts * TILE_DEV)
        group = lax.bitwise_xor(group, lax.axis_index("frames"))
        return group, lax.bitwise_xor(tile // TILE_DEV, mine), tile % TILE_DEV

    half = groups // 2
    group, part, tile = relative(ids_x)
    spot_x = jnp.where(part == 0, ((group & 1) * half + (group >> 1)) * TILE_DEV + tile, -1)
    group, part, tile = relative(ids_y)
    here = ((group & 1) == 0) & ((part & 1) == 0)
    spot_y = jnp.where(here, ((part >> 1) * half + (group >> 1)) * TILE_DEV + tile, -1)

    weights, state = bands_of(frames, weight_map, seam_mask)
    bit = 1
    while bit < groups:
        got = swap(strips, "frames", bit)
        if bit == 1:
            got, weights, state = tie((got, weights, state))
            far, near = swap(weights, "tiles", 2), swap(weights, "tiles", 1)
        if bit == 2:
            got, far, near = tie((got, far, near))
        if bit == half:
            got, spot_x, spot_y = tie((got, spot_x, spot_y))
        strips = jnp.where((mask & bit) != 0, got, strips)
        bit *= 2

    def gather(routes, *rows):
        return gather_rows(routes, rows, groups * TILE_DEV)

    def along(own, *away):
        return [own] + [swap(part, "frames", 2 * (j + 1)) for j, part in enumerate(away)]

    first, second = blend(strip_cell, strips, state)
    first, second, spot_x, spot_y, far = tie((first, second, spot_x, spot_y, far))
    far_first, near_first = swap(first, "tiles", 2), swap(first, "tiles", 1)
    far_second, near_second = swap(second, "frames", 1), swap(second, "tiles", 1)
    routes_x, routes_y = routes_of(spot_x), routes_of(spot_y)
    home_w, away_w = gather(routes_x, weights, near, far, swap(far, "tiles", 1))
    got_w = swap(away_w, "frames", 1)
    far_second, home_w, routes_y = tie((far_second, home_w, routes_y))
    home_s, away_s = gather(routes_y, second, near_second, far_second, swap(far_second, "tiles", 1))
    got_s = swap(away_s, "tiles", 2)
    far_first, home_s, got_w = tie((far_first, home_s, got_w))
    far_near = swap(far_first, "tiles", 1)
    sums_w = add_halves(home_w, got_w)
    far_near, sums_w = tie((far_near, sums_w))
    got_weights = along(*sums_w)
    home_f, away_f = gather(routes_x, first, near_first, far_first, far_near)
    got_f = swap(away_f, "frames", 1)
    sums_s = add_halves(home_s, got_s)
    got_f, sums_s, got_weights = tie((got_f, sums_s, got_weights))
    got_second = along(*sums_s)
    got_first = along(*add_halves(home_f, got_f))
    return collapse(got_weights, got_first, got_second)


def solution(mesh):
    in_specs = (
        P(("frames", "tiles"), None, None, None),
        P(("frames", "tiles"), None, None),
        P(("frames", "tiles"), None, None),
        P(("frames", "tiles")),
        P(("frames", "tiles")),
        P(("frames", "tiles"), None, None),
        P(("frames", "tiles"), None),
    )
    out_specs = P(("frames", "tiles"), None, None)
    return jax.shard_map(local, mesh=mesh, in_specs=in_specs, out_specs=out_specs, check_vma=False)
```

```python
import functools

import jax
import jax.numpy as jnp
import numpy as np
from jax import lax
from jax.experimental import pallas as pl
from jax.experimental.pallas import tpu as pltpu
from jax.sharding import PartitionSpec as P

COLOURS = 3
FH = 128
FW = 1024
QB = 32
WIN = 256
TILE_DEV = 4
VMEM = 30 << 20
ROUTE = 4096
F32 = jnp.float32
BF16 = jnp.bfloat16


def shrink_matrix(n):
    m = np.zeros((n // 2, n), np.float32)
    for i in range(n // 2):
        for d, tap in zip(range(-2, 3), (1, 4, 6, 4, 1)):
            m[i, min(max(2 * i + d, 0), n - 1)] += tap / 16.0
    return m


def grow_matrix(n):
    m = np.zeros((2 * n, n), np.float32)
    for i in range(n):
        lo, hi = max(i - 1, 0), min(i + 1, n - 1)
        m[2 * i, lo] += 1 / 8
        m[2 * i, i] += 6 / 8
        m[2 * i, hi] += 1 / 8
        m[2 * i + 1, i] += 1 / 2
        m[2 * i + 1, hi] += 1 / 2
    return m


def padded(m, rows, cols):
    return np.pad(m, ((0, rows - m.shape[0]), (0, cols - m.shape[1])))


def row_order():
    m = np.zeros((FH, FH), np.float32)
    for r in range(2):
        for par in range(2):
            for i in range(32):
                m[r * 64 + par * 32 + i, r * 64 + 2 * i + par] = 1
    return m


def vertical():
    v = {1: shrink_matrix(128), 2: shrink_matrix(64), 3: shrink_matrix(32)}
    spread = np.zeros((16, 8), np.float32)
    for r in range(2):
        for i in range(4):
            spread[r * 8 + i, r * 4 + i] = 1
    v[4] = spread @ shrink_matrix(16)
    g = {0: row_order() @ grow_matrix(64), 1: grow_matrix(32), 2: grow_matrix(16)}
    g[3] = grow_matrix(8) @ spread.T
    return v, g


def horizontal(width):
    s = {k: shrink_matrix(width >> (k - 1)).T for k in range(1, 5)}
    g = {k: grow_matrix(width >> (k + 1)).T for k in range(4)}
    return s, g


def shrink_window():
    m = np.zeros((512, 128), np.float32)
    for i in range(128):
        for d, tap in zip(range(-2, 3), (1, 4, 6, 4, 1)):
            m[128 + 2 * i + d, i] = tap / 16.0
    return m


def grow_window():
    m = np.zeros((384, 256), np.float32)
    for i in range(128):
        for d, tap in zip(range(-1, 2), (1, 6, 1)):
            m[128 + i + d, 2 * i] = tap / 8.0
        m[128 + i, 2 * i + 1] = m[128 + i + 1, 2 * i + 1] = 0.5
    return m


def pack(mats, width):
    places, row, col, height = {}, 0, 0, 0
    for name in sorted(mats, key=lambda n: (-mats[n].shape[0], -mats[n].shape[1], n)):
        h, w = mats[name].shape
        wide = -(-w // 128) * 128
        if col + wide > width:
            row, col, height = row + height, 0, 0
        height = max(height, -(-h // 16) * 16)
        places[name] = (row, col, h, w)
        col += wide
    out = np.zeros((row + height, width), np.float32)
    for name, (r, c, h, w) in places.items():
        out[r : r + h, c : c + w] = mats[name]
    return jnp.asarray(out, BF16), places


def unpack(ref, places):
    return {name: ref[r : r + h, c : c + w] for name, (r, c, h, w) in places.items()}


def small_matrices():
    v, g = vertical()
    s, gh = horizontal(WIN)
    sm, _ = horizontal(64)
    mats = {f"v{k}": m for k, m in v.items()} | {f"g{k}": m for k, m in g.items()}
    mats |= {f"s{k}": m for k, m in s.items()} | {f"h{k}": m for k, m in gh.items()}
    mats |= {f"m{k}": m for k, m in sm.items()} | {"order": row_order()}
    return pack(mats, 512)


def large_matrices():
    mats = {"shrink": shrink_window(), "grow": grow_window()}
    mats["last"] = padded(shrink_matrix(128).T, 128, 128)
    mats["least"] = padded(grow_matrix(64).T, 128, 128)
    return pack(mats, 640)


def levels_of(mats, letter):
    return {int(n[1:]): m for n, m in mats.items() if n[0] == letter and n[1:].isdigit()}


def mm(a, b):
    return jnp.dot(a, b, preferred_element_type=F32)


def split(v):
    hi = v.astype(BF16)
    return hi, (v - hi.astype(F32)).astype(BF16)


def rdot(v, m):
    hi, lo = split(v)
    return mm(hi, m) + mm(lo, m)


def ldot(m, v):
    hi, lo = split(v)
    return mm(m, hi) + mm(m, lo)


def mmt(a, b):
    return lax.dot_general(a, b, (((1,), (1,)), ((), ())), preferred_element_type=F32)


def windows(v, m, step):
    rows, width = v.shape
    both = jnp.concatenate(split(v), axis=0)
    left = jnp.broadcast_to(both[:, :1], (2 * rows, 128))
    right = jnp.broadcast_to(both[:, width - 1 :], (2 * rows, 128))
    both = jnp.concatenate([left, both, right], axis=1)
    pieces = []
    for n in range(width // step):
        piece = mm(both[:, n * step : n * step + step + 256], m)
        pieces.append(piece[:rows] + piece[rows:])
    return jnp.concatenate(pieces, axis=1)


def right_of(m):
    return lambda v: rdot(v, m)


def pyramid(planes, v, shrinks, product=mm):
    n = len(planes)
    t = jnp.concatenate([product(v[1], p) for p in planes], axis=0)
    levels = {1: shrinks[1](t)}
    for k in range(2, 5):
        prev = levels[k - 1]
        rows = prev.shape[0] // n
        t = jnp.concatenate([ldot(v[k], prev[i * rows : (i + 1) * rows]) for i in range(n)], axis=0)
        levels[k] = shrinks[k](t)
    return levels


def grown(level, n, gv, grow):
    h = grow(level)
    rows = level.shape[0] // n
    return [ldot(gv, h[i * rows : (i + 1) * rows]) for i in range(n)]


def place(rows, cols, base, width, offset):
    i = lax.broadcasted_iota(jnp.int32, (rows, cols), 0)
    c = lax.broadcasted_iota(jnp.int32, (rows, cols), 1)
    hit = (i >= base) & (i < base + width) & (c - i == offset - base)
    return jnp.where(hit, 1.0, 0.0).astype(BF16)


def strips_kernel(places, cell, xa, xb, packed, out, acc):
    mats = unpack(packed, places)
    v, gv, s, gh = (levels_of(mats, letter) for letter in "vgsh")
    s, gh = ({k: right_of(m) for k, m in each.items()} for each in (s, gh))
    order = mats["order"]
    first = window_tile(cell[0]) * 128
    planes = [jnp.concatenate([xa[0, c], xb[0, c]], axis=1) for c in range(COLOURS)]
    levels = pyramid(planes, v, s)
    back = grown(levels[1], COLOURS, gv[0], gh[0])
    b0 = jnp.concatenate([mm(order, planes[c]) - back[c] for c in range(COLOURS)], axis=0)
    bands = [b0.astype(BF16)]
    for k in range(1, 4):
        back = grown(levels[k + 1], COLOURS, gv[k], gh[k])
        bands.append((levels[k] - jnp.concatenate(back, axis=0)).astype(BF16))
    bands.append(levels[4].astype(BF16))
    start = cell[0] * 16 - first

    def pick(band, base, k):
        i = lax.broadcasted_iota(jnp.int32, (band.shape[1], 128), 0)
        c = lax.broadcasted_iota(jnp.int32, (band.shape[1], 128), 1)
        hit = (c >= base) & (c < base + (64 >> k)) & (i - c == (start >> k) - base)
        return mm(band, jnp.where(hit, 1.0, 0.0).astype(BF16))

    out[0:192, :] = (pick(bands[0][0:192], 0, 0) + pick(bands[0][192:384], 64, 0)).astype(BF16)
    acc[...] = pick(bands[1][0:96], 0, 1) + pick(bands[1][96:192], 32, 1) + pick(bands[2], 64, 2)
    acc[0:48, :] = acc[0:48, :] + pick(bands[3], 80, 3) + pick(bands[4], 88, 4)
    out[192:288, :] = acc[...].astype(BF16)


def window_tile(cell):
    return jnp.clip((cell - 3) >> 3, 0, (FW - WIN) // 128)


def full_spec(a):
    return pl.BlockSpec(a.shape, lambda *_: (0,) * a.ndim)


def strips_of(frames, cell):
    packed, places = small_matrices()
    grid_spec = pltpu.PrefetchScalarGridSpec(
        num_scalar_prefetch=1,
        grid=(1,),
        in_specs=[
            pl.BlockSpec((1, COLOURS, FH, 128), lambda i, c: (0, 0, 0, window_tile(c[0]))),
            pl.BlockSpec((1, COLOURS, FH, 128), lambda i, c: (0, 0, 0, window_tile(c[0]) + 1)),
        ]
        + [full_spec(packed)],
        out_specs=pl.BlockSpec((288, 128), lambda i, c: (0, 0)),
        scratch_shapes=[pltpu.VMEM((96, 128), F32)],
    )
    return pl.pallas_call(
        functools.partial(strips_kernel, places),
        grid_spec=grid_spec,
        out_shape=jax.ShapeDtypeStruct((288, 128), BF16),
        compiler_params=pltpu.CompilerParams(vmem_limit_bytes=VMEM),
        cost_estimate=pl.CostEstimate(flops=2 * 10**9, bytes_accessed=10**6, transcendentals=0),
        name="strips",
    )(cell, frames, frames, packed)


def lane_index():
    return lax.broadcasted_iota(jnp.int32, (1, 128), 1)


def fold_level0(p, store):
    left = lane_index() < 64
    for r in range(2):
        for j in range(8):
            even = p[r * 64 : r * 64 + 32, j * 128 : j * 128 + 128]
            odd = p[r * 64 + 32 : r * 64 + 64, j * 128 : j * 128 + 128]
            store(r * 16 + 2 * j, jnp.where(left, even, pltpu.roll(odd, 64, 1)))
            store(r * 16 + 2 * j + 1, jnp.where(left, pltpu.roll(even, 64, 1), odd))


def gather_channels(parts, width, cc, base):
    groups = 128 // width
    group = lane_index() // width
    out = jnp.zeros_like(parts[0])
    for ch in range(4):
        out = jnp.where(group == (cc + ch) % groups, parts[ch], out)
    return pltpu.roll(out, (base - cc * width) % 128, 1)


STATE_ROWS = 816


def state_views(state):
    at = lambda r, h, c, w: (slice(r, r + h), slice(c, c + w))
    b0 = [at(128 * c, 128, 0, 1024) for c in range(3)]
    l1 = [at(384, 64, 0, 512), at(384, 64, 512, 512), at(448, 64, 0, 512), at(448, 64, 512, 512)]
    l2 = [at(512, 32, 256 * c, 256) for c in range(4)]
    l3 = [at(544, 16, 128 * c, 128) for c in range(4)]
    l4 = [at(544, 16, 512 + 128 * c, 128) for c in range(4)]
    levels = [b0 + [at(560, 128, 0, 1024)], l1, l2, l3, l4]
    masks = [at(688, 128 >> k, 128 * k, 64 >> k) for k in range(4)] + [at(688, 16, 512, 4)]
    return levels, masks


def bands_kernel(small_places, large_places, x, w, m, small, large, wblocks, state):
    mats = unpack(small, small_places)
    v, gv, sm = (levels_of(mats, letter) for letter in "vgm")
    order = mats["order"]
    sm = {k: right_of(each) for k, each in sm.items()}
    mats = unpack(large, large_places)
    half = lambda each: windows(each, mats["shrink"], 256)
    twice = lambda each: windows(each, mats["grow"], 128)
    s = {1: half, 2: half, 3: half, 4: right_of(mats["last"])}
    gh = {0: twice, 1: twice, 2: twice, 3: right_of(mats["least"])}
    views, mask_views = state_views(state)
    planes = [x[0, c] for c in range(COLOURS)] + [w[0]]
    weights = mm(order, planes[3])
    state[views[0][3]] = weights

    def store(q, piece):
        wblocks[q] = piece.astype(BF16)

    fold_level0(weights, store)
    levels = pyramid(planes, v, s)
    for k in range(1, 5):
        rows = levels[k].shape[0] // 4
        state[views[k][3]] = levels[k][3 * rows :]
    back = grown(levels[1][: 3 * 64], COLOURS, gv[0], gh[0])
    for c in range(COLOURS):
        state[views[0][c]] = mm(order, planes[c]) - back[c]
    for k in range(1, 4):
        rows = levels[k].shape[0] // 4
        below = levels[k + 1].shape[0] // 4
        back = grown(levels[k + 1][: 3 * below], COLOURS, gv[k], gh[k])
        for c in range(COLOURS):
            state[views[k][c]] = levels[k][c * rows : (c + 1) * rows] - back[c]
    for c in range(COLOURS):
        state[views[4][c]] = levels[4][c * 16 : (c + 1) * 16]
    other = (1.0 - m[0].astype(F32)).astype(BF16)
    state[mask_views[0]] = mmt(order, other)
    masks = pyramid([other], v, sm, mmt)
    for k in range(1, 5):
        state[mask_views[k]] = masks[k]


def bands_of(frames, weight_map, seam_mask):
    small, small_places = small_matrices()
    large, large_places = large_matrices()
    return pl.pallas_call(
        functools.partial(bands_kernel, small_places, large_places),
        out_shape=[jax.ShapeDtypeStruct((QB, 32, 128), BF16), jax.ShapeDtypeStruct((STATE_ROWS, FW), F32)],
        compiler_params=pltpu.CompilerParams(vmem_limit_bytes=VMEM),
        cost_estimate=pl.CostEstimate(flops=8 * 10**9, bytes_accessed=6 * 10**6, transcendentals=0),
        name="bands",
    )(frames, weight_map, jnp.swapaxes(seam_mask, 1, 2), small, large)


def blend_kernel(cell, strips, state, first, second):
    views, mask_views = state_views(state)
    (b0, b1, b2, b3, b4) = [[state[view] for view in views[k][:3]] for k in range(5)]
    (wp, w1, w2, w3, w4) = [state[views[k][3]] for k in range(5)]
    (n0, n1, n2, n3, n4) = [state[view] for view in mask_views]
    start = cell[0] * 16
    low = strips[192:288]

    def mixed(band, remote, share):
        return band + share * (remote - band)

    widths = (1024, 512, 256, 128, 128)
    share0 = mm(n0.astype(BF16), place(64, 1024, 0, 64, start))
    share = [share0]
    for k, ref in enumerate((n1, n2, n3, n4)):
        share.append(rdot(ref, place(64 >> (k + 1), widths[k + 1], 0, 64 >> (k + 1), start >> (k + 1))))
    top = strips[0:192]
    remote0 = [mm(top, place(128, 1024, 0, 64, start)), mm(top, place(128, 1024, 64, 64, start))]
    remote0 = jnp.concatenate(remote0, axis=0)
    weights = wp
    for c in range(COLOURS):
        p = weights * mixed(b0[c], remote0[c * 128 : (c + 1) * 128], share[0])
        out, row = (first, 0) if c == 0 else (second, 32 * (c - 1))

        def store(q, piece, out=out, row=row):
            out[q, row : row + 32, :] = piece.astype(BF16)

        fold_level0(p, store)
    remote1 = [mm(low, place(128, 512, 0, 32, start >> 1)), mm(low, place(128, 512, 32, 32, start >> 1))]
    remote1 = jnp.concatenate(remote1, axis=0)
    parts = [w1 * mixed(b1[c], remote1[c * 64 : (c + 1) * 64], share[1]) for c in range(COLOURS)] + [w1]
    for r in range(2):
        for j in range(4):
            turned = [parts[ch][r * 32 : r * 32 + 32, j * 128 : j * 128 + 128] for ch in range(4)]
            turned = [turned[0]] + [pltpu.roll(turned[ch], 32 * ch, 1) for ch in range(1, 4)]
            for cc in range(4):
                first[r * 16 + 4 * j + cc, 32:64, :] = gather_channels(turned, 32, cc, 0).astype(BF16)
    remote2 = mm(low, place(128, 256, 64, 16, start >> 2))
    remote3 = mm(low[0:48], place(128, 128, 80, 8, start >> 3))
    remote4 = mm(low[0:48], place(128, 128, 88, 4, start >> 4))
    parts2 = [w2 * mixed(b2[c], remote2[c * 32 : (c + 1) * 32], share[2]) for c in range(COLOURS)] + [w2]
    parts3 = [w3 * mixed(b3[c], remote3[c * 16 : (c + 1) * 16], share[3]) for c in range(COLOURS)] + [w3]
    parts4 = [w4 * mixed(b4[c], remote4[c * 16 : (c + 1) * 16], share[4]) for c in range(COLOURS)] + [w4]
    lane = lane_index()
    for r in range(2):
        turned3 = [pltpu.roll(parts3[ch][r * 8 : r * 8 + 8], 8 * ch, 1) for ch in range(4)]
        turned4 = [pltpu.roll(parts4[ch][r * 8 : r * 8 + 8], 4 * ch, 1) for ch in range(4)]
        for j in range(2):
            turned2 = [parts2[ch][r * 16 : r * 16 + 16, j * 128 : j * 128 + 128] for ch in range(4)]
            turned2 = [pltpu.roll(turned2[ch], 16 * ch, 1) for ch in range(4)]
            for cc in range(8):
                c = j * 8 + cc
                two = gather_channels(turned2, 16, cc, 0)
                three = gather_channels(turned3, 8, c, 64)
                four = gather_channels(turned4, 4, c, 96)
                head = jnp.where(lane < 64, two[0:8], jnp.where(lane < 96, three, four))
                tail = jnp.where(lane < 64, two[8:16], 0.0)
                first[r * 16 + c, 64:80, :] = jnp.concatenate([head, tail], axis=0).astype(BF16)


def blend(cell, strips, state):
    vmem = pl.BlockSpec(memory_space=pltpu.VMEM)
    return pl.pallas_call(
        blend_kernel,
        in_specs=[pl.BlockSpec(memory_space=pltpu.SMEM)] + [vmem] * 2,
        out_shape=[jax.ShapeDtypeStruct((QB, 80, 128), BF16), jax.ShapeDtypeStruct((QB, 64, 128), BF16)],
        compiler_params=pltpu.CompilerParams(vmem_limit_bytes=VMEM),
        cost_estimate=pl.CostEstimate(flops=10**6, bytes_accessed=10**4, transcendentals=0),
        name="blend",
    )(cell, strips, state)


def routes_kernel(spot, lists, counts):
    for source in range(4):

        def body(q, count, source=source):
            at = spot[source, q]
            lists[source, count] = q * ROUTE + at
            return jnp.where(at >= 0, count + 1, count)

        counts[source] = lax.fori_loop(0, QB, body, 0, unroll=True)


def routes_of(spot):
    smem = pl.BlockSpec(memory_space=pltpu.SMEM)
    return pl.pallas_call(
        routes_kernel,
        in_specs=[smem],
        out_specs=[smem, smem],
        out_shape=[jax.ShapeDtypeStruct((4, QB + 1), jnp.int32), jax.ShapeDtypeStruct((4,), jnp.int32)],
        name="routes",
    )(spot)


def gather_kernel(lists, counts, a, b, c, d, home, away, acc):
    acc[...] = jnp.zeros_like(acc)
    for source, ref in enumerate((a, b, c, d)):

        def body(i, carry, source=source, ref=ref):
            entry = lists[source, i]
            q, at = entry // ROUTE, entry % ROUTE
            acc[at] = acc[at] + ref[q].astype(F32)
            return carry

        lax.fori_loop(0, counts[source], body, 0)
    tiles = home.shape[0]
    home[...] = acc[0:tiles]
    away[...] = acc[tiles : 2 * tiles].astype(BF16)


def gather_rows(routes, rows, tiles):
    height = rows[0].shape[1]
    vmem = pl.BlockSpec(memory_space=pltpu.VMEM)
    shape = (tiles // 2, height, 128)
    return pl.pallas_call(
        gather_kernel,
        in_specs=[pl.BlockSpec(memory_space=pltpu.SMEM)] * 2 + [vmem] * 4,
        out_shape=[jax.ShapeDtypeStruct(shape, F32), jax.ShapeDtypeStruct(shape, BF16)],
        scratch_shapes=[pltpu.VMEM((tiles, height, 128), F32)],
        compiler_params=pltpu.CompilerParams(vmem_limit_bytes=VMEM),
        cost_estimate=pl.CostEstimate(flops=10**6, bytes_accessed=10**4, transcendentals=0),
        name="gather_rows",
    )(*routes, *rows)


def add_kernel(home, got, own, *away):
    for j in range(len(away) + 1):
        lo = j * TILE_DEV
        total = home[lo : lo + TILE_DEV] + got[lo : lo + TILE_DEV].astype(F32)
        if j == 0:
            own[...] = total
        else:
            away[j - 1][...] = total.astype(BF16)


def add_halves(home, got):
    shape = (TILE_DEV,) + home.shape[1:]
    others = home.shape[0] // TILE_DEV - 1
    return pl.pallas_call(
        add_kernel,
        out_shape=[jax.ShapeDtypeStruct(shape, F32)] + [jax.ShapeDtypeStruct(shape, BF16)] * others,
        compiler_params=pltpu.CompilerParams(vmem_limit_bytes=VMEM),
        cost_estimate=pl.CostEstimate(flops=10**6, bytes_accessed=10**4, transcendentals=0),
        name="add_halves",
    )(home, got)


def collapse_matrices():
    def across(src, dst, width):
        g = grow_matrix(width).T
        m = np.zeros((128, 128), np.float32)
        for ch in range(COLOURS):
            m[src + ch * width : src + (ch + 1) * width, dst + ch * 2 * width : dst + (ch + 1) * 2 * width] = g
        return m

    last = np.zeros((128, 384), np.float32)
    g = grow_matrix(32).T
    for ch in range(COLOURS):
        for half in range(2):
            last[ch * 32 : ch * 32 + 32, ch * 128 + half * 64 : ch * 128 + half * 64 + 64] = g

    def down(n, rows_in, rows_out, pick=None):
        g = grow_matrix(n)
        g = g if pick is None else g[pick::2]
        m = np.zeros((TILE_DEV * rows_out, TILE_DEV * rows_in), np.float32)
        for t in range(TILE_DEV):
            m[t * rows_out : t * rows_out + g.shape[0], t * rows_in : t * rows_in + n] = g
        return m

    mats = {"m43": across(96, 64, 4), "m32": across(64, 0, 8), "m21": across(0, 0, 16), "m10": last}
    mats |= {"d43": down(4, 16, 16), "d32": down(8, 16, 16), "d21": down(16, 16, 32)}
    mats |= {"even": down(32, 32, 32, 0), "odd": down(32, 32, 32, 1)}
    return pack(mats, 1280)


def collapse_kernel(places, each, packed, *refs):
    mats = unpack(packed, places)
    a, b, c = (refs[i * each : (i + 1) * each] for i in range(3))
    out, level0 = refs[3 * each :]

    def total(sources, lo, hi):
        acc = sources[0][:, lo:hi, :]
        for source in sources[1:]:
            acc = acc + source[:, lo:hi, :].astype(F32)
        return acc.reshape(TILE_DEV * (hi - lo), 128)

    lane = lane_index()
    small = total(b, 64, 80)
    bottom = small
    for lo, width, chans in ((0, 16, 3), (64, 8, 3), (96, 4, 3)):
        for ch in range(chans):
            inside = (lane >= lo + ch * width) & (lane < lo + (ch + 1) * width)
            bottom = jnp.where(inside, pltpu.roll(small, (128 - (3 - ch) * width) % 128, 1), bottom)
    small = small / jnp.maximum(bottom, 1.0)
    three = small + ldot(mats["d43"], rdot(small, mats["m43"]))
    two = small + ldot(mats["d32"], rdot(three, mats["m32"]))
    one = total(b, 32, 64)
    bottom = one
    for ch in range(3):
        inside = (lane >= ch * 32) & (lane < (ch + 1) * 32)
        bottom = jnp.where(inside, pltpu.roll(one, (128 - (3 - ch) * 32) % 128, 1), bottom)
    one = one / jnp.maximum(bottom, 1.0) + ldot(mats["d21"], rdot(two, mats["m21"]))
    wide = rdot(one, mats["m10"])
    hi, lo = split(wide)
    up = mm(mats["even"], hi) + mm(mats["even"], lo)
    down = mm(mats["odd"], hi) + mm(mats["odd"], lo)
    bottom = jnp.maximum(total(a, 0, 32), 1.0)
    for ch in range(COLOURS):
        own = total(b, 0, 32) if ch == 0 else total(c, 32 * (ch - 1), 32 * ch)
        back = jnp.where(lane < 64, up[:, ch * 128 : ch * 128 + 128], down[:, ch * 128 : ch * 128 + 128])
        level0[ch * 128 : ch * 128 + 128, :] = own / bottom + back
    for ch in range(COLOURS):
        for row in range(32):
            out[ch, :, row * 128 : row * 128 + 128] = level0[pl.ds(ch * 128 + row, TILE_DEV, stride=32), :]


def collapse(a, b, c):
    packed, places = collapse_matrices()
    tiles = pl.pallas_call(
        functools.partial(collapse_kernel, places, len(a)),
        out_shape=jax.ShapeDtypeStruct((COLOURS, TILE_DEV, 4096), F32),
        scratch_shapes=[pltpu.VMEM((COLOURS * 128, 128), F32)],
        compiler_params=pltpu.CompilerParams(vmem_limit_bytes=VMEM),
        cost_estimate=pl.CostEstimate(flops=10**6, bytes_accessed=10**4, transcendentals=0),
        name="collapse",
    )(packed, *a, *b, *c)
    return jnp.swapaxes(tiles, 0, 1)


def swap(value, axis, bit):
    size = lax.axis_size(axis)
    return lax.ppermute(value, axis, [(i, i ^ bit) for i in range(size)])


def local(frames, weight_map, seam_mask, strip_cell, partner, tile_group, tile_position_in_group):
    groups = lax.axis_size("frames")
    parts = lax.axis_size("tiles")
    mine = lax.axis_index("tiles")
    mask = lax.bitwise_xor(partner[0] // parts, lax.axis_index("frames"))

    tie = lax.optimization_barrier
    strips = strips_of(frames, strip_cell)
    ids = tile_group.reshape(QB) * (parts * TILE_DEV) + tile_position_in_group.reshape(QB)
    strips, frames, ids = tie((strips, frames, ids))
    ids = jnp.stack([ids, swap(ids, "tiles", 1)])
    ids_x = jnp.concatenate([ids, swap(ids, "tiles", 2)])
    ids_y = jnp.concatenate([ids, swap(ids, "frames", 1)])

    def relative(ids):
        group, tile = ids // (parts * TILE_DEV), ids % (parts * TILE_DEV)
        group = lax.bitwise_xor(group, lax.axis_index("frames"))
        return group, lax.bitwise_xor(tile // TILE_DEV, mine), tile % TILE_DEV

    half = groups // 2
    group, part, tile = relative(ids_x)
    spot_x = jnp.where(part == 0, ((group & 1) * half + (group >> 1)) * TILE_DEV + tile, -1)
    group, part, tile = relative(ids_y)
    here = ((group & 1) == 0) & ((part & 1) == 0)
    spot_y = jnp.where(here, ((part >> 1) * half + (group >> 1)) * TILE_DEV + tile, -1)

    weights, state = bands_of(frames, weight_map, seam_mask)
    bit = 1
    while bit < groups:
        got = swap(strips, "frames", bit)
        if bit == 1:
            got, weights, state = tie((got, weights, state))
            far, near = swap(weights, "tiles", 2), swap(weights, "tiles", 1)
        if bit == half:
            far_near = swap(far, "tiles", 1)
            got, far, near, far_near, routes_x, spot_y = tie((got, far, near, far_near, routes_of(spot_x), spot_y))
        strips = jnp.where((mask & bit) != 0, got, strips)
        bit *= 2

    def gather(routes, *rows):
        return gather_rows(routes, rows, groups * TILE_DEV)

    def along(own, *away):
        return [own] + [swap(part, "frames", 2 * (j + 1)) for j, part in enumerate(away)]

    first, second = blend(strip_cell, strips, state)
    first, second, near, spot_y = tie((first, second, near, spot_y))
    far_first, near_first = swap(first, "tiles", 2), swap(first, "tiles", 1)
    far_second, near_second = swap(second, "frames", 1), swap(second, "tiles", 1)
    home_w, away_w = gather(routes_x, weights, near, far, far_near)
    got_w = swap(away_w, "frames", 1)
    near_first, near_second, got_w, routes_y = tie((near_first, near_second, got_w, routes_of(spot_y)))
    sums_w = add_halves(home_w, got_w)
    far_second, sums_w = tie((far_second, sums_w))
    got_weights = along(*sums_w)
    home_s, away_s = gather(routes_y, second, near_second, far_second, swap(far_second, "tiles", 1))
    got_s = swap(away_s, "tiles", 2)
    far_first, home_s, got_weights = tie((far_first, home_s, got_weights))
    far_near, got_s = tie((swap(far_first, "tiles", 1), got_s))
    home_f, away_f = gather(routes_x, first, near_first, far_first, far_near)
    got_f = swap(away_f, "frames", 1)
    got_second = along(*add_halves(home_s, got_s))
    got_f, got_second = tie((got_f, got_second))
    got_first = along(*add_halves(home_f, got_f))
    return collapse(got_weights, got_first, got_second)


def solution(mesh):
    in_specs = (
        P(("frames", "tiles"), None, None, None),
        P(("frames", "tiles"), None, None),
        P(("frames", "tiles"), None, None),
        P(("frames", "tiles")),
        P(("frames", "tiles")),
        P(("frames", "tiles"), None, None),
        P(("frames", "tiles"), None),
    )
    out_specs = P(("frames", "tiles"), None, None)
    return jax.shard_map(local, mesh=mesh, in_specs=in_specs, out_specs=out_specs, check_vma=False)
```

```python
import functools

import jax
import jax.numpy as jnp
import numpy as np
from jax import lax
from jax.experimental import pallas as pl
from jax.experimental.pallas import tpu as pltpu
from jax.sharding import PartitionSpec as P

COLOURS = 3
FH = 128
FW = 1024
QB = 32
WIN = 256
TILE_DEV = 4
VMEM = 30 << 20
ROUTE = 4096
F32 = jnp.float32
BF16 = jnp.bfloat16


def shrink_matrix(n):
    m = np.zeros((n // 2, n), np.float32)
    for i in range(n // 2):
        for d, tap in zip(range(-2, 3), (1, 4, 6, 4, 1)):
            m[i, min(max(2 * i + d, 0), n - 1)] += tap / 16.0
    return m


def grow_matrix(n):
    m = np.zeros((2 * n, n), np.float32)
    for i in range(n):
        lo, hi = max(i - 1, 0), min(i + 1, n - 1)
        m[2 * i, lo] += 1 / 8
        m[2 * i, i] += 6 / 8
        m[2 * i, hi] += 1 / 8
        m[2 * i + 1, i] += 1 / 2
        m[2 * i + 1, hi] += 1 / 2
    return m


def padded(m, rows, cols):
    return np.pad(m, ((0, rows - m.shape[0]), (0, cols - m.shape[1])))


def row_order():
    m = np.zeros((FH, FH), np.float32)
    for r in range(2):
        for par in range(2):
            for i in range(32):
                m[r * 64 + par * 32 + i, r * 64 + 2 * i + par] = 1
    return m


def vertical():
    v = {1: shrink_matrix(128), 2: shrink_matrix(64), 3: shrink_matrix(32)}
    spread = np.zeros((16, 8), np.float32)
    for r in range(2):
        for i in range(4):
            spread[r * 8 + i, r * 4 + i] = 1
    v[4] = spread @ shrink_matrix(16)
    g = {0: row_order() @ grow_matrix(64), 1: grow_matrix(32), 2: grow_matrix(16)}
    g[3] = grow_matrix(8) @ spread.T
    return v, g


def horizontal(width):
    s = {k: shrink_matrix(width >> (k - 1)).T for k in range(1, 5)}
    g = {k: grow_matrix(width >> (k + 1)).T for k in range(4)}
    return s, g


def shrink_window():
    m = np.zeros((512, 128), np.float32)
    for i in range(128):
        for d, tap in zip(range(-2, 3), (1, 4, 6, 4, 1)):
            m[128 + 2 * i + d, i] = tap / 16.0
    return m


def grow_window():
    m = np.zeros((384, 256), np.float32)
    for i in range(128):
        for d, tap in zip(range(-1, 2), (1, 6, 1)):
            m[128 + i + d, 2 * i] = tap / 8.0
        m[128 + i, 2 * i + 1] = m[128 + i + 1, 2 * i + 1] = 0.5
    return m


def pack(mats, width):
    places, row, col, height = {}, 0, 0, 0
    for name in sorted(mats, key=lambda n: (-mats[n].shape[0], -mats[n].shape[1], n)):
        h, w = mats[name].shape
        wide = -(-w // 128) * 128
        if col + wide > width:
            row, col, height = row + height, 0, 0
        height = max(height, -(-h // 16) * 16)
        places[name] = (row, col, h, w)
        col += wide
    out = np.zeros((row + height, width), np.float32)
    for name, (r, c, h, w) in places.items():
        out[r : r + h, c : c + w] = mats[name]
    return jnp.asarray(out, BF16), places


def unpack(ref, places):
    return {name: ref[r : r + h, c : c + w] for name, (r, c, h, w) in places.items()}


def small_matrices():
    v, g = vertical()
    s, gh = horizontal(WIN)
    sm, _ = horizontal(64)
    mats = {f"v{k}": m for k, m in v.items()} | {f"g{k}": m for k, m in g.items()}
    mats |= {f"s{k}": m for k, m in s.items()} | {f"h{k}": m for k, m in gh.items()}
    mats |= {f"m{k}": m for k, m in sm.items()} | {"order": row_order()}
    return pack(mats, 512)


def large_matrices():
    mats = {"shrink": shrink_window(), "grow": grow_window()}
    mats["last"] = padded(shrink_matrix(128).T, 128, 128)
    mats["least"] = padded(grow_matrix(64).T, 128, 128)
    return pack(mats, 640)


def levels_of(mats, letter):
    return {int(n[1:]): m for n, m in mats.items() if n[0] == letter and n[1:].isdigit()}


def mm(a, b):
    return jnp.dot(a, b, preferred_element_type=F32)


def split(v):
    hi = v.astype(BF16)
    return hi, (v - hi.astype(F32)).astype(BF16)


def rdot(v, m):
    hi, lo = split(v)
    return mm(hi, m) + mm(lo, m)


def ldot(m, v):
    hi, lo = split(v)
    return mm(m, hi) + mm(m, lo)


def mmt(a, b):
    return lax.dot_general(a, b, (((1,), (1,)), ((), ())), preferred_element_type=F32)


def windows(v, m, step):
    rows, width = v.shape
    both = jnp.concatenate(split(v), axis=0)
    left = jnp.broadcast_to(both[:, :1], (2 * rows, 128))
    right = jnp.broadcast_to(both[:, width - 1 :], (2 * rows, 128))
    both = jnp.concatenate([left, both, right], axis=1)
    pieces = []
    for n in range(width // step):
        piece = mm(both[:, n * step : n * step + step + 256], m)
        pieces.append(piece[:rows] + piece[rows:])
    return jnp.concatenate(pieces, axis=1)


def right_of(m):
    return lambda v: rdot(v, m)


def pyramid(planes, v, shrinks, product=mm):
    n = len(planes)
    t = jnp.concatenate([product(v[1], p) for p in planes], axis=0)
    levels = {1: shrinks[1](t)}
    for k in range(2, 5):
        prev = levels[k - 1]
        rows = prev.shape[0] // n
        t = jnp.concatenate([ldot(v[k], prev[i * rows : (i + 1) * rows]) for i in range(n)], axis=0)
        levels[k] = shrinks[k](t)
    return levels


def grown(level, n, gv, grow):
    h = grow(level)
    rows = level.shape[0] // n
    return [ldot(gv, h[i * rows : (i + 1) * rows]) for i in range(n)]


def place(rows, cols, base, width, offset):
    i = lax.broadcasted_iota(jnp.int32, (rows, cols), 0)
    c = lax.broadcasted_iota(jnp.int32, (rows, cols), 1)
    hit = (i >= base) & (i < base + width) & (c - i == offset - base)
    return jnp.where(hit, 1.0, 0.0).astype(BF16)


def strips_kernel(places, cell, xa, xb, packed, out, acc):
    mats = unpack(packed, places)
    v, gv, s, gh = (levels_of(mats, letter) for letter in "vgsh")
    s, gh = ({k: right_of(m) for k, m in each.items()} for each in (s, gh))
    order = mats["order"]
    first = window_tile(cell[0]) * 128
    planes = [jnp.concatenate([xa[0, c], xb[0, c]], axis=1) for c in range(COLOURS)]
    levels = pyramid(planes, v, s)
    back = grown(levels[1], COLOURS, gv[0], gh[0])
    b0 = jnp.concatenate([mm(order, planes[c]) - back[c] for c in range(COLOURS)], axis=0)
    bands = [b0.astype(BF16)]
    for k in range(1, 4):
        back = grown(levels[k + 1], COLOURS, gv[k], gh[k])
        bands.append((levels[k] - jnp.concatenate(back, axis=0)).astype(BF16))
    bands.append(levels[4].astype(BF16))
    start = cell[0] * 16 - first

    def pick(band, base, k):
        i = lax.broadcasted_iota(jnp.int32, (band.shape[1], 128), 0)
        c = lax.broadcasted_iota(jnp.int32, (band.shape[1], 128), 1)
        hit = (c >= base) & (c < base + (64 >> k)) & (i - c == (start >> k) - base)
        return mm(band, jnp.where(hit, 1.0, 0.0).astype(BF16))

    out[0:192, :] = (pick(bands[0][0:192], 0, 0) + pick(bands[0][192:384], 64, 0)).astype(BF16)
    acc[...] = pick(bands[1][0:96], 0, 1) + pick(bands[1][96:192], 32, 1) + pick(bands[2], 64, 2)
    acc[0:48, :] = acc[0:48, :] + pick(bands[3], 80, 3) + pick(bands[4], 88, 4)
    out[192:288, :] = acc[...].astype(BF16)


def window_tile(cell):
    return jnp.clip((cell - 3) >> 3, 0, (FW - WIN) // 128)


def full_spec(a):
    return pl.BlockSpec(a.shape, lambda *_: (0,) * a.ndim)


def strips_of(frames, cell):
    packed, places = small_matrices()
    grid_spec = pltpu.PrefetchScalarGridSpec(
        num_scalar_prefetch=1,
        grid=(1,),
        in_specs=[
            pl.BlockSpec((1, COLOURS, FH, 128), lambda i, c: (0, 0, 0, window_tile(c[0]))),
            pl.BlockSpec((1, COLOURS, FH, 128), lambda i, c: (0, 0, 0, window_tile(c[0]) + 1)),
        ]
        + [full_spec(packed)],
        out_specs=pl.BlockSpec((288, 128), lambda i, c: (0, 0)),
        scratch_shapes=[pltpu.VMEM((96, 128), F32)],
    )
    return pl.pallas_call(
        functools.partial(strips_kernel, places),
        grid_spec=grid_spec,
        out_shape=jax.ShapeDtypeStruct((288, 128), BF16),
        compiler_params=pltpu.CompilerParams(vmem_limit_bytes=VMEM),
        cost_estimate=pl.CostEstimate(flops=2 * 10**9, bytes_accessed=10**6, transcendentals=0),
        name="strips",
    )(cell, frames, frames, packed)


def lane_index():
    return lax.broadcasted_iota(jnp.int32, (1, 128), 1)


def fold_level0(p, store):
    left = lane_index() < 64
    for r in range(2):
        for j in range(8):
            even = p[r * 64 : r * 64 + 32, j * 128 : j * 128 + 128]
            odd = p[r * 64 + 32 : r * 64 + 64, j * 128 : j * 128 + 128]
            store(r * 16 + 2 * j, jnp.where(left, even, pltpu.roll(odd, 64, 1)))
            store(r * 16 + 2 * j + 1, jnp.where(left, pltpu.roll(even, 64, 1), odd))


def gather_channels(parts, width, cc, base):
    groups = 128 // width
    group = lane_index() // width
    out = jnp.zeros_like(parts[0])
    for ch in range(4):
        out = jnp.where(group == (cc + ch) % groups, parts[ch], out)
    return pltpu.roll(out, (base - cc * width) % 128, 1)


STATE_ROWS = 816


def state_views(state):
    at = lambda r, h, c, w: (slice(r, r + h), slice(c, c + w))
    b0 = [at(128 * c, 128, 0, 1024) for c in range(3)]
    l1 = [at(384, 64, 0, 512), at(384, 64, 512, 512), at(448, 64, 0, 512), at(448, 64, 512, 512)]
    l2 = [at(512, 32, 256 * c, 256) for c in range(4)]
    l3 = [at(544, 16, 128 * c, 128) for c in range(4)]
    l4 = [at(544, 16, 512 + 128 * c, 128) for c in range(4)]
    levels = [b0 + [at(560, 128, 0, 1024)], l1, l2, l3, l4]
    masks = [at(688, 128 >> k, 128 * k, 64 >> k) for k in range(4)] + [at(688, 16, 512, 4)]
    return levels, masks


def bands_kernel(small_places, large_places, x, w, m, small, large, wblocks, state):
    mats = unpack(small, small_places)
    v, gv, sm = (levels_of(mats, letter) for letter in "vgm")
    order = mats["order"]
    sm = {k: right_of(each) for k, each in sm.items()}
    mats = unpack(large, large_places)
    half = lambda each: windows(each, mats["shrink"], 256)
    twice = lambda each: windows(each, mats["grow"], 128)
    s = {1: half, 2: half, 3: half, 4: right_of(mats["last"])}
    gh = {0: twice, 1: twice, 2: twice, 3: right_of(mats["least"])}
    views, mask_views = state_views(state)
    planes = [x[0, c] for c in range(COLOURS)] + [w[0]]
    weights = mm(order, planes[3])
    state[views[0][3]] = weights

    def store(q, piece):
        wblocks[q] = piece.astype(BF16)

    fold_level0(weights, store)
    levels = pyramid(planes, v, s)
    for k in range(1, 5):
        rows = levels[k].shape[0] // 4
        state[views[k][3]] = levels[k][3 * rows :]
    back = grown(levels[1][: 3 * 64], COLOURS, gv[0], gh[0])
    for c in range(COLOURS):
        state[views[0][c]] = mm(order, planes[c]) - back[c]
    for k in range(1, 4):
        rows = levels[k].shape[0] // 4
        below = levels[k + 1].shape[0] // 4
        back = grown(levels[k + 1][: 3 * below], COLOURS, gv[k], gh[k])
        for c in range(COLOURS):
            state[views[k][c]] = levels[k][c * rows : (c + 1) * rows] - back[c]
    for c in range(COLOURS):
        state[views[4][c]] = levels[4][c * 16 : (c + 1) * 16]
    other = (1.0 - m[0].astype(F32)).astype(BF16)
    state[mask_views[0]] = mmt(order, other)
    masks = pyramid([other], v, sm, mmt)
    for k in range(1, 5):
        state[mask_views[k]] = masks[k]


def bands_of(frames, weight_map, seam_mask):
    small, small_places = small_matrices()
    large, large_places = large_matrices()
    return pl.pallas_call(
        functools.partial(bands_kernel, small_places, large_places),
        out_shape=[jax.ShapeDtypeStruct((QB, 32, 128), BF16), jax.ShapeDtypeStruct((STATE_ROWS, FW), F32)],
        compiler_params=pltpu.CompilerParams(vmem_limit_bytes=VMEM),
        cost_estimate=pl.CostEstimate(flops=8 * 10**9, bytes_accessed=6 * 10**6, transcendentals=0),
        name="bands",
    )(frames, weight_map, jnp.swapaxes(seam_mask, 1, 2), small, large)


def blend_kernel(cell, strips, state, first, second):
    views, mask_views = state_views(state)
    (b0, b1, b2, b3, b4) = [[state[view] for view in views[k][:3]] for k in range(5)]
    (wp, w1, w2, w3, w4) = [state[views[k][3]] for k in range(5)]
    (n0, n1, n2, n3, n4) = [state[view] for view in mask_views]
    start = cell[0] * 16
    low = strips[192:288]

    def mixed(band, remote, share):
        return band + share * (remote - band)

    widths = (1024, 512, 256, 128, 128)
    share0 = mm(n0.astype(BF16), place(64, 1024, 0, 64, start))
    share = [share0]
    for k, ref in enumerate((n1, n2, n3, n4)):
        share.append(rdot(ref, place(64 >> (k + 1), widths[k + 1], 0, 64 >> (k + 1), start >> (k + 1))))
    top = strips[0:192]
    remote0 = [mm(top, place(128, 1024, 0, 64, start)), mm(top, place(128, 1024, 64, 64, start))]
    remote0 = jnp.concatenate(remote0, axis=0)
    weights = wp
    for c in range(COLOURS):
        p = weights * mixed(b0[c], remote0[c * 128 : (c + 1) * 128], share[0])
        out, row = (first, 0) if c == 0 else (second, 32 * (c - 1))

        def store(q, piece, out=out, row=row):
            out[q, row : row + 32, :] = piece.astype(BF16)

        fold_level0(p, store)
    remote1 = [mm(low, place(128, 512, 0, 32, start >> 1)), mm(low, place(128, 512, 32, 32, start >> 1))]
    remote1 = jnp.concatenate(remote1, axis=0)
    parts = [w1 * mixed(b1[c], remote1[c * 64 : (c + 1) * 64], share[1]) for c in range(COLOURS)] + [w1]
    for r in range(2):
        for j in range(4):
            turned = [parts[ch][r * 32 : r * 32 + 32, j * 128 : j * 128 + 128] for ch in range(4)]
            turned = [turned[0]] + [pltpu.roll(turned[ch], 32 * ch, 1) for ch in range(1, 4)]
            for cc in range(4):
                first[r * 16 + 4 * j + cc, 32:64, :] = gather_channels(turned, 32, cc, 0).astype(BF16)
    remote2 = mm(low, place(128, 256, 64, 16, start >> 2))
    remote3 = mm(low[0:48], place(128, 128, 80, 8, start >> 3))
    remote4 = mm(low[0:48], place(128, 128, 88, 4, start >> 4))
    parts2 = [w2 * mixed(b2[c], remote2[c * 32 : (c + 1) * 32], share[2]) for c in range(COLOURS)] + [w2]
    parts3 = [w3 * mixed(b3[c], remote3[c * 16 : (c + 1) * 16], share[3]) for c in range(COLOURS)] + [w3]
    parts4 = [w4 * mixed(b4[c], remote4[c * 16 : (c + 1) * 16], share[4]) for c in range(COLOURS)] + [w4]
    lane = lane_index()
    for r in range(2):
        turned3 = [pltpu.roll(parts3[ch][r * 8 : r * 8 + 8], 8 * ch, 1) for ch in range(4)]
        turned4 = [pltpu.roll(parts4[ch][r * 8 : r * 8 + 8], 4 * ch, 1) for ch in range(4)]
        for j in range(2):
            turned2 = [parts2[ch][r * 16 : r * 16 + 16, j * 128 : j * 128 + 128] for ch in range(4)]
            turned2 = [pltpu.roll(turned2[ch], 16 * ch, 1) for ch in range(4)]
            for cc in range(8):
                c = j * 8 + cc
                two = gather_channels(turned2, 16, cc, 0)
                three = gather_channels(turned3, 8, c, 64)
                four = gather_channels(turned4, 4, c, 96)
                head = jnp.where(lane < 64, two[0:8], jnp.where(lane < 96, three, four))
                tail = jnp.where(lane < 64, two[8:16], 0.0)
                first[r * 16 + c, 64:80, :] = jnp.concatenate([head, tail], axis=0).astype(BF16)


def blend(cell, strips, state):
    vmem = pl.BlockSpec(memory_space=pltpu.VMEM)
    return pl.pallas_call(
        blend_kernel,
        in_specs=[pl.BlockSpec(memory_space=pltpu.SMEM)] + [vmem] * 2,
        out_shape=[jax.ShapeDtypeStruct((QB, 80, 128), BF16), jax.ShapeDtypeStruct((QB, 64, 128), BF16)],
        compiler_params=pltpu.CompilerParams(vmem_limit_bytes=VMEM),
        cost_estimate=pl.CostEstimate(flops=10**6, bytes_accessed=10**4, transcendentals=0),
        name="blend",
    )(cell, strips, state)


def routes_kernel(spot, lists, counts):
    for source in range(4):

        def body(q, count, source=source):
            at = spot[source, q]
            lists[source, count] = q * ROUTE + at
            return jnp.where(at >= 0, count + 1, count)

        counts[source] = lax.fori_loop(0, QB, body, 0, unroll=True)


def routes_of(spot):
    smem = pl.BlockSpec(memory_space=pltpu.SMEM)
    return pl.pallas_call(
        routes_kernel,
        in_specs=[smem],
        out_specs=[smem, smem],
        out_shape=[jax.ShapeDtypeStruct((4, QB + 1), jnp.int32), jax.ShapeDtypeStruct((4,), jnp.int32)],
        name="routes",
    )(spot)


def gather_kernel(lists, counts, *refs):
    home, away, acc = refs[-3:]
    acc[...] = jnp.zeros_like(acc)
    for source in range(4):

        def body(i, carry, source=source):
            entry = lists[source, i]
            q, at = entry // ROUTE, entry % ROUTE
            lo = 0
            for ref in refs[source:-3:4]:
                hi = lo + ref.shape[1]
                acc[at, lo:hi, :] = acc[at, lo:hi, :] + ref[q].astype(F32)
                lo = hi
            return carry

        lax.fori_loop(0, counts[source], body, 0)
    tiles = home.shape[0]
    home[...] = acc[0:tiles]
    away[...] = acc[tiles : 2 * tiles].astype(BF16)


def gather_rows(routes, rows, tiles):
    height = sum(each.shape[1] for each in rows[::4])
    vmem = pl.BlockSpec(memory_space=pltpu.VMEM)
    shape = (tiles // 2, height, 128)
    return pl.pallas_call(
        gather_kernel,
        in_specs=[pl.BlockSpec(memory_space=pltpu.SMEM)] * 2 + [vmem] * len(rows),
        out_shape=[jax.ShapeDtypeStruct(shape, F32), jax.ShapeDtypeStruct(shape, BF16)],
        scratch_shapes=[pltpu.VMEM((tiles, height, 128), F32)],
        compiler_params=pltpu.CompilerParams(vmem_limit_bytes=VMEM),
        cost_estimate=pl.CostEstimate(flops=10**6, bytes_accessed=10**4, transcendentals=0),
        name="gather_rows",
    )(*routes, *rows)


def add_kernel(home, got, own, *away):
    for j in range(len(away) + 1):
        lo = j * TILE_DEV
        total = home[lo : lo + TILE_DEV] + got[lo : lo + TILE_DEV].astype(F32)
        if j == 0:
            own[...] = total
        else:
            away[j - 1][...] = total.astype(BF16)


def add_halves(home, got):
    shape = (TILE_DEV,) + home.shape[1:]
    others = home.shape[0] // TILE_DEV - 1
    return pl.pallas_call(
        add_kernel,
        out_shape=[jax.ShapeDtypeStruct(shape, F32)] + [jax.ShapeDtypeStruct(shape, BF16)] * others,
        compiler_params=pltpu.CompilerParams(vmem_limit_bytes=VMEM),
        cost_estimate=pl.CostEstimate(flops=10**6, bytes_accessed=10**4, transcendentals=0),
        name="add_halves",
    )(home, got)


def collapse_matrices():
    def across(src, dst, width):
        g = grow_matrix(width).T
        m = np.zeros((128, 128), np.float32)
        for ch in range(COLOURS):
            m[src + ch * width : src + (ch + 1) * width, dst + ch * 2 * width : dst + (ch + 1) * 2 * width] = g
        return m

    last = np.zeros((128, 384), np.float32)
    g = grow_matrix(32).T
    for ch in range(COLOURS):
        for half in range(2):
            last[ch * 32 : ch * 32 + 32, ch * 128 + half * 64 : ch * 128 + half * 64 + 64] = g

    def down(n, rows_in, rows_out, pick=None):
        g = grow_matrix(n)
        g = g if pick is None else g[pick::2]
        m = np.zeros((TILE_DEV * rows_out, TILE_DEV * rows_in), np.float32)
        for t in range(TILE_DEV):
            m[t * rows_out : t * rows_out + g.shape[0], t * rows_in : t * rows_in + n] = g
        return m

    mats = {"m43": across(96, 64, 4), "m32": across(64, 0, 8), "m21": across(0, 0, 16), "m10": last}
    mats |= {"d43": down(4, 16, 16), "d32": down(8, 16, 16), "d21": down(16, 16, 32)}
    mats |= {"even": down(32, 32, 32, 0), "odd": down(32, 32, 32, 1)}
    return pack(mats, 1280)


def collapse_kernel(places, each, packed, *refs):
    mats = unpack(packed, places)
    b, c = (refs[i * each : (i + 1) * each] for i in range(2))
    out, level0 = refs[2 * each :]

    def total(sources, lo, hi):
        acc = sources[0][:, lo:hi, :]
        for source in sources[1:]:
            acc = acc + source[:, lo:hi, :].astype(F32)
        return acc.reshape(TILE_DEV * (hi - lo), 128)

    lane = lane_index()
    small = total(b, 64, 80)
    bottom = small
    for lo, width, chans in ((0, 16, 3), (64, 8, 3), (96, 4, 3)):
        for ch in range(chans):
            inside = (lane >= lo + ch * width) & (lane < lo + (ch + 1) * width)
            bottom = jnp.where(inside, pltpu.roll(small, (128 - (3 - ch) * width) % 128, 1), bottom)
    small = small / jnp.maximum(bottom, 1.0)
    three = small + ldot(mats["d43"], rdot(small, mats["m43"]))
    two = small + ldot(mats["d32"], rdot(three, mats["m32"]))
    one = total(b, 32, 64)
    bottom = one
    for ch in range(3):
        inside = (lane >= ch * 32) & (lane < (ch + 1) * 32)
        bottom = jnp.where(inside, pltpu.roll(one, (128 - (3 - ch) * 32) % 128, 1), bottom)
    one = one / jnp.maximum(bottom, 1.0) + ldot(mats["d21"], rdot(two, mats["m21"]))
    wide = rdot(one, mats["m10"])
    hi, lo = split(wide)
    up = mm(mats["even"], hi) + mm(mats["even"], lo)
    down = mm(mats["odd"], hi) + mm(mats["odd"], lo)
    bottom = jnp.maximum(total(c, 64, 96), 1.0)
    for ch in range(COLOURS):
        own = total(b, 0, 32) if ch == 0 else total(c, 32 * (ch - 1), 32 * ch)
        back = jnp.where(lane < 64, up[:, ch * 128 : ch * 128 + 128], down[:, ch * 128 : ch * 128 + 128])
        level0[ch * 128 : ch * 128 + 128, :] = own / bottom + back
    for ch in range(COLOURS):
        for row in range(32):
            out[ch, :, row * 128 : row * 128 + 128] = level0[pl.ds(ch * 128 + row, TILE_DEV, stride=32), :]


def collapse(b, c):
    packed, places = collapse_matrices()
    tiles = pl.pallas_call(
        functools.partial(collapse_kernel, places, len(b)),
        out_shape=jax.ShapeDtypeStruct((COLOURS, TILE_DEV, 4096), F32),
        scratch_shapes=[pltpu.VMEM((COLOURS * 128, 128), F32)],
        compiler_params=pltpu.CompilerParams(vmem_limit_bytes=VMEM),
        cost_estimate=pl.CostEstimate(flops=10**6, bytes_accessed=10**4, transcendentals=0),
        name="collapse",
    )(packed, *b, *c)
    return jnp.swapaxes(tiles, 0, 1)


def swap(value, axis, bit):
    size = lax.axis_size(axis)
    return lax.ppermute(value, axis, [(i, i ^ bit) for i in range(size)])


def local(frames, weight_map, seam_mask, strip_cell, partner, tile_group, tile_position_in_group):
    groups = lax.axis_size("frames")
    parts = lax.axis_size("tiles")
    mine = lax.axis_index("tiles")
    mask = lax.bitwise_xor(partner[0] // parts, lax.axis_index("frames"))

    tie = lax.optimization_barrier
    strips = strips_of(frames, strip_cell)
    ids = tile_group.reshape(QB) * (parts * TILE_DEV) + tile_position_in_group.reshape(QB)
    strips, frames, ids = tie((strips, frames, ids))
    ids = jnp.stack([ids, swap(ids, "tiles", 1)])
    ids_x = jnp.concatenate([ids, swap(ids, "tiles", 2)])
    ids_y = jnp.concatenate([ids, swap(ids, "frames", 1)])

    def relative(ids):
        group, tile = ids // (parts * TILE_DEV), ids % (parts * TILE_DEV)
        group = lax.bitwise_xor(group, lax.axis_index("frames"))
        return group, lax.bitwise_xor(tile // TILE_DEV, mine), tile % TILE_DEV

    half = groups // 2
    group, part, tile = relative(ids_x)
    spot_x = jnp.where(part == 0, ((group & 1) * half + (group >> 1)) * TILE_DEV + tile, -1)
    group, part, tile = relative(ids_y)
    here = ((group & 1) == 0) & ((part & 1) == 0)
    spot_y = jnp.where(here, ((part >> 1) * half + (group >> 1)) * TILE_DEV + tile, -1)

    weights, state = bands_of(frames, weight_map, seam_mask)
    bit = 1
    while bit < groups:
        got = swap(strips, "frames", bit)
        if bit == 1:
            got, weights, state = tie((got, weights, state))
            far, near = swap(weights, "frames", 1), swap(weights, "tiles", 1)
        if bit == half:
            far_near = swap(far, "tiles", 1)
            got, far, near, far_near, spot_x, spot_y = tie((got, far, near, far_near, spot_x, spot_y))
        strips = jnp.where((mask & bit) != 0, got, strips)
        bit *= 2

    def gather(routes, *rows):
        return gather_rows(routes, rows, groups * TILE_DEV)

    def along(own, *away):
        return [own] + [swap(part, "frames", 2 * (j + 1)) for j, part in enumerate(away)]

    first, second = blend(strip_cell, strips, state)
    first, second, spot_x, spot_y = tie((first, second, spot_x, spot_y))
    far_first, near_first = swap(first, "tiles", 2), swap(first, "tiles", 1)
    far_second, near_second = swap(second, "frames", 1), swap(second, "tiles", 1)
    routes_x, routes_y = routes_of(spot_x), routes_of(spot_y)
    far_second, routes_x, routes_y, near_first = tie((far_second, routes_x, routes_y, near_first))
    rows = (second, near_second, far_second, swap(far_second, "tiles", 1))
    home_s, away_s = gather(routes_y, *rows, weights, near, far, far_near)
    got_s = swap(away_s, "tiles", 2)
    far_first, home_s = tie((far_first, home_s))
    far_near, got_s = tie((swap(far_first, "tiles", 1), got_s))
    home_f, away_f = gather(routes_x, first, near_first, far_first, far_near)
    got_f = swap(away_f, "frames", 1)
    got_second = along(*add_halves(home_s, got_s))
    got_f, got_second = tie((got_f, got_second))
    got_first = along(*add_halves(home_f, got_f))
    return collapse(got_first, got_second)


def solution(mesh):
    in_specs = (
        P(("frames", "tiles"), None, None, None),
        P(("frames", "tiles"), None, None),
        P(("frames", "tiles"), None, None),
        P(("frames", "tiles")),
        P(("frames", "tiles")),
        P(("frames", "tiles"), None, None),
        P(("frames", "tiles"), None),
    )
    out_specs = P(("frames", "tiles"), None, None)
    return jax.shard_map(local, mesh=mesh, in_specs=in_specs, out_specs=out_specs, check_vma=False)
```

```python
import functools

import jax
import jax.numpy as jnp
import numpy as np
from jax import lax
from jax.experimental import pallas as pl
from jax.experimental.pallas import tpu as pltpu
from jax.sharding import PartitionSpec as P

COLOURS = 3
FH = 128
FW = 1024
QB = 32
WIN = 256
TILE_DEV = 4
VMEM = 30 << 20
ROUTE = 4096
F32 = jnp.float32
BF16 = jnp.bfloat16


def shrink_matrix(n):
    m = np.zeros((n // 2, n), np.float32)
    for i in range(n // 2):
        for d, tap in zip(range(-2, 3), (1, 4, 6, 4, 1)):
            m[i, min(max(2 * i + d, 0), n - 1)] += tap / 16.0
    return m


def grow_matrix(n):
    m = np.zeros((2 * n, n), np.float32)
    for i in range(n):
        lo, hi = max(i - 1, 0), min(i + 1, n - 1)
        m[2 * i, lo] += 1 / 8
        m[2 * i, i] += 6 / 8
        m[2 * i, hi] += 1 / 8
        m[2 * i + 1, i] += 1 / 2
        m[2 * i + 1, hi] += 1 / 2
    return m


def padded(m, rows, cols):
    return np.pad(m, ((0, rows - m.shape[0]), (0, cols - m.shape[1])))


def row_order():
    m = np.zeros((FH, FH), np.float32)
    for r in range(2):
        for par in range(2):
            for i in range(32):
                m[r * 64 + par * 32 + i, r * 64 + 2 * i + par] = 1
    return m


def vertical():
    v = {1: shrink_matrix(128), 2: shrink_matrix(64), 3: shrink_matrix(32)}
    spread = np.zeros((16, 8), np.float32)
    for r in range(2):
        for i in range(4):
            spread[r * 8 + i, r * 4 + i] = 1
    v[4] = spread @ shrink_matrix(16)
    g = {0: row_order() @ grow_matrix(64), 1: grow_matrix(32), 2: grow_matrix(16)}
    g[3] = grow_matrix(8) @ spread.T
    return v, g


def horizontal(width):
    s = {k: shrink_matrix(width >> (k - 1)).T for k in range(1, 5)}
    g = {k: grow_matrix(width >> (k + 1)).T for k in range(4)}
    return s, g


def shrink_window():
    m = np.zeros((512, 128), np.float32)
    for i in range(128):
        for d, tap in zip(range(-2, 3), (1, 4, 6, 4, 1)):
            m[128 + 2 * i + d, i] = tap / 16.0
    return m


def grow_window():
    m = np.zeros((384, 256), np.float32)
    for i in range(128):
        for d, tap in zip(range(-1, 2), (1, 6, 1)):
            m[128 + i + d, 2 * i] = tap / 8.0
        m[128 + i, 2 * i + 1] = m[128 + i + 1, 2 * i + 1] = 0.5
    return m


def pack(mats, width):
    places, row, col, height = {}, 0, 0, 0
    for name in sorted(mats, key=lambda n: (-mats[n].shape[0], -mats[n].shape[1], n)):
        h, w = mats[name].shape
        wide = -(-w // 128) * 128
        if col + wide > width:
            row, col, height = row + height, 0, 0
        height = max(height, -(-h // 16) * 16)
        places[name] = (row, col, h, w)
        col += wide
    out = np.zeros((row + height, width), np.float32)
    for name, (r, c, h, w) in places.items():
        out[r : r + h, c : c + w] = mats[name]
    return jnp.asarray(out, BF16), places


def unpack(ref, places):
    return {name: ref[r : r + h, c : c + w] for name, (r, c, h, w) in places.items()}


def small_matrices():
    v, g = vertical()
    s, gh = horizontal(WIN)
    sm, _ = horizontal(64)
    mats = {f"v{k}": m for k, m in v.items()} | {f"g{k}": m for k, m in g.items()}
    mats |= {f"s{k}": m for k, m in s.items()} | {f"h{k}": m for k, m in gh.items()}
    mats |= {f"m{k}": m for k, m in sm.items()} | {"order": row_order()}
    return pack(mats, 512)


def large_matrices():
    mats = {"shrink": shrink_window(), "grow": grow_window()}
    mats["last"] = padded(shrink_matrix(128).T, 128, 128)
    mats["least"] = padded(grow_matrix(64).T, 128, 128)
    return pack(mats, 640)


def levels_of(mats, letter):
    return {int(n[1:]): m for n, m in mats.items() if n[0] == letter and n[1:].isdigit()}


def mm(a, b):
    return jnp.dot(a, b, preferred_element_type=F32)


def split(v):
    hi = v.astype(BF16)
    return hi, (v - hi.astype(F32)).astype(BF16)


def rdot(v, m):
    hi, lo = split(v)
    return mm(hi, m) + mm(lo, m)


def ldot(m, v):
    hi, lo = split(v)
    return mm(m, hi) + mm(m, lo)


def mmt(a, b):
    return lax.dot_general(a, b, (((1,), (1,)), ((), ())), preferred_element_type=F32)


def windows(v, m, step):
    rows, width = v.shape
    both = jnp.concatenate(split(v), axis=0)
    left = jnp.broadcast_to(both[:, :1], (2 * rows, 128))
    right = jnp.broadcast_to(both[:, width - 1 :], (2 * rows, 128))
    both = jnp.concatenate([left, both, right], axis=1)
    pieces = []
    for n in range(width // step):
        piece = mm(both[:, n * step : n * step + step + 256], m)
        pieces.append(piece[:rows] + piece[rows:])
    return jnp.concatenate(pieces, axis=1)


def right_of(m):
    return lambda v: rdot(v, m)


def pyramid(planes, v, shrinks, product=mm):
    n = len(planes)
    t = jnp.concatenate([product(v[1], p) for p in planes], axis=0)
    levels = {1: shrinks[1](t)}
    for k in range(2, 5):
        prev = levels[k - 1]
        rows = prev.shape[0] // n
        t = jnp.concatenate([ldot(v[k], prev[i * rows : (i + 1) * rows]) for i in range(n)], axis=0)
        levels[k] = shrinks[k](t)
    return levels


def grown(level, n, gv, grow):
    h = grow(level)
    rows = level.shape[0] // n
    return [ldot(gv, h[i * rows : (i + 1) * rows]) for i in range(n)]


def place(rows, cols, base, width, offset):
    i = lax.broadcasted_iota(jnp.int32, (rows, cols), 0)
    c = lax.broadcasted_iota(jnp.int32, (rows, cols), 1)
    hit = (i >= base) & (i < base + width) & (c - i == offset - base)
    return jnp.where(hit, 1.0, 0.0).astype(BF16)


def strips_kernel(places, cell, xa, xb, packed, out, acc):
    mats = unpack(packed, places)
    v, gv, s, gh = (levels_of(mats, letter) for letter in "vgsh")
    s, gh = ({k: right_of(m) for k, m in each.items()} for each in (s, gh))
    order = mats["order"]
    first = window_tile(cell[0]) * 128
    planes = [jnp.concatenate([xa[0, c], xb[0, c]], axis=1) for c in range(COLOURS)]
    levels = pyramid(planes, v, s)
    back = grown(levels[1], COLOURS, gv[0], gh[0])
    b0 = jnp.concatenate([mm(order, planes[c]) - back[c] for c in range(COLOURS)], axis=0)
    bands = [b0.astype(BF16)]
    for k in range(1, 4):
        back = grown(levels[k + 1], COLOURS, gv[k], gh[k])
        bands.append((levels[k] - jnp.concatenate(back, axis=0)).astype(BF16))
    bands.append(levels[4].astype(BF16))
    start = cell[0] * 16 - first

    def pick(band, base, k):
        i = lax.broadcasted_iota(jnp.int32, (band.shape[1], 128), 0)
        c = lax.broadcasted_iota(jnp.int32, (band.shape[1], 128), 1)
        hit = (c >= base) & (c < base + (64 >> k)) & (i - c == (start >> k) - base)
        return mm(band, jnp.where(hit, 1.0, 0.0).astype(BF16))

    out[0:192, :] = (pick(bands[0][0:192], 0, 0) + pick(bands[0][192:384], 64, 0)).astype(BF16)
    acc[...] = pick(bands[1][0:96], 0, 1) + pick(bands[1][96:192], 32, 1) + pick(bands[2], 64, 2)
    acc[0:48, :] = acc[0:48, :] + pick(bands[3], 80, 3) + pick(bands[4], 88, 4)
    out[192:288, :] = acc[...].astype(BF16)


def window_tile(cell):
    return jnp.clip((cell - 3) >> 3, 0, (FW - WIN) // 128)


def full_spec(a):
    return pl.BlockSpec(a.shape, lambda *_: (0,) * a.ndim)


def strips_of(frames, cell):
    packed, places = small_matrices()
    grid_spec = pltpu.PrefetchScalarGridSpec(
        num_scalar_prefetch=1,
        grid=(1,),
        in_specs=[
            pl.BlockSpec((1, COLOURS, FH, 128), lambda i, c: (0, 0, 0, window_tile(c[0]))),
            pl.BlockSpec((1, COLOURS, FH, 128), lambda i, c: (0, 0, 0, window_tile(c[0]) + 1)),
        ]
        + [full_spec(packed)],
        out_specs=pl.BlockSpec((288, 128), lambda i, c: (0, 0)),
        scratch_shapes=[pltpu.VMEM((96, 128), F32)],
    )
    return pl.pallas_call(
        functools.partial(strips_kernel, places),
        grid_spec=grid_spec,
        out_shape=jax.ShapeDtypeStruct((288, 128), BF16),
        compiler_params=pltpu.CompilerParams(vmem_limit_bytes=VMEM),
        cost_estimate=pl.CostEstimate(flops=2 * 10**9, bytes_accessed=10**6, transcendentals=0),
        name="strips",
    )(cell, frames, frames, packed)


def lane_index():
    return lax.broadcasted_iota(jnp.int32, (1, 128), 1)


def fold_level0(p, store):
    left = lane_index() < 64
    for r in range(2):
        for j in range(8):
            even = p[r * 64 : r * 64 + 32, j * 128 : j * 128 + 128]
            odd = p[r * 64 + 32 : r * 64 + 64, j * 128 : j * 128 + 128]
            store(r * 16 + 2 * j, jnp.where(left, even, pltpu.roll(odd, 64, 1)))
            store(r * 16 + 2 * j + 1, jnp.where(left, pltpu.roll(even, 64, 1), odd))


def gather_channels(parts, width, cc, base):
    groups = 128 // width
    group = lane_index() // width
    out = jnp.zeros_like(parts[0])
    for ch in range(4):
        out = jnp.where(group == (cc + ch) % groups, parts[ch], out)
    return pltpu.roll(out, (base - cc * width) % 128, 1)


STATE_ROWS = 816


def state_views(state):
    at = lambda r, h, c, w: (slice(r, r + h), slice(c, c + w))
    b0 = [at(128 * c, 128, 0, 1024) for c in range(3)]
    l1 = [at(384, 64, 0, 512), at(384, 64, 512, 512), at(448, 64, 0, 512), at(448, 64, 512, 512)]
    l2 = [at(512, 32, 256 * c, 256) for c in range(4)]
    l3 = [at(544, 16, 128 * c, 128) for c in range(4)]
    l4 = [at(544, 16, 512 + 128 * c, 128) for c in range(4)]
    levels = [b0 + [at(560, 128, 0, 1024)], l1, l2, l3, l4]
    masks = [at(688, 128 >> k, 128 * k, 64 >> k) for k in range(4)] + [at(688, 16, 512, 4)]
    return levels, masks


def bands_kernel(small_places, large_places, x, w, m, small, large, wblocks, state):
    mats = unpack(small, small_places)
    v, gv, sm = (levels_of(mats, letter) for letter in "vgm")
    order = mats["order"]
    sm = {k: right_of(each) for k, each in sm.items()}
    mats = unpack(large, large_places)
    half = lambda each: windows(each, mats["shrink"], 256)
    twice = lambda each: windows(each, mats["grow"], 128)
    s = {1: half, 2: half, 3: half, 4: right_of(mats["last"])}
    gh = {0: twice, 1: twice, 2: twice, 3: right_of(mats["least"])}
    views, mask_views = state_views(state)
    planes = [x[0, c] for c in range(COLOURS)] + [w[0]]
    weights = mm(order, planes[3])
    state[views[0][3]] = weights

    def store(q, piece):
        wblocks[q] = piece.astype(BF16)

    fold_level0(weights, store)
    levels = pyramid(planes, v, s)
    for k in range(1, 5):
        rows = levels[k].shape[0] // 4
        state[views[k][3]] = levels[k][3 * rows :]
    back = grown(levels[1][: 3 * 64], COLOURS, gv[0], gh[0])
    for c in range(COLOURS):
        state[views[0][c]] = mm(order, planes[c]) - back[c]
    for k in range(1, 4):
        rows = levels[k].shape[0] // 4
        below = levels[k + 1].shape[0] // 4
        back = grown(levels[k + 1][: 3 * below], COLOURS, gv[k], gh[k])
        for c in range(COLOURS):
            state[views[k][c]] = levels[k][c * rows : (c + 1) * rows] - back[c]
    for c in range(COLOURS):
        state[views[4][c]] = levels[4][c * 16 : (c + 1) * 16]
    other = (1.0 - m[0].astype(F32)).astype(BF16)
    state[mask_views[0]] = mmt(order, other)
    masks = pyramid([other], v, sm, mmt)
    for k in range(1, 5):
        state[mask_views[k]] = masks[k]


def bands_of(frames, weight_map, seam_mask):
    small, small_places = small_matrices()
    large, large_places = large_matrices()
    return pl.pallas_call(
        functools.partial(bands_kernel, small_places, large_places),
        out_shape=[jax.ShapeDtypeStruct((QB, 32, 128), BF16), jax.ShapeDtypeStruct((STATE_ROWS, FW), F32)],
        compiler_params=pltpu.CompilerParams(vmem_limit_bytes=VMEM),
        cost_estimate=pl.CostEstimate(flops=8 * 10**9, bytes_accessed=6 * 10**6, transcendentals=0),
        name="bands",
    )(frames, weight_map, jnp.swapaxes(seam_mask, 1, 2), small, large)


def blend_kernel(cell, strips, state, first, second):
    views, mask_views = state_views(state)
    (b0, b1, b2, b3, b4) = [[state[view] for view in views[k][:3]] for k in range(5)]
    (wp, w1, w2, w3, w4) = [state[views[k][3]] for k in range(5)]
    (n0, n1, n2, n3, n4) = [state[view] for view in mask_views]
    start = cell[0] * 16
    low = strips[192:288]

    def mixed(band, remote, share):
        return band + share * (remote - band)

    widths = (1024, 512, 256, 128, 128)
    share0 = mm(n0.astype(BF16), place(64, 1024, 0, 64, start))
    share = [share0]
    for k, ref in enumerate((n1, n2, n3, n4)):
        share.append(rdot(ref, place(64 >> (k + 1), widths[k + 1], 0, 64 >> (k + 1), start >> (k + 1))))
    top = strips[0:192]
    remote0 = [mm(top, place(128, 1024, 0, 64, start)), mm(top, place(128, 1024, 64, 64, start))]
    remote0 = jnp.concatenate(remote0, axis=0)
    weights = wp
    for c in range(COLOURS):
        p = weights * mixed(b0[c], remote0[c * 128 : (c + 1) * 128], share[0])
        out, row = (first, 0) if c == 0 else (second, 32 * (c - 1))

        def store(q, piece, out=out, row=row):
            out[q, row : row + 32, :] = piece.astype(BF16)

        fold_level0(p, store)
    remote1 = [mm(low, place(128, 512, 0, 32, start >> 1)), mm(low, place(128, 512, 32, 32, start >> 1))]
    remote1 = jnp.concatenate(remote1, axis=0)
    parts = [w1 * mixed(b1[c], remote1[c * 64 : (c + 1) * 64], share[1]) for c in range(COLOURS)] + [w1]
    for r in range(2):
        for j in range(4):
            turned = [parts[ch][r * 32 : r * 32 + 32, j * 128 : j * 128 + 128] for ch in range(4)]
            turned = [turned[0]] + [pltpu.roll(turned[ch], 32 * ch, 1) for ch in range(1, 4)]
            for cc in range(4):
                first[r * 16 + 4 * j + cc, 32:64, :] = gather_channels(turned, 32, cc, 0).astype(BF16)
    remote2 = mm(low, place(128, 256, 64, 16, start >> 2))
    remote3 = mm(low[0:48], place(128, 128, 80, 8, start >> 3))
    remote4 = mm(low[0:48], place(128, 128, 88, 4, start >> 4))
    parts2 = [w2 * mixed(b2[c], remote2[c * 32 : (c + 1) * 32], share[2]) for c in range(COLOURS)] + [w2]
    parts3 = [w3 * mixed(b3[c], remote3[c * 16 : (c + 1) * 16], share[3]) for c in range(COLOURS)] + [w3]
    parts4 = [w4 * mixed(b4[c], remote4[c * 16 : (c + 1) * 16], share[4]) for c in range(COLOURS)] + [w4]
    lane = lane_index()
    for r in range(2):
        turned3 = [pltpu.roll(parts3[ch][r * 8 : r * 8 + 8], 8 * ch, 1) for ch in range(4)]
        turned4 = [pltpu.roll(parts4[ch][r * 8 : r * 8 + 8], 4 * ch, 1) for ch in range(4)]
        for j in range(2):
            turned2 = [parts2[ch][r * 16 : r * 16 + 16, j * 128 : j * 128 + 128] for ch in range(4)]
            turned2 = [pltpu.roll(turned2[ch], 16 * ch, 1) for ch in range(4)]
            for cc in range(8):
                c = j * 8 + cc
                two = gather_channels(turned2, 16, cc, 0)
                three = gather_channels(turned3, 8, c, 64)
                four = gather_channels(turned4, 4, c, 96)
                head = jnp.where(lane < 64, two[0:8], jnp.where(lane < 96, three, four))
                tail = jnp.where(lane < 64, two[8:16], 0.0)
                first[r * 16 + c, 64:80, :] = jnp.concatenate([head, tail], axis=0).astype(BF16)


def blend(cell, strips, state):
    vmem = pl.BlockSpec(memory_space=pltpu.VMEM)
    return pl.pallas_call(
        blend_kernel,
        in_specs=[pl.BlockSpec(memory_space=pltpu.SMEM)] + [vmem] * 2,
        out_shape=[jax.ShapeDtypeStruct((QB, 80, 128), BF16), jax.ShapeDtypeStruct((QB, 64, 128), BF16)],
        compiler_params=pltpu.CompilerParams(vmem_limit_bytes=VMEM),
        cost_estimate=pl.CostEstimate(flops=10**6, bytes_accessed=10**4, transcendentals=0),
        name="blend",
    )(cell, strips, state)


def routes_kernel(spot, lists, counts):
    for source in range(4):

        def body(q, count, source=source):
            at = spot[source, q]
            lists[source, count] = q * ROUTE + at
            return jnp.where(at >= 0, count + 1, count)

        counts[source] = lax.fori_loop(0, QB, body, 0, unroll=True)


def routes_of(spot):
    smem = pl.BlockSpec(memory_space=pltpu.SMEM)
    return pl.pallas_call(
        routes_kernel,
        in_specs=[smem],
        out_specs=[smem, smem],
        out_shape=[jax.ShapeDtypeStruct((4, QB + 1), jnp.int32), jax.ShapeDtypeStruct((4,), jnp.int32)],
        name="routes",
    )(spot)


def gather_kernel(lists, counts, *refs):
    home, away, acc = refs[-3:]
    acc[...] = jnp.zeros_like(acc)
    for source in range(4):

        def body(i, carry, source=source):
            entry = lists[source, i]
            q, at = entry // ROUTE, entry % ROUTE
            lo = 0
            for ref in refs[source:-3:4]:
                hi = lo + ref.shape[1]
                acc[at, lo:hi, :] = acc[at, lo:hi, :] + ref[q].astype(F32)
                lo = hi
            return carry

        lax.fori_loop(0, counts[source], body, 0)
    tiles = home.shape[0]
    home[...] = acc[0:tiles]
    away[...] = acc[tiles : 2 * tiles].astype(BF16)


def gather_rows(routes, rows, tiles):
    height = sum(each.shape[1] for each in rows[::4])
    vmem = pl.BlockSpec(memory_space=pltpu.VMEM)
    shape = (tiles // 2, height, 128)
    return pl.pallas_call(
        gather_kernel,
        in_specs=[pl.BlockSpec(memory_space=pltpu.SMEM)] * 2 + [vmem] * len(rows),
        out_shape=[jax.ShapeDtypeStruct(shape, F32), jax.ShapeDtypeStruct(shape, BF16)],
        scratch_shapes=[pltpu.VMEM((tiles, height, 128), F32)],
        compiler_params=pltpu.CompilerParams(vmem_limit_bytes=VMEM),
        cost_estimate=pl.CostEstimate(flops=10**6, bytes_accessed=10**4, transcendentals=0),
        name="gather_rows",
    )(*routes, *rows)


def add_kernel(pairs, *refs):
    out = refs[2 * pairs :]
    lo = 0
    for home, got in zip(refs[:pairs], refs[pairs : 2 * pairs]):
        hi = lo + home.shape[1]
        for j, ref in enumerate(out):
            tiles = slice(j * TILE_DEV, (j + 1) * TILE_DEV)
            ref[:, lo:hi, :] = (home[tiles] + got[tiles].astype(F32)).astype(ref.dtype)
        lo = hi


def add_halves(homes, gots):
    shape = (TILE_DEV, sum(home.shape[1] for home in homes), 128)
    others = homes[0].shape[0] // TILE_DEV - 1
    return pl.pallas_call(
        functools.partial(add_kernel, len(homes)),
        out_shape=[jax.ShapeDtypeStruct(shape, F32)] + [jax.ShapeDtypeStruct(shape, BF16)] * others,
        compiler_params=pltpu.CompilerParams(vmem_limit_bytes=VMEM),
        cost_estimate=pl.CostEstimate(flops=10**6, bytes_accessed=10**4, transcendentals=0),
        name="add_halves",
    )(*homes, *gots)


def collapse_matrices():
    def across(src, dst, width):
        g = grow_matrix(width).T
        m = np.zeros((128, 128), np.float32)
        for ch in range(COLOURS):
            m[src + ch * width : src + (ch + 1) * width, dst + ch * 2 * width : dst + (ch + 1) * 2 * width] = g
        return m

    last = np.zeros((128, 384), np.float32)
    g = grow_matrix(32).T
    for ch in range(COLOURS):
        for half in range(2):
            last[ch * 32 : ch * 32 + 32, ch * 128 + half * 64 : ch * 128 + half * 64 + 64] = g

    def down(n, rows_in, rows_out, pick=None):
        g = grow_matrix(n)
        g = g if pick is None else g[pick::2]
        m = np.zeros((TILE_DEV * rows_out, TILE_DEV * rows_in), np.float32)
        for t in range(TILE_DEV):
            m[t * rows_out : t * rows_out + g.shape[0], t * rows_in : t * rows_in + n] = g
        return m

    mats = {"m43": across(96, 64, 4), "m32": across(64, 0, 8), "m21": across(0, 0, 16), "m10": last}
    mats |= {"d43": down(4, 16, 16), "d32": down(8, 16, 16), "d21": down(16, 16, 32)}
    mats |= {"even": down(32, 32, 32, 0), "odd": down(32, 32, 32, 1)}
    return pack(mats, 1280)


def collapse_kernel(places, each, packed, *refs):
    mats = unpack(packed, places)
    b, c = (refs[i * each : (i + 1) * each] for i in range(2))
    out, level0 = refs[2 * each :]

    def total(sources, lo, hi):
        acc = sources[0][:, lo:hi, :]
        for source in sources[1:]:
            acc = acc + source[:, lo:hi, :].astype(F32)
        return acc.reshape(TILE_DEV * (hi - lo), 128)

    lane = lane_index()
    small = total(b, 64, 80)
    bottom = small
    for lo, width, chans in ((0, 16, 3), (64, 8, 3), (96, 4, 3)):
        for ch in range(chans):
            inside = (lane >= lo + ch * width) & (lane < lo + (ch + 1) * width)
            bottom = jnp.where(inside, pltpu.roll(small, (128 - (3 - ch) * width) % 128, 1), bottom)
    small = small / jnp.maximum(bottom, 1.0)
    three = small + ldot(mats["d43"], rdot(small, mats["m43"]))
    two = small + ldot(mats["d32"], rdot(three, mats["m32"]))
    one = total(b, 32, 64)
    bottom = one
    for ch in range(3):
        inside = (lane >= ch * 32) & (lane < (ch + 1) * 32)
        bottom = jnp.where(inside, pltpu.roll(one, (128 - (3 - ch) * 32) % 128, 1), bottom)
    one = one / jnp.maximum(bottom, 1.0) + ldot(mats["d21"], rdot(two, mats["m21"]))
    wide = rdot(one, mats["m10"])
    hi, lo = split(wide)
    up = mm(mats["even"], hi) + mm(mats["even"], lo)
    down = mm(mats["odd"], hi) + mm(mats["odd"], lo)
    bottom = jnp.maximum(total(c, 64, 96), 1.0)
    for ch in range(COLOURS):
        own = total(b, 0, 32) if ch == 0 else total(c, 32 * (ch - 1), 32 * ch)
        back = jnp.where(lane < 64, up[:, ch * 128 : ch * 128 + 128], down[:, ch * 128 : ch * 128 + 128])
        level0[ch * 128 : ch * 128 + 128, :] = own / bottom + back
    for ch in range(COLOURS):
        for row in range(32):
            out[ch, :, row * 128 : row * 128 + 128] = level0[pl.ds(ch * 128 + row, TILE_DEV, stride=32), :]


def collapse(b, c):
    packed, places = collapse_matrices()
    tiles = pl.pallas_call(
        functools.partial(collapse_kernel, places, len(b)),
        out_shape=jax.ShapeDtypeStruct((COLOURS, TILE_DEV, 4096), F32),
        scratch_shapes=[pltpu.VMEM((COLOURS * 128, 128), F32)],
        compiler_params=pltpu.CompilerParams(vmem_limit_bytes=VMEM),
        cost_estimate=pl.CostEstimate(flops=10**6, bytes_accessed=10**4, transcendentals=0),
        name="collapse",
    )(packed, *b, *c)
    return jnp.swapaxes(tiles, 0, 1)


def swap(value, axis, bit):
    size = lax.axis_size(axis)
    return lax.ppermute(value, axis, [(i, i ^ bit) for i in range(size)])


def local(frames, weight_map, seam_mask, strip_cell, partner, tile_group, tile_position_in_group):
    groups = lax.axis_size("frames")
    parts = lax.axis_size("tiles")
    mine = lax.axis_index("tiles")
    mask = lax.bitwise_xor(partner[0] // parts, lax.axis_index("frames"))

    tie = lax.optimization_barrier
    strips = strips_of(frames, strip_cell)
    ids = tile_group.reshape(QB) * (parts * TILE_DEV) + tile_position_in_group.reshape(QB)
    strips, frames, ids = tie((strips, frames, ids))
    ids = jnp.stack([ids, swap(ids, "tiles", 1)])
    ids_x = jnp.concatenate([ids, swap(ids, "tiles", 2)])
    ids_y = jnp.concatenate([ids, swap(ids, "frames", 1)])

    def relative(ids):
        group, tile = ids // (parts * TILE_DEV), ids % (parts * TILE_DEV)
        group = lax.bitwise_xor(group, lax.axis_index("frames"))
        return group, lax.bitwise_xor(tile // TILE_DEV, mine), tile % TILE_DEV

    half = groups // 2
    group, part, tile = relative(ids_x)
    spot_x = jnp.where(part == 0, ((group & 1) * half + (group >> 1)) * TILE_DEV + tile, -1)
    group, part, tile = relative(ids_y)
    here = ((group & 1) == 0) & ((part & 1) == 0)
    spot_y = jnp.where(here, ((part >> 1) * half + (group >> 1)) * TILE_DEV + tile, -1)

    weights, state = bands_of(frames, weight_map, seam_mask)
    bit = 1
    while bit < groups:
        got = swap(strips, "frames", bit)
        if bit == 1:
            got, weights, state = tie((got, weights, state))
            far, near = swap(weights, "tiles", 2), swap(weights, "tiles", 1)
        if bit == 2:
            got, far, near = tie((got, far, near))
        if bit == half:
            got, spot_x, spot_y = tie((got, spot_x, spot_y))
        strips = jnp.where((mask & bit) != 0, got, strips)
        bit *= 2

    def gather(routes, *rows):
        return gather_rows(routes, rows, groups * TILE_DEV)

    def along(own, *away):
        return [own] + [swap(part, "frames", 2 * (j + 1)) for j, part in enumerate(away)]

    first, second = blend(strip_cell, strips, state)
    first, second, spot_x, spot_y, far = tie((first, second, spot_x, spot_y, far))
    far_first, near_first = swap(first, "tiles", 2), swap(first, "tiles", 1)
    far_second, near_second = swap(second, "frames", 1), swap(second, "tiles", 1)
    routes_x, routes_y = routes_of(spot_x), routes_of(spot_y)
    home_w, away_w = gather(routes_x, weights, near, far, swap(far, "tiles", 1))
    got_w = swap(away_w, "frames", 1)
    far_second, home_w, routes_y = tie((far_second, home_w, routes_y))
    home_s, away_s = gather(routes_y, second, near_second, far_second, swap(far_second, "tiles", 1))
    got_s = swap(away_s, "tiles", 2)
    far_first, home_s, got_w = tie((far_first, home_s, got_w))
    far_near, got_s = tie((swap(far_first, "tiles", 1), got_s))
    home_f, away_f = gather(routes_x, first, near_first, far_first, far_near)
    got_f = swap(away_f, "frames", 1)
    got_second = along(*add_halves((home_s, home_w), (got_s, got_w)))
    got_f, got_second = tie((got_f, got_second))
    got_first = along(*add_halves((home_f,), (got_f,)))
    return collapse(got_first, got_second)


def solution(mesh):
    in_specs = (
        P(("frames", "tiles"), None, None, None),
        P(("frames", "tiles"), None, None),
        P(("frames", "tiles"), None, None),
        P(("frames", "tiles")),
        P(("frames", "tiles")),
        P(("frames", "tiles"), None, None),
        P(("frames", "tiles"), None),
    )
    out_specs = P(("frames", "tiles"), None, None)
    return jax.shard_map(local, mesh=mesh, in_specs=in_specs, out_specs=out_specs, check_vma=False)
```

```python
import functools

import jax
import jax.numpy as jnp
import numpy as np
from jax import lax
from jax.experimental import pallas as pl
from jax.experimental.pallas import tpu as pltpu
from jax.sharding import PartitionSpec as P

COLOURS = 3
FH = 128
FW = 1024
QB = 32
WIN = 256
TILE_DEV = 4
VMEM = 20 << 20
ROUTE = 4096
F32 = jnp.float32
BF16 = jnp.bfloat16


def shrink_matrix(n):
    m = np.zeros((n // 2, n), np.float32)
    for i in range(n // 2):
        for d, tap in zip(range(-2, 3), (1, 4, 6, 4, 1)):
            m[i, min(max(2 * i + d, 0), n - 1)] += tap / 16.0
    return m


def grow_matrix(n):
    m = np.zeros((2 * n, n), np.float32)
    for i in range(n):
        lo, hi = max(i - 1, 0), min(i + 1, n - 1)
        m[2 * i, lo] += 1 / 8
        m[2 * i, i] += 6 / 8
        m[2 * i, hi] += 1 / 8
        m[2 * i + 1, i] += 1 / 2
        m[2 * i + 1, hi] += 1 / 2
    return m


def padded(m, rows, cols):
    return np.pad(m, ((0, rows - m.shape[0]), (0, cols - m.shape[1])))


def row_order():
    m = np.zeros((FH, FH), np.float32)
    for r in range(2):
        for par in range(2):
            for i in range(32):
                m[r * 64 + par * 32 + i, r * 64 + 2 * i + par] = 1
    return m


def vertical():
    v = {1: shrink_matrix(128), 2: shrink_matrix(64), 3: shrink_matrix(32)}
    spread = np.zeros((16, 8), np.float32)
    for r in range(2):
        for i in range(4):
            spread[r * 8 + i, r * 4 + i] = 1
    v[4] = spread @ shrink_matrix(16)
    g = {0: row_order() @ grow_matrix(64), 1: grow_matrix(32), 2: grow_matrix(16)}
    g[3] = grow_matrix(8) @ spread.T
    return v, g


def horizontal(width):
    s = {k: shrink_matrix(width >> (k - 1)).T for k in range(1, 5)}
    g = {k: grow_matrix(width >> (k + 1)).T for k in range(4)}
    return s, g


def shrink_window():
    m = np.zeros((512, 128), np.float32)
    for i in range(128):
        for d, tap in zip(range(-2, 3), (1, 4, 6, 4, 1)):
            m[128 + 2 * i + d, i] = tap / 16.0
    return m


def grow_window():
    m = np.zeros((384, 256), np.float32)
    for i in range(128):
        for d, tap in zip(range(-1, 2), (1, 6, 1)):
            m[128 + i + d, 2 * i] = tap / 8.0
        m[128 + i, 2 * i + 1] = m[128 + i + 1, 2 * i + 1] = 0.5
    return m


def pack(mats, width):
    places, row, col, height = {}, 0, 0, 0
    for name in sorted(mats, key=lambda n: (-mats[n].shape[0], -mats[n].shape[1], n)):
        h, w = mats[name].shape
        wide = -(-w // 128) * 128
        if col + wide > width:
            row, col, height = row + height, 0, 0
        height = max(height, -(-h // 16) * 16)
        places[name] = (row, col, h, w)
        col += wide
    out = np.zeros((row + height, width), np.float32)
    for name, (r, c, h, w) in places.items():
        out[r : r + h, c : c + w] = mats[name]
    return jnp.asarray(out, BF16), places


def unpack(ref, places):
    return {name: ref[r : r + h, c : c + w] for name, (r, c, h, w) in places.items()}


def small_matrices():
    v, g = vertical()
    s, gh = horizontal(WIN)
    sm, _ = horizontal(64)
    mats = {f"v{k}": m for k, m in v.items()} | {f"g{k}": m for k, m in g.items()}
    mats |= {f"s{k}": m for k, m in s.items()} | {f"h{k}": m for k, m in gh.items()}
    mats |= {f"m{k}": m for k, m in sm.items()} | {"order": row_order()}
    return pack(mats, 512)


def large_matrices():
    mats = {"shrink": shrink_window(), "grow": grow_window()}
    mats["last"] = padded(shrink_matrix(128).T, 128, 128)
    mats["least"] = padded(grow_matrix(64).T, 128, 128)
    return pack(mats, 640)


def levels_of(mats, letter):
    return {int(n[1:]): m for n, m in mats.items() if n[0] == letter and n[1:].isdigit()}


def mm(a, b):
    return jnp.dot(a, b, preferred_element_type=F32)


def split(v):
    hi = v.astype(BF16)
    return hi, (v - hi.astype(F32)).astype(BF16)


def rdot(v, m):
    hi, lo = split(v)
    return mm(hi, m) + mm(lo, m)


def ldot(m, v):
    hi, lo = split(v)
    return mm(m, hi) + mm(m, lo)


def mmt(a, b):
    return lax.dot_general(a, b, (((1,), (1,)), ((), ())), preferred_element_type=F32)


def windows(v, m, step):
    rows, width = v.shape
    both = jnp.concatenate(split(v), axis=0)
    left = jnp.broadcast_to(both[:, :1], (2 * rows, 128))
    right = jnp.broadcast_to(both[:, width - 1 :], (2 * rows, 128))
    both = jnp.concatenate([left, both, right], axis=1)
    pieces = []
    for n in range(width // step):
        piece = mm(both[:, n * step : n * step + step + 256], m)
        pieces.append(piece[:rows] + piece[rows:])
    return jnp.concatenate(pieces, axis=1)


def right_of(m):
    return lambda v: rdot(v, m)


def pyramid(planes, v, shrinks, product=mm):
    n = len(planes)
    t = jnp.concatenate([product(v[1], p) for p in planes], axis=0)
    levels = {1: shrinks[1](t)}
    for k in range(2, 5):
        prev = levels[k - 1]
        rows = prev.shape[0] // n
        t = jnp.concatenate([ldot(v[k], prev[i * rows : (i + 1) * rows]) for i in range(n)], axis=0)
        levels[k] = shrinks[k](t)
    return levels


def grown(level, n, gv, grow):
    h = grow(level)
    rows = level.shape[0] // n
    return [ldot(gv, h[i * rows : (i + 1) * rows]) for i in range(n)]


def place(rows, cols, base, width, offset):
    i = lax.broadcasted_iota(jnp.int32, (rows, cols), 0)
    c = lax.broadcasted_iota(jnp.int32, (rows, cols), 1)
    hit = (i >= base) & (i < base + width) & (c - i == offset - base)
    return jnp.where(hit, 1.0, 0.0).astype(BF16)


def strips_kernel(places, cell, xa, xb, packed, out, acc):
    mats = unpack(packed, places)
    v, gv, s, gh = (levels_of(mats, letter) for letter in "vgsh")
    s, gh = ({k: right_of(m) for k, m in each.items()} for each in (s, gh))
    order = mats["order"]
    first = window_tile(cell[0]) * 128
    planes = [jnp.concatenate([xa[0, c], xb[0, c]], axis=1) for c in range(COLOURS)]
    levels = pyramid(planes, v, s)
    back = grown(levels[1], COLOURS, gv[0], gh[0])
    b0 = jnp.concatenate([mm(order, planes[c]) - back[c] for c in range(COLOURS)], axis=0)
    bands = [b0.astype(BF16)]
    for k in range(1, 4):
        back = grown(levels[k + 1], COLOURS, gv[k], gh[k])
        bands.append((levels[k] - jnp.concatenate(back, axis=0)).astype(BF16))
    bands.append(levels[4].astype(BF16))
    start = cell[0] * 16 - first

    def pick(band, base, k):
        i = lax.broadcasted_iota(jnp.int32, (band.shape[1], 128), 0)
        c = lax.broadcasted_iota(jnp.int32, (band.shape[1], 128), 1)
        hit = (c >= base) & (c < base + (64 >> k)) & (i - c == (start >> k) - base)
        return mm(band, jnp.where(hit, 1.0, 0.0).astype(BF16))

    out[0:192, :] = (pick(bands[0][0:192], 0, 0) + pick(bands[0][192:384], 64, 0)).astype(BF16)
    acc[...] = pick(bands[1][0:96], 0, 1) + pick(bands[1][96:192], 32, 1) + pick(bands[2], 64, 2)
    acc[0:48, :] = acc[0:48, :] + pick(bands[3], 80, 3) + pick(bands[4], 88, 4)
    out[192:288, :] = acc[...].astype(BF16)


def window_tile(cell):
    return jnp.clip((cell - 3) >> 3, 0, (FW - WIN) // 128)


def full_spec(a):
    return pl.BlockSpec(a.shape, lambda *_: (0,) * a.ndim)


def strips_of(frames, cell):
    packed, places = small_matrices()
    grid_spec = pltpu.PrefetchScalarGridSpec(
        num_scalar_prefetch=1,
        grid=(1,),
        in_specs=[
            pl.BlockSpec((1, COLOURS, FH, 128), lambda i, c: (0, 0, 0, window_tile(c[0]))),
            pl.BlockSpec((1, COLOURS, FH, 128), lambda i, c: (0, 0, 0, window_tile(c[0]) + 1)),
        ]
        + [full_spec(packed)],
        out_specs=pl.BlockSpec((288, 128), lambda i, c: (0, 0)),
        scratch_shapes=[pltpu.VMEM((96, 128), F32)],
    )
    return pl.pallas_call(
        functools.partial(strips_kernel, places),
        grid_spec=grid_spec,
        out_shape=jax.ShapeDtypeStruct((288, 128), BF16),
        compiler_params=pltpu.CompilerParams(vmem_limit_bytes=VMEM),
        cost_estimate=pl.CostEstimate(flops=2 * 10**9, bytes_accessed=10**6, transcendentals=0),
        name="strips",
    )(cell, frames, frames, packed)


def lane_index():
    return lax.broadcasted_iota(jnp.int32, (1, 128), 1)


def fold_level0(p, store):
    left = lane_index() < 64
    for r in range(2):
        for j in range(8):
            even = p[r * 64 : r * 64 + 32, j * 128 : j * 128 + 128]
            odd = p[r * 64 + 32 : r * 64 + 64, j * 128 : j * 128 + 128]
            store(r * 16 + 2 * j, jnp.where(left, even, pltpu.roll(odd, 64, 1)))
            store(r * 16 + 2 * j + 1, jnp.where(left, pltpu.roll(even, 64, 1), odd))


def gather_channels(parts, width, cc, base):
    groups = 128 // width
    group = lane_index() // width
    out = jnp.zeros_like(parts[0])
    for ch in range(4):
        out = jnp.where(group == (cc + ch) % groups, parts[ch], out)
    return pltpu.roll(out, (base - cc * width) % 128, 1)


STATE_ROWS = 816


def state_views(state):
    at = lambda r, h, c, w: (slice(r, r + h), slice(c, c + w))
    b0 = [at(128 * c, 128, 0, 1024) for c in range(3)]
    l1 = [at(384, 64, 0, 512), at(384, 64, 512, 512), at(448, 64, 0, 512), at(448, 64, 512, 512)]
    l2 = [at(512, 32, 256 * c, 256) for c in range(4)]
    l3 = [at(544, 16, 128 * c, 128) for c in range(4)]
    l4 = [at(544, 16, 512 + 128 * c, 128) for c in range(4)]
    levels = [b0 + [at(560, 128, 0, 1024)], l1, l2, l3, l4]
    masks = [at(688, 128 >> k, 128 * k, 64 >> k) for k in range(4)] + [at(688, 16, 512, 4)]
    return levels, masks


def bands_kernel(small_places, large_places, x, w, m, small, large, wblocks, state):
    mats = unpack(small, small_places)
    v, gv, sm = (levels_of(mats, letter) for letter in "vgm")
    order = mats["order"]
    sm = {k: right_of(each) for k, each in sm.items()}
    mats = unpack(large, large_places)
    half = lambda each: windows(each, mats["shrink"], 256)
    twice = lambda each: windows(each, mats["grow"], 128)
    s = {1: half, 2: half, 3: half, 4: right_of(mats["last"])}
    gh = {0: twice, 1: twice, 2: twice, 3: right_of(mats["least"])}
    views, mask_views = state_views(state)
    planes = [x[0, c] for c in range(COLOURS)] + [w[0]]
    weights = mm(order, planes[3])
    state[views[0][3]] = weights

    def store(q, piece):
        wblocks[q] = piece.astype(BF16)

    fold_level0(weights, store)
    levels = pyramid(planes, v, s)
    for k in range(1, 5):
        rows = levels[k].shape[0] // 4
        state[views[k][3]] = levels[k][3 * rows :]
    back = grown(levels[1][: 3 * 64], COLOURS, gv[0], gh[0])
    for c in range(COLOURS):
        state[views[0][c]] = mm(order, planes[c]) - back[c]
    for k in range(1, 4):
        rows = levels[k].shape[0] // 4
        below = levels[k + 1].shape[0] // 4
        back = grown(levels[k + 1][: 3 * below], COLOURS, gv[k], gh[k])
        for c in range(COLOURS):
            state[views[k][c]] = levels[k][c * rows : (c + 1) * rows] - back[c]
    for c in range(COLOURS):
        state[views[4][c]] = levels[4][c * 16 : (c + 1) * 16]
    other = (1.0 - m[0].astype(F32)).astype(BF16)
    state[mask_views[0]] = mmt(order, other)
    masks = pyramid([other], v, sm, mmt)
    for k in range(1, 5):
        state[mask_views[k]] = masks[k]


def bands_of(frames, weight_map, seam_mask):
    small, small_places = small_matrices()
    large, large_places = large_matrices()
    return pl.pallas_call(
        functools.partial(bands_kernel, small_places, large_places),
        out_shape=[jax.ShapeDtypeStruct((QB, 32, 128), BF16), jax.ShapeDtypeStruct((STATE_ROWS, FW), F32)],
        compiler_params=pltpu.CompilerParams(vmem_limit_bytes=VMEM),
        cost_estimate=pl.CostEstimate(flops=8 * 10**9, bytes_accessed=6 * 10**6, transcendentals=0),
        name="bands",
    )(frames, weight_map, jnp.swapaxes(seam_mask, 1, 2), small, large)


def blend_kernel(cell, strips, state, first, second):
    views, mask_views = state_views(state)
    (b0, b1, b2, b3, b4) = [[state[view] for view in views[k][:3]] for k in range(5)]
    (wp, w1, w2, w3, w4) = [state[views[k][3]] for k in range(5)]
    (n0, n1, n2, n3, n4) = [state[view] for view in mask_views]
    start = cell[0] * 16
    low = strips[192:288]

    def mixed(band, remote, share):
        return band + share * (remote - band)

    widths = (1024, 512, 256, 128, 128)
    share0 = mm(n0.astype(BF16), place(64, 1024, 0, 64, start))
    share = [share0]
    for k, ref in enumerate((n1, n2, n3, n4)):
        share.append(rdot(ref, place(64 >> (k + 1), widths[k + 1], 0, 64 >> (k + 1), start >> (k + 1))))
    top = strips[0:192]
    remote0 = [mm(top, place(128, 1024, 0, 64, start)), mm(top, place(128, 1024, 64, 64, start))]
    remote0 = jnp.concatenate(remote0, axis=0)
    weights = wp
    for c in range(COLOURS):
        p = weights * mixed(b0[c], remote0[c * 128 : (c + 1) * 128], share[0])
        out, row = (first, 0) if c == 0 else (second, 32 * (c - 1))

        def store(q, piece, out=out, row=row):
            out[q, row : row + 32, :] = piece.astype(BF16)

        fold_level0(p, store)
    remote1 = [mm(low, place(128, 512, 0, 32, start >> 1)), mm(low, place(128, 512, 32, 32, start >> 1))]
    remote1 = jnp.concatenate(remote1, axis=0)
    parts = [w1 * mixed(b1[c], remote1[c * 64 : (c + 1) * 64], share[1]) for c in range(COLOURS)] + [w1]
    for r in range(2):
        for j in range(4):
            turned = [parts[ch][r * 32 : r * 32 + 32, j * 128 : j * 128 + 128] for ch in range(4)]
            turned = [turned[0]] + [pltpu.roll(turned[ch], 32 * ch, 1) for ch in range(1, 4)]
            for cc in range(4):
                first[r * 16 + 4 * j + cc, 32:64, :] = gather_channels(turned, 32, cc, 0).astype(BF16)
    remote2 = mm(low, place(128, 256, 64, 16, start >> 2))
    remote3 = mm(low[0:48], place(128, 128, 80, 8, start >> 3))
    remote4 = mm(low[0:48], place(128, 128, 88, 4, start >> 4))
    parts2 = [w2 * mixed(b2[c], remote2[c * 32 : (c + 1) * 32], share[2]) for c in range(COLOURS)] + [w2]
    parts3 = [w3 * mixed(b3[c], remote3[c * 16 : (c + 1) * 16], share[3]) for c in range(COLOURS)] + [w3]
    parts4 = [w4 * mixed(b4[c], remote4[c * 16 : (c + 1) * 16], share[4]) for c in range(COLOURS)] + [w4]
    lane = lane_index()
    for r in range(2):
        turned3 = [pltpu.roll(parts3[ch][r * 8 : r * 8 + 8], 8 * ch, 1) for ch in range(4)]
        turned4 = [pltpu.roll(parts4[ch][r * 8 : r * 8 + 8], 4 * ch, 1) for ch in range(4)]
        for j in range(2):
            turned2 = [parts2[ch][r * 16 : r * 16 + 16, j * 128 : j * 128 + 128] for ch in range(4)]
            turned2 = [pltpu.roll(turned2[ch], 16 * ch, 1) for ch in range(4)]
            for cc in range(8):
                c = j * 8 + cc
                two = gather_channels(turned2, 16, cc, 0)
                three = gather_channels(turned3, 8, c, 64)
                four = gather_channels(turned4, 4, c, 96)
                head = jnp.where(lane < 64, two[0:8], jnp.where(lane < 96, three, four))
                tail = jnp.where(lane < 64, two[8:16], 0.0)
                first[r * 16 + c, 64:80, :] = jnp.concatenate([head, tail], axis=0).astype(BF16)


def blend(cell, strips, state):
    vmem = pl.BlockSpec(memory_space=pltpu.VMEM)
    return pl.pallas_call(
        blend_kernel,
        in_specs=[pl.BlockSpec(memory_space=pltpu.SMEM)] + [vmem] * 2,
        out_shape=[jax.ShapeDtypeStruct((QB, 80, 128), BF16), jax.ShapeDtypeStruct((QB, 64, 128), BF16)],
        compiler_params=pltpu.CompilerParams(vmem_limit_bytes=VMEM),
        cost_estimate=pl.CostEstimate(flops=10**6, bytes_accessed=10**4, transcendentals=0),
        name="blend",
    )(cell, strips, state)


def routes_kernel(spot, lists, counts):
    for source in range(4):

        def body(q, count, source=source):
            at = spot[source, q]
            lists[source, count] = q * ROUTE + at
            return jnp.where(at >= 0, count + 1, count)

        counts[source] = lax.fori_loop(0, QB, body, 0, unroll=True)


def routes_of(spot):
    smem = pl.BlockSpec(memory_space=pltpu.SMEM)
    return pl.pallas_call(
        routes_kernel,
        in_specs=[smem],
        out_specs=[smem, smem],
        out_shape=[jax.ShapeDtypeStruct((4, QB + 1), jnp.int32), jax.ShapeDtypeStruct((4,), jnp.int32)],
        name="routes",
    )(spot)


def gather_kernel(lists, counts, *refs):
    home, away, acc = refs[-3:]
    acc[...] = jnp.zeros_like(acc)
    for source in range(4):

        def body(i, carry, source=source):
            entry = lists[source, i]
            q, at = entry // ROUTE, entry % ROUTE
            lo = 0
            for ref in refs[source:-3:4]:
                hi = lo + ref.shape[1]
                acc[at, lo:hi, :] = acc[at, lo:hi, :] + ref[q].astype(F32)
                lo = hi
            return carry

        lax.fori_loop(0, counts[source], body, 0)
    tiles = home.shape[0]
    home[...] = acc[0:tiles]
    away[...] = acc[tiles : 2 * tiles].astype(BF16)


def gather_rows(routes, rows, tiles):
    height = sum(each.shape[1] for each in rows[::4])
    vmem = pl.BlockSpec(memory_space=pltpu.VMEM)
    shape = (tiles // 2, height, 128)
    return pl.pallas_call(
        gather_kernel,
        in_specs=[pl.BlockSpec(memory_space=pltpu.SMEM)] * 2 + [vmem] * len(rows),
        out_shape=[jax.ShapeDtypeStruct(shape, F32), jax.ShapeDtypeStruct(shape, BF16)],
        scratch_shapes=[pltpu.VMEM((tiles, height, 128), F32)],
        compiler_params=pltpu.CompilerParams(vmem_limit_bytes=VMEM),
        cost_estimate=pl.CostEstimate(flops=10**6, bytes_accessed=10**4, transcendentals=0),
        name="gather_rows",
    )(*routes, *rows)


def add_kernel(pairs, *refs):
    out = refs[2 * pairs :]
    lo = 0
    for home, got in zip(refs[:pairs], refs[pairs : 2 * pairs]):
        hi = lo + home.shape[1]
        for j, ref in enumerate(out):
            tiles = slice(j * TILE_DEV, (j + 1) * TILE_DEV)
            ref[:, lo:hi, :] = (home[tiles] + got[tiles].astype(F32)).astype(ref.dtype)
        lo = hi


def add_halves(homes, gots):
    shape = (TILE_DEV, sum(home.shape[1] for home in homes), 128)
    others = homes[0].shape[0] // TILE_DEV - 1
    return pl.pallas_call(
        functools.partial(add_kernel, len(homes)),
        out_shape=[jax.ShapeDtypeStruct(shape, F32)] + [jax.ShapeDtypeStruct(shape, BF16)] * others,
        compiler_params=pltpu.CompilerParams(vmem_limit_bytes=VMEM),
        cost_estimate=pl.CostEstimate(flops=10**6, bytes_accessed=10**4, transcendentals=0),
        name="add_halves",
    )(*homes, *gots)


def collapse_matrices():
    def across(src, dst, width):
        g = grow_matrix(width).T
        m = np.zeros((128, 128), np.float32)
        for ch in range(COLOURS):
            m[src + ch * width : src + (ch + 1) * width, dst + ch * 2 * width : dst + (ch + 1) * 2 * width] = g
        return m

    last = np.zeros((128, 384), np.float32)
    g = grow_matrix(32).T
    for ch in range(COLOURS):
        for half in range(2):
            last[ch * 32 : ch * 32 + 32, ch * 128 + half * 64 : ch * 128 + half * 64 + 64] = g

    def down(n, rows_in, rows_out, pick=None):
        g = grow_matrix(n)
        g = g if pick is None else g[pick::2]
        m = np.zeros((TILE_DEV * rows_out, TILE_DEV * rows_in), np.float32)
        for t in range(TILE_DEV):
            m[t * rows_out : t * rows_out + g.shape[0], t * rows_in : t * rows_in + n] = g
        return m

    mats = {"m43": across(96, 64, 4), "m32": across(64, 0, 8), "m21": across(0, 0, 16), "m10": last}
    mats |= {"d43": down(4, 16, 16), "d32": down(8, 16, 16), "d21": down(16, 16, 32)}
    mats |= {"even": down(32, 32, 32, 0), "odd": down(32, 32, 32, 1)}
    return pack(mats, 1280)


def collapse_kernel(places, each, packed, *refs):
    mats = unpack(packed, places)
    b, c = (refs[i * each : (i + 1) * each] for i in range(2))
    out, level0 = refs[2 * each :]

    def total(sources, lo, hi):
        acc = sources[0][:, lo:hi, :]
        for source in sources[1:]:
            acc = acc + source[:, lo:hi, :].astype(F32)
        return acc.reshape(TILE_DEV * (hi - lo), 128)

    lane = lane_index()
    small = total(b, 64, 80)
    bottom = small
    for lo, width, chans in ((0, 16, 3), (64, 8, 3), (96, 4, 3)):
        for ch in range(chans):
            inside = (lane >= lo + ch * width) & (lane < lo + (ch + 1) * width)
            bottom = jnp.where(inside, pltpu.roll(small, (128 - (3 - ch) * width) % 128, 1), bottom)
    small = small / jnp.maximum(bottom, 1.0)
    three = small + ldot(mats["d43"], rdot(small, mats["m43"]))
    two = small + ldot(mats["d32"], rdot(three, mats["m32"]))
    one = total(b, 32, 64)
    bottom = one
    for ch in range(3):
        inside = (lane >= ch * 32) & (lane < (ch + 1) * 32)
        bottom = jnp.where(inside, pltpu.roll(one, (128 - (3 - ch) * 32) % 128, 1), bottom)
    one = one / jnp.maximum(bottom, 1.0) + ldot(mats["d21"], rdot(two, mats["m21"]))
    wide = rdot(one, mats["m10"])
    hi, lo = split(wide)
    up = mm(mats["even"], hi) + mm(mats["even"], lo)
    down = mm(mats["odd"], hi) + mm(mats["odd"], lo)
    bottom = jnp.maximum(total(c, 64, 96), 1.0)
    for ch in range(COLOURS):
        own = total(b, 0, 32) if ch == 0 else total(c, 32 * (ch - 1), 32 * ch)
        back = jnp.where(lane < 64, up[:, ch * 128 : ch * 128 + 128], down[:, ch * 128 : ch * 128 + 128])
        level0[ch * 128 : ch * 128 + 128, :] = own / bottom + back
    for ch in range(COLOURS):
        for row in range(32):
            out[ch, :, row * 128 : row * 128 + 128] = level0[pl.ds(ch * 128 + row, TILE_DEV, stride=32), :]


def collapse(b, c):
    packed, places = collapse_matrices()
    tiles = pl.pallas_call(
        functools.partial(collapse_kernel, places, len(b)),
        out_shape=jax.ShapeDtypeStruct((COLOURS, TILE_DEV, 4096), F32),
        scratch_shapes=[pltpu.VMEM((COLOURS * 128, 128), F32)],
        compiler_params=pltpu.CompilerParams(vmem_limit_bytes=VMEM),
        cost_estimate=pl.CostEstimate(flops=10**6, bytes_accessed=10**4, transcendentals=0),
        name="collapse",
    )(packed, *b, *c)
    return jnp.swapaxes(tiles, 0, 1)


def swap(value, axis, bit):
    size = lax.axis_size(axis)
    return lax.ppermute(value, axis, [(i, i ^ bit) for i in range(size)])


def local(frames, weight_map, seam_mask, strip_cell, partner, tile_group, tile_position_in_group):
    groups = lax.axis_size("frames")
    parts = lax.axis_size("tiles")
    mine = lax.axis_index("tiles")
    mask = lax.bitwise_xor(partner[0] // parts, lax.axis_index("frames"))

    tie = lax.optimization_barrier
    strips = strips_of(frames, strip_cell)
    ids = tile_group.reshape(QB) * (parts * TILE_DEV) + tile_position_in_group.reshape(QB)
    strips, frames, ids = tie((strips, frames, ids))
    ids = jnp.stack([ids, swap(ids, "tiles", 1)])
    ids_x = jnp.concatenate([ids, swap(ids, "tiles", 2)])
    ids_y = jnp.concatenate([ids, swap(ids, "frames", 1)])

    def relative(ids):
        group, tile = ids // (parts * TILE_DEV), ids % (parts * TILE_DEV)
        group = lax.bitwise_xor(group, lax.axis_index("frames"))
        return group, lax.bitwise_xor(tile // TILE_DEV, mine), tile % TILE_DEV

    half = groups // 2
    group, part, tile = relative(ids_x)
    spot_x = jnp.where(part == 0, ((group & 1) * half + (group >> 1)) * TILE_DEV + tile, -1)
    group, part, tile = relative(ids_y)
    here = ((group & 1) == 0) & ((part & 1) == 0)
    spot_y = jnp.where(here, ((part >> 1) * half + (group >> 1)) * TILE_DEV + tile, -1)

    weights, state = bands_of(frames, weight_map, seam_mask)
    bit = 1
    while bit < groups:
        got = swap(strips, "frames", bit)
        if bit == 1:
            got, weights, state = tie((got, weights, state))
            far, near = swap(weights, "tiles", 2), swap(weights, "tiles", 1)
        if bit == half:
            got, far, near, spot_x, spot_y = tie((got, far, near, spot_x, spot_y))
        strips = jnp.where((mask & bit) != 0, got, strips)
        bit *= 2

    def gather(routes, *rows):
        return gather_rows(routes, rows, groups * TILE_DEV)

    def along(own, *away):
        return [own] + [swap(part, "frames", 2 * (j + 1)) for j, part in enumerate(away)]

    first, second = blend(strip_cell, strips, state)
    first, second, spot_x, spot_y, far = tie((first, second, spot_x, spot_y, far))
    far_first, near_first = swap(first, "tiles", 2), swap(first, "tiles", 1)
    far_second, near_second = swap(second, "frames", 1), swap(second, "tiles", 1)
    routes_x, routes_y = routes_of(spot_x), routes_of(spot_y)
    home_w, away_w = gather(routes_x, weights, near, far, swap(far, "tiles", 1))
    got_w = swap(away_w, "frames", 1)
    far_second, home_w, routes_y = tie((far_second, home_w, routes_y))
    home_s, away_s = gather(routes_y, second, near_second, far_second, swap(far_second, "tiles", 1))
    got_s = swap(away_s, "tiles", 2)
    far_first, home_s, got_w = tie((far_first, home_s, got_w))
    far_near = swap(far_first, "tiles", 1)
    home_f, away_f = gather(routes_x, first, near_first, far_first, far_near)
    got_f = swap(away_f, "frames", 1)
    got_second = along(*add_halves((home_s, home_w), (got_s, got_w)))
    got_f, got_second = tie((got_f, got_second))
    got_first = along(*add_halves((home_f,), (got_f,)))
    return collapse(got_first, got_second)


def solution(mesh):
    in_specs = (
        P(("frames", "tiles"), None, None, None),
        P(("frames", "tiles"), None, None),
        P(("frames", "tiles"), None, None),
        P(("frames", "tiles")),
        P(("frames", "tiles")),
        P(("frames", "tiles"), None, None),
        P(("frames", "tiles"), None),
    )
    out_specs = P(("frames", "tiles"), None, None)
    return jax.shard_map(local, mesh=mesh, in_specs=in_specs, out_specs=out_specs, check_vma=False)
```

```python
import functools

import jax
import jax.numpy as jnp
import numpy as np
from jax import lax
from jax.experimental import pallas as pl
from jax.experimental.pallas import tpu as pltpu
from jax.sharding import PartitionSpec as P

COLOURS = 3
FH = 128
FW = 1024
QB = 32
WIN = 256
TILE_DEV = 4
VMEM = 20 << 20
ROUTE = 4096
F32 = jnp.float32
BF16 = jnp.bfloat16


def shrink_matrix(n):
    m = np.zeros((n // 2, n), np.float32)
    for i in range(n // 2):
        for d, tap in zip(range(-2, 3), (1, 4, 6, 4, 1)):
            m[i, min(max(2 * i + d, 0), n - 1)] += tap / 16.0
    return m


def grow_matrix(n):
    m = np.zeros((2 * n, n), np.float32)
    for i in range(n):
        lo, hi = max(i - 1, 0), min(i + 1, n - 1)
        m[2 * i, lo] += 1 / 8
        m[2 * i, i] += 6 / 8
        m[2 * i, hi] += 1 / 8
        m[2 * i + 1, i] += 1 / 2
        m[2 * i + 1, hi] += 1 / 2
    return m


def padded(m, rows, cols):
    return np.pad(m, ((0, rows - m.shape[0]), (0, cols - m.shape[1])))


def row_order():
    m = np.zeros((FH, FH), np.float32)
    for r in range(2):
        for par in range(2):
            for i in range(32):
                m[r * 64 + par * 32 + i, r * 64 + 2 * i + par] = 1
    return m


def vertical():
    v = {1: shrink_matrix(128), 2: shrink_matrix(64), 3: shrink_matrix(32)}
    spread = np.zeros((16, 8), np.float32)
    for r in range(2):
        for i in range(4):
            spread[r * 8 + i, r * 4 + i] = 1
    v[4] = spread @ shrink_matrix(16)
    g = {0: row_order() @ grow_matrix(64), 1: grow_matrix(32), 2: grow_matrix(16)}
    g[3] = grow_matrix(8) @ spread.T
    return v, g


def horizontal(width):
    s = {k: shrink_matrix(width >> (k - 1)).T for k in range(1, 5)}
    g = {k: grow_matrix(width >> (k + 1)).T for k in range(4)}
    return s, g


def shrink_window():
    m = np.zeros((512, 128), np.float32)
    for i in range(128):
        for d, tap in zip(range(-2, 3), (1, 4, 6, 4, 1)):
            m[128 + 2 * i + d, i] = tap / 16.0
    return m


def grow_window():
    m = np.zeros((384, 256), np.float32)
    for i in range(128):
        for d, tap in zip(range(-1, 2), (1, 6, 1)):
            m[128 + i + d, 2 * i] = tap / 8.0
        m[128 + i, 2 * i + 1] = m[128 + i + 1, 2 * i + 1] = 0.5
    return m


def pack(mats, width):
    places, row, col, height = {}, 0, 0, 0
    for name in sorted(mats, key=lambda n: (-mats[n].shape[0], -mats[n].shape[1], n)):
        h, w = mats[name].shape
        wide = -(-w // 128) * 128
        if col + wide > width:
            row, col, height = row + height, 0, 0
        height = max(height, -(-h // 16) * 16)
        places[name] = (row, col, h, w)
        col += wide
    out = np.zeros((row + height, width), np.float32)
    for name, (r, c, h, w) in places.items():
        out[r : r + h, c : c + w] = mats[name]
    return jnp.asarray(out, BF16), places


def unpack(ref, places):
    return {name: ref[r : r + h, c : c + w] for name, (r, c, h, w) in places.items()}


def small_matrices():
    v, g = vertical()
    s, gh = horizontal(WIN)
    sm, _ = horizontal(64)
    mats = {f"v{k}": m for k, m in v.items()} | {f"g{k}": m for k, m in g.items()}
    mats |= {f"s{k}": m for k, m in s.items()} | {f"h{k}": m for k, m in gh.items()}
    mats |= {f"m{k}": m for k, m in sm.items()} | {"order": row_order()}
    return pack(mats, 512)


def large_matrices():
    mats = {"shrink": shrink_window(), "grow": grow_window()}
    mats["last"] = padded(shrink_matrix(128).T, 128, 128)
    mats["least"] = padded(grow_matrix(64).T, 128, 128)
    return pack(mats, 640)


def levels_of(mats, letter):
    return {int(n[1:]): m for n, m in mats.items() if n[0] == letter and n[1:].isdigit()}


def mm(a, b):
    return jnp.dot(a, b, preferred_element_type=F32)


def split(v):
    hi = v.astype(BF16)
    return hi, (v - hi.astype(F32)).astype(BF16)


def rdot(v, m):
    hi, lo = split(v)
    return mm(hi, m) + mm(lo, m)


def ldot(m, v):
    hi, lo = split(v)
    return mm(m, hi) + mm(m, lo)


def mmt(a, b):
    return lax.dot_general(a, b, (((1,), (1,)), ((), ())), preferred_element_type=F32)


def windows(v, m, step):
    rows, width = v.shape
    both = jnp.concatenate(split(v), axis=0)
    left = jnp.broadcast_to(both[:, :1], (2 * rows, 128))
    right = jnp.broadcast_to(both[:, width - 1 :], (2 * rows, 128))
    both = jnp.concatenate([left, both, right], axis=1)
    pieces = []
    for n in range(width // step):
        piece = mm(both[:, n * step : n * step + step + 256], m)
        pieces.append(piece[:rows] + piece[rows:])
    return jnp.concatenate(pieces, axis=1)


def right_of(m):
    return lambda v: rdot(v, m)


def pyramid(planes, v, shrinks, product=mm):
    n = len(planes)
    t = jnp.concatenate([product(v[1], p) for p in planes], axis=0)
    levels = {1: shrinks[1](t)}
    for k in range(2, 5):
        prev = levels[k - 1]
        rows = prev.shape[0] // n
        t = jnp.concatenate([ldot(v[k], prev[i * rows : (i + 1) * rows]) for i in range(n)], axis=0)
        levels[k] = shrinks[k](t)
    return levels


def grown(level, n, gv, grow):
    h = grow(level)
    rows = level.shape[0] // n
    return [ldot(gv, h[i * rows : (i + 1) * rows]) for i in range(n)]


def place(rows, cols, base, width, offset):
    i = lax.broadcasted_iota(jnp.int32, (rows, cols), 0)
    c = lax.broadcasted_iota(jnp.int32, (rows, cols), 1)
    hit = (i >= base) & (i < base + width) & (c - i == offset - base)
    return jnp.where(hit, 1.0, 0.0).astype(BF16)


def strips_kernel(places, cell, xa, xb, packed, out, acc):
    mats = unpack(packed, places)
    v, gv, s, gh = (levels_of(mats, letter) for letter in "vgsh")
    s, gh = ({k: right_of(m) for k, m in each.items()} for each in (s, gh))
    order = mats["order"]
    first = window_tile(cell[0]) * 128
    planes = [jnp.concatenate([xa[0, c], xb[0, c]], axis=1) for c in range(COLOURS)]
    levels = pyramid(planes, v, s)
    back = grown(levels[1], COLOURS, gv[0], gh[0])
    b0 = jnp.concatenate([mm(order, planes[c]) - back[c] for c in range(COLOURS)], axis=0)
    bands = [b0.astype(BF16)]
    for k in range(1, 4):
        back = grown(levels[k + 1], COLOURS, gv[k], gh[k])
        bands.append((levels[k] - jnp.concatenate(back, axis=0)).astype(BF16))
    bands.append(levels[4].astype(BF16))
    start = cell[0] * 16 - first

    def pick(band, base, k):
        i = lax.broadcasted_iota(jnp.int32, (band.shape[1], 128), 0)
        c = lax.broadcasted_iota(jnp.int32, (band.shape[1], 128), 1)
        hit = (c >= base) & (c < base + (64 >> k)) & (i - c == (start >> k) - base)
        return mm(band, jnp.where(hit, 1.0, 0.0).astype(BF16))

    out[0:192, :] = (pick(bands[0][0:192], 0, 0) + pick(bands[0][192:384], 64, 0)).astype(BF16)
    acc[...] = pick(bands[1][0:96], 0, 1) + pick(bands[1][96:192], 32, 1) + pick(bands[2], 64, 2)
    acc[0:48, :] = acc[0:48, :] + pick(bands[3], 80, 3) + pick(bands[4], 88, 4)
    out[192:288, :] = acc[...].astype(BF16)


def window_tile(cell):
    return jnp.clip((cell - 3) >> 3, 0, (FW - WIN) // 128)


def full_spec(a):
    return pl.BlockSpec(a.shape, lambda *_: (0,) * a.ndim)


def strips_of(frames, cell):
    packed, places = small_matrices()
    grid_spec = pltpu.PrefetchScalarGridSpec(
        num_scalar_prefetch=1,
        grid=(1,),
        in_specs=[
            pl.BlockSpec((1, COLOURS, FH, 128), lambda i, c: (0, 0, 0, window_tile(c[0]))),
            pl.BlockSpec((1, COLOURS, FH, 128), lambda i, c: (0, 0, 0, window_tile(c[0]) + 1)),
        ]
        + [full_spec(packed)],
        out_specs=pl.BlockSpec((288, 128), lambda i, c: (0, 0)),
        scratch_shapes=[pltpu.VMEM((96, 128), F32)],
    )
    return pl.pallas_call(
        functools.partial(strips_kernel, places),
        grid_spec=grid_spec,
        out_shape=jax.ShapeDtypeStruct((288, 128), BF16),
        compiler_params=pltpu.CompilerParams(vmem_limit_bytes=VMEM),
        cost_estimate=pl.CostEstimate(flops=2 * 10**9, bytes_accessed=10**6, transcendentals=0),
        name="strips",
    )(cell, frames, frames, packed)


def lane_index():
    return lax.broadcasted_iota(jnp.int32, (1, 128), 1)


def fold_level0(p, store):
    left = lane_index() < 64
    for r in range(2):
        for j in range(8):
            even = p[r * 64 : r * 64 + 32, j * 128 : j * 128 + 128]
            odd = p[r * 64 + 32 : r * 64 + 64, j * 128 : j * 128 + 128]
            store(r * 16 + 2 * j, jnp.where(left, even, pltpu.roll(odd, 64, 1)))
            store(r * 16 + 2 * j + 1, jnp.where(left, pltpu.roll(even, 64, 1), odd))


def gather_channels(parts, width, cc, base):
    groups = 128 // width
    group = lane_index() // width
    out = jnp.zeros_like(parts[0])
    for ch in range(4):
        out = jnp.where(group == (cc + ch) % groups, parts[ch], out)
    return pltpu.roll(out, (base - cc * width) % 128, 1)


STATE_ROWS = 816


def state_views(state):
    at = lambda r, h, c, w: (slice(r, r + h), slice(c, c + w))
    b0 = [at(128 * c, 128, 0, 1024) for c in range(3)]
    l1 = [at(384, 64, 0, 512), at(384, 64, 512, 512), at(448, 64, 0, 512), at(448, 64, 512, 512)]
    l2 = [at(512, 32, 256 * c, 256) for c in range(4)]
    l3 = [at(544, 16, 128 * c, 128) for c in range(4)]
    l4 = [at(544, 16, 512 + 128 * c, 128) for c in range(4)]
    levels = [b0 + [at(560, 128, 0, 1024)], l1, l2, l3, l4]
    masks = [at(688, 128 >> k, 128 * k, 64 >> k) for k in range(4)] + [at(688, 16, 512, 4)]
    return levels, masks


def bands_kernel(small_places, large_places, x, w, m, small, large, wblocks, state):
    mats = unpack(small, small_places)
    v, gv, sm = (levels_of(mats, letter) for letter in "vgm")
    order = mats["order"]
    sm = {k: right_of(each) for k, each in sm.items()}
    mats = unpack(large, large_places)
    half = lambda each: windows(each, mats["shrink"], 256)
    twice = lambda each: windows(each, mats["grow"], 128)
    s = {1: half, 2: half, 3: half, 4: right_of(mats["last"])}
    gh = {0: twice, 1: twice, 2: twice, 3: right_of(mats["least"])}
    views, mask_views = state_views(state)
    planes = [x[0, c] for c in range(COLOURS)] + [w[0]]
    weights = mm(order, planes[3])
    state[views[0][3]] = weights

    def store(q, piece):
        wblocks[q] = piece.astype(BF16)

    fold_level0(weights, store)
    levels = pyramid(planes, v, s)
    for k in range(1, 5):
        rows = levels[k].shape[0] // 4
        state[views[k][3]] = levels[k][3 * rows :]
    back = grown(levels[1][: 3 * 64], COLOURS, gv[0], gh[0])
    for c in range(COLOURS):
        state[views[0][c]] = mm(order, planes[c]) - back[c]
    for k in range(1, 4):
        rows = levels[k].shape[0] // 4
        below = levels[k + 1].shape[0] // 4
        back = grown(levels[k + 1][: 3 * below], COLOURS, gv[k], gh[k])
        for c in range(COLOURS):
            state[views[k][c]] = levels[k][c * rows : (c + 1) * rows] - back[c]
    for c in range(COLOURS):
        state[views[4][c]] = levels[4][c * 16 : (c + 1) * 16]
    other = (1.0 - m[0].astype(F32)).astype(BF16)
    state[mask_views[0]] = mmt(order, other)
    masks = pyramid([other], v, sm, mmt)
    for k in range(1, 5):
        state[mask_views[k]] = masks[k]


def bands_of(frames, weight_map, seam_mask):
    small, small_places = small_matrices()
    large, large_places = large_matrices()
    return pl.pallas_call(
        functools.partial(bands_kernel, small_places, large_places),
        out_shape=[jax.ShapeDtypeStruct((QB, 32, 128), BF16), jax.ShapeDtypeStruct((STATE_ROWS, FW), F32)],
        compiler_params=pltpu.CompilerParams(vmem_limit_bytes=VMEM),
        cost_estimate=pl.CostEstimate(flops=8 * 10**9, bytes_accessed=6 * 10**6, transcendentals=0),
        name="bands",
    )(frames, weight_map, jnp.swapaxes(seam_mask, 1, 2), small, large)


def blend_kernel(cell, strips, state, first, second):
    views, mask_views = state_views(state)
    (b0, b1, b2, b3, b4) = [[state[view] for view in views[k][:3]] for k in range(5)]
    (wp, w1, w2, w3, w4) = [state[views[k][3]] for k in range(5)]
    (n0, n1, n2, n3, n4) = [state[view] for view in mask_views]
    start = cell[0] * 16
    low = strips[192:288]

    def mixed(band, remote, share):
        return band + share * (remote - band)

    widths = (1024, 512, 256, 128, 128)
    share0 = mm(n0.astype(BF16), place(64, 1024, 0, 64, start))
    share = [share0]
    for k, ref in enumerate((n1, n2, n3, n4)):
        share.append(rdot(ref, place(64 >> (k + 1), widths[k + 1], 0, 64 >> (k + 1), start >> (k + 1))))
    top = strips[0:192]
    remote0 = [mm(top, place(128, 1024, 0, 64, start)), mm(top, place(128, 1024, 64, 64, start))]
    remote0 = jnp.concatenate(remote0, axis=0)
    weights = wp
    for c in range(COLOURS):
        p = weights * mixed(b0[c], remote0[c * 128 : (c + 1) * 128], share[0])
        out, row = (first, 0) if c == 0 else (second, 32 * (c - 1))

        def store(q, piece, out=out, row=row):
            out[q, row : row + 32, :] = piece.astype(BF16)

        fold_level0(p, store)
    remote1 = [mm(low, place(128, 512, 0, 32, start >> 1)), mm(low, place(128, 512, 32, 32, start >> 1))]
    remote1 = jnp.concatenate(remote1, axis=0)
    parts = [w1 * mixed(b1[c], remote1[c * 64 : (c + 1) * 64], share[1]) for c in range(COLOURS)] + [w1]
    for r in range(2):
        for j in range(4):
            turned = [parts[ch][r * 32 : r * 32 + 32, j * 128 : j * 128 + 128] for ch in range(4)]
            turned = [turned[0]] + [pltpu.roll(turned[ch], 32 * ch, 1) for ch in range(1, 4)]
            for cc in range(4):
                first[r * 16 + 4 * j + cc, 32:64, :] = gather_channels(turned, 32, cc, 0).astype(BF16)
    remote2 = mm(low, place(128, 256, 64, 16, start >> 2))
    remote3 = mm(low[0:48], place(128, 128, 80, 8, start >> 3))
    remote4 = mm(low[0:48], place(128, 128, 88, 4, start >> 4))
    parts2 = [w2 * mixed(b2[c], remote2[c * 32 : (c + 1) * 32], share[2]) for c in range(COLOURS)] + [w2]
    parts3 = [w3 * mixed(b3[c], remote3[c * 16 : (c + 1) * 16], share[3]) for c in range(COLOURS)] + [w3]
    parts4 = [w4 * mixed(b4[c], remote4[c * 16 : (c + 1) * 16], share[4]) for c in range(COLOURS)] + [w4]
    lane = lane_index()
    for r in range(2):
        turned3 = [pltpu.roll(parts3[ch][r * 8 : r * 8 + 8], 8 * ch, 1) for ch in range(4)]
        turned4 = [pltpu.roll(parts4[ch][r * 8 : r * 8 + 8], 4 * ch, 1) for ch in range(4)]
        for j in range(2):
            turned2 = [parts2[ch][r * 16 : r * 16 + 16, j * 128 : j * 128 + 128] for ch in range(4)]
            turned2 = [pltpu.roll(turned2[ch], 16 * ch, 1) for ch in range(4)]
            for cc in range(8):
                c = j * 8 + cc
                two = gather_channels(turned2, 16, cc, 0)
                three = gather_channels(turned3, 8, c, 64)
                four = gather_channels(turned4, 4, c, 96)
                head = jnp.where(lane < 64, two[0:8], jnp.where(lane < 96, three, four))
                tail = jnp.where(lane < 64, two[8:16], 0.0)
                first[r * 16 + c, 64:80, :] = jnp.concatenate([head, tail], axis=0).astype(BF16)


def blend(cell, strips, state):
    vmem = pl.BlockSpec(memory_space=pltpu.VMEM)
    return pl.pallas_call(
        blend_kernel,
        in_specs=[pl.BlockSpec(memory_space=pltpu.SMEM)] + [vmem] * 2,
        out_shape=[jax.ShapeDtypeStruct((QB, 80, 128), BF16), jax.ShapeDtypeStruct((QB, 64, 128), BF16)],
        compiler_params=pltpu.CompilerParams(vmem_limit_bytes=VMEM),
        cost_estimate=pl.CostEstimate(flops=10**6, bytes_accessed=10**4, transcendentals=0),
        name="blend",
    )(cell, strips, state)


def routes_kernel(spot, lists, counts):
    for source in range(4):

        def body(q, count, source=source):
            at = spot[source, q]
            lists[source, count] = q * ROUTE + at
            return jnp.where(at >= 0, count + 1, count)

        counts[source] = lax.fori_loop(0, QB, body, 0, unroll=True)


def routes_of(spot):
    smem = pl.BlockSpec(memory_space=pltpu.SMEM)
    return pl.pallas_call(
        routes_kernel,
        in_specs=[smem],
        out_specs=[smem, smem],
        out_shape=[jax.ShapeDtypeStruct((4, QB + 1), jnp.int32), jax.ShapeDtypeStruct((4,), jnp.int32)],
        name="routes",
    )(spot)


def gather_kernel(lists, counts, *refs):
    home, away, acc = refs[-3:]
    acc[...] = jnp.zeros_like(acc)
    for source in range(4):

        def body(i, carry, source=source):
            entry = lists[source, i]
            q, at = entry // ROUTE, entry % ROUTE
            lo = 0
            for ref in refs[source:-3:4]:
                hi = lo + ref.shape[1]
                acc[at, lo:hi, :] = acc[at, lo:hi, :] + ref[q].astype(F32)
                lo = hi
            return carry

        lax.fori_loop(0, counts[source], body, 0)
    tiles = home.shape[0]
    home[...] = acc[0:tiles]
    away[...] = acc[tiles : 2 * tiles].astype(BF16)


def gather_rows(routes, rows, tiles):
    height = sum(each.shape[1] for each in rows[::4])
    vmem = pl.BlockSpec(memory_space=pltpu.VMEM)
    shape = (tiles // 2, height, 128)
    return pl.pallas_call(
        gather_kernel,
        in_specs=[pl.BlockSpec(memory_space=pltpu.SMEM)] * 2 + [vmem] * len(rows),
        out_shape=[jax.ShapeDtypeStruct(shape, F32), jax.ShapeDtypeStruct(shape, BF16)],
        scratch_shapes=[pltpu.VMEM((tiles, height, 128), F32)],
        compiler_params=pltpu.CompilerParams(vmem_limit_bytes=VMEM),
        cost_estimate=pl.CostEstimate(flops=10**6, bytes_accessed=10**4, transcendentals=0),
        name="gather_rows",
    )(*routes, *rows)


def add_kernel(pairs, *refs):
    out = refs[2 * pairs :]
    lo = 0
    for home, got in zip(refs[:pairs], refs[pairs : 2 * pairs]):
        hi = lo + home.shape[1]
        for j, ref in enumerate(out):
            tiles = slice(j * TILE_DEV, (j + 1) * TILE_DEV)
            ref[:, lo:hi, :] = (home[tiles] + got[tiles].astype(F32)).astype(ref.dtype)
        lo = hi


def add_halves(homes, gots):
    shape = (TILE_DEV, sum(home.shape[1] for home in homes), 128)
    others = homes[0].shape[0] // TILE_DEV - 1
    return pl.pallas_call(
        functools.partial(add_kernel, len(homes)),
        out_shape=[jax.ShapeDtypeStruct(shape, F32)] + [jax.ShapeDtypeStruct(shape, BF16)] * others,
        compiler_params=pltpu.CompilerParams(vmem_limit_bytes=VMEM),
        cost_estimate=pl.CostEstimate(flops=10**6, bytes_accessed=10**4, transcendentals=0),
        name="add_halves",
    )(*homes, *gots)


def collapse_matrices():
    def across(src, dst, width):
        g = grow_matrix(width).T
        m = np.zeros((128, 128), np.float32)
        for ch in range(COLOURS):
            m[src + ch * width : src + (ch + 1) * width, dst + ch * 2 * width : dst + (ch + 1) * 2 * width] = g
        return m

    last = np.zeros((128, 384), np.float32)
    g = grow_matrix(32).T
    for ch in range(COLOURS):
        for half in range(2):
            last[ch * 32 : ch * 32 + 32, ch * 128 + half * 64 : ch * 128 + half * 64 + 64] = g

    def down(n, rows_in, rows_out, pick=None):
        g = grow_matrix(n)
        g = g if pick is None else g[pick::2]
        m = np.zeros((TILE_DEV * rows_out, TILE_DEV * rows_in), np.float32)
        for t in range(TILE_DEV):
            m[t * rows_out : t * rows_out + g.shape[0], t * rows_in : t * rows_in + n] = g
        return m

    mats = {"m43": across(96, 64, 4), "m32": across(64, 0, 8), "m21": across(0, 0, 16), "m10": last}
    mats |= {"d43": down(4, 16, 16), "d32": down(8, 16, 16), "d21": down(16, 16, 32)}
    mats |= {"even": down(32, 32, 32, 0), "odd": down(32, 32, 32, 1)}
    return pack(mats, 1280)


def collapse_kernel(places, each, packed, *refs):
    mats = unpack(packed, places)
    b, c = (refs[i * each : (i + 1) * each] for i in range(2))
    out, level0 = refs[2 * each :]

    def total(sources, lo, hi):
        acc = sources[0][:, lo:hi, :]
        for source in sources[1:]:
            acc = acc + source[:, lo:hi, :].astype(F32)
        return acc.reshape(TILE_DEV * (hi - lo), 128)

    lane = lane_index()
    small = total(b, 64, 80)
    bottom = small
    for lo, width, chans in ((0, 16, 3), (64, 8, 3), (96, 4, 3)):
        for ch in range(chans):
            inside = (lane >= lo + ch * width) & (lane < lo + (ch + 1) * width)
            bottom = jnp.where(inside, pltpu.roll(small, (128 - (3 - ch) * width) % 128, 1), bottom)
    small = small / jnp.maximum(bottom, 1.0)
    three = small + ldot(mats["d43"], rdot(small, mats["m43"]))
    two = small + ldot(mats["d32"], rdot(three, mats["m32"]))
    one = total(b, 32, 64)
    bottom = one
    for ch in range(3):
        inside = (lane >= ch * 32) & (lane < (ch + 1) * 32)
        bottom = jnp.where(inside, pltpu.roll(one, (128 - (3 - ch) * 32) % 128, 1), bottom)
    one = one / jnp.maximum(bottom, 1.0) + ldot(mats["d21"], rdot(two, mats["m21"]))
    wide = rdot(one, mats["m10"])
    hi, lo = split(wide)
    up = mm(mats["even"], hi) + mm(mats["even"], lo)
    down = mm(mats["odd"], hi) + mm(mats["odd"], lo)
    bottom = jnp.maximum(total(c, 64, 96), 1.0)
    for ch in range(COLOURS):
        own = total(b, 0, 32) if ch == 0 else total(c, 32 * (ch - 1), 32 * ch)
        back = jnp.where(lane < 64, up[:, ch * 128 : ch * 128 + 128], down[:, ch * 128 : ch * 128 + 128])
        level0[ch * 128 : ch * 128 + 128, :] = own / bottom + back
    for ch in range(COLOURS):
        for row in range(32):
            out[ch, :, row * 128 : row * 128 + 128] = level0[pl.ds(ch * 128 + row, TILE_DEV, stride=32), :]


def collapse(b, c):
    packed, places = collapse_matrices()
    tiles = pl.pallas_call(
        functools.partial(collapse_kernel, places, len(b)),
        out_shape=jax.ShapeDtypeStruct((COLOURS, TILE_DEV, 4096), F32),
        scratch_shapes=[pltpu.VMEM((COLOURS * 128, 128), F32)],
        compiler_params=pltpu.CompilerParams(vmem_limit_bytes=VMEM),
        cost_estimate=pl.CostEstimate(flops=10**6, bytes_accessed=10**4, transcendentals=0),
        name="collapse",
    )(packed, *b, *c)
    return jnp.swapaxes(tiles, 0, 1)


def swap(value, axis, bit):
    size = lax.axis_size(axis)
    return lax.ppermute(value, axis, [(i, i ^ bit) for i in range(size)])


def local(frames, weight_map, seam_mask, strip_cell, partner, tile_group, tile_position_in_group):
    groups = lax.axis_size("frames")
    parts = lax.axis_size("tiles")
    mine = lax.axis_index("tiles")
    mask = lax.bitwise_xor(partner[0] // parts, lax.axis_index("frames"))

    tie = lax.optimization_barrier
    strips = strips_of(frames, strip_cell)
    ids = tile_group.reshape(QB) * (parts * TILE_DEV) + tile_position_in_group.reshape(QB)
    strips, frames, ids = tie((strips, frames, ids))
    ids = jnp.stack([ids, swap(ids, "tiles", 1)])
    ids_x = jnp.concatenate([ids, swap(ids, "tiles", 2)])
    ids_y = jnp.concatenate([ids, swap(ids, "frames", 1)])

    def relative(ids):
        group, tile = ids // (parts * TILE_DEV), ids % (parts * TILE_DEV)
        group = lax.bitwise_xor(group, lax.axis_index("frames"))
        return group, lax.bitwise_xor(tile // TILE_DEV, mine), tile % TILE_DEV

    half = groups // 2
    group, part, tile = relative(ids_x)
    spot_x = jnp.where(part == 0, ((group & 1) * half + (group >> 1)) * TILE_DEV + tile, -1)
    group, part, tile = relative(ids_y)
    here = ((group & 1) == 0) & ((part & 1) == 0)
    spot_y = jnp.where(here, ((part >> 1) * half + (group >> 1)) * TILE_DEV + tile, -1)

    weights, state = bands_of(frames, weight_map, seam_mask)
    bit = 1
    while bit < groups:
        got = swap(strips, "frames", bit)
        if bit == 1:
            got, weights, state = tie((got, weights, state))
            far, near = swap(weights, "tiles", 2), swap(weights, "tiles", 1)
        if bit == half:
            got, far, near, spot_x, spot_y = tie((got, far, near, spot_x, spot_y))
        strips = jnp.where((mask & bit) != 0, got, strips)
        bit *= 2

    def gather(routes, *rows):
        return gather_rows(routes, rows, groups * TILE_DEV)

    def along(own, *away):
        return [own] + [swap(part, "frames", 2 * (j + 1)) for j, part in enumerate(away)]

    first, second = blend(strip_cell, strips, state)
    first, second, spot_x, spot_y, far = tie((first, second, spot_x, spot_y, far))
    far_first, near_first = swap(first, "tiles", 2), swap(first, "tiles", 1)
    far_second, near_second = swap(second, "frames", 1), swap(second, "tiles", 1)
    routes_x, routes_y = routes_of(spot_x), routes_of(spot_y)
    home_w, away_w = gather(routes_x, weights, near, far, swap(far, "tiles", 1))
    got_w = swap(away_w, "frames", 1)
    far_second, home_w, routes_y = tie((far_second, home_w, routes_y))
    home_s, away_s = gather(routes_y, second, near_second, far_second, swap(far_second, "tiles", 1))
    got_s = swap(away_s, "tiles", 2)
    far_first, home_s, got_w = tie((far_first, home_s, got_w))
    far_near = swap(far_first, "tiles", 1)
    home_f, away_f = gather(routes_x, first, near_first, far_first, far_near)
    got_f = swap(away_f, "frames", 1)
    got_second = along(*add_halves((home_s, home_w), (got_s, got_w)))
    got_f, got_second[1] = tie((got_f, got_second[1]))
    got_first = along(*add_halves((home_f,), (got_f,)))
    return collapse(got_first, got_second)


def solution(mesh):
    in_specs = (
        P(("frames", "tiles"), None, None, None),
        P(("frames", "tiles"), None, None),
        P(("frames", "tiles"), None, None),
        P(("frames", "tiles")),
        P(("frames", "tiles")),
        P(("frames", "tiles"), None, None),
        P(("frames", "tiles"), None),
    )
    out_specs = P(("frames", "tiles"), None, None)
    return jax.shard_map(local, mesh=mesh, in_specs=in_specs, out_specs=out_specs, check_vma=False)
```

```python
import functools

import jax
import jax.numpy as jnp
import numpy as np
from jax import lax
from jax.experimental import pallas as pl
from jax.experimental.pallas import tpu as pltpu
from jax.sharding import PartitionSpec as P

COLOURS = 3
FH = 128
FW = 1024
QB = 32
WIN = 256
TILE_DEV = 4
VMEM = 20 << 20
ROUTE = 4096
F32 = jnp.float32
BF16 = jnp.bfloat16


def shrink_matrix(n):
    m = np.zeros((n // 2, n), np.float32)
    for i in range(n // 2):
        for d, tap in zip(range(-2, 3), (1, 4, 6, 4, 1)):
            m[i, min(max(2 * i + d, 0), n - 1)] += tap / 16.0
    return m


def grow_matrix(n):
    m = np.zeros((2 * n, n), np.float32)
    for i in range(n):
        lo, hi = max(i - 1, 0), min(i + 1, n - 1)
        m[2 * i, lo] += 1 / 8
        m[2 * i, i] += 6 / 8
        m[2 * i, hi] += 1 / 8
        m[2 * i + 1, i] += 1 / 2
        m[2 * i + 1, hi] += 1 / 2
    return m


def padded(m, rows, cols):
    return np.pad(m, ((0, rows - m.shape[0]), (0, cols - m.shape[1])))


def row_order():
    m = np.zeros((FH, FH), np.float32)
    for r in range(2):
        for par in range(2):
            for i in range(32):
                m[r * 64 + par * 32 + i, r * 64 + 2 * i + par] = 1
    return m


def vertical():
    v = {1: shrink_matrix(128), 2: shrink_matrix(64), 3: shrink_matrix(32)}
    spread = np.zeros((16, 8), np.float32)
    for r in range(2):
        for i in range(4):
            spread[r * 8 + i, r * 4 + i] = 1
    v[4] = spread @ shrink_matrix(16)
    g = {0: row_order() @ grow_matrix(64), 1: grow_matrix(32), 2: grow_matrix(16)}
    g[3] = grow_matrix(8) @ spread.T
    return v, g


def horizontal(width):
    s = {k: shrink_matrix(width >> (k - 1)).T for k in range(1, 5)}
    g = {k: grow_matrix(width >> (k + 1)).T for k in range(4)}
    return s, g


def shrink_window():
    m = np.zeros((512, 128), np.float32)
    for i in range(128):
        for d, tap in zip(range(-2, 3), (1, 4, 6, 4, 1)):
            m[128 + 2 * i + d, i] = tap / 16.0
    return m


def grow_window():
    m = np.zeros((384, 256), np.float32)
    for i in range(128):
        for d, tap in zip(range(-1, 2), (1, 6, 1)):
            m[128 + i + d, 2 * i] = tap / 8.0
        m[128 + i, 2 * i + 1] = m[128 + i + 1, 2 * i + 1] = 0.5
    return m


def pack(mats, width):
    places, row, col, height = {}, 0, 0, 0
    for name in sorted(mats, key=lambda n: (-mats[n].shape[0], -mats[n].shape[1], n)):
        h, w = mats[name].shape
        wide = -(-w // 128) * 128
        if col + wide > width:
            row, col, height = row + height, 0, 0
        height = max(height, -(-h // 16) * 16)
        places[name] = (row, col, h, w)
        col += wide
    out = np.zeros((row + height, width), np.float32)
    for name, (r, c, h, w) in places.items():
        out[r : r + h, c : c + w] = mats[name]
    return jnp.asarray(out, BF16), places


def unpack(ref, places):
    return {name: ref[r : r + h, c : c + w] for name, (r, c, h, w) in places.items()}


def small_matrices():
    v, g = vertical()
    s, gh = horizontal(WIN)
    sm, _ = horizontal(64)
    mats = {f"v{k}": m for k, m in v.items()} | {f"g{k}": m for k, m in g.items()}
    mats |= {f"s{k}": m for k, m in s.items()} | {f"h{k}": m for k, m in gh.items()}
    mats |= {f"m{k}": m for k, m in sm.items()} | {"order": row_order()}
    return pack(mats, 512)


def large_matrices():
    mats = {"shrink": shrink_window(), "grow": grow_window()}
    mats["last"] = padded(shrink_matrix(128).T, 128, 128)
    mats["least"] = padded(grow_matrix(64).T, 128, 128)
    return pack(mats, 640)


def levels_of(mats, letter):
    return {int(n[1:]): m for n, m in mats.items() if n[0] == letter and n[1:].isdigit()}


def mm(a, b):
    return jnp.dot(a, b, preferred_element_type=F32)


def split(v):
    hi = v.astype(BF16)
    return hi, (v - hi.astype(F32)).astype(BF16)


def rdot(v, m):
    hi, lo = split(v)
    return mm(hi, m) + mm(lo, m)


def ldot(m, v):
    hi, lo = split(v)
    return mm(m, hi) + mm(m, lo)


def mmt(a, b):
    return lax.dot_general(a, b, (((1,), (1,)), ((), ())), preferred_element_type=F32)


def windows(v, m, step):
    rows, width = v.shape
    both = jnp.concatenate(split(v), axis=0)
    left = jnp.broadcast_to(both[:, :1], (2 * rows, 128))
    right = jnp.broadcast_to(both[:, width - 1 :], (2 * rows, 128))
    both = jnp.concatenate([left, both, right], axis=1)
    pieces = []
    for n in range(width // step):
        piece = mm(both[:, n * step : n * step + step + 256], m)
        pieces.append(piece[:rows] + piece[rows:])
    return jnp.concatenate(pieces, axis=1)


def right_of(m):
    return lambda v: rdot(v, m)


def pyramid(planes, v, shrinks, product=mm):
    n = len(planes)
    t = jnp.concatenate([product(v[1], p) for p in planes], axis=0)
    levels = {1: shrinks[1](t)}
    for k in range(2, 5):
        prev = levels[k - 1]
        rows = prev.shape[0] // n
        t = jnp.concatenate([ldot(v[k], prev[i * rows : (i + 1) * rows]) for i in range(n)], axis=0)
        levels[k] = shrinks[k](t)
    return levels


def grown(level, n, gv, grow):
    h = grow(level)
    rows = level.shape[0] // n
    return [ldot(gv, h[i * rows : (i + 1) * rows]) for i in range(n)]


def place(rows, cols, base, width, offset):
    i = lax.broadcasted_iota(jnp.int32, (rows, cols), 0)
    c = lax.broadcasted_iota(jnp.int32, (rows, cols), 1)
    hit = (i >= base) & (i < base + width) & (c - i == offset - base)
    return jnp.where(hit, 1.0, 0.0).astype(BF16)


def strips_kernel(places, cell, xa, xb, packed, out, acc):
    mats = unpack(packed, places)
    v, gv, s, gh = (levels_of(mats, letter) for letter in "vgsh")
    s, gh = ({k: right_of(m) for k, m in each.items()} for each in (s, gh))
    order = mats["order"]
    first = window_tile(cell[0]) * 128
    planes = [jnp.concatenate([xa[0, c], xb[0, c]], axis=1) for c in range(COLOURS)]
    levels = pyramid(planes, v, s)
    back = grown(levels[1], COLOURS, gv[0], gh[0])
    b0 = jnp.concatenate([mm(order, planes[c]) - back[c] for c in range(COLOURS)], axis=0)
    bands = [b0.astype(BF16)]
    for k in range(1, 4):
        back = grown(levels[k + 1], COLOURS, gv[k], gh[k])
        bands.append((levels[k] - jnp.concatenate(back, axis=0)).astype(BF16))
    bands.append(levels[4].astype(BF16))
    start = cell[0] * 16 - first

    def pick(band, base, k):
        i = lax.broadcasted_iota(jnp.int32, (band.shape[1], 128), 0)
        c = lax.broadcasted_iota(jnp.int32, (band.shape[1], 128), 1)
        hit = (c >= base) & (c < base + (64 >> k)) & (i - c == (start >> k) - base)
        return mm(band, jnp.where(hit, 1.0, 0.0).astype(BF16))

    out[0:192, :] = (pick(bands[0][0:192], 0, 0) + pick(bands[0][192:384], 64, 0)).astype(BF16)
    acc[...] = pick(bands[1][0:96], 0, 1) + pick(bands[1][96:192], 32, 1) + pick(bands[2], 64, 2)
    acc[0:48, :] = acc[0:48, :] + pick(bands[3], 80, 3) + pick(bands[4], 88, 4)
    out[192:288, :] = acc[...].astype(BF16)


def window_tile(cell):
    return jnp.clip((cell - 3) >> 3, 0, (FW - WIN) // 128)


def full_spec(a):
    return pl.BlockSpec(a.shape, lambda *_: (0,) * a.ndim)


def strips_of(frames, cell):
    packed, places = small_matrices()
    grid_spec = pltpu.PrefetchScalarGridSpec(
        num_scalar_prefetch=1,
        grid=(1,),
        in_specs=[
            pl.BlockSpec((1, COLOURS, FH, 128), lambda i, c: (0, 0, 0, window_tile(c[0]))),
            pl.BlockSpec((1, COLOURS, FH, 128), lambda i, c: (0, 0, 0, window_tile(c[0]) + 1)),
        ]
        + [full_spec(packed)],
        out_specs=pl.BlockSpec((288, 128), lambda i, c: (0, 0)),
        scratch_shapes=[pltpu.VMEM((96, 128), F32)],
    )
    return pl.pallas_call(
        functools.partial(strips_kernel, places),
        grid_spec=grid_spec,
        out_shape=jax.ShapeDtypeStruct((288, 128), BF16),
        compiler_params=pltpu.CompilerParams(vmem_limit_bytes=VMEM),
        cost_estimate=pl.CostEstimate(flops=2 * 10**9, bytes_accessed=10**6, transcendentals=0),
        name="strips",
    )(cell, frames, frames, packed)


def lane_index():
    return lax.broadcasted_iota(jnp.int32, (1, 128), 1)


def fold_level0(p, store):
    left = lane_index() < 64
    for r in range(2):
        for j in range(8):
            even = p[r * 64 : r * 64 + 32, j * 128 : j * 128 + 128]
            odd = p[r * 64 + 32 : r * 64 + 64, j * 128 : j * 128 + 128]
            store(r * 16 + 2 * j, jnp.where(left, even, pltpu.roll(odd, 64, 1)))
            store(r * 16 + 2 * j + 1, jnp.where(left, pltpu.roll(even, 64, 1), odd))


def gather_channels(parts, width, cc, base):
    groups = 128 // width
    group = lane_index() // width
    out = jnp.zeros_like(parts[0])
    for ch in range(4):
        out = jnp.where(group == (cc + ch) % groups, parts[ch], out)
    return pltpu.roll(out, (base - cc * width) % 128, 1)


COLOUR_ROWS = 560
WEIGHT_ROWS = 320


def at(r, h, c, w):
    return slice(r, r + h), slice(c, c + w)


def colour_views():
    levels = [[at(128 * c, 128, 0, 1024) for c in range(3)]]
    levels.append([at(384, 64, 0, 512), at(384, 64, 512, 512), at(448, 64, 0, 512)])
    levels.append([at(512, 32, 256 * c, 256) for c in range(3)])
    levels.append([at(544, 16, 128 * c, 128) for c in range(3)])
    levels.append([at(544, 16, 512 + 128 * c, 128) for c in range(3)])
    return levels


def weight_views():
    levels = [at(0, 128, 0, 1024), at(128, 64, 0, 512), at(128, 32, 512, 256), at(128, 16, 768, 128), at(128, 16, 896, 128)]
    masks = [at(192, 128 >> k, 128 * k, 64 >> k) for k in range(4)] + [at(192, 16, 512, 4)]
    return levels, masks


def filters(small_places, large_places, small, large):
    mats = unpack(small, small_places)
    v, gv, sm = (levels_of(mats, letter) for letter in "vgm")
    order = mats["order"]
    sm = {k: right_of(each) for k, each in sm.items()}
    mats = unpack(large, large_places)
    half = lambda each: windows(each, mats["shrink"], 256)
    twice = lambda each: windows(each, mats["grow"], 128)
    s = {1: half, 2: half, 3: half, 4: right_of(mats["last"])}
    gh = {0: twice, 1: twice, 2: twice, 3: right_of(mats["least"])}
    return v, gv, sm, s, gh, order


def weights_kernel(small_places, large_places, w, m, small, large, wblocks, state):
    v, _, sm, s, _, order = filters(small_places, large_places, small, large)
    views, mask_views = weight_views()
    weights = mm(order, w[0])
    state[views[0]] = weights

    def store(q, piece):
        wblocks[q] = piece.astype(BF16)

    fold_level0(weights, store)
    levels = pyramid([w[0]], v, s)
    for k in range(1, 5):
        state[views[k]] = levels[k]
    other = (1.0 - m[0].astype(F32)).astype(BF16)
    state[mask_views[0]] = mmt(order, other)
    masks = pyramid([other], v, sm, mmt)
    for k in range(1, 5):
        state[mask_views[k]] = masks[k]


def colours_kernel(small_places, large_places, x, small, large, state):
    v, gv, _, s, gh, order = filters(small_places, large_places, small, large)
    views = colour_views()
    planes = [x[0, c] for c in range(COLOURS)]
    levels = pyramid(planes, v, s)
    back = grown(levels[1], COLOURS, gv[0], gh[0])
    for c in range(COLOURS):
        state[views[0][c]] = mm(order, planes[c]) - back[c]
    for k in range(1, 4):
        rows = levels[k].shape[0] // COLOURS
        back = grown(levels[k + 1], COLOURS, gv[k], gh[k])
        for c in range(COLOURS):
            state[views[k][c]] = levels[k][c * rows : (c + 1) * rows] - back[c]
    for c in range(COLOURS):
        state[views[4][c]] = levels[4][c * 16 : (c + 1) * 16]


def weights_of(weight_map, seam_mask):
    small, small_places = small_matrices()
    large, large_places = large_matrices()
    return pl.pallas_call(
        functools.partial(weights_kernel, small_places, large_places),
        out_shape=[jax.ShapeDtypeStruct((QB, 32, 128), BF16), jax.ShapeDtypeStruct((WEIGHT_ROWS, FW), F32)],
        compiler_params=pltpu.CompilerParams(vmem_limit_bytes=VMEM),
        cost_estimate=pl.CostEstimate(flops=4 * 10**9, bytes_accessed=2 * 10**6, transcendentals=0),
        name="weights",
    )(weight_map, jnp.swapaxes(seam_mask, 1, 2), small, large)


def colours_of(frames):
    small, small_places = small_matrices()
    large, large_places = large_matrices()
    return pl.pallas_call(
        functools.partial(colours_kernel, small_places, large_places),
        out_shape=jax.ShapeDtypeStruct((COLOUR_ROWS, FW), F32),
        compiler_params=pltpu.CompilerParams(vmem_limit_bytes=VMEM),
        cost_estimate=pl.CostEstimate(flops=6 * 10**9, bytes_accessed=4 * 10**6, transcendentals=0),
        name="colours",
    )(frames, small, large)


def blend_kernel(cell, strips, colours, masked, first, second):
    views, mask_views = weight_views()
    (b0, b1, b2, b3, b4) = [[colours[view] for view in level] for level in colour_views()]
    (wp, w1, w2, w3, w4) = [masked[view] for view in views]
    (n0, n1, n2, n3, n4) = [masked[view] for view in mask_views]
    start = cell[0] * 16
    low = strips[192:288]

    def mixed(band, remote, share):
        return band + share * (remote - band)

    widths = (1024, 512, 256, 128, 128)
    share0 = mm(n0.astype(BF16), place(64, 1024, 0, 64, start))
    share = [share0]
    for k, ref in enumerate((n1, n2, n3, n4)):
        share.append(rdot(ref, place(64 >> (k + 1), widths[k + 1], 0, 64 >> (k + 1), start >> (k + 1))))
    top = strips[0:192]
    remote0 = [mm(top, place(128, 1024, 0, 64, start)), mm(top, place(128, 1024, 64, 64, start))]
    remote0 = jnp.concatenate(remote0, axis=0)
    weights = wp
    for c in range(COLOURS):
        p = weights * mixed(b0[c], remote0[c * 128 : (c + 1) * 128], share[0])
        out, row = (first, 0) if c == 0 else (second, 32 * (c - 1))

        def store(q, piece, out=out, row=row):
            out[q, row : row + 32, :] = piece.astype(BF16)

        fold_level0(p, store)
    remote1 = [mm(low, place(128, 512, 0, 32, start >> 1)), mm(low, place(128, 512, 32, 32, start >> 1))]
    remote1 = jnp.concatenate(remote1, axis=0)
    parts = [w1 * mixed(b1[c], remote1[c * 64 : (c + 1) * 64], share[1]) for c in range(COLOURS)] + [w1]
    for r in range(2):
        for j in range(4):
            turned = [parts[ch][r * 32 : r * 32 + 32, j * 128 : j * 128 + 128] for ch in range(4)]
            turned = [turned[0]] + [pltpu.roll(turned[ch], 32 * ch, 1) for ch in range(1, 4)]
            for cc in range(4):
                first[r * 16 + 4 * j + cc, 32:64, :] = gather_channels(turned, 32, cc, 0).astype(BF16)
    remote2 = mm(low, place(128, 256, 64, 16, start >> 2))
    remote3 = mm(low[0:48], place(128, 128, 80, 8, start >> 3))
    remote4 = mm(low[0:48], place(128, 128, 88, 4, start >> 4))
    parts2 = [w2 * mixed(b2[c], remote2[c * 32 : (c + 1) * 32], share[2]) for c in range(COLOURS)] + [w2]
    parts3 = [w3 * mixed(b3[c], remote3[c * 16 : (c + 1) * 16], share[3]) for c in range(COLOURS)] + [w3]
    parts4 = [w4 * mixed(b4[c], remote4[c * 16 : (c + 1) * 16], share[4]) for c in range(COLOURS)] + [w4]
    lane = lane_index()
    for r in range(2):
        turned3 = [pltpu.roll(parts3[ch][r * 8 : r * 8 + 8], 8 * ch, 1) for ch in range(4)]
        turned4 = [pltpu.roll(parts4[ch][r * 8 : r * 8 + 8], 4 * ch, 1) for ch in range(4)]
        for j in range(2):
            turned2 = [parts2[ch][r * 16 : r * 16 + 16, j * 128 : j * 128 + 128] for ch in range(4)]
            turned2 = [pltpu.roll(turned2[ch], 16 * ch, 1) for ch in range(4)]
            for cc in range(8):
                c = j * 8 + cc
                two = gather_channels(turned2, 16, cc, 0)
                three = gather_channels(turned3, 8, c, 64)
                four = gather_channels(turned4, 4, c, 96)
                head = jnp.where(lane < 64, two[0:8], jnp.where(lane < 96, three, four))
                tail = jnp.where(lane < 64, two[8:16], 0.0)
                first[r * 16 + c, 64:80, :] = jnp.concatenate([head, tail], axis=0).astype(BF16)


def blend(cell, strips, colours, masked):
    vmem = pl.BlockSpec(memory_space=pltpu.VMEM)
    return pl.pallas_call(
        blend_kernel,
        in_specs=[pl.BlockSpec(memory_space=pltpu.SMEM)] + [vmem] * 3,
        out_shape=[jax.ShapeDtypeStruct((QB, 80, 128), BF16), jax.ShapeDtypeStruct((QB, 64, 128), BF16)],
        compiler_params=pltpu.CompilerParams(vmem_limit_bytes=VMEM),
        cost_estimate=pl.CostEstimate(flops=10**6, bytes_accessed=10**4, transcendentals=0),
        name="blend",
    )(cell, strips, colours, masked)


def routes_kernel(spot, lists, counts):
    for source in range(4):

        def body(q, count, source=source):
            at = spot[source, q]
            lists[source, count] = q * ROUTE + at
            return jnp.where(at >= 0, count + 1, count)

        counts[source] = lax.fori_loop(0, QB, body, 0, unroll=True)


def routes_of(spot):
    smem = pl.BlockSpec(memory_space=pltpu.SMEM)
    return pl.pallas_call(
        routes_kernel,
        in_specs=[smem],
        out_specs=[smem, smem],
        out_shape=[jax.ShapeDtypeStruct((4, QB + 1), jnp.int32), jax.ShapeDtypeStruct((4,), jnp.int32)],
        name="routes",
    )(spot)


def gather_kernel(lists, counts, *refs):
    home, away, acc = refs[-3:]
    acc[...] = jnp.zeros_like(acc)
    for source in range(4):

        def body(i, carry, source=source):
            entry = lists[source, i]
            q, at = entry // ROUTE, entry % ROUTE
            lo = 0
            for ref in refs[source:-3:4]:
                hi = lo + ref.shape[1]
                acc[at, lo:hi, :] = acc[at, lo:hi, :] + ref[q].astype(F32)
                lo = hi
            return carry

        lax.fori_loop(0, counts[source], body, 0)
    tiles = home.shape[0]
    home[...] = acc[0:tiles]
    away[...] = acc[tiles : 2 * tiles].astype(BF16)


def gather_rows(routes, rows, tiles):
    height = sum(each.shape[1] for each in rows[::4])
    vmem = pl.BlockSpec(memory_space=pltpu.VMEM)
    shape = (tiles // 2, height, 128)
    return pl.pallas_call(
        gather_kernel,
        in_specs=[pl.BlockSpec(memory_space=pltpu.SMEM)] * 2 + [vmem] * len(rows),
        out_shape=[jax.ShapeDtypeStruct(shape, F32), jax.ShapeDtypeStruct(shape, BF16)],
        scratch_shapes=[pltpu.VMEM((tiles, height, 128), F32)],
        compiler_params=pltpu.CompilerParams(vmem_limit_bytes=VMEM),
        cost_estimate=pl.CostEstimate(flops=10**6, bytes_accessed=10**4, transcendentals=0),
        name="gather_rows",
    )(*routes, *rows)


def add_kernel(pairs, *refs):
    out = refs[2 * pairs :]
    lo = 0
    for home, got in zip(refs[:pairs], refs[pairs : 2 * pairs]):
        hi = lo + home.shape[1]
        for j, ref in enumerate(out):
            tiles = slice(j * TILE_DEV, (j + 1) * TILE_DEV)
            ref[:, lo:hi, :] = (home[tiles] + got[tiles].astype(F32)).astype(ref.dtype)
        lo = hi


def add_halves(homes, gots):
    shape = (TILE_DEV, sum(home.shape[1] for home in homes), 128)
    others = homes[0].shape[0] // TILE_DEV - 1
    return pl.pallas_call(
        functools.partial(add_kernel, len(homes)),
        out_shape=[jax.ShapeDtypeStruct(shape, F32)] + [jax.ShapeDtypeStruct(shape, BF16)] * others,
        compiler_params=pltpu.CompilerParams(vmem_limit_bytes=VMEM),
        cost_estimate=pl.CostEstimate(flops=10**6, bytes_accessed=10**4, transcendentals=0),
        name="add_halves",
    )(*homes, *gots)


def collapse_matrices():
    def across(src, dst, width):
        g = grow_matrix(width).T
        m = np.zeros((128, 128), np.float32)
        for ch in range(COLOURS):
            m[src + ch * width : src + (ch + 1) * width, dst + ch * 2 * width : dst + (ch + 1) * 2 * width] = g
        return m

    last = np.zeros((128, 384), np.float32)
    g = grow_matrix(32).T
    for ch in range(COLOURS):
        for half in range(2):
            last[ch * 32 : ch * 32 + 32, ch * 128 + half * 64 : ch * 128 + half * 64 + 64] = g

    def down(n, rows_in, rows_out, pick=None):
        g = grow_matrix(n)
        g = g if pick is None else g[pick::2]
        m = np.zeros((TILE_DEV * rows_out, TILE_DEV * rows_in), np.float32)
        for t in range(TILE_DEV):
            m[t * rows_out : t * rows_out + g.shape[0], t * rows_in : t * rows_in + n] = g
        return m

    mats = {"m43": across(96, 64, 4), "m32": across(64, 0, 8), "m21": across(0, 0, 16), "m10": last}
    mats |= {"d43": down(4, 16, 16), "d32": down(8, 16, 16), "d21": down(16, 16, 32)}
    mats |= {"even": down(32, 32, 32, 0), "odd": down(32, 32, 32, 1)}
    return pack(mats, 1280)


def collapse_kernel(places, each, packed, *refs):
    mats = unpack(packed, places)
    b, c = (refs[i * each : (i + 1) * each] for i in range(2))
    out, level0 = refs[2 * each :]

    def total(sources, lo, hi):
        acc = sources[0][:, lo:hi, :]
        for source in sources[1:]:
            acc = acc + source[:, lo:hi, :].astype(F32)
        return acc.reshape(TILE_DEV * (hi - lo), 128)

    lane = lane_index()
    small = total(b, 64, 80)
    bottom = small
    for lo, width, chans in ((0, 16, 3), (64, 8, 3), (96, 4, 3)):
        for ch in range(chans):
            inside = (lane >= lo + ch * width) & (lane < lo + (ch + 1) * width)
            bottom = jnp.where(inside, pltpu.roll(small, (128 - (3 - ch) * width) % 128, 1), bottom)
    small = small / jnp.maximum(bottom, 1.0)
    three = small + ldot(mats["d43"], rdot(small, mats["m43"]))
    two = small + ldot(mats["d32"], rdot(three, mats["m32"]))
    one = total(b, 32, 64)
    bottom = one
    for ch in range(3):
        inside = (lane >= ch * 32) & (lane < (ch + 1) * 32)
        bottom = jnp.where(inside, pltpu.roll(one, (128 - (3 - ch) * 32) % 128, 1), bottom)
    one = one / jnp.maximum(bottom, 1.0) + ldot(mats["d21"], rdot(two, mats["m21"]))
    wide = rdot(one, mats["m10"])
    hi, lo = split(wide)
    up = mm(mats["even"], hi) + mm(mats["even"], lo)
    down = mm(mats["odd"], hi) + mm(mats["odd"], lo)
    bottom = jnp.maximum(total(c, 64, 96), 1.0)
    for ch in range(COLOURS):
        own = total(b, 0, 32) if ch == 0 else total(c, 32 * (ch - 1), 32 * ch)
        back = jnp.where(lane < 64, up[:, ch * 128 : ch * 128 + 128], down[:, ch * 128 : ch * 128 + 128])
        level0[ch * 128 : ch * 128 + 128, :] = own / bottom + back
    for ch in range(COLOURS):
        for row in range(32):
            out[ch, :, row * 128 : row * 128 + 128] = level0[pl.ds(ch * 128 + row, TILE_DEV, stride=32), :]


def collapse(b, c):
    packed, places = collapse_matrices()
    tiles = pl.pallas_call(
        functools.partial(collapse_kernel, places, len(b)),
        out_shape=jax.ShapeDtypeStruct((COLOURS, TILE_DEV, 4096), F32),
        scratch_shapes=[pltpu.VMEM((COLOURS * 128, 128), F32)],
        compiler_params=pltpu.CompilerParams(vmem_limit_bytes=VMEM),
        cost_estimate=pl.CostEstimate(flops=10**6, bytes_accessed=10**4, transcendentals=0),
        name="collapse",
    )(packed, *b, *c)
    return jnp.swapaxes(tiles, 0, 1)


def swap(value, axis, bit):
    size = lax.axis_size(axis)
    return lax.ppermute(value, axis, [(i, i ^ bit) for i in range(size)])


def local(frames, weight_map, seam_mask, strip_cell, partner, tile_group, tile_position_in_group):
    groups = lax.axis_size("frames")
    parts = lax.axis_size("tiles")
    mine = lax.axis_index("tiles")
    mask = lax.bitwise_xor(partner[0] // parts, lax.axis_index("frames"))

    tie = lax.optimization_barrier
    strips = strips_of(frames, strip_cell)
    ids = tile_group.reshape(QB) * (parts * TILE_DEV) + tile_position_in_group.reshape(QB)
    strips, weight_map, ids = tie((strips, weight_map, ids))
    ids = jnp.stack([ids, swap(ids, "tiles", 1)])
    ids_x = jnp.concatenate([ids, swap(ids, "tiles", 2)])
    ids_y = jnp.concatenate([ids, swap(ids, "frames", 1)])

    def relative(ids):
        group, tile = ids // (parts * TILE_DEV), ids % (parts * TILE_DEV)
        group = lax.bitwise_xor(group, lax.axis_index("frames"))
        return group, lax.bitwise_xor(tile // TILE_DEV, mine), tile % TILE_DEV

    half = groups // 2
    group, part, tile = relative(ids_x)
    spot_x = jnp.where(part == 0, ((group & 1) * half + (group >> 1)) * TILE_DEV + tile, -1)
    group, part, tile = relative(ids_y)
    here = ((group & 1) == 0) & ((part & 1) == 0)
    spot_y = jnp.where(here, ((part >> 1) * half + (group >> 1)) * TILE_DEV + tile, -1)

    weights, masked = weights_of(weight_map, seam_mask)
    bit = 1
    while bit < groups:
        got = swap(strips, "frames", bit)
        if bit == 1:
            got, weights, masked = tie((got, weights, masked))
            far, near = swap(weights, "tiles", 2), swap(weights, "tiles", 1)
        if bit == half // 2:
            got, frames = tie((got, frames))
        if bit == half:
            colours = colours_of(frames)
            got, far, near, spot_x, spot_y, colours = tie((got, far, near, spot_x, spot_y, colours))
        strips = jnp.where((mask & bit) != 0, got, strips)
        bit *= 2

    def gather(routes, *rows):
        return gather_rows(routes, rows, groups * TILE_DEV)

    def along(own, *away):
        return [own] + [swap(part, "frames", 2 * (j + 1)) for j, part in enumerate(away)]

    first, second = blend(strip_cell, strips, colours, masked)
    first, second, spot_x, spot_y, far = tie((first, second, spot_x, spot_y, far))
    far_first, near_first = swap(first, "tiles", 2), swap(first, "tiles", 1)
    far_second, near_second = swap(second, "frames", 1), swap(second, "tiles", 1)
    routes_x, routes_y = routes_of(spot_x), routes_of(spot_y)
    home_w, away_w = gather(routes_x, weights, near, far, swap(far, "tiles", 1))
    got_w = swap(away_w, "frames", 1)
    far_second, home_w, routes_y = tie((far_second, home_w, routes_y))
    home_s, away_s = gather(routes_y, second, near_second, far_second, swap(far_second, "tiles", 1))
    got_s = swap(away_s, "tiles", 2)
    far_first, home_s, got_w = tie((far_first, home_s, got_w))
    far_near = swap(far_first, "tiles", 1)
    home_f, away_f = gather(routes_x, first, near_first, far_first, far_near)
    got_f = swap(away_f, "frames", 1)
    got_second = along(*add_halves((home_s, home_w), (got_s, got_w)))
    got_f, got_second[1] = tie((got_f, got_second[1]))
    got_first = along(*add_halves((home_f,), (got_f,)))
    return collapse(got_first, got_second)


def solution(mesh):
    in_specs = (
        P(("frames", "tiles"), None, None, None),
        P(("frames", "tiles"), None, None),
        P(("frames", "tiles"), None, None),
        P(("frames", "tiles")),
        P(("frames", "tiles")),
        P(("frames", "tiles"), None, None),
        P(("frames", "tiles"), None),
    )
    out_specs = P(("frames", "tiles"), None, None)
    return jax.shard_map(local, mesh=mesh, in_specs=in_specs, out_specs=out_specs, check_vma=False)
```

```python
import functools

import jax
import jax.numpy as jnp
import numpy as np
from jax import lax
from jax.experimental import pallas as pl
from jax.experimental.pallas import tpu as pltpu
from jax.sharding import PartitionSpec as P

COLOURS = 3
FH = 128
FW = 1024
QB = 32
WIN = 256
TILE_DEV = 4
VMEM = 20 << 20
ROUTE = 4096
F32 = jnp.float32
BF16 = jnp.bfloat16


def shrink_matrix(n):
    m = np.zeros((n // 2, n), np.float32)
    for i in range(n // 2):
        for d, tap in zip(range(-2, 3), (1, 4, 6, 4, 1)):
            m[i, min(max(2 * i + d, 0), n - 1)] += tap / 16.0
    return m


def grow_matrix(n):
    m = np.zeros((2 * n, n), np.float32)
    for i in range(n):
        lo, hi = max(i - 1, 0), min(i + 1, n - 1)
        m[2 * i, lo] += 1 / 8
        m[2 * i, i] += 6 / 8
        m[2 * i, hi] += 1 / 8
        m[2 * i + 1, i] += 1 / 2
        m[2 * i + 1, hi] += 1 / 2
    return m


def padded(m, rows, cols):
    return np.pad(m, ((0, rows - m.shape[0]), (0, cols - m.shape[1])))


def row_order():
    m = np.zeros((FH, FH), np.float32)
    for r in range(2):
        for par in range(2):
            for i in range(32):
                m[r * 64 + par * 32 + i, r * 64 + 2 * i + par] = 1
    return m


def vertical():
    v = {1: shrink_matrix(128), 2: shrink_matrix(64), 3: shrink_matrix(32)}
    spread = np.zeros((16, 8), np.float32)
    for r in range(2):
        for i in range(4):
            spread[r * 8 + i, r * 4 + i] = 1
    v[4] = spread @ shrink_matrix(16)
    g = {0: row_order() @ grow_matrix(64), 1: grow_matrix(32), 2: grow_matrix(16)}
    g[3] = grow_matrix(8) @ spread.T
    return v, g


def horizontal(width):
    s = {k: shrink_matrix(width >> (k - 1)).T for k in range(1, 5)}
    g = {k: grow_matrix(width >> (k + 1)).T for k in range(4)}
    return s, g


def shrink_window():
    m = np.zeros((512, 128), np.float32)
    for i in range(128):
        for d, tap in zip(range(-2, 3), (1, 4, 6, 4, 1)):
            m[128 + 2 * i + d, i] = tap / 16.0
    return m


def grow_window():
    m = np.zeros((384, 256), np.float32)
    for i in range(128):
        for d, tap in zip(range(-1, 2), (1, 6, 1)):
            m[128 + i + d, 2 * i] = tap / 8.0
        m[128 + i, 2 * i + 1] = m[128 + i + 1, 2 * i + 1] = 0.5
    return m


def pack(mats, width):
    places, row, col, height = {}, 0, 0, 0
    for name in sorted(mats, key=lambda n: (-mats[n].shape[0], -mats[n].shape[1], n)):
        h, w = mats[name].shape
        wide = -(-w // 128) * 128
        if col + wide > width:
            row, col, height = row + height, 0, 0
        height = max(height, -(-h // 16) * 16)
        places[name] = (row, col, h, w)
        col += wide
    out = np.zeros((row + height, width), np.float32)
    for name, (r, c, h, w) in places.items():
        out[r : r + h, c : c + w] = mats[name]
    return jnp.asarray(out, BF16), places


def unpack(ref, places):
    return {name: ref[r : r + h, c : c + w] for name, (r, c, h, w) in places.items()}


def small_matrices():
    v, g = vertical()
    s, gh = horizontal(WIN)
    sm, _ = horizontal(64)
    mats = {f"v{k}": m for k, m in v.items()} | {f"g{k}": m for k, m in g.items()}
    mats |= {f"s{k}": m for k, m in s.items()} | {f"h{k}": m for k, m in gh.items()}
    mats |= {f"m{k}": m for k, m in sm.items()} | {"order": row_order()}
    return pack(mats, 512)


def large_matrices():
    mats = {"shrink": shrink_window(), "grow": grow_window()}
    mats["last"] = padded(shrink_matrix(128).T, 128, 128)
    mats["least"] = padded(grow_matrix(64).T, 128, 128)
    return pack(mats, 640)


def levels_of(mats, letter):
    return {int(n[1:]): m for n, m in mats.items() if n[0] == letter and n[1:].isdigit()}


def mm(a, b):
    return jnp.dot(a, b, preferred_element_type=F32)


def split(v):
    hi = v.astype(BF16)
    return hi, (v - hi.astype(F32)).astype(BF16)


def rdot(v, m):
    hi, lo = split(v)
    return mm(hi, m) + mm(lo, m)


def ldot(m, v):
    hi, lo = split(v)
    return mm(m, hi) + mm(m, lo)


def mmt(a, b):
    return lax.dot_general(a, b, (((1,), (1,)), ((), ())), preferred_element_type=F32)


def windows(v, m, step):
    rows, width = v.shape
    both = jnp.concatenate(split(v), axis=0)
    left = jnp.broadcast_to(both[:, :1], (2 * rows, 128))
    right = jnp.broadcast_to(both[:, width - 1 :], (2 * rows, 128))
    both = jnp.concatenate([left, both, right], axis=1)
    pieces = []
    for n in range(width // step):
        piece = mm(both[:, n * step : n * step + step + 256], m)
        pieces.append(piece[:rows] + piece[rows:])
    return jnp.concatenate(pieces, axis=1)


def right_of(m):
    return lambda v: rdot(v, m)


def pyramid(planes, v, shrinks, product=mm):
    n = len(planes)
    t = jnp.concatenate([product(v[1], p) for p in planes], axis=0)
    levels = {1: shrinks[1](t)}
    for k in range(2, 5):
        prev = levels[k - 1]
        rows = prev.shape[0] // n
        t = jnp.concatenate([ldot(v[k], prev[i * rows : (i + 1) * rows]) for i in range(n)], axis=0)
        levels[k] = shrinks[k](t)
    return levels


def grown(level, n, gv, grow):
    h = grow(level)
    rows = level.shape[0] // n
    return [ldot(gv, h[i * rows : (i + 1) * rows]) for i in range(n)]


def place(rows, cols, base, width, offset):
    i = lax.broadcasted_iota(jnp.int32, (rows, cols), 0)
    c = lax.broadcasted_iota(jnp.int32, (rows, cols), 1)
    hit = (i >= base) & (i < base + width) & (c - i == offset - base)
    return jnp.where(hit, 1.0, 0.0).astype(BF16)


def strips_kernel(places, cell, xa, xb, packed, out, acc):
    mats = unpack(packed, places)
    v, gv, s, gh = (levels_of(mats, letter) for letter in "vgsh")
    s, gh = ({k: right_of(m) for k, m in each.items()} for each in (s, gh))
    order = mats["order"]
    first = window_tile(cell[0]) * 128
    planes = [jnp.concatenate([xa[0, c], xb[0, c]], axis=1) for c in range(COLOURS)]
    levels = pyramid(planes, v, s)
    back = grown(levels[1], COLOURS, gv[0], gh[0])
    b0 = jnp.concatenate([mm(order, planes[c]) - back[c] for c in range(COLOURS)], axis=0)
    bands = [b0.astype(BF16)]
    for k in range(1, 4):
        back = grown(levels[k + 1], COLOURS, gv[k], gh[k])
        bands.append((levels[k] - jnp.concatenate(back, axis=0)).astype(BF16))
    bands.append(levels[4].astype(BF16))
    start = cell[0] * 16 - first

    def pick(band, base, k):
        i = lax.broadcasted_iota(jnp.int32, (band.shape[1], 128), 0)
        c = lax.broadcasted_iota(jnp.int32, (band.shape[1], 128), 1)
        hit = (c >= base) & (c < base + (64 >> k)) & (i - c == (start >> k) - base)
        return mm(band, jnp.where(hit, 1.0, 0.0).astype(BF16))

    out[0:192, :] = (pick(bands[0][0:192], 0, 0) + pick(bands[0][192:384], 64, 0)).astype(BF16)
    acc[...] = pick(bands[1][0:96], 0, 1) + pick(bands[1][96:192], 32, 1) + pick(bands[2], 64, 2)
    acc[0:48, :] = acc[0:48, :] + pick(bands[3], 80, 3) + pick(bands[4], 88, 4)
    out[192:288, :] = acc[...].astype(BF16)


def window_tile(cell):
    return jnp.clip((cell - 3) >> 3, 0, (FW - WIN) // 128)


def full_spec(a):
    return pl.BlockSpec(a.shape, lambda *_: (0,) * a.ndim)


def strips_of(frames, cell):
    packed, places = small_matrices()
    grid_spec = pltpu.PrefetchScalarGridSpec(
        num_scalar_prefetch=1,
        grid=(1,),
        in_specs=[
            pl.BlockSpec((1, COLOURS, FH, 128), lambda i, c: (0, 0, 0, window_tile(c[0]))),
            pl.BlockSpec((1, COLOURS, FH, 128), lambda i, c: (0, 0, 0, window_tile(c[0]) + 1)),
        ]
        + [full_spec(packed)],
        out_specs=pl.BlockSpec((288, 128), lambda i, c: (0, 0)),
        scratch_shapes=[pltpu.VMEM((96, 128), F32)],
    )
    return pl.pallas_call(
        functools.partial(strips_kernel, places),
        grid_spec=grid_spec,
        out_shape=jax.ShapeDtypeStruct((288, 128), BF16),
        compiler_params=pltpu.CompilerParams(vmem_limit_bytes=VMEM),
        cost_estimate=pl.CostEstimate(flops=2 * 10**9, bytes_accessed=10**6, transcendentals=0),
        name="strips",
    )(cell, frames, frames, packed)


def lane_index():
    return lax.broadcasted_iota(jnp.int32, (1, 128), 1)


def fold_level0(p, store):
    left = lane_index() < 64
    for r in range(2):
        for j in range(8):
            even = p[r * 64 : r * 64 + 32, j * 128 : j * 128 + 128]
            odd = p[r * 64 + 32 : r * 64 + 64, j * 128 : j * 128 + 128]
            store(r * 16 + 2 * j, jnp.where(left, even, pltpu.roll(odd, 64, 1)))
            store(r * 16 + 2 * j + 1, jnp.where(left, pltpu.roll(even, 64, 1), odd))


def gather_channels(parts, width, cc, base):
    groups = 128 // width
    group = lane_index() // width
    out = jnp.zeros_like(parts[0])
    for ch in range(4):
        out = jnp.where(group == (cc + ch) % groups, parts[ch], out)
    return pltpu.roll(out, (base - cc * width) % 128, 1)


COLOUR_ROWS = 560
WEIGHT_ROWS = 320


def at(r, h, c, w):
    return slice(r, r + h), slice(c, c + w)


def colour_views():
    levels = [[at(128 * c, 128, 0, 1024) for c in range(3)]]
    levels.append([at(384, 64, 0, 512), at(384, 64, 512, 512), at(448, 64, 0, 512)])
    levels.append([at(512, 32, 256 * c, 256) for c in range(3)])
    levels.append([at(544, 16, 128 * c, 128) for c in range(3)])
    levels.append([at(544, 16, 512 + 128 * c, 128) for c in range(3)])
    return levels


def weight_views():
    levels = [at(0, 128, 0, 1024), at(128, 64, 0, 512), at(128, 32, 512, 256), at(128, 16, 768, 128), at(128, 16, 896, 128)]
    masks = [at(192, 128 >> k, 128 * k, 64 >> k) for k in range(4)] + [at(192, 16, 512, 4)]
    return levels, masks


def filters(small_places, large_places, small, large):
    mats = unpack(small, small_places)
    v, gv, sm = (levels_of(mats, letter) for letter in "vgm")
    order = mats["order"]
    sm = {k: right_of(each) for k, each in sm.items()}
    mats = unpack(large, large_places)
    half = lambda each: windows(each, mats["shrink"], 256)
    twice = lambda each: windows(each, mats["grow"], 128)
    s = {1: half, 2: half, 3: half, 4: right_of(mats["last"])}
    gh = {0: twice, 1: twice, 2: twice, 3: right_of(mats["least"])}
    return v, gv, sm, s, gh, order


def weights_kernel(small_places, large_places, w, m, small, large, wblocks, state):
    v, _, sm, s, _, order = filters(small_places, large_places, small, large)
    views, mask_views = weight_views()
    weights = mm(order, w[0])
    state[views[0]] = weights

    def store(q, piece):
        wblocks[q] = piece.astype(BF16)

    fold_level0(weights, store)
    levels = pyramid([w[0]], v, s)
    for k in range(1, 5):
        state[views[k]] = levels[k]
    other = (1.0 - m[0].astype(F32)).astype(BF16)
    state[mask_views[0]] = mmt(order, other)
    masks = pyramid([other], v, sm, mmt)
    for k in range(1, 5):
        state[mask_views[k]] = masks[k]


def colours_kernel(small_places, large_places, x, small, large, state):
    v, gv, _, s, gh, order = filters(small_places, large_places, small, large)
    views = colour_views()
    planes = [x[0, c] for c in range(COLOURS)]
    levels = pyramid(planes, v, s)
    back = grown(levels[1], COLOURS, gv[0], gh[0])
    for c in range(COLOURS):
        state[views[0][c]] = mm(order, planes[c]) - back[c]
    for k in range(1, 4):
        rows = levels[k].shape[0] // COLOURS
        back = grown(levels[k + 1], COLOURS, gv[k], gh[k])
        for c in range(COLOURS):
            state[views[k][c]] = levels[k][c * rows : (c + 1) * rows] - back[c]
    for c in range(COLOURS):
        state[views[4][c]] = levels[4][c * 16 : (c + 1) * 16]


def weights_of(weight_map, seam_mask):
    small, small_places = small_matrices()
    large, large_places = large_matrices()
    return pl.pallas_call(
        functools.partial(weights_kernel, small_places, large_places),
        out_shape=[jax.ShapeDtypeStruct((QB, 32, 128), BF16), jax.ShapeDtypeStruct((WEIGHT_ROWS, FW), F32)],
        compiler_params=pltpu.CompilerParams(vmem_limit_bytes=VMEM),
        cost_estimate=pl.CostEstimate(flops=4 * 10**9, bytes_accessed=2 * 10**6, transcendentals=0),
        name="weights",
    )(weight_map, jnp.swapaxes(seam_mask, 1, 2), small, large)


def colours_of(frames):
    small, small_places = small_matrices()
    large, large_places = large_matrices()
    return pl.pallas_call(
        functools.partial(colours_kernel, small_places, large_places),
        out_shape=jax.ShapeDtypeStruct((COLOUR_ROWS, FW), F32),
        compiler_params=pltpu.CompilerParams(vmem_limit_bytes=VMEM),
        cost_estimate=pl.CostEstimate(flops=6 * 10**9, bytes_accessed=4 * 10**6, transcendentals=0),
        name="colours",
    )(frames, small, large)


def blend_kernel(cell, strips, colours, masked, first, second):
    views, mask_views = weight_views()
    (b0, b1, b2, b3, b4) = [[colours[view] for view in level] for level in colour_views()]
    (wp, w1, w2, w3, w4) = [masked[view] for view in views]
    (n0, n1, n2, n3, n4) = [masked[view] for view in mask_views]
    start = cell[0] * 16
    low = strips[192:288]

    def mixed(band, remote, share):
        return band + share * (remote - band)

    widths = (1024, 512, 256, 128, 128)
    share0 = mm(n0.astype(BF16), place(64, 1024, 0, 64, start))
    share = [share0]
    for k, ref in enumerate((n1, n2, n3, n4)):
        share.append(rdot(ref, place(64 >> (k + 1), widths[k + 1], 0, 64 >> (k + 1), start >> (k + 1))))
    top = strips[0:192]
    remote0 = [mm(top, place(128, 1024, 0, 64, start)), mm(top, place(128, 1024, 64, 64, start))]
    remote0 = jnp.concatenate(remote0, axis=0)
    weights = wp
    for c in range(COLOURS):
        p = weights * mixed(b0[c], remote0[c * 128 : (c + 1) * 128], share[0])
        out, row = (first, 0) if c == 0 else (second, 32 * (c - 1))

        def store(q, piece, out=out, row=row):
            out[q, row : row + 32, :] = piece.astype(BF16)

        fold_level0(p, store)
    remote1 = [mm(low, place(128, 512, 0, 32, start >> 1)), mm(low, place(128, 512, 32, 32, start >> 1))]
    remote1 = jnp.concatenate(remote1, axis=0)
    parts = [w1 * mixed(b1[c], remote1[c * 64 : (c + 1) * 64], share[1]) for c in range(COLOURS)] + [w1]
    for r in range(2):
        for j in range(4):
            turned = [parts[ch][r * 32 : r * 32 + 32, j * 128 : j * 128 + 128] for ch in range(4)]
            turned = [turned[0]] + [pltpu.roll(turned[ch], 32 * ch, 1) for ch in range(1, 4)]
            for cc in range(4):
                first[r * 16 + 4 * j + cc, 32:64, :] = gather_channels(turned, 32, cc, 0).astype(BF16)
    remote2 = mm(low, place(128, 256, 64, 16, start >> 2))
    remote3 = mm(low[0:48], place(128, 128, 80, 8, start >> 3))
    remote4 = mm(low[0:48], place(128, 128, 88, 4, start >> 4))
    parts2 = [w2 * mixed(b2[c], remote2[c * 32 : (c + 1) * 32], share[2]) for c in range(COLOURS)] + [w2]
    parts3 = [w3 * mixed(b3[c], remote3[c * 16 : (c + 1) * 16], share[3]) for c in range(COLOURS)] + [w3]
    parts4 = [w4 * mixed(b4[c], remote4[c * 16 : (c + 1) * 16], share[4]) for c in range(COLOURS)] + [w4]
    lane = lane_index()
    for r in range(2):
        turned3 = [pltpu.roll(parts3[ch][r * 8 : r * 8 + 8], 8 * ch, 1) for ch in range(4)]
        turned4 = [pltpu.roll(parts4[ch][r * 8 : r * 8 + 8], 4 * ch, 1) for ch in range(4)]
        for j in range(2):
            turned2 = [parts2[ch][r * 16 : r * 16 + 16, j * 128 : j * 128 + 128] for ch in range(4)]
            turned2 = [pltpu.roll(turned2[ch], 16 * ch, 1) for ch in range(4)]
            for cc in range(8):
                c = j * 8 + cc
                two = gather_channels(turned2, 16, cc, 0)
                three = gather_channels(turned3, 8, c, 64)
                four = gather_channels(turned4, 4, c, 96)
                head = jnp.where(lane < 64, two[0:8], jnp.where(lane < 96, three, four))
                tail = jnp.where(lane < 64, two[8:16], 0.0)
                first[r * 16 + c, 64:80, :] = jnp.concatenate([head, tail], axis=0).astype(BF16)


def blend(cell, strips, colours, masked):
    vmem = pl.BlockSpec(memory_space=pltpu.VMEM)
    return pl.pallas_call(
        blend_kernel,
        in_specs=[pl.BlockSpec(memory_space=pltpu.SMEM)] + [vmem] * 3,
        out_shape=[jax.ShapeDtypeStruct((QB, 80, 128), BF16), jax.ShapeDtypeStruct((QB, 64, 128), BF16)],
        compiler_params=pltpu.CompilerParams(vmem_limit_bytes=VMEM),
        cost_estimate=pl.CostEstimate(flops=10**6, bytes_accessed=10**4, transcendentals=0),
        name="blend",
    )(cell, strips, colours, masked)


def routes_kernel(spot, lists, counts):
    for source in range(4):

        def body(q, count, source=source):
            at = spot[source, q]
            lists[source, count] = q * ROUTE + at
            return jnp.where(at >= 0, count + 1, count)

        counts[source] = lax.fori_loop(0, QB, body, 0, unroll=True)


def routes_of(spot):
    smem = pl.BlockSpec(memory_space=pltpu.SMEM)
    return pl.pallas_call(
        routes_kernel,
        in_specs=[smem],
        out_specs=[smem, smem],
        out_shape=[jax.ShapeDtypeStruct((4, QB + 1), jnp.int32), jax.ShapeDtypeStruct((4,), jnp.int32)],
        name="routes",
    )(spot)


def gather_kernel(lists, counts, *refs):
    home, away, acc = refs[-3:]
    acc[...] = jnp.zeros_like(acc)
    for source in range(4):

        def body(i, carry, source=source):
            entry = lists[source, i]
            q, at = entry // ROUTE, entry % ROUTE
            lo = 0
            for ref in refs[source:-3:4]:
                hi = lo + ref.shape[1]
                acc[at, lo:hi, :] = acc[at, lo:hi, :] + ref[q].astype(F32)
                lo = hi
            return carry

        lax.fori_loop(0, counts[source], body, 0)
    tiles = home.shape[0]
    home[...] = acc[0:tiles]
    away[...] = acc[tiles : 2 * tiles].astype(BF16)


def gather_rows(routes, rows, tiles):
    height = sum(each.shape[1] for each in rows[::4])
    vmem = pl.BlockSpec(memory_space=pltpu.VMEM)
    shape = (tiles // 2, height, 128)
    return pl.pallas_call(
        gather_kernel,
        in_specs=[pl.BlockSpec(memory_space=pltpu.SMEM)] * 2 + [vmem] * len(rows),
        out_shape=[jax.ShapeDtypeStruct(shape, F32), jax.ShapeDtypeStruct(shape, BF16)],
        scratch_shapes=[pltpu.VMEM((tiles, height, 128), F32)],
        compiler_params=pltpu.CompilerParams(vmem_limit_bytes=VMEM),
        cost_estimate=pl.CostEstimate(flops=10**6, bytes_accessed=10**4, transcendentals=0),
        name="gather_rows",
    )(*routes, *rows)


def add_kernel(pairs, *refs):
    out = refs[2 * pairs :]
    lo = 0
    for home, got in zip(refs[:pairs], refs[pairs : 2 * pairs]):
        hi = lo + home.shape[1]
        for j, ref in enumerate(out):
            tiles = slice(j * TILE_DEV, (j + 1) * TILE_DEV)
            ref[:, lo:hi, :] = (home[tiles] + got[tiles].astype(F32)).astype(ref.dtype)
        lo = hi


def add_halves(homes, gots):
    shape = (TILE_DEV, sum(home.shape[1] for home in homes), 128)
    others = homes[0].shape[0] // TILE_DEV - 1
    return pl.pallas_call(
        functools.partial(add_kernel, len(homes)),
        out_shape=[jax.ShapeDtypeStruct(shape, F32)] + [jax.ShapeDtypeStruct(shape, BF16)] * others,
        compiler_params=pltpu.CompilerParams(vmem_limit_bytes=VMEM),
        cost_estimate=pl.CostEstimate(flops=10**6, bytes_accessed=10**4, transcendentals=0),
        name="add_halves",
    )(*homes, *gots)


def collapse_matrices():
    def across(src, dst, width):
        g = grow_matrix(width).T
        m = np.zeros((128, 128), np.float32)
        for ch in range(COLOURS):
            m[src + ch * width : src + (ch + 1) * width, dst + ch * 2 * width : dst + (ch + 1) * 2 * width] = g
        return m

    last = np.zeros((128, 384), np.float32)
    g = grow_matrix(32).T
    for ch in range(COLOURS):
        for half in range(2):
            last[ch * 32 : ch * 32 + 32, ch * 128 + half * 64 : ch * 128 + half * 64 + 64] = g

    def down(n, rows_in, rows_out, pick=None):
        g = grow_matrix(n)
        g = g if pick is None else g[pick::2]
        m = np.zeros((TILE_DEV * rows_out, TILE_DEV * rows_in), np.float32)
        for t in range(TILE_DEV):
            m[t * rows_out : t * rows_out + g.shape[0], t * rows_in : t * rows_in + n] = g
        return m

    mats = {"m43": across(96, 64, 4), "m32": across(64, 0, 8), "m21": across(0, 0, 16), "m10": last}
    mats |= {"d43": down(4, 16, 16), "d32": down(8, 16, 16), "d21": down(16, 16, 32)}
    mats |= {"even": down(32, 32, 32, 0), "odd": down(32, 32, 32, 1)}
    return pack(mats, 1280)


def collapse_kernel(places, each, packed, *refs):
    mats = unpack(packed, places)
    a, b, c = (refs[i * each : (i + 1) * each] for i in range(3))
    out, level0 = refs[3 * each :]

    def total(sources, lo, hi):
        acc = sources[0][:, lo:hi, :]
        for source in sources[1:]:
            acc = acc + source[:, lo:hi, :].astype(F32)
        return acc.reshape(TILE_DEV * (hi - lo), 128)

    lane = lane_index()
    small = total(b, 64, 80)
    bottom = small
    for lo, width, chans in ((0, 16, 3), (64, 8, 3), (96, 4, 3)):
        for ch in range(chans):
            inside = (lane >= lo + ch * width) & (lane < lo + (ch + 1) * width)
            bottom = jnp.where(inside, pltpu.roll(small, (128 - (3 - ch) * width) % 128, 1), bottom)
    small = small / jnp.maximum(bottom, 1.0)
    three = small + ldot(mats["d43"], rdot(small, mats["m43"]))
    two = small + ldot(mats["d32"], rdot(three, mats["m32"]))
    one = total(b, 32, 64)
    bottom = one
    for ch in range(3):
        inside = (lane >= ch * 32) & (lane < (ch + 1) * 32)
        bottom = jnp.where(inside, pltpu.roll(one, (128 - (3 - ch) * 32) % 128, 1), bottom)
    one = one / jnp.maximum(bottom, 1.0) + ldot(mats["d21"], rdot(two, mats["m21"]))
    wide = rdot(one, mats["m10"])
    hi, lo = split(wide)
    up = mm(mats["even"], hi) + mm(mats["even"], lo)
    down = mm(mats["odd"], hi) + mm(mats["odd"], lo)
    bottom = jnp.maximum(total(a, 0, 32), 1.0)
    for ch in range(COLOURS):
        own = total(b, 0, 32) if ch == 0 else total(c, 32 * (ch - 1), 32 * ch)
        back = jnp.where(lane < 64, up[:, ch * 128 : ch * 128 + 128], down[:, ch * 128 : ch * 128 + 128])
        level0[ch * 128 : ch * 128 + 128, :] = own / bottom + back
    for ch in range(COLOURS):
        for row in range(32):
            out[ch, :, row * 128 : row * 128 + 128] = level0[pl.ds(ch * 128 + row, TILE_DEV, stride=32), :]


def collapse(a, b, c):
    packed, places = collapse_matrices()
    tiles = pl.pallas_call(
        functools.partial(collapse_kernel, places, len(a)),
        out_shape=jax.ShapeDtypeStruct((COLOURS, TILE_DEV, 4096), F32),
        scratch_shapes=[pltpu.VMEM((COLOURS * 128, 128), F32)],
        compiler_params=pltpu.CompilerParams(vmem_limit_bytes=VMEM),
        cost_estimate=pl.CostEstimate(flops=10**6, bytes_accessed=10**4, transcendentals=0),
        name="collapse",
    )(packed, *a, *b, *c)
    return jnp.swapaxes(tiles, 0, 1)


def swap(value, axis, bit):
    size = lax.axis_size(axis)
    return lax.ppermute(value, axis, [(i, i ^ bit) for i in range(size)])


def local(frames, weight_map, seam_mask, strip_cell, partner, tile_group, tile_position_in_group):
    groups = lax.axis_size("frames")
    parts = lax.axis_size("tiles")
    mine = lax.axis_index("tiles")
    mask = lax.bitwise_xor(partner[0] // parts, lax.axis_index("frames"))

    tie = lax.optimization_barrier
    strips = strips_of(frames, strip_cell)
    ids = tile_group.reshape(QB) * (parts * TILE_DEV) + tile_position_in_group.reshape(QB)
    strips, weight_map, ids = tie((strips, weight_map, ids))
    ids = jnp.stack([ids, swap(ids, "tiles", 1)])
    ids_x = jnp.concatenate([ids, swap(ids, "tiles", 2)])
    ids_y = jnp.concatenate([ids, swap(ids, "frames", 1)])

    def relative(ids):
        group, tile = ids // (parts * TILE_DEV), ids % (parts * TILE_DEV)
        group = lax.bitwise_xor(group, lax.axis_index("frames"))
        return group, lax.bitwise_xor(tile // TILE_DEV, mine), tile % TILE_DEV

    half = groups // 2
    group, part, tile = relative(ids_x)
    spot_x = jnp.where(part == 0, ((group & 1) * half + (group >> 1)) * TILE_DEV + tile, -1)
    group, part, tile = relative(ids_y)
    here = ((group & 1) == 0) & ((part & 1) == 0)
    spot_y = jnp.where(here, ((part >> 1) * half + (group >> 1)) * TILE_DEV + tile, -1)

    weights, masked = weights_of(weight_map, seam_mask)
    bit = 1
    while bit < groups:
        got = swap(strips, "frames", bit)
        if bit == 1:
            got, weights, masked = tie((got, weights, masked))
            far, near = swap(weights, "tiles", 2), swap(weights, "tiles", 1)
        if bit == half // 2:
            got, frames = tie((got, frames))
        if bit == half:
            colours = colours_of(frames)
            got, far, near, spot_x, spot_y, colours = tie((got, far, near, spot_x, spot_y, colours))
        strips = jnp.where((mask & bit) != 0, got, strips)
        bit *= 2

    def gather(routes, *rows):
        return gather_rows(routes, rows, groups * TILE_DEV)

    def along(own, *away):
        return [own] + [swap(part, "frames", 2 * (j + 1)) for j, part in enumerate(away)]

    first, second = blend(strip_cell, strips, colours, masked)
    first, second, spot_x, spot_y, far = tie((first, second, spot_x, spot_y, far))
    far_first, near_first = swap(first, "tiles", 2), swap(first, "tiles", 1)
    far_second, near_second = swap(second, "frames", 1), swap(second, "tiles", 1)
    routes_x, routes_y = routes_of(spot_x), routes_of(spot_y)
    home_w, away_w = gather(routes_x, weights, near, far, swap(far, "tiles", 1))
    got_w = swap(away_w, "frames", 1)
    far_second, home_w, routes_y = tie((far_second, home_w, routes_y))
    home_s, away_s = gather(routes_y, second, near_second, far_second, swap(far_second, "tiles", 1))
    got_s = swap(away_s, "tiles", 2)
    far_first, home_s, got_w = tie((far_first, home_s, got_w))
    far_near = swap(far_first, "tiles", 1)
    home_f, away_f = gather(routes_x, first, near_first, far_first, far_near)
    got_f = swap(away_f, "frames", 1)
    home_w, home_f = tie((home_w, home_f))
    got_weights = along(*add_halves((home_w,), (got_w,)))
    got_s, got_weights = tie((got_s, got_weights))
    got_second = along(*add_halves((home_s,), (got_s,)))
    got_f, got_second[1], got_second[2] = tie((got_f, got_second[1], got_second[2]))
    got_first = along(*add_halves((home_f,), (got_f,)))
    return collapse(got_weights, got_first, got_second)


def solution(mesh):
    in_specs = (
        P(("frames", "tiles"), None, None, None),
        P(("frames", "tiles"), None, None),
        P(("frames", "tiles"), None, None),
        P(("frames", "tiles")),
        P(("frames", "tiles")),
        P(("frames", "tiles"), None, None),
        P(("frames", "tiles"), None),
    )
    out_specs = P(("frames", "tiles"), None, None)
    return jax.shard_map(local, mesh=mesh, in_specs=in_specs, out_specs=out_specs, check_vma=False)
```

```python
import functools

import jax
import jax.numpy as jnp
import numpy as np
from jax import lax
from jax.experimental import pallas as pl
from jax.experimental.pallas import tpu as pltpu
from jax.sharding import PartitionSpec as P

COLOURS = 3
FH = 128
FW = 1024
QB = 32
WIN = 256
TILE_DEV = 4
VMEM = 20 << 20
ROUTE = 4096
F32 = jnp.float32
BF16 = jnp.bfloat16


def shrink_matrix(n):
    m = np.zeros((n // 2, n), np.float32)
    for i in range(n // 2):
        for d, tap in zip(range(-2, 3), (1, 4, 6, 4, 1)):
            m[i, min(max(2 * i + d, 0), n - 1)] += tap / 16.0
    return m


def grow_matrix(n):
    m = np.zeros((2 * n, n), np.float32)
    for i in range(n):
        lo, hi = max(i - 1, 0), min(i + 1, n - 1)
        m[2 * i, lo] += 1 / 8
        m[2 * i, i] += 6 / 8
        m[2 * i, hi] += 1 / 8
        m[2 * i + 1, i] += 1 / 2
        m[2 * i + 1, hi] += 1 / 2
    return m


def padded(m, rows, cols):
    return np.pad(m, ((0, rows - m.shape[0]), (0, cols - m.shape[1])))


def row_order():
    m = np.zeros((FH, FH), np.float32)
    for r in range(2):
        for par in range(2):
            for i in range(32):
                m[r * 64 + par * 32 + i, r * 64 + 2 * i + par] = 1
    return m


def vertical():
    v = {1: shrink_matrix(128), 2: shrink_matrix(64), 3: shrink_matrix(32)}
    spread = np.zeros((16, 8), np.float32)
    for r in range(2):
        for i in range(4):
            spread[r * 8 + i, r * 4 + i] = 1
    v[4] = spread @ shrink_matrix(16)
    g = {0: row_order() @ grow_matrix(64), 1: grow_matrix(32), 2: grow_matrix(16)}
    g[3] = grow_matrix(8) @ spread.T
    return v, g


def horizontal(width):
    s = {k: shrink_matrix(width >> (k - 1)).T for k in range(1, 5)}
    g = {k: grow_matrix(width >> (k + 1)).T for k in range(4)}
    return s, g


def shrink_window():
    m = np.zeros((512, 128), np.float32)
    for i in range(128):
        for d, tap in zip(range(-2, 3), (1, 4, 6, 4, 1)):
            m[128 + 2 * i + d, i] = tap / 16.0
    return m


def grow_window():
    m = np.zeros((384, 256), np.float32)
    for i in range(128):
        for d, tap in zip(range(-1, 2), (1, 6, 1)):
            m[128 + i + d, 2 * i] = tap / 8.0
        m[128 + i, 2 * i + 1] = m[128 + i + 1, 2 * i + 1] = 0.5
    return m


def pack(mats, width):
    places, row, col, height = {}, 0, 0, 0
    for name in sorted(mats, key=lambda n: (-mats[n].shape[0], -mats[n].shape[1], n)):
        h, w = mats[name].shape
        wide = -(-w // 128) * 128
        if col + wide > width:
            row, col, height = row + height, 0, 0
        height = max(height, -(-h // 16) * 16)
        places[name] = (row, col, h, w)
        col += wide
    out = np.zeros((row + height, width), np.float32)
    for name, (r, c, h, w) in places.items():
        out[r : r + h, c : c + w] = mats[name]
    return jnp.asarray(out, BF16), places


def unpack(ref, places):
    return {name: ref[r : r + h, c : c + w] for name, (r, c, h, w) in places.items()}


def small_matrices():
    v, g = vertical()
    s, gh = horizontal(WIN)
    sm, _ = horizontal(64)
    mats = {f"v{k}": m for k, m in v.items()} | {f"g{k}": m for k, m in g.items()}
    mats |= {f"s{k}": m for k, m in s.items()} | {f"h{k}": m for k, m in gh.items()}
    mats |= {f"m{k}": m for k, m in sm.items()} | {"order": row_order()}
    return pack(mats, 512)


def large_matrices():
    mats = {"shrink": shrink_window(), "grow": grow_window()}
    mats["last"] = padded(shrink_matrix(128).T, 128, 128)
    mats["least"] = padded(grow_matrix(64).T, 128, 128)
    return pack(mats, 640)


def levels_of(mats, letter):
    return {int(n[1:]): m for n, m in mats.items() if n[0] == letter and n[1:].isdigit()}


def mm(a, b):
    return jnp.dot(a, b, preferred_element_type=F32)


def split(v):
    hi = v.astype(BF16)
    return hi, (v - hi.astype(F32)).astype(BF16)


def rdot(v, m):
    hi, lo = split(v)
    return mm(hi, m) + mm(lo, m)


def ldot(m, v):
    hi, lo = split(v)
    return mm(m, hi) + mm(m, lo)


def mmt(a, b):
    return lax.dot_general(a, b, (((1,), (1,)), ((), ())), preferred_element_type=F32)


def windows(v, m, step):
    rows, width = v.shape
    both = jnp.concatenate(split(v), axis=0)
    left = jnp.broadcast_to(both[:, :1], (2 * rows, 128))
    right = jnp.broadcast_to(both[:, width - 1 :], (2 * rows, 128))
    both = jnp.concatenate([left, both, right], axis=1)
    pieces = []
    for n in range(width // step):
        piece = mm(both[:, n * step : n * step + step + 256], m)
        pieces.append(piece[:rows] + piece[rows:])
    return jnp.concatenate(pieces, axis=1)


def right_of(m):
    return lambda v: rdot(v, m)


def pyramid(planes, v, shrinks, product=mm):
    n = len(planes)
    t = jnp.concatenate([product(v[1], p) for p in planes], axis=0)
    levels = {1: shrinks[1](t)}
    for k in range(2, 5):
        prev = levels[k - 1]
        rows = prev.shape[0] // n
        t = jnp.concatenate([ldot(v[k], prev[i * rows : (i + 1) * rows]) for i in range(n)], axis=0)
        levels[k] = shrinks[k](t)
    return levels


def grown(level, n, gv, grow):
    h = grow(level)
    rows = level.shape[0] // n
    return [ldot(gv, h[i * rows : (i + 1) * rows]) for i in range(n)]


def place(rows, cols, base, width, offset):
    i = lax.broadcasted_iota(jnp.int32, (rows, cols), 0)
    c = lax.broadcasted_iota(jnp.int32, (rows, cols), 1)
    hit = (i >= base) & (i < base + width) & (c - i == offset - base)
    return jnp.where(hit, 1.0, 0.0).astype(BF16)


def strips_kernel(places, cell, xa, xb, packed, out, acc):
    mats = unpack(packed, places)
    v, gv, s, gh = (levels_of(mats, letter) for letter in "vgsh")
    s, gh = ({k: right_of(m) for k, m in each.items()} for each in (s, gh))
    order = mats["order"]
    first = window_tile(cell[0]) * 128
    planes = [jnp.concatenate([xa[0, c], xb[0, c]], axis=1) for c in range(COLOURS)]
    levels = pyramid(planes, v, s)
    back = grown(levels[1], COLOURS, gv[0], gh[0])
    b0 = jnp.concatenate([mm(order, planes[c]) - back[c] for c in range(COLOURS)], axis=0)
    bands = [b0.astype(BF16)]
    for k in range(1, 4):
        back = grown(levels[k + 1], COLOURS, gv[k], gh[k])
        bands.append((levels[k] - jnp.concatenate(back, axis=0)).astype(BF16))
    bands.append(levels[4].astype(BF16))
    start = cell[0] * 16 - first

    def pick(band, base, k):
        i = lax.broadcasted_iota(jnp.int32, (band.shape[1], 128), 0)
        c = lax.broadcasted_iota(jnp.int32, (band.shape[1], 128), 1)
        hit = (c >= base) & (c < base + (64 >> k)) & (i - c == (start >> k) - base)
        return mm(band, jnp.where(hit, 1.0, 0.0).astype(BF16))

    out[0:192, :] = (pick(bands[0][0:192], 0, 0) + pick(bands[0][192:384], 64, 0)).astype(BF16)
    acc[...] = pick(bands[1][0:96], 0, 1) + pick(bands[1][96:192], 32, 1) + pick(bands[2], 64, 2)
    acc[0:48, :] = acc[0:48, :] + pick(bands[3], 80, 3) + pick(bands[4], 88, 4)
    out[192:288, :] = acc[...].astype(BF16)


def window_tile(cell):
    return jnp.clip((cell - 3) >> 3, 0, (FW - WIN) // 128)


def full_spec(a):
    return pl.BlockSpec(a.shape, lambda *_: (0,) * a.ndim)


def strips_of(frames, cell):
    packed, places = small_matrices()
    grid_spec = pltpu.PrefetchScalarGridSpec(
        num_scalar_prefetch=1,
        grid=(1,),
        in_specs=[
            pl.BlockSpec((1, COLOURS, FH, 128), lambda i, c: (0, 0, 0, window_tile(c[0]))),
            pl.BlockSpec((1, COLOURS, FH, 128), lambda i, c: (0, 0, 0, window_tile(c[0]) + 1)),
        ]
        + [full_spec(packed)],
        out_specs=pl.BlockSpec((288, 128), lambda i, c: (0, 0)),
        scratch_shapes=[pltpu.VMEM((96, 128), F32)],
    )
    return pl.pallas_call(
        functools.partial(strips_kernel, places),
        grid_spec=grid_spec,
        out_shape=jax.ShapeDtypeStruct((288, 128), BF16),
        compiler_params=pltpu.CompilerParams(vmem_limit_bytes=VMEM),
        cost_estimate=pl.CostEstimate(flops=2 * 10**9, bytes_accessed=10**6, transcendentals=0),
        name="strips",
    )(cell, frames, frames, packed)


def lane_index():
    return lax.broadcasted_iota(jnp.int32, (1, 128), 1)


def fold_level0(p, store):
    left = lane_index() < 64
    for r in range(2):
        for j in range(8):
            even = p[r * 64 : r * 64 + 32, j * 128 : j * 128 + 128]
            odd = p[r * 64 + 32 : r * 64 + 64, j * 128 : j * 128 + 128]
            store(r * 16 + 2 * j, jnp.where(left, even, pltpu.roll(odd, 64, 1)))
            store(r * 16 + 2 * j + 1, jnp.where(left, pltpu.roll(even, 64, 1), odd))


def gather_channels(parts, width, cc, base):
    groups = 128 // width
    group = lane_index() // width
    out = jnp.zeros_like(parts[0])
    for ch in range(4):
        out = jnp.where(group == (cc + ch) % groups, parts[ch], out)
    return pltpu.roll(out, (base - cc * width) % 128, 1)


COLOUR_ROWS = 560
WEIGHT_ROWS = 320


def at(r, h, c, w):
    return slice(r, r + h), slice(c, c + w)


def colour_views():
    levels = [[at(128 * c, 128, 0, 1024) for c in range(3)]]
    levels.append([at(384, 64, 0, 512), at(384, 64, 512, 512), at(448, 64, 0, 512)])
    levels.append([at(512, 32, 256 * c, 256) for c in range(3)])
    levels.append([at(544, 16, 128 * c, 128) for c in range(3)])
    levels.append([at(544, 16, 512 + 128 * c, 128) for c in range(3)])
    return levels


def weight_views():
    levels = [at(0, 128, 0, 1024), at(128, 64, 0, 512), at(128, 32, 512, 256), at(128, 16, 768, 128), at(128, 16, 896, 128)]
    masks = [at(192, 128 >> k, 128 * k, 64 >> k) for k in range(4)] + [at(192, 16, 512, 4)]
    return levels, masks


def filters(small_places, large_places, small, large):
    mats = unpack(small, small_places)
    v, gv, sm = (levels_of(mats, letter) for letter in "vgm")
    order = mats["order"]
    sm = {k: right_of(each) for k, each in sm.items()}
    mats = unpack(large, large_places)
    half = lambda each: windows(each, mats["shrink"], 256)
    twice = lambda each: windows(each, mats["grow"], 128)
    s = {1: half, 2: half, 3: half, 4: right_of(mats["last"])}
    gh = {0: twice, 1: twice, 2: twice, 3: right_of(mats["least"])}
    return v, gv, sm, s, gh, order


def weights_kernel(small_places, large_places, w, m, small, large, wblocks, state):
    v, _, sm, s, _, order = filters(small_places, large_places, small, large)
    views, mask_views = weight_views()
    weights = mm(order, w[0])
    state[views[0]] = weights

    def store(q, piece):
        wblocks[q] = piece.astype(BF16)

    fold_level0(weights, store)
    levels = pyramid([w[0]], v, s)
    for k in range(1, 5):
        state[views[k]] = levels[k]
    other = (1.0 - m[0].astype(F32)).astype(BF16)
    state[mask_views[0]] = mmt(order, other)
    masks = pyramid([other], v, sm, mmt)
    for k in range(1, 5):
        state[mask_views[k]] = masks[k]


def colours_kernel(small_places, large_places, x, small, large, state):
    v, gv, _, s, gh, order = filters(small_places, large_places, small, large)
    views = colour_views()
    planes = [x[0, c] for c in range(COLOURS)]
    levels = pyramid(planes, v, s)
    back = grown(levels[1], COLOURS, gv[0], gh[0])
    for c in range(COLOURS):
        state[views[0][c]] = mm(order, planes[c]) - back[c]
    for k in range(1, 4):
        rows = levels[k].shape[0] // COLOURS
        back = grown(levels[k + 1], COLOURS, gv[k], gh[k])
        for c in range(COLOURS):
            state[views[k][c]] = levels[k][c * rows : (c + 1) * rows] - back[c]
    for c in range(COLOURS):
        state[views[4][c]] = levels[4][c * 16 : (c + 1) * 16]


def weights_of(weight_map, seam_mask):
    small, small_places = small_matrices()
    large, large_places = large_matrices()
    return pl.pallas_call(
        functools.partial(weights_kernel, small_places, large_places),
        out_shape=[jax.ShapeDtypeStruct((QB, 32, 128), BF16), jax.ShapeDtypeStruct((WEIGHT_ROWS, FW), F32)],
        compiler_params=pltpu.CompilerParams(vmem_limit_bytes=VMEM),
        cost_estimate=pl.CostEstimate(flops=4 * 10**9, bytes_accessed=2 * 10**6, transcendentals=0),
        name="weights",
    )(weight_map, jnp.swapaxes(seam_mask, 1, 2), small, large)


def colours_of(frames):
    small, small_places = small_matrices()
    large, large_places = large_matrices()
    return pl.pallas_call(
        functools.partial(colours_kernel, small_places, large_places),
        out_shape=jax.ShapeDtypeStruct((COLOUR_ROWS, FW), F32),
        compiler_params=pltpu.CompilerParams(vmem_limit_bytes=VMEM),
        cost_estimate=pl.CostEstimate(flops=6 * 10**9, bytes_accessed=4 * 10**6, transcendentals=0),
        name="colours",
    )(frames, small, large)


def blend_kernel(cell, strips, colours, masked, first, second):
    views, mask_views = weight_views()
    (b0, b1, b2, b3, b4) = [[colours[view] for view in level] for level in colour_views()]
    (wp, w1, w2, w3, w4) = [masked[view] for view in views]
    (n0, n1, n2, n3, n4) = [masked[view] for view in mask_views]
    start = cell[0] * 16
    low = strips[192:288]

    def mixed(band, remote, share):
        return band + share * (remote - band)

    widths = (1024, 512, 256, 128, 128)
    share0 = mm(n0.astype(BF16), place(64, 1024, 0, 64, start))
    share = [share0]
    for k, ref in enumerate((n1, n2, n3, n4)):
        share.append(rdot(ref, place(64 >> (k + 1), widths[k + 1], 0, 64 >> (k + 1), start >> (k + 1))))
    top = strips[0:192]
    remote0 = [mm(top, place(128, 1024, 0, 64, start)), mm(top, place(128, 1024, 64, 64, start))]
    remote0 = jnp.concatenate(remote0, axis=0)
    weights = wp
    for c in range(COLOURS):
        p = weights * mixed(b0[c], remote0[c * 128 : (c + 1) * 128], share[0])
        out, row = (first, 0) if c == 0 else (second, 32 * (c - 1))

        def store(q, piece, out=out, row=row):
            out[q, row : row + 32, :] = piece.astype(BF16)

        fold_level0(p, store)
    remote1 = [mm(low, place(128, 512, 0, 32, start >> 1)), mm(low, place(128, 512, 32, 32, start >> 1))]
    remote1 = jnp.concatenate(remote1, axis=0)
    parts = [w1 * mixed(b1[c], remote1[c * 64 : (c + 1) * 64], share[1]) for c in range(COLOURS)] + [w1]
    for r in range(2):
        for j in range(4):
            turned = [parts[ch][r * 32 : r * 32 + 32, j * 128 : j * 128 + 128] for ch in range(4)]
            turned = [turned[0]] + [pltpu.roll(turned[ch], 32 * ch, 1) for ch in range(1, 4)]
            for cc in range(4):
                first[r * 16 + 4 * j + cc, 32:64, :] = gather_channels(turned, 32, cc, 0).astype(BF16)
    remote2 = mm(low, place(128, 256, 64, 16, start >> 2))
    remote3 = mm(low[0:48], place(128, 128, 80, 8, start >> 3))
    remote4 = mm(low[0:48], place(128, 128, 88, 4, start >> 4))
    parts2 = [w2 * mixed(b2[c], remote2[c * 32 : (c + 1) * 32], share[2]) for c in range(COLOURS)] + [w2]
    parts3 = [w3 * mixed(b3[c], remote3[c * 16 : (c + 1) * 16], share[3]) for c in range(COLOURS)] + [w3]
    parts4 = [w4 * mixed(b4[c], remote4[c * 16 : (c + 1) * 16], share[4]) for c in range(COLOURS)] + [w4]
    lane = lane_index()
    for r in range(2):
        turned3 = [pltpu.roll(parts3[ch][r * 8 : r * 8 + 8], 8 * ch, 1) for ch in range(4)]
        turned4 = [pltpu.roll(parts4[ch][r * 8 : r * 8 + 8], 4 * ch, 1) for ch in range(4)]
        for j in range(2):
            turned2 = [parts2[ch][r * 16 : r * 16 + 16, j * 128 : j * 128 + 128] for ch in range(4)]
            turned2 = [pltpu.roll(turned2[ch], 16 * ch, 1) for ch in range(4)]
            for cc in range(8):
                c = j * 8 + cc
                two = gather_channels(turned2, 16, cc, 0)
                three = gather_channels(turned3, 8, c, 64)
                four = gather_channels(turned4, 4, c, 96)
                head = jnp.where(lane < 64, two[0:8], jnp.where(lane < 96, three, four))
                tail = jnp.where(lane < 64, two[8:16], 0.0)
                first[r * 16 + c, 64:80, :] = jnp.concatenate([head, tail], axis=0).astype(BF16)


def blend(cell, strips, colours, masked):
    vmem = pl.BlockSpec(memory_space=pltpu.VMEM)
    return pl.pallas_call(
        blend_kernel,
        in_specs=[pl.BlockSpec(memory_space=pltpu.SMEM)] + [vmem] * 3,
        out_shape=[jax.ShapeDtypeStruct((QB, 80, 128), BF16), jax.ShapeDtypeStruct((QB, 64, 128), BF16)],
        compiler_params=pltpu.CompilerParams(vmem_limit_bytes=VMEM),
        cost_estimate=pl.CostEstimate(flops=10**6, bytes_accessed=10**4, transcendentals=0),
        name="blend",
    )(cell, strips, colours, masked)


def routes_kernel(spot, lists, counts):
    for source in range(4):

        def body(q, count, source=source):
            at = spot[source, q]
            lists[source, count] = q * ROUTE + at
            return jnp.where(at >= 0, count + 1, count)

        counts[source] = lax.fori_loop(0, QB, body, 0, unroll=True)


def routes_of(spot):
    smem = pl.BlockSpec(memory_space=pltpu.SMEM)
    return pl.pallas_call(
        routes_kernel,
        in_specs=[smem],
        out_specs=[smem, smem],
        out_shape=[jax.ShapeDtypeStruct((4, QB + 1), jnp.int32), jax.ShapeDtypeStruct((4,), jnp.int32)],
        name="routes",
    )(spot)


def gather_kernel(lists, counts, *refs):
    home, away, acc = refs[-3:]
    acc[...] = jnp.zeros_like(acc)
    for source in range(4):

        def body(i, carry, source=source):
            entry = lists[source, i]
            q, at = entry // ROUTE, entry % ROUTE
            lo = 0
            for ref in refs[source:-3:4]:
                hi = lo + ref.shape[1]
                acc[at, lo:hi, :] = acc[at, lo:hi, :] + ref[q].astype(F32)
                lo = hi
            return carry

        lax.fori_loop(0, counts[source], body, 0)
    tiles = home.shape[0]
    home[...] = acc[0:tiles]
    away[...] = acc[tiles : 2 * tiles].astype(BF16)


def gather_rows(routes, rows, tiles):
    height = sum(each.shape[1] for each in rows[::4])
    vmem = pl.BlockSpec(memory_space=pltpu.VMEM)
    shape = (tiles // 2, height, 128)
    return pl.pallas_call(
        gather_kernel,
        in_specs=[pl.BlockSpec(memory_space=pltpu.SMEM)] * 2 + [vmem] * len(rows),
        out_shape=[jax.ShapeDtypeStruct(shape, F32), jax.ShapeDtypeStruct(shape, BF16)],
        scratch_shapes=[pltpu.VMEM((tiles, height, 128), F32)],
        compiler_params=pltpu.CompilerParams(vmem_limit_bytes=VMEM),
        cost_estimate=pl.CostEstimate(flops=10**6, bytes_accessed=10**4, transcendentals=0),
        name="gather_rows",
    )(*routes, *rows)


def add_kernel(pairs, *refs):
    out = refs[2 * pairs :]
    lo = 0
    for home, got in zip(refs[:pairs], refs[pairs : 2 * pairs]):
        hi = lo + home.shape[1]
        for j, ref in enumerate(out):
            tiles = slice(j * TILE_DEV, (j + 1) * TILE_DEV)
            ref[:, lo:hi, :] = (home[tiles] + got[tiles].astype(F32)).astype(ref.dtype)
        lo = hi


def add_halves(homes, gots):
    shape = (TILE_DEV, sum(home.shape[1] for home in homes), 128)
    others = homes[0].shape[0] // TILE_DEV - 1
    return pl.pallas_call(
        functools.partial(add_kernel, len(homes)),
        out_shape=[jax.ShapeDtypeStruct(shape, F32)] + [jax.ShapeDtypeStruct(shape, BF16)] * others,
        compiler_params=pltpu.CompilerParams(vmem_limit_bytes=VMEM),
        cost_estimate=pl.CostEstimate(flops=10**6, bytes_accessed=10**4, transcendentals=0),
        name="add_halves",
    )(*homes, *gots)


def collapse_matrices():
    def across(src, dst, width):
        g = grow_matrix(width).T
        m = np.zeros((128, 128), np.float32)
        for ch in range(COLOURS):
            m[src + ch * width : src + (ch + 1) * width, dst + ch * 2 * width : dst + (ch + 1) * 2 * width] = g
        return m

    last = np.zeros((128, 384), np.float32)
    g = grow_matrix(32).T
    for ch in range(COLOURS):
        for half in range(2):
            last[ch * 32 : ch * 32 + 32, ch * 128 + half * 64 : ch * 128 + half * 64 + 64] = g

    def down(n, rows_in, rows_out, pick=None):
        g = grow_matrix(n)
        g = g if pick is None else g[pick::2]
        m = np.zeros((TILE_DEV * rows_out, TILE_DEV * rows_in), np.float32)
        for t in range(TILE_DEV):
            m[t * rows_out : t * rows_out + g.shape[0], t * rows_in : t * rows_in + n] = g
        return m

    mats = {"m43": across(96, 64, 4), "m32": across(64, 0, 8), "m21": across(0, 0, 16), "m10": last}
    mats |= {"d43": down(4, 16, 16), "d32": down(8, 16, 16), "d21": down(16, 16, 32)}
    mats |= {"even": down(32, 32, 32, 0), "odd": down(32, 32, 32, 1)}
    return pack(mats, 1280)


def collapse_kernel(places, each, packed, *refs):
    mats = unpack(packed, places)
    b, c = (refs[i * each : (i + 1) * each] for i in range(2))
    out, level0 = refs[2 * each :]

    def total(sources, lo, hi):
        acc = sources[0][:, lo:hi, :]
        for source in sources[1:]:
            acc = acc + source[:, lo:hi, :].astype(F32)
        return acc.reshape(TILE_DEV * (hi - lo), 128)

    lane = lane_index()
    small = total(b, 64, 80)
    bottom = small
    for lo, width, chans in ((0, 16, 3), (64, 8, 3), (96, 4, 3)):
        for ch in range(chans):
            inside = (lane >= lo + ch * width) & (lane < lo + (ch + 1) * width)
            bottom = jnp.where(inside, pltpu.roll(small, (128 - (3 - ch) * width) % 128, 1), bottom)
    small = small / jnp.maximum(bottom, 1.0)
    three = small + ldot(mats["d43"], rdot(small, mats["m43"]))
    two = small + ldot(mats["d32"], rdot(three, mats["m32"]))
    one = total(b, 32, 64)
    bottom = one
    for ch in range(3):
        inside = (lane >= ch * 32) & (lane < (ch + 1) * 32)
        bottom = jnp.where(inside, pltpu.roll(one, (128 - (3 - ch) * 32) % 128, 1), bottom)
    one = one / jnp.maximum(bottom, 1.0) + ldot(mats["d21"], rdot(two, mats["m21"]))
    wide = rdot(one, mats["m10"])
    hi, lo = split(wide)
    up = mm(mats["even"], hi) + mm(mats["even"], lo)
    down = mm(mats["odd"], hi) + mm(mats["odd"], lo)
    bottom = jnp.maximum(total(c, 64, 96), 1.0)
    for ch in range(COLOURS):
        own = total(b, 0, 32) if ch == 0 else total(c, 32 * (ch - 1), 32 * ch)
        back = jnp.where(lane < 64, up[:, ch * 128 : ch * 128 + 128], down[:, ch * 128 : ch * 128 + 128])
        level0[ch * 128 : ch * 128 + 128, :] = own / bottom + back
    for ch in range(COLOURS):
        for row in range(32):
            out[ch, :, row * 128 : row * 128 + 128] = level0[pl.ds(ch * 128 + row, TILE_DEV, stride=32), :]


def collapse(b, c):
    packed, places = collapse_matrices()
    tiles = pl.pallas_call(
        functools.partial(collapse_kernel, places, len(b)),
        out_shape=jax.ShapeDtypeStruct((COLOURS, TILE_DEV, 4096), F32),
        scratch_shapes=[pltpu.VMEM((COLOURS * 128, 128), F32)],
        compiler_params=pltpu.CompilerParams(vmem_limit_bytes=VMEM),
        cost_estimate=pl.CostEstimate(flops=10**6, bytes_accessed=10**4, transcendentals=0),
        name="collapse",
    )(packed, *b, *c)
    return jnp.swapaxes(tiles, 0, 1)


def swap(value, axis, bit):
    size = lax.axis_size(axis)
    return lax.ppermute(value, axis, [(i, i ^ bit) for i in range(size)])


def local(frames, weight_map, seam_mask, strip_cell, partner, tile_group, tile_position_in_group):
    groups = lax.axis_size("frames")
    parts = lax.axis_size("tiles")
    mine = lax.axis_index("tiles")
    mask = lax.bitwise_xor(partner[0] // parts, lax.axis_index("frames"))

    tie = lax.optimization_barrier
    strips = strips_of(frames, strip_cell)
    ids = tile_group.reshape(QB) * (parts * TILE_DEV) + tile_position_in_group.reshape(QB)
    strips, weight_map, ids = tie((strips, weight_map, ids))
    ids = jnp.stack([ids, swap(ids, "tiles", 1)])
    ids_x = jnp.concatenate([ids, swap(ids, "tiles", 2)])
    ids_y = jnp.concatenate([ids, swap(ids, "frames", 1)])

    def relative(ids):
        group, tile = ids // (parts * TILE_DEV), ids % (parts * TILE_DEV)
        group = lax.bitwise_xor(group, lax.axis_index("frames"))
        return group, lax.bitwise_xor(tile // TILE_DEV, mine), tile % TILE_DEV

    half = groups // 2
    weights, masked = weights_of(weight_map, seam_mask)
    bit = 1
    while bit < groups:
        got = swap(strips, "frames", bit)
        if bit == 1:
            got, weights, masked = tie((got, weights, masked))
            far, near = swap(weights, "tiles", 2), swap(weights, "tiles", 1)
        if bit == half // 2:
            got, frames = tie((got, frames))
        if bit == half:
            colours = colours_of(frames)
            got, far, near, ids_x, ids_y, colours = tie((got, far, near, ids_x, ids_y, colours))
        strips = jnp.where((mask & bit) != 0, got, strips)
        bit *= 2

    def gather(routes, *rows):
        return gather_rows(routes, rows, groups * TILE_DEV)

    def along(own, *away):
        return [own] + [swap(part, "frames", 2 * (j + 1)) for j, part in enumerate(away)]

    first, second = blend(strip_cell, strips, colours, masked)
    first, second, ids_x, ids_y, far = tie((first, second, ids_x, ids_y, far))
    group, part, tile = relative(ids_x)
    spot_x = jnp.where(part == 0, ((group & 1) * half + (group >> 1)) * TILE_DEV + tile, -1)
    group, part, tile = relative(ids_y)
    here = ((group & 1) == 0) & ((part & 1) == 0)
    spot_y = jnp.where(here, ((part >> 1) * half + (group >> 1)) * TILE_DEV + tile, -1)
    far_first, near_first = swap(first, "tiles", 2), swap(first, "tiles", 1)
    far_second, near_second = swap(second, "frames", 1), swap(second, "tiles", 1)
    routes_x, routes_y = routes_of(spot_x), routes_of(spot_y)
    home_w, away_w = gather(routes_x, weights, near, far, swap(far, "tiles", 1))
    got_w = swap(away_w, "frames", 1)
    far_second, home_w, routes_y = tie((far_second, home_w, routes_y))
    home_s, away_s = gather(routes_y, second, near_second, far_second, swap(far_second, "tiles", 1))
    got_s = swap(away_s, "tiles", 2)
    far_first, home_s, got_w = tie((far_first, home_s, got_w))
    far_near = swap(far_first, "tiles", 1)
    home_f, away_f = gather(routes_x, first, near_first, far_first, far_near)
    got_f = swap(away_f, "frames", 1)
    got_second = along(*add_halves((home_s, home_w), (got_s, got_w)))
    got_f, got_second[1] = tie((got_f, got_second[1]))
    got_first = along(*add_halves((home_f,), (got_f,)))
    return collapse(got_first, got_second)


def solution(mesh):
    in_specs = (
        P(("frames", "tiles"), None, None, None),
        P(("frames", "tiles"), None, None),
        P(("frames", "tiles"), None, None),
        P(("frames", "tiles")),
        P(("frames", "tiles")),
        P(("frames", "tiles"), None, None),
        P(("frames", "tiles"), None),
    )
    out_specs = P(("frames", "tiles"), None, None)
    return jax.shard_map(local, mesh=mesh, in_specs=in_specs, out_specs=out_specs, check_vma=False)
```
